32 devices in a mesh: seq: 16 (over z, y, x), head: 2 (over core).
Axes of the slice: x: 2, y: 2, z: 4, core: 2. Of those that a mesh axis runs over, the one named last changes fastest.
Arguments:
- tokens: bfloat16 [4096, 2048], P('seq'), may hold values from -6 to 6
- cotangent: bfloat16 [4096, 2048], P('seq'), may hold values from -6 to 6
- lengths: int32 [13], replicated, may hold values from 1 to 3898, as said below
- attn_gain: bfloat16 [2048], P('seq'), may hold values from 0.5 to 1.5
- ffn_gain: bfloat16 [2048], P('seq'), may hold values from 0.5 to 1.5
- mixer_in: bfloat16 [4, 2048, 2048], P(None, 'seq', 'head'), may hold values from -0.125 to 0.125
- decay_down: bfloat16 [2048, 16], P('seq'), may hold values from -0.125 to 0.125
- decay_up: bfloat16 [16, 2048], P(None, 'head'), may hold values from -1.5 to 1.5
- decay_bias: float32 [2048], P('head'), may hold values from -2 to 12
- head_gain: float32 [512], replicated, may hold values from 0.5 to 1.5
- mixer_out: bfloat16 [2048, 2048], P('head', 'seq'), may hold values from -0.25 to 0.25
- ffn_in: bfloat16 [2, 2048, 5632], P(None, 'seq', 'head'), may hold values from -0.125 to 0.125
- ffn_out: bfloat16 [5632, 2048], P('head', 'seq'), may hold values from -0.15625 to 0.15625
Outputs:
- out: bfloat16 [4096, 2048], P('seq')
- tokens_grad: bfloat16 [4096, 2048], P('seq')
- attn_gain_grad: float32 [2048], P('seq')
- ffn_gain_grad: float32 [2048], P('seq')
- mixer_in_grad: float32 [4, 2048, 2048], P(None, 'seq', 'head')
- decay_down_grad: float32 [2048, 16], P('seq')
- decay_up_grad: float32 [16, 2048], P(None, 'head')
- decay_bias_grad: float32 [2048], P('head')
- head_gain_grad: float32 [512], replicated
- mixer_out_grad: float32 [2048, 2048], P('head', 'seq')
- ffn_in_grad: float32 [2, 2048, 5632], P(None, 'seq', 'head')
- ffn_out_grad: float32 [5632, 2048], P('head', 'seq')
The draws below stay inside these ranges and needn't reach their ends.
Inputs may be any that keep to these rules, and one draw needn't show every extreme that they name: The lengths sum to 4096; item 6, counting from 0, is the longest, starts within the first 256 tokens and ends within the last 256 tokens; every other item has at most 32 tokens.
All inputs are finite; a program needn't handle non-finite values.
Results may differ from the reference program's by a relative error of at most 0.017.
The reference program's roundings to bfloat16 on the way count: a program that leaves them out, or rounds other values in their place, can miss the bound.
Values may be sent and summed in bfloat16 or wider, within the bound.
A program may use at most 448 MiB of HBM per device.

```python
import jax
import jax.numpy as jnp
from jax import lax

D = 2048
HEADS = 4
FF = 5632
RANK = 16
HD = 512
GROUP = 64
EDGE = 6
SHORT = 32
TOKENS = 4096


def draw_lengths(key, part):
    key = jax.random.fold_in(key, 7)
    before = jax.random.randint(key, (EDGE,), 1, SHORT + 1, dtype=jnp.int32)
    after = (SHORT + 1 - before[::-1]).astype(jnp.int32)
    middle_item = jnp.full((1,), TOKENS - EDGE * (SHORT + 1), jnp.int32)
    return jnp.concatenate([before, middle_item, after]).astype(jnp.int32)


def levels(key, shape, cuts, smallest, largest):
    factor_of = 1.0
    for dim, shards_of in cuts:
        heights = jax.random.uniform(jax.random.fold_in(jax.random.fold_in(key, 6), dim), (shards_of,), jnp.float32, smallest / len(cuts), largest / len(cuts))
        factor_of = factor_of * jnp.repeat(jnp.exp(heights), shape[dim] // shards_of).reshape((-1,) + (1,) * (len(shape) - 1 - dim))
    return factor_of


def bell_draw(rng, shape, spread, reach, pieces=(), kind=jnp.bfloat16):
    level = levels(rng, shape, pieces, -0.22, 0.18) if pieces else 1.0
    entries = jax.random.normal(rng, shape, jnp.float32) * spread * level
    return jnp.minimum(jnp.maximum(entries, -reach), reach).astype(kind)


def setup_inputs(seed: int = 0) -> dict:
    keys = jax.random.split(jax.random.key(seed), 14)
    tokens = bell_draw(keys[0], (TOKENS, D), 1.0, 6.0, ((0, 16),))
    cotangent = bell_draw(keys[1], (TOKENS, D), 1.0, 6.0, ((0, 16),))
    lengths = draw_lengths(jax.random.fold_in(keys[13], 71), 0)
    attn_gain = jnp.clip(1.0 + 0.1 * jax.random.normal(keys[3], (D,), jnp.float32), 0.5, 1.5).astype(jnp.bfloat16)
    ffn_gain = jnp.clip(1.0 + 0.1 * jax.random.normal(keys[4], (D,), jnp.float32), 0.5, 1.5).astype(jnp.bfloat16)
    mixer_in = bell_draw(keys[5], (4, D, D), D ** -0.5, 0.125, ((1, 16), (2, 2)))
    decay_down = bell_draw(keys[6], (D, RANK), D ** -0.5, 0.125, ((0, 16),))
    decay_up = bell_draw(keys[7], (RANK, D), RANK ** -0.5, 1.5, ((1, 2),))
    decay_bias = jnp.clip(-2.0 + 14.0 * jax.random.uniform(keys[8], (D,), jnp.float32) ** levels(keys[8], (D,), ((0, 2),), -0.2, 0.2), -2.0, 12.0)
    head_gain = jnp.clip(1.0 + 0.1 * jax.random.normal(keys[9], (HD,), jnp.float32), 0.5, 1.5)
    mixer_out = bell_draw(keys[10], (D, D), (D // 4) ** -0.5, 0.25, ((0, 2), (1, 16)))
    ffn_in = bell_draw(keys[11], (2, D, FF), D ** -0.5, 0.125, ((1, 16), (2, 2)))
    ffn_out = bell_draw(keys[12], (FF, D), (FF // 4) ** -0.5, 0.15625, ((0, 2), (1, 16)))
    return dict(tokens=tokens, cotangent=cotangent, lengths=lengths, attn_gain=attn_gain, ffn_gain=ffn_gain, mixer_in=mixer_in, decay_down=decay_down, decay_up=decay_up, decay_bias=decay_bias, head_gain=head_gain, mixer_out=mixer_out, ffn_in=ffn_in, ffn_out=ffn_out)


EPSILON = 1e-06
HEAD_FLOOR = 1.0
MAXIMUM_PRECISION = lax.Precision.HIGHEST

@jax.custom_vjp
def low(v):
    return lax.optimization_barrier(v.astype(jnp.bfloat16)).astype(jnp.float32)

@jax.custom_vjp
def low_back(v):
    return v

def low_keep(v):
    return (low(v), None)

def low_pass(kept, grad):
    return (grad,)

def back_keep(v):
    return (v, None)

def back_low(kept, grad):
    return (low(grad),)
low.defvjp(low_keep, low_pass)
low_back.defvjp(back_keep, back_low)

def high_dot(left_matrix, right_matrix):
    return jnp.dot(left_matrix, right_matrix, precision=MAXIMUM_PRECISION)

def group_masks(resets):
    counted = jnp.cumsum(resets, axis=1).astype(jnp.int32)
    position = jnp.arange(resets.shape[1])
    causal = position[:, None] >= position[None, :]
    pair_mask = (causal[None] & (counted[:, :, None] == counted[:, None, :])).astype(jnp.float32)
    state_visible_mask = (counted == 0).astype(jnp.float32)
    keeps_state = (counted[:, -1] == 0).astype(jnp.float32)
    in_last = (counted == counted[:, -1:]).astype(jnp.float32)
    return (pair_mask, state_visible_mask, keeps_state, in_last)

def group_step(state_carried_in, group_items):
    queries, key_rows, value_rows, log_gates, resets = group_items
    cumulated = jnp.cumsum(log_gates, axis=0)
    pair_mask, state_visible_mask, keeps_state, in_last = group_masks(resets[None])
    pair_mask, state_visible_mask, keeps_state, in_last = (pair_mask[0], state_visible_mask[0], keeps_state[0], in_last[0])
    growth = jnp.exp(cumulated)
    decayed_query_rows = queries * growth
    key_decayed = key_rows * jnp.exp(-cumulated)
    last_sum = cumulated[-1]
    carried_key_rows = key_rows * jnp.exp(last_sum[None] - cumulated) * in_last[:, None, None]
    scores = jnp.einsum('ihk,jhk->hij', decayed_query_rows, key_decayed, precision=MAXIMUM_PRECISION) * pair_mask[None]
    layer_output = jnp.einsum('hij,jhv->ihv', scores, value_rows, precision=MAXIMUM_PRECISION)
    layer_output = layer_output + state_visible_mask[:, None, None] * jnp.einsum('cwb,wbs->cws', decayed_query_rows, state_carried_in, precision=MAXIMUM_PRECISION)
    updated_state = keeps_state * jnp.exp(last_sum)[:, :, None] * state_carried_in
    updated_state = updated_state + jnp.einsum('nfe,nfu->feu', carried_key_rows, value_rows, precision=MAXIMUM_PRECISION)
    return (updated_state, layer_output)

def mixer_scan(queries, key_rows, value_rows, log_gates, resets):
    groups_all = queries.shape[0] // GROUP

    def split_groups(whole_array):
        return whole_array.reshape(groups_all, GROUP, HEADS, HD)
    zero_state = jnp.zeros((HEADS, HD, HD), jnp.float32)
    final_state, outputs = lax.scan(jax.checkpoint(group_step), zero_state, (split_groups(queries), split_groups(key_rows), split_groups(value_rows), split_groups(log_gates), resets.reshape(groups_all, GROUP)))
    return outputs.reshape(-1, HEADS, HD)

def reference(tokens, cotangent, lengths, attn_gain, ffn_gain, mixer_in, decay_down, decay_up, decay_bias, head_gain, mixer_out, ffn_in, ffn_out):
    item_starts = (jnp.cumsum(lengths) - lengths).astype(jnp.int32)
    position = jnp.arange(TOKENS, dtype=jnp.int32)
    resets = jnp.any(position[:, None] == item_starts[None, :], axis=1).astype(jnp.int32)

    def layer_forward(inputs, gain_one, gain_two, weights_in, rank_down, rank_up, gate_bias, gain_head, weights_out, ffn_pair, ffn_down):
        scale_one = lax.rsqrt(lax.optimization_barrier(jnp.mean(inputs * inputs, -1, keepdims=True)) + EPSILON)
        hidden_one = low(inputs * scale_one * gain_one)
        projected = low_back(jnp.einsum('td,jde->jte', hidden_one, weights_in, precision=MAXIMUM_PRECISION))
        queries = projected[0].reshape(-1, HEADS, HD) * HD ** (-0.5)
        key_rows = projected[1].reshape(-1, HEADS, HD)
        value_rows = projected[2].reshape(-1, HEADS, HD)
        out_gate = projected[3].reshape(-1, HEADS, HD)
        low_rank = low(low_back(high_dot(hidden_one, rank_down)))
        gate_input = low_back(high_dot(low_rank, rank_up)) + gate_bias
        log_gates = (jax.nn.log_sigmoid(gate_input) / 16.0).reshape(-1, HEADS, HD)
        mixed = mixer_scan(queries, key_rows, value_rows, log_gates, resets)
        head_scale = lax.rsqrt(lax.optimization_barrier(jnp.mean(mixed * mixed, -1, keepdims=True)) + HEAD_FLOOR)
        gated_rows = low(mixed * head_scale * gain_head * jax.nn.silu(out_gate)).reshape(-1, D)
        branch = low_back(high_dot(gated_rows, weights_out))
        middle = inputs + branch
        scale_two = lax.rsqrt(lax.optimization_barrier(jnp.mean(middle * middle, -1, keepdims=True)) + EPSILON)
        hidden_two = low(middle * scale_two * gain_two)
        up_pair = low_back(jnp.einsum('td,jdf->jtf', hidden_two, ffn_pair, precision=MAXIMUM_PRECISION))
        activated = low(jax.nn.silu(up_pair[0]) * up_pair[1])
        return middle + high_dot(activated, ffn_down)
    floats = [whole.astype(jnp.float32) for whole in (tokens, attn_gain, ffn_gain, mixer_in, decay_down, decay_up, decay_bias, head_gain, mixer_out, ffn_in, ffn_out)]
    result, pullback = jax.vjp(layer_forward, *floats)
    gradients = pullback(cotangent.astype(jnp.float32))
    return (result.astype(jnp.bfloat16), gradients[0].astype(jnp.bfloat16), gradients[1], gradients[2], gradients[3], gradients[4], gradients[5], gradients[6], gradients[7], gradients[8], gradients[9], gradients[10])
```

```python
import jax
import jax.numpy as jnp
from jax import lax
from jax.sharding import Mesh, PartitionSpec as P

HD = 512
CHUNK = 128
EPSILON = 1e-06
HEAD_FLOOR = 1.0
TEAM = 4

BF = jnp.bfloat16
F32 = jnp.float32


def dot(a, b):
    return jnp.dot(a, b, preferred_element_type=F32)


def dot_rows(a, b):
    return lax.dot_general(a, b, (((0,), (0,)), ((), ())), preferred_element_type=F32)


def dot_last(a, b):
    return lax.dot_general(a, b, (((1,), (1,)), ((), ())), preferred_element_type=F32)


def swap_cores(parts):
    return lax.all_to_all(parts, "c", 0, 0)


def gather_weights(pack):
    rows, _, cols = pack.shape
    pieces = pack.reshape(2, rows // 2, 2, cols)
    pieces = swap_cores(pieces)
    pieces = pieces.transpose(0, 2, 1, 3).reshape(TEAM, rows // 2, cols)
    pieces = lax.all_to_all(pieces, "t", 0, 0)
    everything = lax.all_gather(pieces, "g")
    everything = lax.all_gather(everything, "c", axis=2)
    return everything.reshape(-1, cols)


def scatter_grads(grad):
    groups = lax.axis_size("g")
    cols = grad.shape[1]
    rows = grad.shape[0] // (groups * TEAM)
    part = grad.astype(BF).reshape(groups, TEAM, 2, rows // 2, cols)
    part = part.transpose(2, 0, 1, 3, 4)
    part = lax.psum_scatter(part, "c", scatter_dimension=0, tiled=False)
    part = lax.psum_scatter(part, "g", scatter_dimension=0, tiled=False)
    part = lax.all_to_all(part, "t", 0, 0)
    part = part.reshape(2, 2, rows // 2, cols)
    part = swap_cores(part)
    return part.transpose(0, 2, 1, 3).reshape(rows, 2, cols).astype(F32)


def blocks_to_owners(partial):
    width = partial.shape[1]
    parts = partial.astype(BF).reshape(2, 2, -1, width).transpose(1, 0, 2, 3)
    parts = swap_cores(parts).reshape(TEAM, -1, width)
    return lax.psum_scatter(parts, "t", scatter_dimension=0, tiled=False).astype(F32)


def owners_to_blocks(rows):
    width = rows.shape[1]
    parts = lax.all_gather(rows, "t").reshape(2, 2, -1, width)
    parts = swap_cores(parts)
    return parts.transpose(1, 0, 2, 3).reshape(-1, width)


def chunk_masks(resets):
    counted = jnp.cumsum(resets)
    position = jnp.arange(resets.shape[0])
    pair = (position[:, None] >= position[None, :]) & (counted[:, None] == counted[None, :])
    visible = (counted == 0).astype(F32)[:, None]
    keep = (counted[-1] == 0).astype(F32)
    last = (counted == counted[-1]).astype(F32)[:, None]
    return pair, visible, keep, last


def low(v):
    return v.astype(BF)


def shards(
    tokens,
    cotangent,
    lengths,
    attn_gain,
    ffn_gain,
    mixer_in,
    decay_down,
    decay_up,
    decay_bias,
    head_gain,
    mixer_out,
    ffn_in,
    ffn_out,
):
    g, t, c = lax.axis_index("g"), lax.axis_index("t"), lax.axis_index("c")
    groups = lax.axis_size("g")
    block, width = tokens.shape
    half = block // 2
    rows = mixer_in.shape[1]
    units = ffn_out.shape[0] // 2
    team_tokens = 2 * block
    chunks = team_tokens // CHUNK

    small = jnp.concatenate([attn_gain[:, None], ffn_gain[:, None], decay_down], axis=1)
    small = lax.all_gather(small, ("g", "t"), axis=0, tiled=True)
    gain_one, gain_two, rank_down = small[:, 0].astype(F32), small[:, 1].astype(F32), small[:, 2:]

    mixer_pack = jnp.concatenate(
        [
            mixer_in.transpose(1, 0, 2).reshape(rows, 4, 2, HD),
            mixer_out.T.reshape(rows, 1, 2, HD),
        ],
        axis=1,
    )
    mixer_pack = mixer_pack.transpose(0, 2, 1, 3).reshape(rows, 2, 5 * HD)
    ffn_pack = jnp.concatenate(
        [
            ffn_in.transpose(1, 0, 2).reshape(rows, 2, 2, units),
            ffn_out.T.reshape(rows, 1, 2, units),
        ],
        axis=1,
    )
    ffn_pack = ffn_pack.transpose(0, 2, 1, 3).reshape(rows, 2, 3 * units)
    mixer_w = gather_weights(mixer_pack)
    ffn_w = gather_weights(ffn_pack)

    inputs = lax.all_gather(tokens, "t")
    inputs = lax.dynamic_slice_in_dim(inputs, 2 * c, 2, 0).reshape(team_tokens, width).astype(F32)
    own = lax.dynamic_slice_in_dim(tokens, half * c, half, 0).astype(F32)
    own_dy = lax.dynamic_slice_in_dim(cotangent, half * c, half, 0)
    ffn_dy = lax.all_gather(own_dy, "t", axis=0, tiled=True)
    scale_one = lax.rsqrt(jnp.mean(inputs * inputs, -1, keepdims=True) + EPSILON)
    hidden_one = low(inputs * scale_one * gain_one)

    up_head = lax.dynamic_slice_in_dim(decay_up, HD * (t % 2), HD, 1)
    bias_head = lax.dynamic_slice_in_dim(decay_bias, HD * (t % 2), HD, 0)
    ups = lax.all_gather(up_head, "c")
    biases = lax.all_gather(bias_head, "c")
    up_head, bias_head = ups[t // 2], biases[t // 2]

    first = (g * 2 + c) * team_tokens
    starts = jnp.cumsum(lengths) - lengths
    position = first + jnp.arange(team_tokens, dtype=jnp.int32)
    resets = jnp.any(position[:, None] == starts[None, :], axis=1).astype(jnp.int32)

    projected = dot(hidden_one, mixer_w[:, : 4 * HD])
    queries = projected[:, :HD] * HD ** (-0.5)
    keys = projected[:, HD : 2 * HD]
    values = projected[:, 2 * HD : 3 * HD]
    out_gate = projected[:, 3 * HD :]
    low_rank = low(dot(hidden_one, rank_down))
    gate_input = dot(low_rank, up_head) + bias_head
    log_gates = jax.nn.log_sigmoid(gate_input) / 16.0

    ones = (jnp.arange(CHUNK)[:, None] >= jnp.arange(CHUNK)[None, :]).astype(F32)
    cumulated = jnp.einsum(
        "ij,cjk->cik", ones, log_gates.reshape(chunks, CHUNK, HD), precision=lax.Precision.HIGHEST
    )
    items = []
    for n in range(chunks):
        at = slice(n * CHUNK, (n + 1) * CHUNK)
        q, k, v, b = queries[at], keys[at], values[at], cumulated[n]
        pair, visible, keep, last = chunk_masks(resets[at])
        middle, end = b[CHUNK // 2 - 1], b[-1]
        eq, ek, eb = jnp.exp(b - middle), jnp.exp(middle - b), jnp.exp(b) * visible
        el = jnp.exp(end - b) * last
        qh, kh, qd, kc = low(q * eq), low(k * ek), low(q * eb), k * el
        scores = low(jnp.where(pair, dot_last(qh, kh), 0.0))
        carry = keep * jnp.exp(end)
        update = dot_rows(low(kc), low(v))
        items.append((q, k, low(v), pair, eq, ek, eb, el, qh, kh, qd, kc, scores, carry, update))

    state = jnp.zeros((HD, HD), F32)
    decay = jnp.ones((HD,), F32)
    for it in items:
        state = it[13][:, None] * state + it[14]
        decay = decay * it[13]
    all_states = lax.all_gather(state, ("g", "c"))
    all_decays = lax.all_gather(decay, ("g", "c"))
    index = g * 2 + c
    segments = 2 * groups

    def enter(n, s):
        new = all_decays[n][:, None] * s + all_states[n]
        return jnp.where(n < index, new, s)

    state = lax.fori_loop(0, segments, enter, jnp.zeros((HD, HD), F32))
    outs, states = [], []
    for it in items:
        states.append(state)
        outs.append(dot(it[12], it[2]) + dot(it[10], low(state)))
        state = it[13][:, None] * state + it[14]
    mixed = jnp.concatenate(outs, axis=0)
    head_scale = lax.rsqrt(jnp.mean(mixed * mixed, -1, keepdims=True) + HEAD_FLOOR)
    head_normed = mixed * head_scale
    normed_heads = head_normed * head_gain
    gate_sig = jax.nn.sigmoid(out_gate)
    gate_silu = out_gate * gate_sig
    gated = low(normed_heads * gate_silu)
    branch = blocks_to_owners(dot_last(gated, mixer_w[:, 4 * HD :]))
    middle = own + branch
    scale_two = lax.rsqrt(jnp.mean(middle * middle, -1, keepdims=True) + EPSILON)
    normed_two = middle * scale_two
    hidden_two = lax.all_gather(low(normed_two * gain_two), "t", axis=0, tiled=True)

    up_a = dot(hidden_two, ffn_w[:, :units])
    up_b = dot(hidden_two, ffn_w[:, units : 2 * units])
    ffn_sig = jax.nn.sigmoid(up_a)
    ffn_silu = up_a * ffn_sig
    activated = low(ffn_silu * up_b)
    down = dot_last(activated, ffn_w[:, 2 * units :]).astype(BF)
    down = lax.psum_scatter(down, "t", scatter_dimension=0, tiled=True).astype(F32)
    result = lax.all_gather((middle + down).astype(BF), "c", axis=0, tiled=True)

    grad_act = dot(ffn_dy, ffn_w[:, 2 * units :])
    grad_gate = low(grad_act * up_b * ffn_sig * (1.0 + up_a * (1.0 - ffn_sig)))
    grad_upper = low(grad_act * ffn_silu)
    back = dot_last(grad_gate, ffn_w[:, :units]) + dot_last(grad_upper, ffn_w[:, units : 2 * units])
    grad_hidden_two = lax.psum_scatter(
        back.astype(BF), "t", scatter_dimension=0, tiled=True
    ).astype(F32)
    grad_ffn = jnp.concatenate(
        [
            dot_rows(hidden_two, grad_gate),
            dot_rows(hidden_two, grad_upper),
            dot_rows(ffn_dy, activated),
        ],
        axis=1,
    )
    grad_gain_two = jnp.sum(grad_hidden_two * normed_two, axis=0)
    scaled_two = grad_hidden_two * gain_two
    grad_middle = own_dy.astype(F32) + scale_two * (
        scaled_two - normed_two * jnp.mean(scaled_two * normed_two, -1, keepdims=True)
    )
    grad_branch = owners_to_blocks(low(grad_middle))
    grad_out_proj = dot_rows(grad_branch, gated)
    grad_gated = dot(grad_branch, mixer_w[:, 4 * HD :])
    grad_normed = grad_gated * gate_silu
    grad_out_gate = grad_gated * normed_heads * gate_sig * (1.0 + out_gate * (1.0 - gate_sig))
    grad_head_gain = jnp.sum(grad_normed * head_normed, axis=0)
    scaled_heads = grad_normed * head_gain
    grad_mixed = head_scale * (
        scaled_heads - head_normed * jnp.mean(scaled_heads * head_normed, -1, keepdims=True)
    )

    douts = [low(grad_mixed[n * CHUNK : (n + 1) * CHUNK]) for n in range(chunks)]
    outgoing = [dot_rows(it[10], d) for it, d in zip(items, douts)]
    dstate = jnp.zeros((HD, HD), F32)
    for it, o in zip(items[::-1], outgoing[::-1]):
        dstate = it[13][:, None] * dstate + o
    all_states = lax.all_gather(low(dstate), ("g", "c"))

    def leave(n, s):
        at = segments - 1 - n
        new = all_decays[at][:, None] * s + all_states[at].astype(F32)
        return jnp.where(at > index, new, s)

    dstate = lax.fori_loop(0, segments, leave, jnp.zeros((HD, HD), F32))
    grads = []
    for n in range(chunks - 1, -1, -1):
        q, k, v, pair, eq, ek, eb, el, qh, kh, qd, kc, scores, carry, update = items[n]
        do, state, ds = douts[n], states[n], low(dstate)
        gs = low(jnp.where(pair, dot_last(do, v), 0.0))
        dv = dot_rows(scores, do) + dot(low(kc), ds)
        dq = dot(gs, kh) * eq + dot_last(do, low(state)) * eb
        gkc = dot_last(v, ds)
        dk = dot_rows(gs, qh) * ek + gkc * el
        dcum = dq * q - dk * k
        extra = jnp.sum(gkc * kc, axis=0) + carry * jnp.sum(state * dstate, axis=-1)
        dcum = dcum.at[-1].add(extra)
        dlog = jnp.einsum("ji,jk->ik", ones, dcum, precision=lax.Precision.HIGHEST)
        dstate = carry[:, None] * dstate + outgoing[n]
        grads.append((dq, dk, dv, dlog))
    grads = grads[::-1]
    grad_queries, grad_keys, grad_values, grad_logs = (
        jnp.concatenate([gr[i] for gr in grads], axis=0) for i in range(4)
    )
    grad_gate_input = grad_logs * jax.nn.sigmoid(-gate_input) / 16.0
    grad_bias = jnp.sum(grad_gate_input, axis=0)
    grad_input_low = low(grad_gate_input)
    grad_decay_up = dot_rows(low_rank, grad_input_low)
    grad_rank_part = dot_last(grad_input_low, up_head)
    grad_proj = jnp.concatenate(
        [
            low(grad_queries * HD ** (-0.5)),
            low(grad_keys),
            low(grad_values),
            low(grad_out_gate),
        ],
        axis=1,
    )
    grad_mixer = jnp.concatenate([dot_rows(hidden_one, grad_proj), grad_out_proj], axis=1)
    hidden_part = dot_last(grad_proj, mixer_w[:, : 4 * HD])
    grad_rank = low(lax.psum(grad_rank_part, "t"))
    grad_rank_down = dot_rows(hidden_one, grad_rank) / TEAM
    hidden_part = jnp.concatenate([hidden_part, jnp.zeros((team_tokens, 0), F32)], axis=1)
    grad_hidden_one = blocks_to_owners(hidden_part)
    rank_own = swap_cores(grad_rank.reshape(2, 2, half, -1).transpose(1, 0, 2, 3))
    rank_own = rank_own.reshape(TEAM, half, -1)[t]
    grad_hidden_one = grad_hidden_one + dot_last(rank_own, rank_down)
    scale_own = lax.rsqrt(jnp.mean(own * own, -1, keepdims=True) + EPSILON)
    normed_own = own * scale_own
    grad_gain_one = jnp.sum(grad_hidden_one * normed_own, axis=0)
    scaled_one = grad_hidden_one * gain_one
    grad_inputs = grad_middle + scale_own * (
        scaled_one - normed_own * jnp.mean(scaled_one * normed_own, -1, keepdims=True)
    )
    grad_inputs = lax.all_gather(grad_inputs.astype(BF), "c", axis=0, tiled=True)

    mixer_home = scatter_grads(grad_mixer).reshape(rows, 2, 5, HD)
    ffn_home = scatter_grads(grad_ffn).reshape(rows, 2, 3, units)
    small_home = jnp.concatenate(
        [grad_gain_one[:, None], grad_gain_two[:, None], grad_rank_down], axis=1
    )
    small_home = lax.psum_scatter(
        lax.psum(small_home, "c"), ("g", "t"), scatter_dimension=0, tiled=True
    )
    head_small = jnp.concatenate([grad_decay_up, grad_bias[None], grad_head_gain[None]], axis=0)
    head_small = lax.psum(head_small, ("g", "c"))
    head_small = lax.all_gather(head_small, "t")
    pair_small = lax.dynamic_slice_in_dim(head_small, 2 * c, 2, 0)
    decay_up_home = pair_small[:, :-2].transpose(1, 0, 2).reshape(-1, 2 * HD)
    bias_home = pair_small[:, -2].reshape(2 * HD)
    head_gain_home = jnp.sum(head_small[:, -1], axis=0)
    return (
        result,
        grad_inputs,
        small_home[:, 0],
        small_home[:, 1],
        mixer_home[:, :, :4].transpose(2, 0, 1, 3).reshape(4, rows, 2 * HD),
        small_home[:, 2:],
        decay_up_home,
        bias_home,
        head_gain_home,
        mixer_home[:, :, 4].reshape(rows, 2 * HD).T,
        ffn_home[:, :, :2].transpose(2, 0, 1, 3).reshape(2, rows, 2 * units),
        ffn_home[:, :, 2].reshape(rows, 2 * units).T,
    )


def solution(mesh):
    devices = mesh.devices
    inner = Mesh(devices.reshape(devices.shape[0] // TEAM, TEAM, devices.shape[1]), ("g", "t", "c"))
    seq = ("g", "t")
    in_specs = (
        P(seq, None),
        P(seq, None),
        P(),
        P(seq),
        P(seq),
        P(None, seq, "c"),
        P(seq, None),
        P(None, "c"),
        P("c"),
        P(),
        P("c", seq),
        P(None, seq, "c"),
        P("c", seq),
    )
    out_specs = (
        P(seq, None),
        P(seq, None),
        P(seq),
        P(seq),
        P(None, seq, "c"),
        P(seq, None),
        P(None, "c"),
        P("c"),
        P(),
        P("c", seq),
        P(None, seq, "c"),
        P("c", seq),
    )
    return jax.shard_map(shards, mesh=inner, in_specs=in_specs, out_specs=out_specs, check_vma=False)
```

```python
import functools

import jax
import jax.numpy as jnp
from jax import lax
from jax.experimental import pallas as pl
from jax.experimental.pallas import tpu as pltpu
from jax.sharding import Mesh, PartitionSpec as P

HD = 512
CHUNK = 128
EPSILON = 1e-06
HEAD_FLOOR = 1.0
TEAM = 4

BF = jnp.bfloat16
F32 = jnp.float32
MESH = pl.DeviceIdType.MESH
ANY = pl.BlockSpec(memory_space=pl.ANY)
VMEM = pl.BlockSpec(memory_space=pltpu.VMEM)
DMA = pltpu.SemaphoreType.DMA

SEQ = ("g", "y", "x")
FLIPS = ((1, 1), (0, 1), (1, 0), (0, 0))


def dot(a, b):
    return jnp.dot(a, b, preferred_element_type=F32)


def dot_rows(a, b):
    return lax.dot_general(a, b, (((0,), (0,)), ((), ())), preferred_element_type=F32)


def dot_last(a, b):
    return lax.dot_general(a, b, (((1,), (1,)), ((), ())), preferred_element_type=F32)


def low(v):
    return v.astype(BF)


def flip(index, by):
    return 1 - index if by else index


class Place:
    def __init__(self):
        self.y, self.x, self.c = lax.axis_index("y"), lax.axis_index("x"), lax.axis_index("c")
        self.member = self.y * 2 + self.x


def greet_team(me):
    barrier = pltpu.get_barrier_semaphore()
    for n in range(1, 8):
        to = {"y": flip(me.y, n & 1), "x": flip(me.x, n & 2), "c": flip(me.c, n & 4)}
        pl.semaphore_signal(barrier, inc=1, device_id=to, device_id_type=MESH)
    pl.semaphore_wait(barrier, 7)


def greet_all(me):
    barrier = pltpu.get_barrier_semaphore()
    g, groups = lax.axis_index("g"), lax.axis_size("g")
    for k in range(groups):
        for n in range(8):
            if k == 0 and n == 0:
                continue
            to = {
                "g": lax.rem(g + k, groups),
                "y": flip(me.y, n & 1),
                "x": flip(me.x, n & 2),
                "c": flip(me.c, n & 4),
            }
            pl.semaphore_signal(barrier, inc=1, device_id=to, device_id_type=MESH)
    pl.semaphore_wait(barrier, groups * 8 - 1)


def route_member(me):
    out, arrive = [], []
    for fy, fx in FLIPS:
        y, x = flip(me.y, fy), flip(me.x, fx)
        own = (fy, fx) == (0, 0)
        out.append((y * 2 + x, me.member, {"y": y, "x": x}, own))
        arrive.append((y * 2 + x, own))
    return out, arrive


def route_all(me):
    g, groups = lax.axis_index("g"), lax.axis_size("g")
    out, arrive = [], []
    for k in range(groups):
        for fy, fx in FLIPS:
            to_g, y, x = lax.rem(g + k, groups), flip(me.y, fy), flip(me.x, fx)
            own = k == 0 and (fy, fx) == (0, 0)
            chip = to_g * 4 + y * 2 + x
            out.append((chip, g * 4 + me.member, {"g": to_g, "y": y, "x": x}, own))
            arrive.append((chip, own))
    return out, arrive


def route_halves(me):
    mine = me.c == me.y
    out, arrive = [], []
    for fy, fx in FLIPS:
        y, x = flip(me.y, fy), flip(me.x, fx)
        own = mine if (fy, fx) == (0, 0) else False
        out.append((0, me.x * 2 + me.c, {"y": y, "x": x, "c": me.y}, own))
    for fc, fx in FLIPS:
        c, x = flip(me.c, fc), flip(me.x, fx)
        own = mine if (fc, fx) == (0, 0) else False
        arrive.append((x * 2 + c, own))
    return out, arrive


def route_owners(me):
    mine = me.c == me.y
    out, arrive = [], []
    for fc, fx in FLIPS:
        c, x = flip(me.c, fc), flip(me.x, fx)
        own = mine if (fc, fx) == (0, 0) else False
        out.append((x * 2 + c, me.member, {"y": me.c, "x": x, "c": c}, own))
    for fy, fx in FLIPS:
        y, x = flip(me.y, fy), flip(me.x, fx)
        own = mine if (fy, fx) == (0, 0) else False
        arrive.append((y * 2 + x, own))
    return out, arrive


def route_weights(me):
    mine = (me.c == me.y) & (me.c == me.x)
    out, arrive = [], []
    for f in (1, 0):
        x = flip(me.x, f)
        own = (me.c == me.y) & (me.c == x) & (me.x == me.c) if not f else False
        out.append((x, me.y, {"y": me.c, "x": x, "c": me.x}, own))
    for f in (1, 0):
        y = flip(me.y, f)
        own = mine if not f else False
        arrive.append((y, own))
    return out, arrive


def route_weights_home(me):
    mine = (me.c == me.y) & (me.c == me.x)
    out, arrive = [], []
    for f in (1, 0):
        y = flip(me.y, f)
        own = mine if not f else False
        out.append((y, me.x, {"y": y, "x": me.c, "c": me.y}, own))
    for f in (1, 0):
        x = flip(me.x, f)
        own = mine if not f else False
        arrive.append((x, own))
    return out, arrive


def when(condition, run):
    if condition is True:
        run()
    elif condition is not False:
        pl.when(condition)(run)


def unless(condition, run):
    if condition is False:
        run()
    elif condition is not True:
        pl.when(jnp.logical_not(condition))(run)


class Transfer:
    def __init__(self, route, source, target, send, arrive):
        self.route, self.source, self.target, self.send, self.arrive = route, source, target, send, arrive

    def _remote(self, n):
        index, slot, to, own = self.route[0][n]
        return pltpu.make_async_remote_copy(
            src_ref=self.source(index),
            dst_ref=self.target(slot),
            send_sem=self.send.at[n],
            recv_sem=self.arrive.at[slot],
            device_id=to,
            device_id_type=MESH,
        )

    def _local(self, n):
        index, slot, to, own = self.route[0][n]
        return pltpu.make_async_copy(self.source(index), self.target(slot), self.send.at[n])

    def start(self):
        for n, (_, _, _, own) in enumerate(self.route[0]):
            unless(own, lambda: self._remote(n).start())
            when(own, lambda: self._local(n).start())

    def wait_arrive(self):
        for slot, own in self.route[1]:
            ref = self.target(slot)

            def arrived():
                pltpu.make_async_copy(ref, ref, self.arrive.at[slot]).wait()

            unless(own, arrived)

    def wait_local(self):
        for n, (_, _, _, own) in enumerate(self.route[0]):
            when(own, lambda: self._local(n).wait())

    def wait_sent(self):
        for n, (_, _, _, own) in enumerate(self.route[0]):
            unless(own, lambda: self._remote(n).wait_send())

    def wait(self):
        self.wait_arrive()
        self.wait_local()
        self.wait_sent()


def exchange_kernel(routes, everyone, *refs):
    count = len(routes)
    ins, outs = refs[:count], refs[count : 2 * count]
    sems = refs[2 * count :]
    me = Place()
    if everyone:
        greet_all(me)
    else:
        greet_team(me)
    transfers = []
    for n, (route, whole) in enumerate(routes):
        i, o = ins[n], outs[n]
        transfer = Transfer(
            route(me),
            (lambda _, i=i: i) if whole else (lambda k, i=i: i.at[k]),
            lambda k, o=o: o.at[k],
            sems[2 * n],
            sems[2 * n + 1],
        )
        transfer.start()
        transfers.append(transfer)
    for transfer in transfers:
        transfer.wait()


def exchange(call_id, *parts, everyone=False):
    routes = [(route, whole) for route, _, _, whole in parts]
    arrays = [array for _, array, _, _ in parts]
    shapes = []
    size = 0
    for _, array, slots, whole in parts:
        shape = array.shape if whole else array.shape[1:]
        shapes.append(jax.ShapeDtypeStruct((slots,) + shape, array.dtype))
        size += (array.size + shapes[-1].size) * array.dtype.itemsize
    scratch = []
    for _, _, slots, _ in parts:
        scratch += [DMA((slots,)), DMA((slots,))]
    return pl.pallas_call(
        functools.partial(exchange_kernel, routes, everyone),
        out_shape=shapes,
        in_specs=[VMEM] * len(parts),
        out_specs=[VMEM] * len(parts),
        scratch_shapes=scratch,
        compiler_params=pltpu.CompilerParams(
            collective_id=call_id, has_side_effects=True, vmem_limit_bytes=size + (8 << 20)
        ),
        name=f"exchange_{call_id}",
    )(*arrays)


def norm_forward_kernel(partial, own, gain, hidden, middle, got, line, send, arrive, send2, arrive2):
    me = Place()
    greet_team(me)
    steps = send.shape[0]
    rows = own.shape[0] // steps

    def part(ref, k, n):
        return ref.at[k, pl.ds(n * rows, rows)]

    sums = [
        Transfer(
            route_owners(me),
            lambda k, n=n: part(partial, k, n),
            lambda k, n=n: part(got, k, n),
            send.at[n],
            arrive.at[n],
        )
        for n in range(steps)
    ]
    spreads = [
        Transfer(
            route_member(me),
            lambda k, n=n: line.at[pl.ds(n * rows, rows)],
            lambda k, n=n: part(hidden, k, n),
            send2.at[n],
            arrive2.at[n],
        )
        for n in range(steps)
    ]
    for transfer in sums:
        transfer.start()
    for n in range(steps):
        sums[n].wait_arrive()
        sums[n].wait_local()
        at = pl.ds(n * rows, rows)
        total = own[at].astype(F32)
        for k in range(TEAM):
            total = total + got[k, at].astype(F32)
        middle[at] = total
        scale = lax.rsqrt(jnp.mean(total * total, -1, keepdims=True) + EPSILON)
        line[at] = low(total * scale * gain[...])
        spreads[n].start()
    for transfer in sums:
        transfer.wait_sent()
    for transfer in spreads:
        transfer.wait()


STEPS = 4


def norm_forward(partial, own, gain):
    rows, width = own.shape
    return pl.pallas_call(
        norm_forward_kernel,
        out_shape=(
            jax.ShapeDtypeStruct((TEAM, rows, width), BF),
            jax.ShapeDtypeStruct((rows, width), F32),
        ),
        in_specs=[VMEM, VMEM, VMEM],
        out_specs=(VMEM, VMEM),
        scratch_shapes=[
            pltpu.VMEM((TEAM, rows, width), BF),
            pltpu.VMEM((rows, width), BF),
            DMA((STEPS, TEAM)),
            DMA((STEPS, TEAM)),
            DMA((STEPS, TEAM)),
            DMA((STEPS, TEAM)),
        ],
        compiler_params=pltpu.CompilerParams(
            collective_id=2, has_side_effects=True, vmem_limit_bytes=32 << 20
        ),
        name="norm_forward",
    )(partial, own, gain)


def norm_backward_kernel(
    partial, cot, middle, gain, branch, grad, gain_grad, got, line, send, arrive, send2, arrive2
):
    me = Place()
    greet_team(me)
    steps = send.shape[0]
    rows = cot.shape[0] // steps

    def part(ref, k, n):
        return ref.at[k, pl.ds(n * rows, rows)]

    sums = [
        Transfer(
            route_member(me),
            lambda k, n=n: part(partial, k, n),
            lambda k, n=n: part(got, k, n),
            send.at[n],
            arrive.at[n],
        )
        for n in range(steps)
    ]
    spreads = [
        Transfer(
            route_halves(me),
            lambda k, n=n: line.at[pl.ds(n * rows, rows)],
            lambda k, n=n: part(branch, k, n),
            send2.at[n],
            arrive2.at[n],
        )
        for n in range(steps)
    ]
    for transfer in sums:
        transfer.start()
    for n in range(steps):
        at = pl.ds(n * rows, rows)
        mid = middle[at]
        scale = lax.rsqrt(jnp.mean(mid * mid, -1, keepdims=True) + EPSILON)
        normed = mid * scale
        sums[n].wait_arrive()
        sums[n].wait_local()
        total = got[0, at].astype(F32)
        for k in range(1, TEAM):
            total = total + got[k, at].astype(F32)
        gsum = jnp.sum(total * normed, axis=0, keepdims=True)
        gain_grad[...] = gsum if n == 0 else gain_grad[...] + gsum
        scaled = total * gain[...]
        out = cot[at].astype(F32) + scale * (
            scaled - normed * jnp.mean(scaled * normed, -1, keepdims=True)
        )
        grad[at] = out
        line[at] = low(out)
        spreads[n].start()
    for transfer in sums:
        transfer.wait_sent()
    for transfer in spreads:
        transfer.wait()


def norm_backward(partial, cot, middle, gain):
    rows, width = cot.shape
    return pl.pallas_call(
        norm_backward_kernel,
        out_shape=(
            jax.ShapeDtypeStruct((TEAM, rows, width), BF),
            jax.ShapeDtypeStruct((rows, width), F32),
            jax.ShapeDtypeStruct((1, width), F32),
        ),
        in_specs=[VMEM] * 4,
        out_specs=(VMEM, VMEM, VMEM),
        scratch_shapes=[
            pltpu.VMEM((TEAM, rows, width), BF),
            pltpu.VMEM((rows, width), BF),
            DMA((STEPS, TEAM)),
            DMA((STEPS, TEAM)),
            DMA((STEPS, TEAM)),
            DMA((STEPS, TEAM)),
        ],
        compiler_params=pltpu.CompilerParams(
            collective_id=3, has_side_effects=True, vmem_limit_bytes=32 << 20
        ),
        name="norm_backward",
    )(partial, cot, middle, gain)


def first_norm_kernel(
    partial, own, grad_middle, gain, down, out, gain_grad, rank_grad, got, line, send, arrive, send2, arrive2
):
    me = Place()
    greet_team(me)
    steps = send.shape[0]
    rows, width = own.shape[0] // steps, own.shape[1]

    def part(ref, k, n):
        return ref.at[k, pl.ds(n * rows, rows)]

    sums = [
        Transfer(
            route_owners(me),
            lambda k, n=n: part(partial, k, n),
            lambda k, n=n: part(got, k, n),
            send.at[n],
            arrive.at[n],
        )
        for n in range(steps)
    ]
    other = {"c": 1 - me.c}

    def twin(n):
        return pltpu.make_async_remote_copy(
            src_ref=line.at[pl.ds(n * rows, rows)],
            dst_ref=part(out, me.c, n),
            send_sem=send2.at[n],
            recv_sem=arrive2.at[n],
            device_id=other,
            device_id_type=MESH,
        )

    def mine(n):
        return pltpu.make_async_copy(
            line.at[pl.ds(n * rows, rows)], part(out, me.c, n), arrive2.at[steps + n]
        )

    for transfer in sums:
        transfer.start()
    for n in range(steps):
        at = pl.ds(n * rows, rows)
        x = own[at].astype(F32)
        scale = lax.rsqrt(jnp.mean(x * x, -1, keepdims=True) + EPSILON)
        normed = x * scale
        sums[n].wait_arrive()
        sums[n].wait_local()
        total = got[0, at].astype(F32)
        for k in range(1, TEAM):
            total = total + got[k, at].astype(F32)
        rank = low(total[:, width:])
        total = total[:, :width] + dot(rank, down[...])
        gsum = jnp.sum(total * normed, axis=0, keepdims=True)
        hidden = low(normed * gain[...])
        rsum = dot_rows(rank, hidden)
        gain_grad[...] = gsum if n == 0 else gain_grad[...] + gsum
        rank_grad[...] = rsum if n == 0 else rank_grad[...] + rsum
        scaled = total * gain[...]
        line[at] = low(
            grad_middle[at]
            + scale * (scaled - normed * jnp.mean(scaled * normed, -1, keepdims=True))
        )
        twin(n).start()
        mine(n).start()
    for transfer in sums:
        transfer.wait_sent()
    for n in range(steps):
        twin(n).wait()
        mine(n).wait()


def first_norm(partial, own, grad_middle, gain, down):
    rows, width = own.shape
    lanes = partial.shape[-1] - width
    return pl.pallas_call(
        first_norm_kernel,
        out_shape=(
            jax.ShapeDtypeStruct((2, rows, width), BF),
            jax.ShapeDtypeStruct((1, width), F32),
            jax.ShapeDtypeStruct((lanes, width), F32),
        ),
        in_specs=[VMEM] * 5,
        out_specs=(VMEM, VMEM, VMEM),
        scratch_shapes=[
            pltpu.VMEM((TEAM, rows, width + lanes), BF),
            pltpu.VMEM((rows, width), BF),
            DMA((STEPS, TEAM)),
            DMA((STEPS, TEAM)),
            DMA((STEPS,)),
            DMA((2 * STEPS,)),
        ],
        compiler_params=pltpu.CompilerParams(
            collective_id=4, has_side_effects=True, vmem_limit_bytes=40 << 20
        ),
        name="first_norm",
    )(partial, own, grad_middle, gain, down)


def join_kernel(piece, out, send, arrive, here):
    c = lax.axis_index("c")
    barrier = pltpu.get_barrier_semaphore()
    pl.semaphore_signal(barrier, inc=1, device_id={"c": 1 - c}, device_id_type=MESH)
    pl.semaphore_wait(barrier, 1)
    copies = []
    for n in range(piece.shape[0]):
        place = out.at[n, :, c]
        copies.append(
            pltpu.make_async_remote_copy(
                src_ref=piece.at[n],
                dst_ref=place,
                send_sem=send.at[n],
                recv_sem=arrive.at[n],
                device_id={"c": 1 - c},
                device_id_type=MESH,
            )
        )
        copies.append(pltpu.make_async_copy(piece.at[n], place, here.at[n]))
    for copy in copies:
        copy.start()
    for copy in copies:
        copy.wait()


def join_pieces(call_id, piece):
    groups, _, rows, cols = piece.shape
    size = piece.size * 4
    out = pl.pallas_call(
        join_kernel,
        out_shape=jax.ShapeDtypeStruct((groups, 2, 2, rows, cols), BF),
        in_specs=[ANY],
        out_specs=VMEM,
        scratch_shapes=[DMA((groups,)), DMA((groups,)), DMA((groups,))],
        compiler_params=pltpu.CompilerParams(
            collective_id=call_id, has_side_effects=True, vmem_limit_bytes=size + (8 << 20)
        ),
        name=f"join_{call_id}",
    )(piece)
    return out.reshape(-1, cols)


def sum_pieces(grad):
    groups = lax.axis_size("g")
    cols = grad.shape[1]
    c = lax.axis_index("c")
    rows = grad.shape[0] // (groups * 4)
    part = low(grad).reshape(groups, 2, 2, rows, cols)
    away = lax.dynamic_index_in_dim(part, 1 - c, 2, keepdims=False)
    keep = lax.dynamic_index_in_dim(part, c, 2, keepdims=False)
    got = lax.ppermute(away, "c", [(0, 1), (1, 0)])
    part = low(keep.astype(F32) + got.astype(F32))
    return lax.psum_scatter(part, "g", scatter_dimension=0, tiled=False)


def states_kernel(
    back, local, decay, out, pair, pair_decay, sums, sum_decays, stage, stage_decay, entering,
    near, far_send, far_arrive, far_send2, far_arrive2,
):
    g, c = lax.axis_index("g"), lax.axis_index("c")
    groups = lax.axis_size("g")
    half = local.shape[0] // 2
    sibling = {"c": 1 - c}
    barrier = pltpu.get_barrier_semaphore()
    pl.semaphore_signal(barrier, inc=1, device_id=sibling, device_id_type=MESH)
    for n in range(1, groups):
        to = {"g": lax.rem(g + n, groups)}
        pl.semaphore_signal(barrier, inc=1, device_id=to, device_id_type=MESH)
    pl.semaphore_wait(barrier, groups)

    def remote(src, dst, send, arrive, to):
        return pltpu.make_async_remote_copy(
            src_ref=src, dst_ref=dst, send_sem=send, recv_sem=arrive, device_id=to, device_id_type=MESH
        )

    first = [
        remote(local.at[pl.ds((1 - c) * half, half)], pair, near.at[0], near.at[1], sibling),
        remote(decay, pair_decay, near.at[2], near.at[3], sibling),
    ]
    for copy in first:
        copy.start()
    for copy in first:
        copy.wait()
    leads = (c == 1) if back else (c == 0)
    mine, theirs = local[pl.ds(c * half, half)], pair[...]
    my_decay, their_decay = decay[...], pair_decay[...]
    early = jnp.where(leads, mine, theirs)
    late = jnp.where(leads, theirs, mine)
    early_decay = jnp.where(leads, my_decay, their_decay)[:1]
    late_decay = jnp.where(leads, their_decay, my_decay)[:1]
    stage[...] = low(late_decay * early + late)
    stage_decay[...] = jnp.broadcast_to(early_decay * late_decay, stage_decay.shape)

    def needs(source, target):
        return (source > target) if back else (source < target)

    for n in range(1, groups):
        to = lax.rem(g + n, groups)

        @pl.when(needs(g, to))
        def _(n=n, to=to):
            remote(stage, sums.at[g], far_send.at[n], far_arrive.at[g], {"g": to}).start()
            remote(stage_decay, sum_decays.at[g], far_send2.at[n], far_arrive2.at[g], {"g": to}).start()

    entering[...] = jnp.zeros_like(entering)
    for n in range(groups):
        k = groups - 1 - n if back else n

        @pl.when(needs(k, g))
        def _(k=k):
            pltpu.make_async_copy(sums.at[k], sums.at[k], far_arrive.at[k]).wait()
            pltpu.make_async_copy(sum_decays.at[k], sum_decays.at[k], far_arrive2.at[k]).wait()
            entering[...] = sum_decays[k][:1] * entering[...] + sums[k].astype(F32)

    at_early = entering[...]
    at_late = early_decay * at_early + early
    out[pl.ds(c * half, half)] = jnp.where(leads, at_early, at_late)
    pair[...] = jnp.where(leads, at_late, at_early)
    last = remote(pair, out.at[pl.ds(c * half, half)], near.at[4], near.at[5], sibling)
    last.start()
    last.wait()
    for n in range(1, groups):
        to = lax.rem(g + n, groups)

        @pl.when(needs(g, to))
        def _(n=n, to=to):
            remote(stage, sums.at[g], far_send.at[n], far_arrive.at[g], {"g": to}).wait_send()
            remote(
                stage_decay, sum_decays.at[g], far_send2.at[n], far_arrive2.at[g], {"g": to}
            ).wait_send()


def states(call_id, back, local, decay):
    groups = lax.axis_size("g")
    rows, cols = local.shape
    half = rows // 2
    return pl.pallas_call(
        functools.partial(states_kernel, back),
        out_shape=jax.ShapeDtypeStruct((rows, cols), F32),
        in_specs=[VMEM, VMEM],
        out_specs=VMEM,
        scratch_shapes=[
            pltpu.VMEM((half, cols), F32),
            pltpu.VMEM((8, cols), F32),
            pltpu.VMEM((groups, half, cols), BF),
            pltpu.VMEM((groups, 8, cols), F32),
            pltpu.VMEM((half, cols), BF),
            pltpu.VMEM((8, cols), F32),
            pltpu.VMEM((half, cols), F32),
            DMA((6,)),
            DMA((groups,)),
            DMA((groups,)),
            DMA((groups,)),
            DMA((groups,)),
        ],
        compiler_params=pltpu.CompilerParams(
            collective_id=call_id, has_side_effects=True, vmem_limit_bytes=32 << 20
        ),
        name="states_back" if back else "states",
    )(local, jnp.broadcast_to(decay, (8, cols)))


def finish_kernel(wide, heads, wide_out, heads_out, gains_out, wide_got, heads_got, line, twin, *sems):
    wide_send, wide_arrive, heads_send, heads_arrive, near, out_send, out_arrive, gain_send, gain_arrive = sems
    me = Place()
    g, groups = lax.axis_index("g"), lax.axis_size("g")
    greet_all(me)
    owners = groups * 4

    def remote(src, dst, send, arrive, to):
        return pltpu.make_async_remote_copy(
            src_ref=src, dst_ref=dst, send_sem=send, recv_sem=arrive, device_id=to, device_id_type=MESH
        )

    mine = g * 4 + me.member
    spreads = Transfer(
        route_all(me),
        lambda k: wide.at[k],
        lambda k: wide_got.at[k],
        wide_send,
        wide_arrive,
    )
    spreads.start()
    group_out, group_arrive = [], []
    for n in range(groups):
        for f in range(2):
            to_g, to_c = lax.rem(g + n, groups), flip(me.c, f)
            own = n == 0 and f == 0
            group_out.append((0, g * 2 + me.c, {"g": to_g, "c": to_c}, own))
            group_arrive.append((to_g * 2 + to_c, own))
    heads_move = Transfer(
        (group_out, group_arrive), lambda _: heads, lambda k: heads_got.at[k], heads_send, heads_arrive
    )
    heads_move.start()
    heads_move.wait()
    total = heads_got[0]
    for n in range(1, groups * 2):
        total = total + heads_got[n]
    line[...] = total
    member_out, member_arrive = route_member(me)
    gain_rows = line.shape[0] - gains_out.shape[1]
    gains = Transfer(
        (member_out, member_arrive),
        lambda _: line.at[pl.ds(gain_rows, gains_out.shape[1])],
        lambda k: gains_out.at[k],
        gain_send,
        gain_arrive,
    )
    gains.start()
    for n, (fy, fx) in enumerate(FLIPS):
        to = {"y": flip(me.y, fy), "x": flip(me.x, fx)}
        if (fy, fx) == (0, 0):
            continue

        @pl.when(me.c == me.y)
        def _(n=n, to=to):
            remote(line, heads_out.at[me.x], out_send.at[n], out_arrive.at[me.x], to).start()

    @pl.when(me.c == me.y)
    def _():
        heads_out[me.x] = line[...]

    spreads.wait()
    total = wide_got[0]
    for n in range(1, owners):
        total = total + wide_got[n]
    wide_got[0] = total
    last = remote(wide_got.at[0], twin, near.at[0], near.at[1], {"c": 1 - me.c})
    last.start()
    for k in range(2):
        own = (me.c == me.y) & (me.x == k)

        @pl.when(jnp.logical_not(own))
        def _(k=k):
            pltpu.make_async_copy(heads_out.at[k], heads_out.at[k], out_arrive.at[k]).wait()

    for n, (fy, fx) in enumerate(FLIPS):
        to = {"y": flip(me.y, fy), "x": flip(me.x, fx)}
        if (fy, fx) == (0, 0):
            continue

        @pl.when(me.c == me.y)
        def _(n=n, to=to):
            remote(line, heads_out.at[me.x], out_send.at[n], out_arrive.at[me.x], to).wait_send()

    gains.wait()
    last.wait()
    wide_out[...] = wide_got[0] + twin[...]


def finish(wide, heads):
    owners, r, rows = wide.shape
    groups = owners // 4
    return pl.pallas_call(
        finish_kernel,
        out_shape=(
            jax.ShapeDtypeStruct((r, rows), F32),
            jax.ShapeDtypeStruct((2,) + heads.shape, F32),
            jax.ShapeDtypeStruct((TEAM, 8, heads.shape[1]), F32),
        ),
        in_specs=[VMEM, VMEM],
        out_specs=(VMEM, VMEM, VMEM),
        scratch_shapes=[
            pltpu.VMEM((owners, r, rows), F32),
            pltpu.VMEM((groups * 2,) + heads.shape, F32),
            pltpu.VMEM(heads.shape, F32),
            pltpu.VMEM((r, rows), F32),
            DMA((owners,)),
            DMA((owners,)),
            DMA((groups * 2,)),
            DMA((groups * 2,)),
            DMA((2,)),
            DMA((TEAM,)),
            DMA((2,)),
            DMA((TEAM,)),
            DMA((TEAM,)),
        ],
        compiler_params=pltpu.CompilerParams(
            collective_id=11, has_side_effects=True, vmem_limit_bytes=32 << 20
        ),
        name="finish",
    )(wide, heads)


def chunk_masks(resets):
    counted = jnp.cumsum(resets)
    position = jnp.arange(resets.shape[0])
    pair = (position[:, None] >= position[None, :]) & (counted[:, None] == counted[None, :])
    visible = (counted == 0).astype(F32)[:, None]
    keep = (counted[-1] == 0).astype(F32)
    last = (counted == counted[-1]).astype(F32)[:, None]
    return pair, visible, keep, last


def shards(
    tokens,
    cotangent,
    lengths,
    attn_gain,
    ffn_gain,
    mixer_in,
    decay_down,
    decay_up,
    decay_bias,
    head_gain,
    mixer_out,
    ffn_in,
    ffn_out,
):
    g, y, x, c = (lax.axis_index(a) for a in SEQ + ("c",))
    groups = lax.axis_size("g")
    block, width = tokens.shape
    half = block // 2
    rows = mixer_in.shape[1]
    units = ffn_out.shape[0] // 2
    team_tokens = 2 * block
    chunks = team_tokens // CHUNK
    rank = decay_down.shape[1]

    mixer_pack = jnp.concatenate(
        [
            mixer_in.transpose(1, 0, 2).reshape(rows, 4, 2, HD),
            mixer_out.T.reshape(rows, 1, 2, HD),
        ],
        axis=1,
    )
    mixer_pack = mixer_pack.transpose(2, 0, 1, 3).reshape(2, rows, 5 * HD)
    small = jnp.concatenate([attn_gain[None], ffn_gain[None], decay_down.T], axis=0)
    small = jnp.pad(small, ((0, 32 - small.shape[0]), (0, 0)))
    mixer_piece, small = exchange(
        0, (route_weights, mixer_pack, 2, False), (route_all, small, 4 * groups, True), everyone=True
    )
    small = small.transpose(1, 0, 2).reshape(32, width)
    gain_one, gain_two = small[0].astype(F32), small[1].astype(F32)
    rank_down = small[2 : 2 + rank]
    mixer_w = lax.all_gather(mixer_piece, "g")
    ffn_pack = jnp.concatenate(
        [
            ffn_in.transpose(1, 0, 2).reshape(rows, 2, 2, units),
            ffn_out.T.reshape(rows, 1, 2, units),
        ],
        axis=1,
    )
    ffn_pack = ffn_pack.transpose(2, 0, 1, 3).reshape(2, rows, 3 * units)
    own = lax.dynamic_slice_in_dim(tokens, half * c, half, 0)
    own_dy = lax.dynamic_slice_in_dim(cotangent, half * c, half, 0)
    ffn_piece, inputs, ffn_dy = exchange(
        1,
        (route_weights, ffn_pack, 2, False),
        (route_halves, own, 4, True),
        (route_member, own_dy, 4, True),
    )
    ffn_w = lax.all_gather(ffn_piece, "g")
    mixer_w = join_pieces(5, mixer_w)

    inputs = inputs.reshape(team_tokens, width).astype(F32)
    ffn_dy = ffn_dy.reshape(team_tokens, width)
    scale_one = lax.rsqrt(jnp.mean(inputs * inputs, -1, keepdims=True) + EPSILON)
    hidden_one = low(inputs * scale_one * gain_one)

    up_head = lax.dynamic_slice_in_dim(decay_up, HD * x, HD, 1)
    bias_head = lax.dynamic_slice_in_dim(decay_bias, HD * x, HD, 0)
    cross = [(0, 1), (1, 0)]
    up_head = jnp.where(c == y, up_head, lax.ppermute(up_head, "c", cross))
    bias_head = jnp.where(c == y, bias_head, lax.ppermute(bias_head, "c", cross))

    first = (g * 2 + c) * team_tokens
    starts = jnp.cumsum(lengths) - lengths
    position = first + jnp.arange(team_tokens, dtype=jnp.int32)
    resets = jnp.any(position[:, None] == starts[None, :], axis=1).astype(jnp.int32)

    projected = dot(hidden_one, mixer_w[:, : 4 * HD])
    queries = projected[:, :HD] * HD ** (-0.5)
    keys = projected[:, HD : 2 * HD]
    values = projected[:, 2 * HD : 3 * HD]
    out_gate = projected[:, 3 * HD :]
    low_rank = low(dot_last(hidden_one, rank_down))
    gate_input = dot(low_rank, up_head) + bias_head
    log_gates = jax.nn.log_sigmoid(gate_input) / 16.0

    ones = (jnp.arange(CHUNK)[:, None] >= jnp.arange(CHUNK)[None, :]).astype(F32)
    cumulated = jnp.einsum(
        "ij,cjk->cik", ones, log_gates.reshape(chunks, CHUNK, HD), precision=lax.Precision.HIGHEST
    )
    items = []
    state = jnp.zeros((HD, HD), F32)
    decay = jnp.ones((1, HD), F32)
    for n in range(chunks):
        at = slice(n * CHUNK, (n + 1) * CHUNK)
        q, k, v, b = queries[at], keys[at], values[at], cumulated[n]
        pair, visible, keep, last = chunk_masks(resets[at])
        middle, end = b[CHUNK // 2 - 1], b[-1:]
        eq, ek, eb = jnp.exp(b - middle), jnp.exp(middle - b), jnp.exp(b) * visible
        el = jnp.exp(end - b) * last
        qh, kh, qd, kc = low(q * eq), low(k * ek), low(q * eb), k * el
        scores = low(jnp.where(pair, dot_last(qh, kh), 0.0))
        carry = keep * jnp.exp(end)
        update = dot_rows(low(v), low(kc))
        state = carry * state + update
        decay = decay * carry
        items.append((q, k, low(v), pair, eq, ek, eb, el, qh, kh, qd, kc, scores, carry, update))
    state = states(9, False, state, decay)
    outs, befores = [], []
    for it in items:
        befores.append(state)
        outs.append(dot(it[12], it[2]) + dot_last(it[10], low(state)))
        state = it[13] * state + it[14]
    mixed = jnp.concatenate(outs, axis=0)
    head_scale = lax.rsqrt(jnp.mean(mixed * mixed, -1, keepdims=True) + HEAD_FLOOR)
    head_normed = mixed * head_scale
    normed_heads = head_normed * head_gain
    gate_sig = jax.nn.sigmoid(out_gate)
    gate_silu = out_gate * gate_sig
    gated = low(normed_heads * gate_silu)
    branch = low(dot_last(gated, mixer_w[:, 4 * HD :])).reshape(TEAM, half, width)
    hidden_two, middle = norm_forward(branch, own, gain_two[None])
    hidden_two = hidden_two.reshape(team_tokens, width)

    ffn_w = join_pieces(6, ffn_w)
    up_a = dot(hidden_two, ffn_w[:, :units])
    up_b = dot(hidden_two, ffn_w[:, units : 2 * units])
    ffn_sig = jax.nn.sigmoid(up_a)
    ffn_silu = up_a * ffn_sig
    activated = low(ffn_silu * up_b)
    down = dot_last(activated, ffn_w[:, 2 * units :]).astype(BF)
    down = lax.psum_scatter(down, ("y", "x"), scatter_dimension=0, tiled=True).astype(F32)
    result = lax.all_gather((middle + down).astype(BF), "c", axis=0, tiled=True)

    grad_act = dot(ffn_dy, ffn_w[:, 2 * units :])
    grad_gate = low(grad_act * up_b * ffn_sig * (1.0 + up_a * (1.0 - ffn_sig)))
    grad_upper = low(grad_act * ffn_silu)
    back = dot_last(grad_gate, ffn_w[:, :units]) + dot_last(grad_upper, ffn_w[:, units : 2 * units])
    grad_ffn_parts = [
        sum_pieces(dot_rows(ffn_dy, activated)),
        sum_pieces(dot_rows(hidden_two, jnp.concatenate([grad_gate, grad_upper], axis=1))),
    ]
    back = low(back).reshape(TEAM, half, width)
    grad_branch, grad_middle, grad_gain_two = norm_backward(back, own_dy, middle, gain_two[None])
    grad_branch = grad_branch.reshape(team_tokens, width)
    grad_out_proj = dot_rows(grad_branch, gated)
    grad_gated = dot(grad_branch, mixer_w[:, 4 * HD :])
    grad_normed = grad_gated * gate_silu
    grad_out_gate = grad_gated * normed_heads * gate_sig * (1.0 + out_gate * (1.0 - gate_sig))
    grad_head_gain = jnp.sum(grad_normed * head_normed, axis=0)
    scaled_heads = grad_normed * head_gain
    grad_mixed = head_scale * (
        scaled_heads - head_normed * jnp.mean(scaled_heads * head_normed, -1, keepdims=True)
    )

    douts = [low(grad_mixed[n * CHUNK : (n + 1) * CHUNK]) for n in range(chunks)]
    outgoing = [dot_rows(d, it[10]) for it, d in zip(items, douts)]
    dstate = jnp.zeros((HD, HD), F32)
    for it, o in zip(items[::-1], outgoing[::-1]):
        dstate = it[13] * dstate + o
    dstate = states(10, True, dstate, decay)
    grads = []
    for n in range(chunks - 1, -1, -1):
        q, k, v, pair, eq, ek, eb, el, qh, kh, qd, kc, scores, carry, update = items[n]
        do, state, ds = douts[n], befores[n], low(dstate)
        gs = low(jnp.where(pair, dot_last(do, v), 0.0))
        dv = dot_rows(scores, do) + dot_last(low(kc), ds)
        dq = dot(gs, kh) * eq + dot(do, low(state)) * eb
        gkc = dot(v, ds)
        dk = dot_rows(gs, qh) * ek + gkc * el
        dcum = dq * q - dk * k
        extra = jnp.sum(gkc * kc, axis=0) + carry[0] * jnp.sum(state * dstate, axis=0)
        dcum = dcum.at[-1].add(extra)
        dlog = jnp.einsum("ji,jk->ik", ones, dcum, precision=lax.Precision.HIGHEST)
        dstate = carry * dstate + outgoing[n]
        grads.append((dq, dk, dv, dlog))
    grads = grads[::-1]
    grad_queries, grad_keys, grad_values, grad_logs = (
        jnp.concatenate([gr[i] for gr in grads], axis=0) for i in range(4)
    )
    grad_gate_input = grad_logs * jax.nn.sigmoid(-gate_input) / 16.0
    grad_bias = jnp.sum(grad_gate_input, axis=0)
    grad_input_low = low(grad_gate_input)
    grad_decay_up = dot_rows(low_rank, grad_input_low)
    grad_proj = jnp.concatenate(
        [
            low(grad_queries * HD ** (-0.5)),
            low(grad_keys),
            low(grad_values),
            low(grad_out_gate),
        ],
        axis=1,
    )
    grad_rank_part = dot_last(grad_input_low, up_head)
    hidden_part = dot_last(grad_proj, mixer_w[:, : 4 * HD])
    lanes = 128
    hidden_part = jnp.concatenate(
        [low(hidden_part), jnp.pad(low(grad_rank_part), ((0, 0), (0, lanes - rank)))], axis=1
    ).reshape(TEAM, half, width + lanes)
    grad_mixer = sum_pieces(
        jnp.concatenate([dot_rows(hidden_one, grad_proj), grad_out_proj], axis=1)
    )
    down_pad = jnp.pad(rank_down, ((0, lanes - rank), (0, 0)))
    grad_inputs, grad_gain_one, grad_rank_down = first_norm(
        hidden_part, own, grad_middle, gain_one[None], down_pad
    )
    grad_inputs = grad_inputs.reshape(block, width)

    wide = jnp.concatenate([grad_gain_one, grad_gain_two, grad_rank_down[:rank]], axis=0)
    wide = jnp.pad(wide, ((0, 24 - wide.shape[0]), (0, 0)))
    wide = wide.reshape(24, 4 * groups, rows).transpose(1, 0, 2)
    heads = jnp.concatenate([grad_decay_up, grad_bias[None], grad_head_gain[None]], axis=0)
    heads = jnp.pad(heads, ((0, 24 - heads.shape[0]), (0, 0)))
    wide, heads, gains = finish(wide, heads)
    homes = exchange(7, *((route_weights_home, a, 2, False) for a in grad_ffn_parts))
    (mixer_home,) = exchange(8, (route_weights_home, grad_mixer, 2, False))
    ffn_down, ffn_pair = (a.astype(F32) for a in homes)
    mixer_home = mixer_home.reshape(2, rows, 5, HD).astype(F32)
    return (
        result,
        grad_inputs,
        wide[0],
        wide[1],
        mixer_home[:, :, :4].transpose(2, 1, 0, 3).reshape(4, rows, 2 * HD),
        wide[2 : 2 + rank].T,
        heads[:, :rank].transpose(1, 0, 2).reshape(rank, 2 * HD),
        heads[:, rank].reshape(2 * HD),
        jnp.sum(gains[:, rank + 1 - 16], axis=0),
        mixer_home[:, :, 4].transpose(0, 2, 1).reshape(2 * HD, rows),
        ffn_pair.reshape(2, rows, 2, units).transpose(2, 1, 0, 3).reshape(2, rows, 2 * units),
        ffn_down.transpose(0, 2, 1).reshape(2 * units, rows),
    )


def solution(mesh):
    devices = mesh.devices
    inner = Mesh(devices.reshape(devices.shape[0] // 4, 2, 2, devices.shape[1]), SEQ + ("c",))
    in_specs = (
        P(SEQ, None),
        P(SEQ, None),
        P(),
        P(SEQ),
        P(SEQ),
        P(None, SEQ, "c"),
        P(SEQ, None),
        P(None, "c"),
        P("c"),
        P(),
        P("c", SEQ),
        P(None, SEQ, "c"),
        P("c", SEQ),
    )
    out_specs = (
        P(SEQ, None),
        P(SEQ, None),
        P(SEQ),
        P(SEQ),
        P(None, SEQ, "c"),
        P(SEQ, None),
        P(None, "c"),
        P("c"),
        P(),
        P("c", SEQ),
        P(None, SEQ, "c"),
        P("c", SEQ),
    )
    return jax.shard_map(shards, mesh=inner, in_specs=in_specs, out_specs=out_specs, check_vma=False)
```

```python
import functools

import jax
import jax.numpy as jnp
from jax import lax
from jax.experimental import pallas as pl
from jax.experimental.pallas import tpu as pltpu
from jax.sharding import Mesh, PartitionSpec as P

HD = 512
CHUNK = 128
EPSILON = 1e-06
HEAD_FLOOR = 1.0
TEAM = 4

BF = jnp.bfloat16
F32 = jnp.float32
MESH = pl.DeviceIdType.MESH
ANY = pl.BlockSpec(memory_space=pl.ANY)
VMEM = pl.BlockSpec(memory_space=pltpu.VMEM)
DMA = pltpu.SemaphoreType.DMA

SEQ = ("zh", "zl", "y", "x")
FLIPS = ((1, 1), (0, 1), (1, 0), (0, 0))


def dot(a, b):
    return jnp.dot(a, b, preferred_element_type=F32)


def dot_rows(a, b):
    return lax.dot_general(a, b, (((0,), (0,)), ((), ())), preferred_element_type=F32)


def dot_last(a, b):
    return lax.dot_general(a, b, (((1,), (1,)), ((), ())), preferred_element_type=F32)


def low(v):
    return v.astype(BF)


def flip(index, by):
    return 1 - index if by else index


class Place:
    def __init__(self):
        self.zl, self.x, self.c = lax.axis_index("zl"), lax.axis_index("x"), lax.axis_index("c")
        self.member = self.zl * 2 + self.x


def greet_team(me, more=0):
    barrier = pltpu.get_barrier_semaphore()
    for n in range(1, 8):
        to = {"zl": flip(me.zl, n & 1), "x": flip(me.x, n & 2), "c": flip(me.c, n & 4)}
        pl.semaphore_signal(barrier, inc=1, device_id=to, device_id_type=MESH)
    pl.semaphore_wait(barrier, 7 + more)


def others(me):
    zh, y, highs = lax.axis_index("zh"), lax.axis_index("y"), lax.axis_size("zh")
    for k in range(highs):
        for n in range(8):
            yield lax.rem(zh + k, highs), flip(me.zl, n & 1), flip(y, n & 2), flip(me.x, n & 4), k + n == 0


def greet_all(me):
    barrier = pltpu.get_barrier_semaphore()
    count = 0
    for zh, zl, y, x, own in others(me):
        for f in range(2):
            if own and not f:
                continue
            to = {"zh": zh, "zl": zl, "y": y, "x": x, "c": flip(me.c, f)}
            pl.semaphore_signal(barrier, inc=1, device_id=to, device_id_type=MESH)
            count += 1
    pl.semaphore_wait(barrier, count)


def route_member(me):
    out, arrive = [], []
    for fz, fx in FLIPS:
        zl, x = flip(me.zl, fz), flip(me.x, fx)
        own = (fz, fx) == (0, 0)
        out.append((zl * 2 + x, me.member, {"zl": zl, "x": x}, own))
        arrive.append((zl * 2 + x, own))
    return out, arrive


def chip_index(zh, zl, y, x):
    return ((zh * 2 + zl) * 2 + y) * 2 + x


def route_all(me):
    mine = chip_index(lax.axis_index("zh"), me.zl, lax.axis_index("y"), me.x)
    out, arrive = [], []
    for zh, zl, y, x, own in others(me):
        chip = chip_index(zh, zl, y, x)
        out.append((chip, mine, {"zh": zh, "zl": zl, "y": y, "x": x}, own))
        arrive.append((chip, own))
    return out, arrive


def route_halves(me):
    mine = me.c == me.zl
    out, arrive = [], []
    for fz, fx in FLIPS:
        zl, x = flip(me.zl, fz), flip(me.x, fx)
        own = mine if (fz, fx) == (0, 0) else False
        out.append((0, me.x * 2 + me.c, {"zl": zl, "x": x, "c": me.zl}, own))
    for fc, fx in FLIPS:
        c, x = flip(me.c, fc), flip(me.x, fx)
        own = mine if (fc, fx) == (0, 0) else False
        arrive.append((x * 2 + c, own))
    return out, arrive


def route_owners(me):
    mine = me.c == me.zl
    out, arrive = [], []
    for fc, fx in FLIPS:
        c, x = flip(me.c, fc), flip(me.x, fx)
        own = mine if (fc, fx) == (0, 0) else False
        out.append((x * 2 + c, me.member, {"zl": me.c, "x": x, "c": c}, own))
    for fz, fx in FLIPS:
        zl, x = flip(me.zl, fz), flip(me.x, fx)
        own = mine if (fz, fx) == (0, 0) else False
        arrive.append((zl * 2 + x, own))
    return out, arrive


def route_weights(me):
    mine = (me.c == me.zl) & (me.c == me.x)
    out, arrive = [], []
    for f in (1, 0):
        x = flip(me.x, f)
        own = (me.c == me.zl) & (me.c == x) & (me.x == me.c) if not f else False
        out.append((x, me.zl, {"zl": me.c, "x": x, "c": me.x}, own))
    for f in (1, 0):
        zl = flip(me.zl, f)
        own = mine if not f else False
        arrive.append((zl, own))
    return out, arrive


def route_weights_home(me):
    mine = (me.c == me.zl) & (me.c == me.x)
    out, arrive = [], []
    for f in (1, 0):
        zl = flip(me.zl, f)
        own = mine if not f else False
        out.append((zl, me.x, {"zl": zl, "x": me.c, "c": me.zl}, own))
    for f in (1, 0):
        x = flip(me.x, f)
        own = mine if not f else False
        arrive.append((x, own))
    return out, arrive


def when(condition, run):
    if condition is True:
        run()
    elif condition is not False:
        pl.when(condition)(run)


def unless(condition, run):
    if condition is False:
        run()
    elif condition is not True:
        pl.when(jnp.logical_not(condition))(run)


class Transfer:
    def __init__(self, route, source, target, send, arrive):
        self.route, self.source, self.target, self.send, self.arrive = route, source, target, send, arrive

    def _remote(self, n):
        index, slot, to, own = self.route[0][n]
        return pltpu.make_async_remote_copy(
            src_ref=self.source(index),
            dst_ref=self.target(slot),
            send_sem=self.send.at[n],
            recv_sem=self.arrive.at[slot],
            device_id=to,
            device_id_type=MESH,
        )

    def _local(self, n):
        index, slot, to, own = self.route[0][n]
        return pltpu.make_async_copy(self.source(index), self.target(slot), self.send.at[n])

    def start(self):
        for n, (_, _, _, own) in enumerate(self.route[0]):
            unless(own, lambda: self._remote(n).start())
            when(own, lambda: self._local(n).start())

    def wait_arrive(self):
        for slot, own in self.route[1]:
            ref = self.target(slot)

            def arrived():
                pltpu.make_async_copy(ref, ref, self.arrive.at[slot]).wait()

            unless(own, arrived)

    def wait_local(self):
        for n, (_, _, _, own) in enumerate(self.route[0]):
            when(own, lambda: self._local(n).wait())

    def wait_sent(self):
        for n, (_, _, _, own) in enumerate(self.route[0]):
            unless(own, lambda: self._remote(n).wait_send())

    def wait(self):
        self.wait_arrive()
        self.wait_local()
        self.wait_sent()


def copy_to(src, dst, send, arrive, to):
    return pltpu.make_async_remote_copy(
        src_ref=src, dst_ref=dst, send_sem=send, recv_sem=arrive, device_id=to, device_id_type=MESH
    )


def wait_for(ref, sem):
    pltpu.make_async_copy(ref, ref, sem).wait()


def member_slots(me, two):
    along = me.zl * 2 + 1 - me.x, {"x": 1 - me.x}
    over = (1 - me.zl) * 2 + me.x, {"zl": 1 - me.zl}
    one, double = (over, along) if two == "x" else (along, over)
    return one[0], double[0], (1 - me.zl) * 2 + 1 - me.x, one[1], double[1]


class MemberSpread:
    def __init__(self, me, source, target, send, arrive, two="x"):
        self.target, self.arrive = target, arrive
        mine = me.member
        one, double, across, to_one, to_double = member_slots(me, two)
        self.slots = one, double, across
        self.direct = [
            copy_to(source, target(mine), send.at[0], arrive.at[mine], to_one),
            copy_to(source, target(mine), send.at[1], arrive.at[mine], to_double),
        ]
        self.local = pltpu.make_async_copy(source, target(mine), arrive.at[mine])
        self.forward = copy_to(target(one), target(one), send.at[2], arrive.at[one], to_double)

    def start(self):
        for copy in self.direct:
            copy.start()
        self.local.start()

    def relay(self):
        wait_for(self.target(self.slots[0]), self.arrive.at[self.slots[0]])
        self.forward.start()

    def wait(self):
        for slot in self.slots[1:]:
            wait_for(self.target(slot), self.arrive.at[slot])
        self.local.wait()
        for copy in self.direct + [self.forward]:
            copy.wait_send()


class HalvesSpread:
    def __init__(self, me, source, target, send, arrive):
        self.me, self.target, self.arrive = me, target, arrive
        mine = me.x * 2 + me.c
        self.home = me.c == me.zl
        self.direct = [
            copy_to(source, target(mine), send.at[0], arrive.at[mine], {"zl": 1 - me.zl, "c": me.zl}),
            copy_to(source, target(mine), send.at[1], arrive.at[mine], {"x": 1 - me.x, "c": me.zl}),
        ]
        self.near = copy_to(source, target(mine), send.at[2], arrive.at[mine], {"c": 1 - me.c})
        self.local = pltpu.make_async_copy(source, target(mine), send.at[2])
        self.near_slots = [me.x * 2 + c for c in range(2)]
        self.far_slots = [(1 - me.x) * 2 + c for c in range(2)]
        self.forwards = [
            copy_to(target(slot), target(slot), send.at[3 + c], arrive.at[slot], {"x": 1 - me.x})
            for c, slot in enumerate(self.near_slots)
        ]

    def start(self):
        for copy in self.direct:
            copy.start()
        pl.when(self.home)(self.local.start)
        unless(self.home, self.near.start)

    def relay(self):
        @pl.when(jnp.logical_not(self.home))
        def _():
            for slot, forward in zip(self.near_slots, self.forwards):
                wait_for(self.target(slot), self.arrive.at[slot])
                forward.start()

    def wait(self):
        me = self.me

        @pl.when(self.home)
        def _():
            self.local.wait()
            slot = me.x * 2 + 1 - me.c
            wait_for(self.target(slot), self.arrive.at[slot])

        for slot in self.far_slots:
            wait_for(self.target(slot), self.arrive.at[slot])
        for copy in self.direct:
            copy.wait_send()

        @pl.when(jnp.logical_not(self.home))
        def _():
            self.near.wait_send()
            for forward in self.forwards:
                forward.wait_send()


class MemberSum:
    def __init__(self, me, source, got, relayed, staged, send, arrive, two="x"):
        self.me, self.source, self.got, self.relayed, self.staged = me, source, got, relayed, staged
        self.arrive = arrive
        self.one, double, across, to_one, to_double = member_slots(me, two)
        self.direct = [
            copy_to(source(across), relayed(0), send.at[0], arrive.at[0], to_double),
            copy_to(source(double), got(0), send.at[1], arrive.at[1], to_double),
        ]
        self.onward = copy_to(staged(0), got(1), send.at[2], arrive.at[2], to_one)

    def start(self):
        for copy in self.direct:
            copy.start()

    def relay(self):
        wait_for(self.relayed(0), self.arrive.at[0])
        own = self.source(self.one)[...].astype(F32)
        self.staged(0)[...] = low(own + self.relayed(0)[...].astype(F32))
        self.onward.start()

    def total(self):
        wait_for(self.got(0), self.arrive.at[1])
        wait_for(self.got(1), self.arrive.at[2])
        total = self.source(self.me.member)[...].astype(F32)
        return total + self.got(0)[...].astype(F32) + self.got(1)[...].astype(F32)

    def wait_sent(self):
        for copy in self.direct + [self.onward]:
            copy.wait_send()


class OwnersSum:
    def __init__(self, me, source, got, relayed, staged, send, arrive):
        self.me, self.source, self.got, self.relayed, self.staged = me, source, got, relayed, staged
        self.arrive = arrive
        self.home = me.c == me.zl
        mine, other = me.x * 2, (1 - me.x) * 2
        self.near = copy_to(source(mine + 1 - me.c), got(0), send.at[0], arrive.at[0], {"c": 1 - me.c})
        self.local = pltpu.make_async_copy(source(mine + me.c), got(0), send.at[1])
        self.across = [
            copy_to(source(other + c), got(1), send.at[2 + c], arrive.at[1], {"x": 1 - me.x, "c": c})
            for c in range(2)
        ]
        self.first = [
            copy_to(source(other + c), relayed(c), send.at[2 + c], arrive.at[3 + c], {"x": 1 - me.x})
            for c in range(2)
        ]
        self.onward = [
            copy_to(staged(c), got(2), send.at[4 + c], arrive.at[2], {"zl": me.c, "c": c})
            for c in range(2)
        ]

    def start(self):
        @pl.when(self.home)
        def _():
            for copy in self.across + [self.near, self.local]:
                copy.start()

        @pl.when(jnp.logical_not(self.home))
        def _():
            for copy in self.first:
                copy.start()

    def relay(self):
        @pl.when(jnp.logical_not(self.home))
        def _():
            for c in range(2):
                wait_for(self.relayed(c), self.arrive.at[3 + c])
                own = self.source(self.me.x * 2 + c)[...].astype(F32)
                self.staged(c)[...] = low(own + self.relayed(c)[...].astype(F32))
                self.onward[c].start()

    def total(self):
        pl.when(self.home)(self.local.wait)
        unless(self.home, lambda: wait_for(self.got(0), self.arrive.at[0]))
        wait_for(self.got(1), self.arrive.at[1])
        wait_for(self.got(2), self.arrive.at[2])
        return sum(self.got(k)[...].astype(F32) for k in range(3))

    def wait_sent(self):
        @pl.when(self.home)
        def _():
            for copy in self.across + [self.near]:
                copy.wait_send()

        @pl.when(jnp.logical_not(self.home))
        def _():
            for copy in self.first + self.onward:
                copy.wait_send()


class Placed(Transfer):
    def __init__(self, route, source, there, target, send, arrive):
        super().__init__(route, source, target, send, arrive)
        self.there = there

    def _remote(self, n):
        index, slot, to, own = self.route[0][n]
        return pltpu.make_async_remote_copy(
            src_ref=self.source(index),
            dst_ref=self.there(slot),
            send_sem=self.send.at[n],
            recv_sem=self.arrive.at[slot],
            device_id=to,
            device_id_type=MESH,
        )


LANES = 128


def keyed_mask(start, starts_row, starts_column):
    rows = lax.broadcasted_iota(jnp.int32, (CHUNK, CHUNK), 0)
    columns = lax.broadcasted_iota(jnp.int32, (CHUNK, CHUNK), 1)
    ids = jnp.sum((rows + start >= starts_row[0:1]).astype(F32), axis=1, keepdims=True)
    places = lax.broadcasted_iota(jnp.int32, starts_column.shape, 1)
    ids_row = jnp.sum((places + start >= starts_column[...]).astype(F32), axis=0, keepdims=True)
    before = jnp.sum((starts_row[0:1] < start).astype(F32), axis=1, keepdims=True)
    final = ids_row[:, CHUNK - 1 :]
    pair = (rows >= columns) & (ids == ids_row)
    visible = (ids == before).astype(F32)
    keep = (final == before).astype(F32)
    return pair, visible, keep, (ids == final).astype(F32)


class StatePass:
    def __init__(self, back, local, decay, out, rounded, got, got_decay, sums, sum_decays, stage, stage_decay,
                 entering, leave, enter, send, arrive, far_send, far_arrive, leave_send, leave_arrive):
        self.__dict__.update(locals())
        self.zh, c, y = lax.axis_index("zh"), lax.axis_index("c"), lax.axis_index("y")
        self.highs = lax.axis_size("zh")
        self.mine = c * 2 + y
        self.quarter = local.shape[0] // 4
        self.partners = []
        for fc, fy in ((1, 1), (0, 1), (1, 0)):
            to_c, to_y = flip(c, fc), flip(y, fy)
            self.partners.append((to_c * 2 + to_y, {"c": to_c, "y": to_y}))
        self.order = range(3, -1, -1) if back else range(4)
        self.moves, self.outs = [], []

    def begin(self):
        self.rounded[...] = low(self.local[...])
        for n, (index, to) in enumerate(self.partners):
            rows = self.rounded.at[pl.ds(index * self.quarter, self.quarter)]
            self.moves.append(copy_to(rows, self.got.at[self.mine], self.send.at[0, n], self.arrive.at[0, self.mine], to))
            self.moves.append(
                copy_to(self.decay, self.got_decay.at[self.mine], self.send.at[1, n], self.arrive.at[1, self.mine], to)
            )
        for move in self.moves:
            move.start()
        self.got[self.mine] = self.rounded[pl.ds(self.mine * self.quarter, self.quarter)]
        self.got_decay[self.mine] = self.decay[...]

    def needs(self, source, target):
        return (source > target) if self.back else (source < target)

    def far(self, n, to):
        zh = self.zh
        return (
            copy_to(self.stage, self.sums.at[zh], self.far_send.at[0, n], self.far_arrive.at[0, zh], {"zh": to}),
            copy_to(
                self.stage_decay, self.sum_decays.at[zh], self.far_send.at[1, n], self.far_arrive.at[1, zh], {"zh": to}
            ),
        )

    def combine(self):
        for index, _ in self.partners:
            wait_for(self.got.at[index], self.arrive.at[0, index])
            wait_for(self.got_decay.at[index], self.arrive.at[1, index])
        total, total_decay = None, None
        for k in self.order:
            piece, d = self.got[k].astype(F32), self.got_decay[k][:1]
            total = piece if total is None else d * total + piece
            total_decay = d if total_decay is None else total_decay * d
        self.stage[...] = low(total)
        self.stage_decay[...] = jnp.broadcast_to(total_decay, self.stage_decay.shape)
        for n in range(1, self.highs):
            to = lax.rem(self.zh + n, self.highs)

            @pl.when(self.needs(self.zh, to))
            def _(n=n, to=to):
                for move in self.far(n, to):
                    move.start()

    def spread(self):
        self.entering[...] = jnp.zeros_like(self.entering)
        for n in range(self.highs):
            k = self.highs - 1 - n if self.back else n

            @pl.when(self.needs(k, self.zh))
            def _(k=k):
                wait_for(self.sums.at[k], self.far_arrive.at[0, k])
                wait_for(self.sum_decays.at[k], self.far_arrive.at[1, k])
                self.entering[...] = self.sum_decays[k][:1] * self.entering[...] + self.sums[k].astype(F32)

        state = self.entering[...]
        for k in self.order:
            self.leave[k] = low(state)
            state = self.got_decay[k][:1] * state + self.got[k].astype(F32)
        for n, (index, to) in enumerate(self.partners):
            self.outs.append(
                copy_to(
                    self.leave.at[index], self.enter.at[self.mine], self.leave_send.at[n],
                    self.leave_arrive.at[self.mine], to,
                )
            )
        for move in self.outs:
            move.start()
        self.enter[self.mine] = self.leave[self.mine]

    def finish(self):
        for index, _ in self.partners:
            wait_for(self.enter.at[index], self.leave_arrive.at[index])
        for k in range(4):
            self.out[pl.ds(k * self.quarter, self.quarter)] = self.enter[k].astype(F32)

    def wait_sent(self):
        for move in self.moves + self.outs:
            move.wait_send()
        for n in range(1, self.highs):
            to = lax.rem(self.zh + n, self.highs)

            @pl.when(self.needs(self.zh, to))
            def _(n=n, to=to):
                for move in self.far(n, to):
                    move.wait_send()


def state_pass_scratch(highs):
    quarter = HD // 4
    return [
        pltpu.VMEM((HD, HD), BF),
        pltpu.VMEM((4, quarter, HD), BF),
        pltpu.VMEM((4, 8, HD), F32),
        pltpu.VMEM((highs, quarter, HD), BF),
        pltpu.VMEM((highs, 8, HD), F32),
        pltpu.VMEM((quarter, HD), BF),
        pltpu.VMEM((8, HD), F32),
        pltpu.VMEM((quarter, HD), F32),
        pltpu.VMEM((4, quarter, HD), BF),
        pltpu.VMEM((4, quarter, HD), BF),
        DMA((2, 3)),
        DMA((2, 4)),
        DMA((2, highs)),
        DMA((2, highs)),
        DMA((3,)),
        DMA((4,)),
    ]


STATE_REFS = 16


def forward_kernel(*refs):
    (
        mixer_in, mixer_out, ffn_in, ffn_out, small, ups, own, cot, starts_row, starts_column, head_gain,
        mixer_w, merge_w, pair_w, down_w, gains, cots, hidden, low_rank, gate, cumulated, projected, mixed, gated,
        befores, decay, second, middle,
        mixer_v, merge_v, projected_v, befores_v, inputs, smalls, ups_got, columns, state, partial, got, relayed, staged, line,
        own_send, own_arrive, far_send, arrive, small_send, small_arrive, ups_sem, inputs_send, inputs_arrive,
        cot_send, cot_arrive, sum_send, sum_arrive, spread_send, spread_arrive, saves,
    ) = refs[:-STATE_REFS]
    me = Place()
    zh, y, highs = lax.axis_index("zh"), lax.axis_index("y"), lax.axis_size("zh")
    units = down_w.shape[-1]
    width = own.shape[1]
    chunks = hidden.shape[0]
    first = ((zh * 2 + me.c) * 2 + y) * (chunks * CHUNK)
    greet_all(me)
    twin, side = {"c": 1 - me.c}, {"y": 1 - y}

    def own_source(part, k):
        if part < 5:
            at = pl.ds(pl.multiple_of(k * HD, HD), HD)
            return mixer_out.at[:, at] if part == 4 else mixer_in.at[part, :, at]
        at = pl.ds(pl.multiple_of(k * units, LANES), units)
        return ffn_out.at[:, at] if part == 7 else ffn_in.at[part - 5, :, at]

    def piece(at_zh, at_y, x, part, zl=slice(None)):
        if part < 4:
            return mixer_v.at[at_zh, zl, at_y, x, :, pl.ds(part * HD, HD)]
        if part == 4:
            return merge_v.at[at_zh, zl, at_y, x]
        if part < 7:
            return pair_w.at[at_zh, zl, at_y, x, :, pl.ds((part - 5) * units, units)]
        return down_w.at[at_zh, zl, at_y, x]

    firsts = [
        Placed(
            route_weights(me),
            lambda k, p=p: own_source(p, k),
            lambda zl, p=p: piece(zh, y, me.x, p, zl),
            lambda zl, p=p: piece(zh, y, me.c, p, zl),
            own_send.at[p],
            own_arrive.at[p],
        )
        for p in range(8)
    ]
    count = [0]
    sent = []

    def forward(at_zh, at_y, part, to):
        place = piece(at_zh, at_y, me.c, part)
        copy = copy_to(place, place, far_send.at[count[0]], arrive.at[at_zh, at_y, me.c, part], to)
        copy.start()
        count[0] += 1
        sent.append(copy)

    def arrived(at_zh, at_y, x, part):
        wait_for(piece(at_zh, at_y, x, part), arrive.at[at_zh, at_y, x, part])

    def send_own(part):
        firsts[part].wait_arrive()
        firsts[part].wait_local()
        for k in range(1, highs):
            forward(zh, y, part, {"zh": lax.rem(zh + k, highs)})
        forward(zh, y, part, side)
        forward(zh, y, part, twin)

    def pass_high(part):
        for k in range(1, highs):
            at_zh = lax.rem(zh + k, highs)
            arrived(at_zh, y, me.c, part)
            forward(at_zh, y, part, side)
            forward(at_zh, y, part, twin)

    def pass_side(part):
        for k in range(highs):
            at_zh = lax.rem(zh + k, highs)
            arrived(at_zh, 1 - y, me.c, part)
            forward(at_zh, 1 - y, part, twin)

    def complete(part):
        for k in range(highs):
            at_zh = lax.rem(zh + k, highs)
            arrived(at_zh, y, 1 - me.c, part)
            arrived(at_zh, 1 - y, 1 - me.c, part)

    save_count = [0]
    saved = []

    def save(source, target):
        copy = pltpu.make_async_copy(source, target, saves.at[save_count[0]])
        copy.start()
        save_count[0] += 1
        saved.append(copy)

    order = (1, 2, 0, 3, 4)
    for part in order:
        firsts[part].start()
    move_small = Transfer(route_all(me), lambda _: small, lambda k: smalls.at[k], small_send, small_arrive)
    move_small.start()
    lend = copy_to(ups, ups_got, ups_sem.at[0], ups_sem.at[1], twin)
    lend.start()
    for part in order:
        send_own(part)
    move_inputs = HalvesSpread(me, own, lambda k: inputs.at[k], inputs_send, inputs_arrive)
    move_cot = MemberSpread(me, cot, lambda k: cots.at[k], cot_send, cot_arrive)
    move_inputs.start()
    for part in (5, 6, 7):
        firsts[part].start()
    move_inputs.relay()
    pass_high(1)
    move_small.wait()
    lend.wait()
    owner_rows = smalls.shape[1]
    for n in range(smalls.shape[0]):
        columns[pl.ds(n * owner_rows, owner_rows)] = smalls[n].astype(F32)
    gains[...] = columns[...].T
    pass_high(2)
    move_inputs.wait()

    up = jnp.where(me.c == me.zl, ups[...], ups_got[...])
    rank_up, bias = low(up[:16]), up[16:17]
    down = low(columns[...])
    lower = (
        lax.broadcasted_iota(jnp.int32, (CHUNK, CHUNK), 0)
        >= lax.broadcasted_iota(jnp.int32, (CHUNK, CHUNK), 1)
    ).astype(F32)

    def gates_step(n, _):
        x = inputs[n].astype(F32)
        scale = lax.rsqrt(jnp.mean(x * x, -1, keepdims=True) + EPSILON)
        h = low(x * scale * gains[0:1])
        hidden[n] = h
        z = low(dot(h, down))
        low_rank[n] = z
        a = dot(z[:, 2:18], rank_up) + bias
        gate[n] = a
        log_gate = (jnp.minimum(a, 0.0) - jnp.log1p(jnp.exp(-jnp.abs(a)))) / 16.0
        cumulated[n] = jnp.dot(
            lower, log_gate, precision=lax.Precision.HIGHEST, preferred_element_type=F32
        )
        return 0

    lax.fori_loop(0, chunks, gates_step, 0)

    def project(part):
        rows = hidden[...].reshape(chunks * CHUNK, width)
        block = mixer_v[:, :, :, :, :, pl.ds(part * HD, HD)].reshape(width, HD)
        result = dot(rows, block)
        if part == 0:
            result = result * HD ** (-0.5)
        projected_v[part] = result.reshape(chunks, CHUNK, HD)
        save(projected_v.at[part], projected.at[part])

    pass_side(1)
    pass_side(2)
    pass_high(0)
    complete(1)
    project(1)
    complete(2)
    project(2)
    pass_high(3)

    state[...] = jnp.zeros_like(state)
    decay[...] = jnp.ones_like(decay)

    def masks(n):
        return keyed_mask(first + n * CHUNK, starts_row, starts_column)

    def local_step(n, _):
        _, _, keep, last = masks(n)
        b = cumulated[n]
        end = b[CHUNK - 1 :]
        kc = low(projected_v[1, n] * jnp.exp(end - b) * last)
        update = dot_rows(low(projected_v[2, n]), kc)
        befores_v[n] = update
        carry = keep * jnp.exp(end)
        state[...] = carry * state[...] + update
        decay[...] = decay[...] * carry
        return 0

    lax.fori_loop(0, chunks, local_step, 0)
    states = StatePass(False, state, decay, state, *refs[-STATE_REFS:])
    states.begin()
    pass_side(0)
    pass_high(4)
    for part in (5, 6, 7):
        send_own(part)
    complete(0)
    project(0)
    states.combine()
    pass_side(3)
    pass_side(4)

    def inner_step(n, _):
        pair, _, _, _ = masks(n)
        b = cumulated[n]
        mid = b[CHUNK // 2 - 1 : CHUNK // 2]
        qh = low(projected_v[0, n] * jnp.exp(b - mid))
        kh = low(projected_v[1, n] * jnp.exp(mid - b))
        scores = low(jnp.where(pair, dot_last(qh, kh), 0.0))
        mixed[n] = dot(scores, low(projected_v[2, n]))
        return 0

    lax.fori_loop(0, chunks, inner_step, 0)
    states.spread()
    complete(3)
    project(3)
    states.finish()

    def outer_step(n, _):
        _, visible, keep, _ = masks(n)
        b = cumulated[n]
        before = state[...]
        qd = low(projected_v[0, n] * jnp.exp(b) * visible)
        out = mixed[n] + dot_last(qd, low(before))
        mixed[n] = out
        update = befores_v[n]
        befores_v[n] = before
        state[...] = keep * jnp.exp(b[CHUNK - 1 :]) * before + update
        scale = lax.rsqrt(jnp.mean(out * out, -1, keepdims=True) + HEAD_FLOOR)
        u = projected_v[3, n]
        gated[n] = low(out * scale * head_gain[...] * (u * jax.nn.sigmoid(u)))
        return 0

    lax.fori_loop(0, chunks, outer_step, 0)
    save(befores_v, befores)
    complete(4)

    def merge_step(n, _):
        partial[n] = low(dot_last(gated[n], merge_v[...].reshape(width, HD)))
        return 0

    lax.fori_loop(0, chunks, merge_step, 0)

    steps = sum_send.shape[0]
    rows = own.shape[0] // steps

    def rows_of(ref, k, n):
        return ref.at[k, pl.ds(n * rows, rows)]

    sums = [
        OwnersSum(
            me,
            lambda k, n=n: rows_of(partial, k, n),
            lambda k, n=n: rows_of(got, k, n),
            lambda k, n=n: rows_of(relayed, k, n),
            lambda k, n=n: rows_of(staged, k, n),
            sum_send.at[n],
            sum_arrive.at[n],
        )
        for n in range(steps)
    ]
    spreads = [
        MemberSpread(
            me,
            line.at[pl.ds(n * rows, rows)],
            lambda k, n=n: rows_of(second, k, n),
            spread_send.at[n],
            spread_arrive.at[n],
        )
        for n in range(steps)
    ]
    for transfer in sums:
        transfer.start()
    pass_high(5)
    for transfer in sums:
        transfer.relay()
    for n in range(steps):
        at = pl.ds(n * rows, rows)
        total = own[at].astype(F32) + sums[n].total()
        middle[at] = total
        scale = lax.rsqrt(jnp.mean(total * total, -1, keepdims=True) + EPSILON)
        line[at] = low(total * scale * gains[1:2])
        spreads[n].start()
        if n:
            spreads[n - 1].relay()
    spreads[steps - 1].relay()
    move_cot.start()
    save(mixer_v, mixer_w)
    save(merge_v, merge_w)
    pass_high(6)
    pass_side(5)
    move_cot.relay()
    pass_high(7)
    for part in (6, 7):
        pass_side(part)
    for part in (5, 6, 7):
        complete(part)
    for transfer in sums:
        transfer.wait_sent()
    for transfer in spreads:
        transfer.wait()
    states.wait_sent()
    move_cot.wait()
    for transfer in firsts:
        transfer.wait_sent()
    for copy in sent:
        copy.wait_send()
    for copy in saved:
        copy.wait()


def starts_arrays(starts):
    starts = jnp.pad(starts, (0, LANES - starts.shape[0]), constant_values=jnp.int32(1 << 30))
    return jnp.broadcast_to(starts[None], (8, LANES)), jnp.broadcast_to(starts[:16, None], (16, LANES))


def forward(mixer_in, mixer_out, ffn_in, ffn_out, small, ups, own, cot, starts, head_gain):
    highs = lax.axis_size("zh")
    chips = highs * 8
    rows, half, width = small.shape[0], own.shape[0], own.shape[1]
    units = ffn_out.shape[1] // 2
    chunks = TEAM * half // CHUNK

    def shape(*dims, kind=BF):
        return jax.ShapeDtypeStruct(dims, kind)

    shapes = [
        (shape(highs, 2, 2, 2, rows, 4 * HD), ANY),
        (shape(highs, 2, 2, 2, rows, HD), ANY),
        (shape(highs, 2, 2, 2, rows, 2 * units), ANY),
        (shape(highs, 2, 2, 2, rows, units), ANY),
        (shape(LANES, width, kind=F32), VMEM),
        (shape(TEAM, half, width), ANY),
        (shape(chunks, CHUNK, width), VMEM),
        (shape(chunks, CHUNK, LANES), VMEM),
        (shape(chunks, CHUNK, HD, kind=F32), VMEM),
        (shape(chunks, CHUNK, HD, kind=F32), VMEM),
        (shape(4, chunks, CHUNK, HD, kind=F32), ANY),
        (shape(chunks, CHUNK, HD, kind=F32), VMEM),
        (shape(chunks, CHUNK, HD), VMEM),
        (shape(chunks, HD, HD, kind=F32), ANY),
        (shape(8, HD, kind=F32), VMEM),
        (shape(TEAM, half, width), VMEM),
        (shape(half, width, kind=F32), VMEM),
    ]
    arrays = [mixer_in, mixer_out, ffn_in, ffn_out, small, ups, own, cot, *starts_arrays(starts), head_gain]
    scratch = [
        shapes[0][0],
        shapes[1][0],
        shapes[10][0],
        shapes[13][0],
        shape(TEAM, half, width),
        shape(chips, rows, LANES),
        shape(*ups.shape, kind=F32),
        shape(width, LANES, kind=F32),
        shape(HD, HD, kind=F32),
        shape(TEAM, half, width),
        shape(3, half, width),
        shape(2, half, width),
        shape(2, half, width),
        shape(half, width),
    ]
    used = arrays + scratch + [a for a, place in shapes if place is VMEM]
    size = sum(a.size * a.dtype.itemsize for a in used)
    forwards = 8 * ((highs - 1) + highs + 2 * highs)
    sems = [
        (8, 2), (8, 2), (forwards,), (highs, 2, 2, 8), (chips,), (chips,), (2,), (5,), (4,), (3,), (4,),
        (STEPS, 6), (STEPS, 5), (STEPS, 3), (STEPS, 4), (7,),
    ]
    return pl.pallas_call(
        forward_kernel,
        out_shape=[a for a, _ in shapes],
        in_specs=[VMEM] * len(arrays),
        out_specs=[place for _, place in shapes],
        scratch_shapes=[pltpu.VMEM(a.shape, a.dtype) for a in scratch]
        + [DMA(n) for n in sems]
        + state_pass_scratch(highs),
        compiler_params=pltpu.CompilerParams(
            collective_id=0, has_side_effects=True, vmem_limit_bytes=min(size + (14 << 20), 62 << 20)
        ),
        name="forward",
    )(*arrays)


STEPS = 4


CROSS = [(0, 1), (1, 0)]


TILE = 256


def grads_kernel(count, *refs):
    lefts, rights = refs[:count], refs[count : 2 * count]
    away, keep = refs[2 * count : 2 * count + 2]
    ordered = refs[2 * count + 2 : 3 * count + 2]
    out, got, send, arrive = refs[3 * count + 2 :]
    zh, y, c = lax.axis_index("zh"), lax.axis_index("y"), lax.axis_index("c")
    highs = lax.axis_size("zh")
    chips, rows, _ = lefts[0].shape
    half = chips // 2 * rows
    quarter = half // 2
    barrier = pltpu.get_barrier_semaphore()
    pl.semaphore_signal(barrier, inc=1, device_id={"c": 1 - c}, device_id_type=MESH)
    for left, order in zip(lefts, ordered):
        n = 0
        for x in (1 - c, c):
            for at_y in (1 - y, y):
                for k in range(highs):
                    for zl in range(2):
                        chip = chip_index(lax.rem(zh + k, highs), zl, at_y, x)
                        order[pl.ds(n * rows, rows)] = left[chip]
                        n += 1
    pl.semaphore_wait(barrier, 1)

    def move(n):
        return pltpu.make_async_remote_copy(
            src_ref=out.at[n],
            dst_ref=got.at[n],
            send_sem=send.at[n],
            recv_sem=arrive.at[n],
            device_id={"c": 1 - c},
            device_id_type=MESH,
        )

    def send_tile(order, right, n, column, width):
        block = dot(order[pl.ds(0, half)], right[:, pl.ds(column, width)])
        if width == TILE:
            out[n] = low(block)
        else:
            out[n, :, pl.ds(0, width)] = low(block)
        move(n).start()

    def add_tile(order, right, n, column, width, start):
        block = dot(order[pl.ds(half, half)], right[:, pl.ds(column, width)])
        move(n).wait_recv()
        block = low(block + got[n, :, pl.ds(0, width)].astype(F32))
        away[:, pl.ds(start + column, width)] = block[:quarter]
        keep[:, pl.ds(start + column, width)] = block[quarter:]

    tile, start = 0, 0
    for order, right in zip(ordered, rights):
        whole, odd = right.shape[1] // TILE, right.shape[1] % TILE

        def send_step(n, _, order=order, right=right, tile=tile):
            send_tile(order, right, tile + n, pl.multiple_of(n * TILE, TILE), TILE)
            return 0

        lax.fori_loop(0, whole, send_step, 0)
        if odd:
            send_tile(order, right, tile + whole, whole * TILE, odd)
        tile += whole + (odd > 0)
    total = tile
    tile = 0
    for order, right in zip(ordered, rights):
        whole, odd = right.shape[1] // TILE, right.shape[1] % TILE

        def add_step(n, _, order=order, right=right, tile=tile, start=start):
            add_tile(order, right, tile + n, pl.multiple_of(n * TILE, TILE), TILE, start)
            return 0

        lax.fori_loop(0, whole, add_step, 0)
        if odd:
            add_tile(order, right, tile + whole, whole * TILE, odd, start)
        tile += whole + (odd > 0)
        start += right.shape[1]

    def sent(n, _):
        move(n).wait_send()
        return 0

    lax.fori_loop(0, total, sent, 0)


def weight_grads(call_id, pairs):
    highs = lax.axis_size("zh")
    count = len(pairs)
    team_tokens, width = pairs[0][0].shape
    chips = highs * 8
    rows = width // chips
    lefts = [left.T.reshape(chips, rows, team_tokens) for left, _ in pairs]
    rights = [right for _, right in pairs]
    cols = sum(r.shape[1] for r in rights)
    tiles = sum(-(-r.shape[1] // TILE) for r in rights)
    half = width // 2
    shape = jax.ShapeDtypeStruct((half // 2, cols), BF)
    size = 4 * count * width * team_tokens + 2 * team_tokens * cols + 2 * half * cols
    size += 4 * half * tiles * TILE
    away, keep = pl.pallas_call(
        functools.partial(grads_kernel, count),
        out_shape=(shape, shape),
        in_specs=[VMEM] * (2 * count),
        out_specs=(VMEM, VMEM),
        scratch_shapes=[pltpu.VMEM((width, team_tokens), BF)] * count
        + [
            pltpu.VMEM((tiles, half, TILE), BF),
            pltpu.VMEM((tiles, half, TILE), BF),
            DMA((tiles,)),
            DMA((tiles,)),
        ],
        compiler_params=pltpu.CompilerParams(
            collective_id=call_id, has_side_effects=True, vmem_limit_bytes=size + (8 << 20)
        ),
        name=f"grads_{call_id}",
    )(*lefts, *rights)
    shape = (highs, 2, rows, cols)
    return away.reshape(shape), keep.reshape(shape)


def together(*values):
    return lax.optimization_barrier(values)


def add_rows(out, *parts):
    def step(n, _):
        at = pl.ds(n * 16, 16)
        total = parts[0][at].astype(F32)
        for part in parts[1:]:
            total = total + part[at].astype(F32)
        out[at] = low(total)
        return 0

    lax.fori_loop(0, out.shape[0] // 16, step, 0)


def backward_kernel(*refs):
    (
        back, cot, middle, gain, pair_away, pair_keep, down_away, down_keep, merge_w, gated, projected, mixed,
        cumulated, gate, befores, decay, low_rank, up_pad, head_gain, hidden, starts_row, starts_column,
        grad_middle, gain_grad, proj, ranks, heads, early_away, early_keep, gate_sum, up_part, down_sum,
        got, relayed, staged, line, branch, left_hidden, left_branch, normed_grad, douts, tiles, tiles_got,
        pair_side, down_side, gate_got, down_got, up_grad, state,
        send, arrive, send2, arrive2, side_send, side_arrive, high_send, high_arrive, tile_send, tile_arrive,
    ) = refs[:-STATE_REFS]
    me = Place()
    zh, y, highs = lax.axis_index("zh"), lax.axis_index("y"), lax.axis_size("zh")
    chunks, _, width = hidden.shape
    units = down_keep.shape[-1]
    first = ((zh * 2 + me.c) * 2 + y) * (chunks * CHUNK)
    greet_all(me)

    def side_part(part, pair, down):
        return down if part == 0 else pair.at[:, :, :, pl.ds((part - 1) * units, units)]

    sides = [
        copy_to(
            side_part(p, pair_away, down_away),
            side_part(p, pair_side, down_side),
            side_send.at[p],
            side_arrive.at[p],
            {"y": 1 - y},
        )
        for p in range(3)
    ]
    highs_moves = [
        [
            copy_to(
                side_part(p, pair_side, down_side).at[k],
                (down_got if p == 0 else gate_got).at[k - 1],
                high_send.at[p, k],
                high_arrive.at[p, k],
                {"zh": lax.rem(zh + k, highs)},
            )
            for k in range(1, highs)
        ]
        for p in range(2)
    ]

    def side_add(part):
        sides[part].wait()
        mine, there = side_part(part, pair_keep, down_keep), side_part(part, pair_side, down_side)
        out = up_part if part == 2 else there
        for k in range(highs):
            for m in range(2):
                add_rows(out.at[k, m], mine.at[k, m], there.at[k, m])

    def high_add(part):
        source, there = side_part(part, pair_side, down_side), (down_got if part == 0 else gate_got)
        out = down_sum if part == 0 else gate_sum
        for k in range(1, highs):
            wait_for(there.at[k - 1], high_arrive.at[part, k])
        for m in range(2):
            add_rows(out.at[m], source.at[0, m], *(there.at[k - 1, m] for k in range(1, highs)))

    sides[0].start()

    steps = send.shape[0]
    rows = cot.shape[0] // steps

    def part(ref, k, n):
        return ref.at[k, pl.ds(n * rows, rows)]

    sums = [
        MemberSum(
            me,
            lambda k, n=n: part(back, k, n),
            lambda k, n=n: part(got, k, n),
            lambda k, n=n: part(relayed, k, n),
            lambda k, n=n: part(staged, k, n),
            send.at[n],
            arrive.at[n],
            two="zl",
        )
        for n in range(steps)
    ]
    spreads = [
        HalvesSpread(
            me,
            line.at[pl.ds(n * rows, rows)],
            lambda k, n=n: part(branch, k, n),
            send2.at[n],
            arrive2.at[n],
        )
        for n in range(steps)
    ]
    for transfer in sums:
        transfer.start()

    owners = highs * 8
    owner_rows = width // owners

    def transpose(source, target):
        for n in range(chunks):
            turned = source[n].T
            for chip in range(owners):
                at_zh, zl, at_y, x = chip // 8, chip // 4 % 2, chip // 2 % 2, chip % 2
                x_place = me.c if x == 1 else 1 - me.c
                x_place = jnp.where(x_place == 1, 1, 0)
                y_place = jnp.where((y if at_y == 1 else 1 - y) == 1, 1, 0)
                place = ((x_place * 2 + y_place) * highs + lax.rem(at_zh - zh + highs, highs)) * 2 + zl
                at = pl.ds(pl.multiple_of(place * owner_rows, owner_rows), owner_rows)
                target[at, n * CHUNK : (n + 1) * CHUNK] = turned[chip * owner_rows : (chip + 1) * owner_rows]

    transpose(hidden, left_hidden)
    for transfer in sums:
        transfer.relay()
    for n in range(steps):
        at = pl.ds(n * rows, rows)
        mid = middle[at]
        scale = lax.rsqrt(jnp.mean(mid * mid, -1, keepdims=True) + EPSILON)
        normed = mid * scale
        total = sums[n].total()
        gsum = jnp.sum(total * normed, axis=0, keepdims=True)
        gain_grad[...] = gsum if n == 0 else gain_grad[...] + gsum
        scaled = total * gain[...]
        out = cot[at].astype(F32) + scale * (
            scaled - normed * jnp.mean(scaled * normed, -1, keepdims=True)
        )
        grad_middle[at] = out
        line[at] = low(out)
        spreads[n].start()
        if n:
            spreads[n - 1].relay()
    spreads[steps - 1].relay()
    side_add(0)
    for move in highs_moves[0]:
        move.start()
    sides[1].start()
    for transfer in spreads:
        transfer.wait()

    heads[...] = jnp.zeros_like(heads)

    def head_step(n, _):
        grad = dot(branch[n], merge_w[...])
        out = mixed[n]
        scale = lax.rsqrt(jnp.mean(out * out, -1, keepdims=True) + HEAD_FLOOR)
        normed = out * scale
        u = projected[3, n]
        sig = jax.nn.sigmoid(u)
        dn = grad * (u * sig)
        proj[n, :, 3 * HD :] = low(grad * normed * head_gain[...] * sig * (1.0 + u * (1.0 - sig)))
        heads[17:18] = heads[17:18] + jnp.sum(dn * normed, axis=0, keepdims=True)
        scaled = dn * head_gain[...]
        douts[n] = low(scale * (scaled - normed * jnp.mean(scaled * normed, -1, keepdims=True)))
        return 0

    lax.fori_loop(0, chunks, head_step, 0)

    def masks(n):
        return keyed_mask(first + n * CHUNK, starts_row, starts_column)

    def query_rows(n, visible):
        return low(projected[0, n] * jnp.exp(cumulated[n]) * visible)

    state[...] = jnp.zeros_like(state)

    def local_step(i, _):
        n = chunks - 1 - i
        _, visible, keep, _ = masks(n)
        carry = keep * jnp.exp(cumulated[n, CHUNK - 1 :])
        state[...] = carry * state[...] + dot_rows(douts[n], query_rows(n, visible))
        return 0

    lax.fori_loop(0, chunks, local_step, 0)
    states = StatePass(True, state, decay, state, *refs[-STATE_REFS:])
    states.begin()

    transpose(branch, left_branch)
    half = width // 2
    quarter = half // 2

    def tile_move(n):
        return copy_to(tiles.at[n], tiles_got.at[n], tile_send.at[n], tile_arrive.at[n], {"c": 1 - me.c})

    def right_tile(kind, n):
        if kind == 0:
            return gated[...].reshape(chunks * CHUNK, HD)[:, n * TILE : (n + 1) * TILE]
        at = 3 * HD + n * TILE
        return proj[...].reshape(chunks * CHUNK, 4 * HD)[:, at : at + TILE]

    lefts = left_branch, left_hidden
    for kind in range(2):
        for n in range(HD // TILE):
            tile = kind * (HD // TILE) + n
            tiles[tile] = low(dot(lefts[kind][pl.ds(0, half)], right_tile(kind, n)))
            tile_move(tile).start()
    states.combine()
    for kind in range(2):
        for n in range(HD // TILE):
            tile = kind * (HD // TILE) + n
            block = dot(lefts[kind][pl.ds(half, half)], right_tile(kind, n))
            tile_move(tile).wait_recv()
            block = low(block + tiles_got[tile].astype(F32))
            at = slice(tile * TILE, (tile + 1) * TILE)
            early_away[:, at] = block[:quarter]
            early_keep[:, at] = block[quarter:]
    states.spread()
    side_add(1)
    for move in highs_moves[1]:
        move.start()
    sides[2].start()
    states.finish()

    upper = (
        lax.broadcasted_iota(jnp.int32, (CHUNK, CHUNK), 0)
        <= lax.broadcasted_iota(jnp.int32, (CHUNK, CHUNK), 1)
    ).astype(F32)
    up_grad[...] = jnp.zeros_like(up_grad)

    def chunk_step(i, _):
        n = chunks - 1 - i
        pair, visible, keep, last = masks(n)
        b = cumulated[n]
        mid, end = b[CHUNK // 2 - 1 : CHUNK // 2], b[CHUNK - 1 :]
        q, k, v = projected[0, n], projected[1, n], low(projected[2, n])
        do = douts[n]
        eq, ek, el = jnp.exp(b - mid), jnp.exp(mid - b), jnp.exp(end - b) * last
        qh, kh, kc = low(q * eq), low(k * ek), k * el
        scores = low(jnp.where(pair, dot_last(qh, kh), 0.0))
        gs = low(jnp.where(pair, dot_last(do, v), 0.0))
        ds = low(state[...])
        proj[n, :, 2 * HD : 3 * HD] = low(dot_rows(scores, do) + dot_last(low(kc), ds))
        dq = dot(gs, kh) * eq + dot(do, low(befores[n])) * (jnp.exp(b) * visible)
        gkc = dot(v, ds)
        dk = dot_rows(gs, qh) * ek + gkc * el
        proj[n, :, :HD] = low(dq * HD ** (-0.5))
        proj[n, :, HD : 2 * HD] = low(dk)
        carry = keep * jnp.exp(end)
        extra = jnp.sum(gkc * kc, axis=0, keepdims=True)
        extra = extra + carry * jnp.sum(befores[n] * state[...], axis=0, keepdims=True)
        dlog = extra + jnp.dot(
            upper, dq * q - dk * k, precision=lax.Precision.HIGHEST, preferred_element_type=F32
        )
        state[...] = carry * state[...] + dot_rows(do, query_rows(n, visible))
        da = dlog * jax.nn.sigmoid(-gate[n]) / 16.0
        heads[16:17] = heads[16:17] + jnp.sum(da, axis=0, keepdims=True)
        dar = low(da)
        up_grad[...] = up_grad[...] + dot_rows(low_rank[n], dar)
        ranks[n] = low(dot_last(dar, up_pad[...]))
        return 0

    lax.fori_loop(0, chunks, chunk_step, 0)
    heads[0:16] = up_grad[2:18]
    high_add(0)
    side_add(2)
    high_add(1)
    for move in highs_moves[0] + highs_moves[1]:
        move.wait_send()
    for transfer in sums:
        transfer.wait_sent()
    for tile in range(tiles.shape[0]):
        tile_move(tile).wait_send()
    states.wait_sent()


def backward(
    back, cot, middle, gain, pair, down, merge_w, gated, projected, mixed, cumulated, gate, befores, decay,
    low_rank, up_pad, head_gain, hidden, starts,
):
    highs, members, owner_rows, units = down[0].shape
    rows, width = cot.shape
    chunks = hidden.shape[0]

    def shape(*dims, kind=BF):
        return jax.ShapeDtypeStruct(dims, kind)

    arrays = [
        back, cot, middle, gain, *pair, *down, merge_w, gated, projected, mixed, cumulated, gate, befores, decay,
        low_rank, up_pad, head_gain, hidden, *starts_arrays(starts),
    ]
    away = {4, 6}
    quarter = width // 4
    shapes = [
        shape(rows, width, kind=F32),
        shape(1, width, kind=F32),
        shape(chunks, CHUNK, 4 * HD),
        shape(chunks, CHUNK, LANES),
        shape(24, HD, kind=F32),
        shape(quarter, 2 * HD),
        shape(quarter, 2 * HD),
        shape(members, owner_rows, units),
        shape(highs, members, owner_rows, units),
        shape(members, owner_rows, units),
    ]
    tiles = 2 * HD // TILE
    scratch = [
        shape(2, rows, width),
        shape(1, rows, width),
        shape(1, rows, width),
        shape(rows, width),
        shape(TEAM, rows, width),
        shape(width, chunks * CHUNK),
        shape(width, chunks * CHUNK),
        shape(8, HD, kind=F32),
        shape(chunks, CHUNK, HD),
        shape(tiles, width // 2, TILE),
        shape(tiles, width // 2, TILE),
        shape(highs, members, owner_rows, 2 * units),
        shape(highs, members, owner_rows, units),
        shape(highs - 1, members, owner_rows, units),
        shape(highs - 1, members, owner_rows, units),
        shape(LANES, HD, kind=F32),
        shape(HD, HD, kind=F32),
    ]
    used = [a for n, a in enumerate(arrays) if n not in away] + shapes + scratch
    size = sum(a.size * a.dtype.itemsize for a in used)
    sems = [
        (STEPS, 3), (STEPS, 3), (STEPS, 5), (STEPS, 4), (3,), (3,), (2, highs), (2, highs), (tiles,), (tiles,),
    ]
    return pl.pallas_call(
        backward_kernel,
        out_shape=shapes,
        in_specs=[ANY if n in away else VMEM for n in range(len(arrays))],
        out_specs=[VMEM] * len(shapes),
        scratch_shapes=[pltpu.VMEM(a.shape, a.dtype) for a in scratch]
        + [DMA(n) for n in sems]
        + state_pass_scratch(highs),
        compiler_params=pltpu.CompilerParams(
            collective_id=3, has_side_effects=True, vmem_limit_bytes=min(size + (14 << 20), 62 << 20)
        ),
        name="backward",
    )(*arrays)


def closing_kernel(*refs):
    (
        partial, own, grad_middle, gain, down, gain_two_grad, heads, late_away, late_keep, early_away, early_keep,
        pair, gates, downs,
        out, late_home, early_home, pair_home, gate_home, down_home, wide_out, heads_out, gains_out,
        got, relayed, staged, line, late_side, late, early_side, early, late_got, early_got, pair_got, late_sum, early_sum, pair_sum,
        wide, wide_got, heads_got, heads_sum, wide_twin, gain_grad, rank_grad,
        send, arrive, twin_send, twin_arrive, here, side_sem, high_send, high_arrive, home_send, home_arrive,
        wide_send, wide_arrive, heads_send, heads_arrive, near, out_send, out_arrive, gain_send, gain_arrive,
    ) = refs
    me = Place()
    zh, y, highs = lax.axis_index("zh"), lax.axis_index("y"), lax.axis_size("zh")
    greet_all(me)
    steps = send.shape[0]
    rows, width = own.shape[0] // steps, own.shape[1]
    twin = {"c": 1 - me.c}

    def high_copies(kind, source, target):
        return [
            copy_to(
                source.at[k],
                target.at[k - 1],
                high_send.at[kind, k],
                high_arrive.at[kind, k],
                {"zh": lax.rem(zh + k, highs)},
            )
            for k in range(1, highs)
        ]

    side = copy_to(late_away, late_side, side_sem.at[0], side_sem.at[1], {"y": 1 - y})
    early_move = copy_to(early_away, early_side, side_sem.at[2], side_sem.at[3], {"y": 1 - y})
    early_move.start()
    side.start()
    early_moves = high_copies(0, early, early_got)
    pair_moves = high_copies(1, pair, pair_got)
    late_moves = high_copies(2, late, late_got)

    def part(ref, k, n):
        return ref.at[k, pl.ds(n * rows, rows)]

    sums = [
        OwnersSum(
            me,
            lambda k, n=n: part(partial, k, n),
            lambda k, n=n: part(got, k, n),
            lambda k, n=n: part(relayed, k, n),
            lambda k, n=n: part(staged, k, n),
            send.at[n],
            arrive.at[n],
        )
        for n in range(steps)
    ]
    for transfer in sums:
        transfer.start()
    for move in pair_moves:
        move.start()

    def home(n, source, target):
        return Transfer(
            route_weights_home(me),
            lambda k: source.at[k],
            lambda k: target.at[k],
            home_send.at[n],
            home_arrive.at[n],
        )

    homes = [
        home(0, downs, down_home),
        home(1, early_sum, early_home),
        home(2, pair_sum, pair_home),
        home(3, late_sum, late_home),
        home(4, gates, gate_home),
    ]

    def twin_copy(n):
        return copy_to(
            line.at[pl.ds(n * rows, rows)], part(out, me.c, n), twin_send.at[n], twin_arrive.at[n], twin
        )

    def own_copy(n):
        return pltpu.make_async_copy(line.at[pl.ds(n * rows, rows)], part(out, me.c, n), here.at[n])

    for transfer in sums:
        transfer.relay()
    homes[0].start()
    homes[4].start()
    early_move.wait()
    for k in range(highs):
        for m in range(2):
            add_rows(early.at[k, m], early_keep.at[k, m], early_side.at[k, m])
    for move in early_moves:
        move.start()
    for n in range(steps):
        at = pl.ds(n * rows, rows)
        x = own[at].astype(F32)
        scale = lax.rsqrt(jnp.mean(x * x, -1, keepdims=True) + EPSILON)
        normed = x * scale
        total = sums[n].total()
        rank = low(total[:, width:])
        total = total[:, :width] + dot(rank, down[...])
        gsum = jnp.sum(total * normed, axis=0, keepdims=True)
        hidden = low(normed * gain[...])
        rsum = dot_rows(rank, hidden)
        gain_grad[...] = gsum if n == 0 else gain_grad[...] + gsum
        rank_grad[...] = rsum if n == 0 else rank_grad[...] + rsum
        scaled = total * gain[...]
        line[at] = low(
            grad_middle[at]
            + scale * (scaled - normed * jnp.mean(scaled * normed, -1, keepdims=True))
        )
        twin_copy(n).start()
        own_copy(n).start()

    owner_rows = wide.shape[2]
    for n in range(wide.shape[0]):
        at = slice(n * owner_rows, (n + 1) * owner_rows)
        wide[n, 0:1] = gain_grad[:, at]
        wide[n, 1:2] = gain_two_grad[:, at]
        wide[n, 2:8] = jnp.zeros((6, owner_rows), F32)
        wide[n, 8:24] = rank_grad[:16, at]
    spreads = Transfer(
        route_all(me), lambda k: wide.at[k], lambda k: wide_got.at[k], wide_send, wide_arrive
    )
    spreads.start()
    group_out, group_arrive = [], []
    for n in range(highs):
        for f in range(4):
            to_zh, to_y, to_c = lax.rem(zh + n, highs), flip(y, f & 2), flip(me.c, f & 1)
            to = {"zh": to_zh, "y": to_y, "c": to_c}
            group_out.append((0, (zh * 2 + y) * 2 + me.c, to, n + f == 0))
            group_arrive.append(((to_zh * 2 + to_y) * 2 + to_c, n + f == 0))
    heads_move = Transfer(
        (group_out, group_arrive), lambda _: heads, lambda k: heads_got.at[k], heads_send, heads_arrive
    )
    heads_move.start()

    side.wait()
    for k in range(highs):
        for m in range(2):
            add_rows(late.at[k, m], late_keep.at[k, m], late_side.at[k, m])
    for move in late_moves:
        move.start()

    heads_move.wait()
    total = heads_got[0]
    for n in range(1, highs * 4):
        total = total + heads_got[n]
    heads_sum[...] = total
    tail = gains_out.shape[1]
    gains = Transfer(
        route_member(me),
        lambda _: heads_sum.at[pl.ds(heads_sum.shape[0] - tail, tail)],
        lambda k: gains_out.at[k],
        gain_send,
        gain_arrive,
    )
    gains.start()
    moves = [
        copy_to(
            heads_sum,
            heads_out.at[me.x],
            out_send.at[n],
            out_arrive.at[me.x],
            {"zl": flip(me.zl, fz), "x": flip(me.x, fx)},
        )
        for n, (fz, fx) in enumerate(FLIPS[:3])
    ]

    @pl.when(me.c == me.zl)
    def _():
        for move in moves:
            move.start()
        heads_out[me.x] = heads_sum[...]

    spreads.wait()
    total = wide_got[0]
    for n in range(1, wide.shape[0]):
        total = total + wide_got[n]
    wide_out[...] = total
    swap = copy_to(wide_out, wide_twin, near.at[0], near.at[1], twin)
    swap.start()

    for n, kind_moves, source, target, total in (
        (2, pair_moves, pair, pair_got, pair_sum),
        (1, early_moves, early, early_got, early_sum),
        (3, late_moves, late, late_got, late_sum),
    ):
        for k in range(1, highs):
            wait_for(target.at[k - 1], high_arrive.at[n - 1, k])
        for m in range(2):
            add_rows(total.at[m], source.at[0, m], *(target.at[k - 1, m] for k in range(1, highs)))
        homes[n].start()
    for k in range(2):
        own_slot = (me.c == me.zl) & (me.x == k)
        unless(own_slot, lambda k=k: wait_for(heads_out.at[k], out_arrive.at[k]))

    @pl.when(me.c == me.zl)
    def _():
        for move in moves:
            move.wait_send()

    swap.wait()
    wide_out[...] = wide_out[...] + wide_twin[...]
    gains.wait()
    for transfer in sums:
        transfer.wait_sent()
    for n in range(steps):
        twin_copy(n).wait()
        own_copy(n).wait()
    for transfer in homes:
        transfer.wait()
    for move in early_moves + pair_moves + late_moves:
        move.wait_send()


def closing(partial, own, grad_middle, gain, down, gain_two_grad, heads, late, early, pair, gates, downs):
    rows, width = own.shape
    lanes = partial.shape[-1] - width
    highs, _, owner_rows, late_cols = late[0].shape
    chips = highs * 8
    arrays = [partial, own, grad_middle, gain, down, gain_two_grad, heads, *late, *early, pair, gates, downs]

    def shape(*dims, kind=BF):
        return jax.ShapeDtypeStruct(dims, kind)

    cols = late_cols, early[0].shape[-1], pair.shape[-1], gates.shape[-1], downs.shape[-1]
    shapes = [shape(2, rows, width)] + [shape(2, owner_rows, n) for n in cols]
    shapes += [
        shape(24, owner_rows, kind=F32),
        shape(2, *heads.shape, kind=F32),
        shape(TEAM, 8, heads.shape[1], kind=F32),
    ]
    scratch = [shape(n, rows, width + lanes) for n in (3, 2, 2)] + [shape(rows, width)]
    scratch += [shape(*late[0].shape)] * 2 + [shape(*early[0].shape)] * 2
    scratch += [shape(highs - 1, 2, owner_rows, n) for n in cols[:3]]
    scratch += [shape(2, owner_rows, n) for n in cols[:3]]
    scratch += [
        shape(chips, 24, owner_rows, kind=F32),
        shape(chips, 24, owner_rows, kind=F32),
        shape(highs * 4, *heads.shape, kind=F32),
        shape(*heads.shape, kind=F32),
        shape(24, owner_rows, kind=F32),
        shape(1, width, kind=F32),
        shape(lanes, width, kind=F32),
    ]
    size = sum(a.size * a.dtype.itemsize for a in arrays + shapes + scratch)
    sems = [
        (STEPS, 6), (STEPS, 5), (STEPS,), (STEPS,), (STEPS,), (4,), (3, highs), (3, highs), (5, 2), (5, 2),
        (chips,), (chips,), (highs * 4,), (highs * 4,), (2,), (3,), (2,), (TEAM,), (TEAM,),
    ]
    return pl.pallas_call(
        closing_kernel,
        out_shape=shapes,
        in_specs=[VMEM] * len(arrays),
        out_specs=[VMEM] * len(shapes),
        scratch_shapes=[pltpu.VMEM(a.shape, a.dtype) for a in scratch] + [DMA(n) for n in sems],
        compiler_params=pltpu.CompilerParams(
            collective_id=4, has_side_effects=True, vmem_limit_bytes=size + (10 << 20)
        ),
        name="closing",
    )(*arrays)


def shards(
    tokens,
    cotangent,
    lengths,
    attn_gain,
    ffn_gain,
    mixer_in,
    decay_down,
    decay_up,
    decay_bias,
    head_gain,
    mixer_out,
    ffn_in,
    ffn_out,
):
    zh, zl, y, x, c = (lax.axis_index(a) for a in SEQ + ("c",))
    block, width = tokens.shape
    half = block // 2
    rows = mixer_in.shape[1]
    units = ffn_out.shape[0] // 2
    team_tokens = 2 * block
    rank = decay_down.shape[1]

    small = jnp.concatenate([attn_gain[:, None], ffn_gain[:, None], decay_down], axis=1)
    small = jnp.pad(small, ((0, 0), (0, LANES - small.shape[1])))
    up_head = lax.dynamic_slice_in_dim(decay_up, HD * x, HD, 1).astype(F32)
    bias_head = lax.dynamic_slice_in_dim(decay_bias, HD * x, HD, 0)
    ups = jnp.concatenate([up_head, bias_head[None], jnp.zeros((7, HD), F32)], axis=0)
    own = lax.dynamic_slice_in_dim(tokens, half * c, half, 0)
    own_dy = lax.dynamic_slice_in_dim(cotangent, half * c, half, 0)
    starts = jnp.cumsum(lengths) - lengths
    (
        mixer_w, merge_w, pair_w, down_w, gains, ffn_dy, hidden_one, low_rank, gate_input, cumulated, projected,
        mixed, gated, befores, decay, hidden_two, middle,
    ) = forward(
        mixer_in, mixer_out.T, ffn_in, ffn_out.T, small, ups, own, own_dy, starts, head_gain[None]
    )
    up_head = jnp.where(c == zl, up_head, lax.ppermute(up_head, "c", CROSS)).astype(BF)
    mixer_w, merge_w = mixer_w.reshape(width, 4 * HD), merge_w.reshape(width, HD)
    pair_w, down_w = pair_w.reshape(width, 2 * units), down_w.reshape(width, units)
    gain_one, gain_two, rank_down = gains[:1], gains[1:2], gains[2 : 2 + rank].astype(BF)
    ffn_dy = ffn_dy.reshape(team_tokens, width)
    hidden_two = hidden_two.reshape(team_tokens, width)

    up_pair = dot(hidden_two, pair_w)
    up_a, up_b = up_pair[:, :units], up_pair[:, units:]
    ffn_sig = jax.nn.sigmoid(up_a)
    ffn_silu = up_a * ffn_sig
    activated = low(ffn_silu * up_b)
    down = dot_last(activated, down_w).astype(BF)
    down = lax.psum_scatter(down, ("zl", "x"), scatter_dimension=0, tiled=True).astype(F32)
    result = (middle + down).astype(BF)
    twin = lax.ppermute(result, "c", CROSS)
    result = jnp.concatenate([jnp.where(c == 0, result, twin), jnp.where(c == 0, twin, result)], axis=0)

    grad_act = dot(ffn_dy, down_w)
    grad_gate = low(grad_act * up_b * ffn_sig * (1.0 + up_a * (1.0 - ffn_sig)))
    grad_upper = low(grad_act * ffn_silu)
    grad_pair = jnp.concatenate([grad_gate, grad_upper], axis=1)
    back = dot_last(grad_pair, pair_w)
    ffn_sums = weight_grads(12, [(ffn_dy, activated)]), weight_grads(13, [(hidden_two, grad_pair)])
    back, ffn_sums = together(back, ffn_sums)
    back = low(back).reshape(TEAM, half, width)
    lanes = LANES
    (
        grad_middle, grad_gain_two, grad_proj, grad_rank_part, heads, early_away, early_keep, gate_sum, up_part, down_sum,
    ) = backward(
        back, own_dy, middle, gain_two, ffn_sums[1], ffn_sums[0], merge_w, gated, projected, mixed, cumulated,
        gate_input, befores, decay, low_rank, jnp.pad(up_head, ((0, lanes - rank), (0, 0))), head_gain[None],
        hidden_one, starts,
    )
    grad_proj = grad_proj.reshape(team_tokens, 4 * HD)
    hidden_part = dot_last(grad_proj, mixer_w)
    hidden_part = jnp.concatenate(
        [low(hidden_part).reshape(TEAM, half, width), grad_rank_part], axis=2
    )
    late_sums = weight_grads(15, [(hidden_one.reshape(team_tokens, width), grad_proj[:, : 3 * HD])])
    early_shape = late_sums[0].shape[:3] + (2 * HD,)
    early_sums = early_away.reshape(early_shape), early_keep.reshape(early_shape)
    down_pad = jnp.pad(rank_down, ((0, lanes - rank), (0, 0)))
    grad_inputs, late_home, early_home, up_home, gate_home, ffn_down, wide, heads, gains = closing(
        hidden_part, own, grad_middle, gain_one, down_pad, grad_gain_two, heads, late_sums, early_sums, up_part,
        gate_sum, down_sum,
    )
    grad_inputs = grad_inputs.reshape(block, width)
    ffn_pair = jnp.stack([gate_home, up_home]).astype(F32)
    ffn_down = ffn_down.astype(F32)
    early_home = early_home.reshape(2, rows, 2, HD).astype(F32)
    late_home = late_home.reshape(2, rows, 3, HD).astype(F32)
    mixer_home = jnp.concatenate([late_home, early_home[:, :, 1:]], axis=2)
    return (
        result,
        grad_inputs,
        wide[0],
        wide[1],
        mixer_home.transpose(2, 1, 0, 3).reshape(4, rows, 2 * HD),
        wide[8 : 8 + rank].T,
        heads[:, :rank].transpose(1, 0, 2).reshape(rank, 2 * HD),
        heads[:, rank].reshape(2 * HD),
        jnp.sum(gains[:, rank + 1 - 16], axis=0),
        early_home[:, :, 0].transpose(0, 2, 1).reshape(2 * HD, rows),
        ffn_pair.transpose(0, 2, 1, 3).reshape(2, rows, 2 * units),
        ffn_down.transpose(0, 2, 1).reshape(2 * units, rows),
    )


def solution(mesh):
    devices = mesh.devices
    inner = Mesh(devices.reshape(devices.shape[0] // 8, 2, 2, 2, devices.shape[1]), SEQ + ("c",))
    in_specs = (
        P(SEQ, None),
        P(SEQ, None),
        P(),
        P(SEQ),
        P(SEQ),
        P(None, SEQ, "c"),
        P(SEQ, None),
        P(None, "c"),
        P("c"),
        P(),
        P("c", SEQ),
        P(None, SEQ, "c"),
        P("c", SEQ),
    )
    out_specs = (
        P(SEQ, None),
        P(SEQ, None),
        P(SEQ),
        P(SEQ),
        P(None, SEQ, "c"),
        P(SEQ, None),
        P(None, "c"),
        P("c"),
        P(),
        P("c", SEQ),
        P(None, SEQ, "c"),
        P("c", SEQ),
    )
    return jax.shard_map(shards, mesh=inner, in_specs=in_specs, out_specs=out_specs, check_vma=False)
```

```python
import functools

import jax
import jax.numpy as jnp
from jax import lax
from jax.experimental import pallas as pl
from jax.experimental.pallas import tpu as pltpu
from jax.sharding import Mesh, PartitionSpec as P

HD = 512
CHUNK = 128
EPSILON = 1e-06
HEAD_FLOOR = 1.0
TEAM = 4

BF = jnp.bfloat16
F32 = jnp.float32
MESH = pl.DeviceIdType.MESH
ANY = pl.BlockSpec(memory_space=pl.ANY)
VMEM = pl.BlockSpec(memory_space=pltpu.VMEM)
DMA = pltpu.SemaphoreType.DMA

SEQ = ("zh", "zl", "y", "x")
FLIPS = ((1, 1), (0, 1), (1, 0), (0, 0))


def dot(a, b):
    return jnp.dot(a, b, preferred_element_type=F32)


def dot_rows(a, b):
    return lax.dot_general(a, b, (((0,), (0,)), ((), ())), preferred_element_type=F32)


def dot_last(a, b):
    return lax.dot_general(a, b, (((1,), (1,)), ((), ())), preferred_element_type=F32)


def low(v):
    return v.astype(BF)


def flip(index, by):
    return 1 - index if by else index


class Place:
    def __init__(self):
        self.zl, self.x, self.c = lax.axis_index("zl"), lax.axis_index("x"), lax.axis_index("c")
        self.member = self.zl * 2 + self.x


def greet_team(me, more=0):
    barrier = pltpu.get_barrier_semaphore()
    for n in range(1, 8):
        to = {"zl": flip(me.zl, n & 1), "x": flip(me.x, n & 2), "c": flip(me.c, n & 4)}
        pl.semaphore_signal(barrier, inc=1, device_id=to, device_id_type=MESH)
    pl.semaphore_wait(barrier, 7 + more)


def others(me):
    zh, y, highs = lax.axis_index("zh"), lax.axis_index("y"), lax.axis_size("zh")
    for k in range(highs):
        for n in range(8):
            yield lax.rem(zh + k, highs), flip(me.zl, n & 1), flip(y, n & 2), flip(me.x, n & 4), k + n == 0


def greet_all(me):
    barrier = pltpu.get_barrier_semaphore()
    count = 0
    for zh, zl, y, x, own in others(me):
        for f in range(2):
            if own and not f:
                continue
            to = {"zh": zh, "zl": zl, "y": y, "x": x, "c": flip(me.c, f)}
            pl.semaphore_signal(barrier, inc=1, device_id=to, device_id_type=MESH)
            count += 1
    pl.semaphore_wait(barrier, count)


def route_member(me):
    out, arrive = [], []
    for fz, fx in FLIPS:
        zl, x = flip(me.zl, fz), flip(me.x, fx)
        own = (fz, fx) == (0, 0)
        out.append((zl * 2 + x, me.member, {"zl": zl, "x": x}, own))
        arrive.append((zl * 2 + x, own))
    return out, arrive


def chip_index(zh, zl, y, x):
    return ((zh * 2 + zl) * 2 + y) * 2 + x


def route_all(me):
    mine = chip_index(lax.axis_index("zh"), me.zl, lax.axis_index("y"), me.x)
    out, arrive = [], []
    for zh, zl, y, x, own in others(me):
        chip = chip_index(zh, zl, y, x)
        out.append((chip, mine, {"zh": zh, "zl": zl, "y": y, "x": x}, own))
        arrive.append((chip, own))
    return out, arrive


def route_halves(me):
    mine = me.c == me.zl
    out, arrive = [], []
    for fz, fx in FLIPS:
        zl, x = flip(me.zl, fz), flip(me.x, fx)
        own = mine if (fz, fx) == (0, 0) else False
        out.append((0, me.x * 2 + me.c, {"zl": zl, "x": x, "c": me.zl}, own))
    for fc, fx in FLIPS:
        c, x = flip(me.c, fc), flip(me.x, fx)
        own = mine if (fc, fx) == (0, 0) else False
        arrive.append((x * 2 + c, own))
    return out, arrive


def route_owners(me):
    mine = me.c == me.zl
    out, arrive = [], []
    for fc, fx in FLIPS:
        c, x = flip(me.c, fc), flip(me.x, fx)
        own = mine if (fc, fx) == (0, 0) else False
        out.append((x * 2 + c, me.member, {"zl": me.c, "x": x, "c": c}, own))
    for fz, fx in FLIPS:
        zl, x = flip(me.zl, fz), flip(me.x, fx)
        own = mine if (fz, fx) == (0, 0) else False
        arrive.append((zl * 2 + x, own))
    return out, arrive


def route_weights(me):
    mine = (me.c == me.zl) & (me.c == me.x)
    out, arrive = [], []
    for f in (1, 0):
        x = flip(me.x, f)
        own = (me.c == me.zl) & (me.c == x) & (me.x == me.c) if not f else False
        out.append((x, me.zl, {"zl": me.c, "x": x, "c": me.x}, own))
    for f in (1, 0):
        zl = flip(me.zl, f)
        own = mine if not f else False
        arrive.append((zl, own))
    return out, arrive


def route_weights_home(me):
    mine = (me.c == me.zl) & (me.c == me.x)
    out, arrive = [], []
    for f in (1, 0):
        zl = flip(me.zl, f)
        own = mine if not f else False
        out.append((zl, me.x, {"zl": zl, "x": me.c, "c": me.zl}, own))
    for f in (1, 0):
        x = flip(me.x, f)
        own = mine if not f else False
        arrive.append((x, own))
    return out, arrive


def when(condition, run):
    if condition is True:
        run()
    elif condition is not False:
        pl.when(condition)(run)


def unless(condition, run):
    if condition is False:
        run()
    elif condition is not True:
        pl.when(jnp.logical_not(condition))(run)


class Transfer:
    def __init__(self, route, source, target, send, arrive):
        self.route, self.source, self.target, self.send, self.arrive = route, source, target, send, arrive

    def _remote(self, n):
        index, slot, to, own = self.route[0][n]
        return pltpu.make_async_remote_copy(
            src_ref=self.source(index),
            dst_ref=self.target(slot),
            send_sem=self.send.at[n],
            recv_sem=self.arrive.at[slot],
            device_id=to,
            device_id_type=MESH,
        )

    def _local(self, n):
        index, slot, to, own = self.route[0][n]
        return pltpu.make_async_copy(self.source(index), self.target(slot), self.send.at[n])

    def start(self):
        for n, (_, _, _, own) in enumerate(self.route[0]):
            unless(own, lambda: self._remote(n).start())
            when(own, lambda: self._local(n).start())

    def wait_arrive(self):
        for slot, own in self.route[1]:
            ref = self.target(slot)

            def arrived():
                pltpu.make_async_copy(ref, ref, self.arrive.at[slot]).wait()

            unless(own, arrived)

    def wait_local(self):
        for n, (_, _, _, own) in enumerate(self.route[0]):
            when(own, lambda: self._local(n).wait())

    def wait_sent(self):
        for n, (_, _, _, own) in enumerate(self.route[0]):
            unless(own, lambda: self._remote(n).wait_send())

    def wait(self):
        self.wait_arrive()
        self.wait_local()
        self.wait_sent()


def copy_to(src, dst, send, arrive, to):
    return pltpu.make_async_remote_copy(
        src_ref=src, dst_ref=dst, send_sem=send, recv_sem=arrive, device_id=to, device_id_type=MESH
    )


def wait_for(ref, sem):
    pltpu.make_async_copy(ref, ref, sem).wait()


def member_slots(me, two):
    along = me.zl * 2 + 1 - me.x, {"x": 1 - me.x}
    over = (1 - me.zl) * 2 + me.x, {"zl": 1 - me.zl}
    one, double = (over, along) if two == "x" else (along, over)
    return one[0], double[0], (1 - me.zl) * 2 + 1 - me.x, one[1], double[1]


class MemberSpread:
    def __init__(self, me, source, target, send, arrive, two="x"):
        self.target, self.arrive = target, arrive
        mine = me.member
        one, double, across, to_one, to_double = member_slots(me, two)
        self.slots = one, double, across
        self.direct = [
            copy_to(source, target(mine), send.at[0], arrive.at[mine], to_one),
            copy_to(source, target(mine), send.at[1], arrive.at[mine], to_double),
        ]
        self.local = pltpu.make_async_copy(source, target(mine), arrive.at[mine])
        self.forward = copy_to(target(one), target(one), send.at[2], arrive.at[one], to_double)

    def start(self):
        for copy in self.direct:
            copy.start()
        self.local.start()

    def relay(self):
        wait_for(self.target(self.slots[0]), self.arrive.at[self.slots[0]])
        self.forward.start()

    def wait(self):
        for slot in self.slots[1:]:
            wait_for(self.target(slot), self.arrive.at[slot])
        self.local.wait()
        for copy in self.direct + [self.forward]:
            copy.wait_send()


class HalvesSpread:
    def __init__(self, me, source, target, send, arrive):
        self.me, self.target, self.arrive = me, target, arrive
        mine = me.x * 2 + me.c
        self.home = me.c == me.zl
        self.direct = [
            copy_to(source, target(mine), send.at[0], arrive.at[mine], {"zl": 1 - me.zl, "c": me.zl}),
            copy_to(source, target(mine), send.at[1], arrive.at[mine], {"x": 1 - me.x, "c": me.zl}),
        ]
        self.near = copy_to(source, target(mine), send.at[2], arrive.at[mine], {"c": 1 - me.c})
        self.local = pltpu.make_async_copy(source, target(mine), send.at[2])
        self.near_slots = [me.x * 2 + c for c in range(2)]
        self.far_slots = [(1 - me.x) * 2 + c for c in range(2)]
        self.forwards = [
            copy_to(target(slot), target(slot), send.at[3 + c], arrive.at[slot], {"x": 1 - me.x})
            for c, slot in enumerate(self.near_slots)
        ]

    def start(self):
        for copy in self.direct:
            copy.start()
        pl.when(self.home)(self.local.start)
        unless(self.home, self.near.start)

    def relay(self):
        @pl.when(jnp.logical_not(self.home))
        def _():
            for slot, forward in zip(self.near_slots, self.forwards):
                wait_for(self.target(slot), self.arrive.at[slot])
                forward.start()

    def wait(self):
        me = self.me

        @pl.when(self.home)
        def _():
            self.local.wait()
            slot = me.x * 2 + 1 - me.c
            wait_for(self.target(slot), self.arrive.at[slot])

        for slot in self.far_slots:
            wait_for(self.target(slot), self.arrive.at[slot])
        for copy in self.direct:
            copy.wait_send()

        @pl.when(jnp.logical_not(self.home))
        def _():
            self.near.wait_send()
            for forward in self.forwards:
                forward.wait_send()


class MemberSum:
    def __init__(self, me, source, got, relayed, staged, send, arrive, two="x"):
        self.me, self.source, self.got, self.relayed, self.staged = me, source, got, relayed, staged
        self.arrive = arrive
        self.one, double, across, to_one, to_double = member_slots(me, two)
        self.direct = [
            copy_to(source(across), relayed(0), send.at[0], arrive.at[0], to_double),
            copy_to(source(double), got(0), send.at[1], arrive.at[1], to_double),
        ]
        self.onward = copy_to(staged(0), got(1), send.at[2], arrive.at[2], to_one)

    def start(self):
        for copy in self.direct:
            copy.start()

    def relay(self):
        wait_for(self.relayed(0), self.arrive.at[0])
        own = self.source(self.one)[...].astype(F32)
        self.staged(0)[...] = low(own + self.relayed(0)[...].astype(F32))
        self.onward.start()

    def total(self):
        wait_for(self.got(0), self.arrive.at[1])
        wait_for(self.got(1), self.arrive.at[2])
        total = self.source(self.me.member)[...].astype(F32)
        return total + self.got(0)[...].astype(F32) + self.got(1)[...].astype(F32)

    def wait_sent(self):
        for copy in self.direct + [self.onward]:
            copy.wait_send()


class OwnersSum:
    def __init__(self, me, source, got, relayed, staged, send, arrive):
        self.me, self.source, self.got, self.relayed, self.staged = me, source, got, relayed, staged
        self.arrive = arrive
        self.home = me.c == me.zl
        mine, other = me.x * 2, (1 - me.x) * 2
        self.near = copy_to(source(mine + 1 - me.c), got(0), send.at[0], arrive.at[0], {"c": 1 - me.c})
        self.local = pltpu.make_async_copy(source(mine + me.c), got(0), send.at[1])
        self.across = [
            copy_to(source(other + c), got(1), send.at[2 + c], arrive.at[1], {"x": 1 - me.x, "c": c})
            for c in range(2)
        ]
        self.first = [
            copy_to(source(other + c), relayed(c), send.at[2 + c], arrive.at[3 + c], {"x": 1 - me.x})
            for c in range(2)
        ]
        self.onward = [
            copy_to(staged(c), got(2), send.at[4 + c], arrive.at[2], {"zl": me.c, "c": c})
            for c in range(2)
        ]

    def start(self):
        @pl.when(self.home)
        def _():
            for copy in self.across + [self.near, self.local]:
                copy.start()

        @pl.when(jnp.logical_not(self.home))
        def _():
            for copy in self.first:
                copy.start()

    def relay(self):
        @pl.when(jnp.logical_not(self.home))
        def _():
            for c in range(2):
                wait_for(self.relayed(c), self.arrive.at[3 + c])
                own = self.source(self.me.x * 2 + c)[...].astype(F32)
                self.staged(c)[...] = low(own + self.relayed(c)[...].astype(F32))
                self.onward[c].start()

    def total(self):
        pl.when(self.home)(self.local.wait)
        unless(self.home, lambda: wait_for(self.got(0), self.arrive.at[0]))
        wait_for(self.got(1), self.arrive.at[1])
        wait_for(self.got(2), self.arrive.at[2])
        return sum(self.got(k)[...].astype(F32) for k in range(3))

    def wait_sent(self):
        @pl.when(self.home)
        def _():
            for copy in self.across + [self.near]:
                copy.wait_send()

        @pl.when(jnp.logical_not(self.home))
        def _():
            for copy in self.first + self.onward:
                copy.wait_send()


class Placed(Transfer):
    def __init__(self, route, source, there, target, send, arrive):
        super().__init__(route, source, target, send, arrive)
        self.there = there

    def _remote(self, n):
        index, slot, to, own = self.route[0][n]
        return pltpu.make_async_remote_copy(
            src_ref=self.source(index),
            dst_ref=self.there(slot),
            send_sem=self.send.at[n],
            recv_sem=self.arrive.at[slot],
            device_id=to,
            device_id_type=MESH,
        )


LANES = 128


def keyed_mask(start, starts_row, starts_column):
    rows = lax.broadcasted_iota(jnp.int32, (CHUNK, CHUNK), 0)
    columns = lax.broadcasted_iota(jnp.int32, (CHUNK, CHUNK), 1)
    ids = jnp.sum((rows + start >= starts_row[0:1]).astype(F32), axis=1, keepdims=True)
    places = lax.broadcasted_iota(jnp.int32, starts_column.shape, 1)
    ids_row = jnp.sum((places + start >= starts_column[...]).astype(F32), axis=0, keepdims=True)
    before = jnp.sum((starts_row[0:1] < start).astype(F32), axis=1, keepdims=True)
    final = ids_row[:, CHUNK - 1 :]
    pair = (rows >= columns) & (ids == ids_row)
    visible = (ids == before).astype(F32)
    keep = (final == before).astype(F32)
    return pair, visible, keep, (ids == final).astype(F32)


class StatePass:
    def __init__(self, back, local, decay, out, rounded, got, got_decay, sums, sum_decays, stage, stage_decay,
                 entering, leave, enter, send, arrive, far_send, far_arrive, leave_send, leave_arrive):
        self.__dict__.update(locals())
        self.zh, c, y = lax.axis_index("zh"), lax.axis_index("c"), lax.axis_index("y")
        self.highs = lax.axis_size("zh")
        self.mine = c * 2 + y
        self.quarter = local.shape[0] // 4
        self.partners = []
        for fc, fy in ((1, 1), (0, 1), (1, 0)):
            to_c, to_y = flip(c, fc), flip(y, fy)
            self.partners.append((to_c * 2 + to_y, {"c": to_c, "y": to_y}))
        self.order = range(3, -1, -1) if back else range(4)
        self.moves, self.outs = [], []

    def begin(self):
        self.rounded[...] = low(self.local[...])
        for n, (index, to) in enumerate(self.partners):
            rows = self.rounded.at[pl.ds(index * self.quarter, self.quarter)]
            self.moves.append(copy_to(rows, self.got.at[self.mine], self.send.at[0, n], self.arrive.at[0, self.mine], to))
            self.moves.append(
                copy_to(self.decay, self.got_decay.at[self.mine], self.send.at[1, n], self.arrive.at[1, self.mine], to)
            )
        for move in self.moves:
            move.start()
        self.got[self.mine] = self.rounded[pl.ds(self.mine * self.quarter, self.quarter)]
        self.got_decay[self.mine] = self.decay[...]

    def needs(self, source, target):
        return (source > target) if self.back else (source < target)

    def far(self, n, to):
        zh = self.zh
        return (
            copy_to(self.stage, self.sums.at[zh], self.far_send.at[0, n], self.far_arrive.at[0, zh], {"zh": to}),
            copy_to(
                self.stage_decay, self.sum_decays.at[zh], self.far_send.at[1, n], self.far_arrive.at[1, zh], {"zh": to}
            ),
        )

    def combine(self):
        for index, _ in self.partners:
            wait_for(self.got.at[index], self.arrive.at[0, index])
            wait_for(self.got_decay.at[index], self.arrive.at[1, index])
        total, total_decay = None, None
        for k in self.order:
            piece, d = self.got[k].astype(F32), self.got_decay[k][:1]
            total = piece if total is None else d * total + piece
            total_decay = d if total_decay is None else total_decay * d
        self.stage[...] = low(total)
        self.stage_decay[...] = jnp.broadcast_to(total_decay, self.stage_decay.shape)
        for n in range(1, self.highs):
            to = lax.rem(self.zh + n, self.highs)

            @pl.when(self.needs(self.zh, to))
            def _(n=n, to=to):
                for move in self.far(n, to):
                    move.start()

    def spread(self):
        self.entering[...] = jnp.zeros_like(self.entering)
        for n in range(self.highs):
            k = self.highs - 1 - n if self.back else n

            @pl.when(self.needs(k, self.zh))
            def _(k=k):
                wait_for(self.sums.at[k], self.far_arrive.at[0, k])
                wait_for(self.sum_decays.at[k], self.far_arrive.at[1, k])
                self.entering[...] = self.sum_decays[k][:1] * self.entering[...] + self.sums[k].astype(F32)

        state = self.entering[...]
        for k in self.order:
            self.leave[k] = low(state)
            state = self.got_decay[k][:1] * state + self.got[k].astype(F32)
        for n, (index, to) in enumerate(self.partners):
            self.outs.append(
                copy_to(
                    self.leave.at[index], self.enter.at[self.mine], self.leave_send.at[n],
                    self.leave_arrive.at[self.mine], to,
                )
            )
        for move in self.outs:
            move.start()
        self.enter[self.mine] = self.leave[self.mine]

    def finish(self):
        for index, _ in self.partners:
            wait_for(self.enter.at[index], self.leave_arrive.at[index])
        for k in range(4):
            self.out[pl.ds(k * self.quarter, self.quarter)] = self.enter[k].astype(F32)

    def wait_sent(self):
        for move in self.moves + self.outs:
            move.wait_send()
        for n in range(1, self.highs):
            to = lax.rem(self.zh + n, self.highs)

            @pl.when(self.needs(self.zh, to))
            def _(n=n, to=to):
                for move in self.far(n, to):
                    move.wait_send()


def state_pass_scratch(highs):
    quarter = HD // 4
    return [
        pltpu.VMEM((HD, HD), BF),
        pltpu.VMEM((4, quarter, HD), BF),
        pltpu.VMEM((4, 8, HD), F32),
        pltpu.VMEM((highs, quarter, HD), BF),
        pltpu.VMEM((highs, 8, HD), F32),
        pltpu.VMEM((quarter, HD), BF),
        pltpu.VMEM((8, HD), F32),
        pltpu.VMEM((quarter, HD), F32),
        pltpu.VMEM((4, quarter, HD), BF),
        pltpu.VMEM((4, quarter, HD), BF),
        DMA((2, 3)),
        DMA((2, 4)),
        DMA((2, highs)),
        DMA((2, highs)),
        DMA((3,)),
        DMA((4,)),
    ]


STATE_REFS = 16


def forward_kernel(*refs):
    (
        mixer_in, mixer_out, ffn_in, ffn_out, small, ups, own, cot, starts_row, starts_column, head_gain,
        mixer_w, merge_w, pair_w, down_w, gains, cots, hidden, low_rank, gate, cumulated, projected, mixed, gated,
        befores, decay, second, middle,
        mixer_v, merge_v, projected_v, updates, inputs, smalls, ups_got, columns, state, partial, got, relayed, staged, line,
        own_send, own_arrive, far_send, arrive, small_send, small_arrive, ups_sem, inputs_send, inputs_arrive,
        cot_send, cot_arrive, sum_send, sum_arrive, spread_send, spread_arrive, saves,
    ) = refs[:-STATE_REFS]
    me = Place()
    zh, y, highs = lax.axis_index("zh"), lax.axis_index("y"), lax.axis_size("zh")
    units = down_w.shape[-1]
    width = own.shape[1]
    chunks = hidden.shape[0]
    first = ((zh * 2 + me.c) * 2 + y) * (chunks * CHUNK)
    greet_all(me)
    twin, side = {"c": 1 - me.c}, {"y": 1 - y}

    def own_source(part, k):
        if part < 5:
            at = pl.ds(pl.multiple_of(k * HD, HD), HD)
            return mixer_out.at[:, at] if part == 4 else mixer_in.at[part, :, at]
        at = pl.ds(pl.multiple_of(k * units, LANES), units)
        return ffn_out.at[:, at] if part == 7 else ffn_in.at[part - 5, :, at]

    def piece(at_zh, at_y, x, part, zl=slice(None)):
        if part < 4:
            return mixer_v.at[at_zh, zl, at_y, x, :, pl.ds(part * HD, HD)]
        if part == 4:
            return merge_v.at[at_zh, zl, at_y, x]
        if part < 7:
            return pair_w.at[at_zh, zl, at_y, x, :, pl.ds((part - 5) * units, units)]
        return down_w.at[at_zh, zl, at_y, x]

    firsts = [
        Placed(
            route_weights(me),
            lambda k, p=p: own_source(p, k),
            lambda zl, p=p: piece(zh, y, me.x, p, zl),
            lambda zl, p=p: piece(zh, y, me.c, p, zl),
            own_send.at[p],
            own_arrive.at[p],
        )
        for p in range(8)
    ]
    count = [0]
    sent = []

    def forward(at_zh, at_y, part, to):
        place = piece(at_zh, at_y, me.c, part)
        copy = copy_to(place, place, far_send.at[count[0]], arrive.at[at_zh, at_y, me.c, part], to)
        copy.start()
        count[0] += 1
        sent.append(copy)

    def arrived(at_zh, at_y, x, part):
        wait_for(piece(at_zh, at_y, x, part), arrive.at[at_zh, at_y, x, part])

    def send_own(part):
        firsts[part].wait_arrive()
        firsts[part].wait_local()
        for k in range(1, highs):
            forward(zh, y, part, {"zh": lax.rem(zh + k, highs)})
        forward(zh, y, part, side)
        forward(zh, y, part, twin)

    def pass_high(part):
        for k in range(1, highs):
            at_zh = lax.rem(zh + k, highs)
            arrived(at_zh, y, me.c, part)
            forward(at_zh, y, part, side)
            forward(at_zh, y, part, twin)

    def pass_side(part):
        for k in range(highs):
            at_zh = lax.rem(zh + k, highs)
            arrived(at_zh, 1 - y, me.c, part)
            forward(at_zh, 1 - y, part, twin)

    def complete(part):
        for k in range(highs):
            at_zh = lax.rem(zh + k, highs)
            arrived(at_zh, y, 1 - me.c, part)
            arrived(at_zh, 1 - y, 1 - me.c, part)

    save_count = [0]
    saved = []

    def save(source, target):
        copy = pltpu.make_async_copy(source, target, saves.at[save_count[0]])
        copy.start()
        save_count[0] += 1
        saved.append(copy)

    order = (1, 2, 0, 3, 4)
    for part in order:
        firsts[part].start()
    move_small = Transfer(route_all(me), lambda _: small, lambda k: smalls.at[k], small_send, small_arrive)
    move_small.start()
    lend = copy_to(ups, ups_got, ups_sem.at[0], ups_sem.at[1], twin)
    lend.start()
    for part in order:
        send_own(part)
    move_inputs = HalvesSpread(me, own, lambda k: inputs.at[k], inputs_send, inputs_arrive)
    move_cot = MemberSpread(me, cot, lambda k: cots.at[k], cot_send, cot_arrive)
    move_inputs.start()
    for part in (5, 6, 7):
        firsts[part].start()
    move_inputs.relay()
    pass_high(1)
    move_small.wait()
    lend.wait()
    owner_rows = smalls.shape[1]
    for n in range(smalls.shape[0]):
        columns[pl.ds(n * owner_rows, owner_rows)] = smalls[n].astype(F32)
    gains[...] = columns[...].T
    pass_high(2)
    move_inputs.wait()

    up = jnp.where(me.c == me.zl, ups[...], ups_got[...])
    rank_up, bias = low(up[:16]), up[16:17]
    down = low(columns[...])
    lower = (
        lax.broadcasted_iota(jnp.int32, (CHUNK, CHUNK), 0)
        >= lax.broadcasted_iota(jnp.int32, (CHUNK, CHUNK), 1)
    ).astype(F32)

    def gates_step(n, _):
        x = inputs[n].astype(F32)
        scale = lax.rsqrt(jnp.mean(x * x, -1, keepdims=True) + EPSILON)
        h = low(x * scale * gains[0:1])
        hidden[n] = h
        z = low(dot(h, down))
        low_rank[n] = z
        a = dot(z[:, 2:18], rank_up) + bias
        gate[n] = a
        log_gate = (jnp.minimum(a, 0.0) - jnp.log1p(jnp.exp(-jnp.abs(a)))) / 16.0
        cumulated[n] = jnp.dot(
            lower, log_gate, precision=lax.Precision.HIGHEST, preferred_element_type=F32
        )
        return 0

    lax.fori_loop(0, chunks, gates_step, 0)

    def project(part):
        rows = hidden[...].reshape(chunks * CHUNK, width)
        block = mixer_v[:, :, :, :, :, pl.ds(part * HD, HD)].reshape(width, HD)
        result = dot(rows, block)
        if part == 0:
            result = result * HD ** (-0.5)
        projected_v[part] = result.reshape(chunks, CHUNK, HD)
        save(projected_v.at[part], projected.at[part])

    pass_side(1)
    pass_side(2)
    pass_high(0)
    for part in (5, 6, 7):
        send_own(part)
    complete(1)
    project(1)
    complete(2)
    project(2)
    pass_high(3)

    state[...] = jnp.zeros_like(state)
    decay[...] = jnp.ones_like(decay)

    def masks(n):
        return keyed_mask(first + n * CHUNK, starts_row, starts_column)

    def local_step(n, _):
        _, _, keep, last = masks(n)
        b = cumulated[n]
        end = b[CHUNK - 1 :]
        kc = low(projected_v[1, n] * jnp.exp(end - b) * last)
        update = dot_rows(low(projected_v[2, n]), kc)
        updates[n] = update
        carry = keep * jnp.exp(end)
        state[...] = carry * state[...] + update
        decay[...] = decay[...] * carry
        return 0

    lax.fori_loop(0, chunks, local_step, 0)
    states = StatePass(False, state, decay, state, *refs[-STATE_REFS:])
    states.begin()
    pass_side(0)
    pass_high(4)
    complete(0)
    project(0)
    states.combine()
    pass_side(3)
    pass_side(4)

    def inner_step(n, _):
        pair, _, _, _ = masks(n)
        b = cumulated[n]
        mid = b[CHUNK // 2 - 1 : CHUNK // 2]
        qh = low(projected_v[0, n] * jnp.exp(b - mid))
        kh = low(projected_v[1, n] * jnp.exp(mid - b))
        scores = low(jnp.where(pair, dot_last(qh, kh), 0.0))
        mixed[n] = dot(scores, low(projected_v[2, n]))
        return 0

    lax.fori_loop(0, chunks, inner_step, 0)
    states.spread()
    complete(3)
    project(3)
    states.finish()

    def outer_step(n, _):
        _, visible, keep, _ = masks(n)
        b = cumulated[n]
        before = state[...]
        qd = low(projected_v[0, n] * jnp.exp(b) * visible)
        out = mixed[n] + dot_last(qd, low(before))
        mixed[n] = out
        befores[n] = low(before)
        state[...] = keep * jnp.exp(b[CHUNK - 1 :]) * before + updates[n]
        scale = lax.rsqrt(jnp.mean(out * out, -1, keepdims=True) + HEAD_FLOOR)
        u = projected_v[3, n]
        gated[n] = low(out * scale * head_gain[...] * (u * jax.nn.sigmoid(u)))
        return 0

    lax.fori_loop(0, chunks, outer_step, 0)
    complete(4)

    def merge_step(n, _):
        partial[n] = low(dot_last(gated[n], merge_v[...].reshape(width, HD)))
        return 0

    lax.fori_loop(0, chunks, merge_step, 0)

    steps = sum_send.shape[0]
    rows = own.shape[0] // steps

    def rows_of(ref, k, n):
        return ref.at[k, pl.ds(n * rows, rows)]

    sums = [
        OwnersSum(
            me,
            lambda k, n=n: rows_of(partial, k, n),
            lambda k, n=n: rows_of(got, k, n),
            lambda k, n=n: rows_of(relayed, k, n),
            lambda k, n=n: rows_of(staged, k, n),
            sum_send.at[n],
            sum_arrive.at[n],
        )
        for n in range(steps)
    ]
    spreads = [
        MemberSpread(
            me,
            line.at[pl.ds(n * rows, rows)],
            lambda k, n=n: rows_of(second, k, n),
            spread_send.at[n],
            spread_arrive.at[n],
        )
        for n in range(steps)
    ]
    for transfer in sums:
        transfer.start()
    pass_high(5)
    for transfer in sums:
        transfer.relay()
    for n in range(steps):
        at = pl.ds(n * rows, rows)
        total = own[at].astype(F32) + sums[n].total()
        middle[at] = total
        scale = lax.rsqrt(jnp.mean(total * total, -1, keepdims=True) + EPSILON)
        line[at] = low(total * scale * gains[1:2])
        spreads[n].start()
        if n:
            spreads[n - 1].relay()
    spreads[steps - 1].relay()
    move_cot.start()
    save(mixer_v, mixer_w)
    save(merge_v, merge_w)
    pass_high(6)
    pass_side(5)
    move_cot.relay()
    pass_high(7)
    for part in (6, 7):
        pass_side(part)
    for part in (5, 6, 7):
        complete(part)
    for transfer in sums:
        transfer.wait_sent()
    for transfer in spreads:
        transfer.wait()
    states.wait_sent()
    move_cot.wait()
    for transfer in firsts:
        transfer.wait_sent()
    for copy in sent:
        copy.wait_send()
    for copy in saved:
        copy.wait()


def starts_arrays(starts):
    starts = jnp.pad(starts, (0, LANES - starts.shape[0]), constant_values=jnp.int32(1 << 30))
    return jnp.broadcast_to(starts[None], (8, LANES)), jnp.broadcast_to(starts[:16, None], (16, LANES))


def forward(mixer_in, mixer_out, ffn_in, ffn_out, small, ups, own, cot, starts, head_gain):
    highs = lax.axis_size("zh")
    chips = highs * 8
    rows, half, width = small.shape[0], own.shape[0], own.shape[1]
    units = ffn_out.shape[1] // 2
    chunks = TEAM * half // CHUNK

    def shape(*dims, kind=BF):
        return jax.ShapeDtypeStruct(dims, kind)

    shapes = [
        (shape(highs, 2, 2, 2, rows, 4 * HD), ANY),
        (shape(highs, 2, 2, 2, rows, HD), ANY),
        (shape(highs, 2, 2, 2, rows, 2 * units), ANY),
        (shape(highs, 2, 2, 2, rows, units), ANY),
        (shape(LANES, width, kind=F32), VMEM),
        (shape(TEAM, half, width), ANY),
        (shape(chunks, CHUNK, width), VMEM),
        (shape(chunks, CHUNK, LANES), VMEM),
        (shape(chunks, CHUNK, HD, kind=F32), VMEM),
        (shape(chunks, CHUNK, HD, kind=F32), VMEM),
        (shape(4, chunks, CHUNK, HD, kind=F32), ANY),
        (shape(chunks, CHUNK, HD, kind=F32), VMEM),
        (shape(chunks, CHUNK, HD), VMEM),
        (shape(chunks, HD, HD), VMEM),
        (shape(8, HD, kind=F32), VMEM),
        (shape(TEAM, half, width), VMEM),
        (shape(half, width, kind=F32), VMEM),
    ]
    arrays = [mixer_in, mixer_out, ffn_in, ffn_out, small, ups, own, cot, *starts_arrays(starts), head_gain]
    scratch = [
        shapes[0][0],
        shapes[1][0],
        shapes[10][0],
        shape(chunks, HD, HD, kind=F32),
        shape(TEAM, half, width),
        shape(chips, rows, LANES),
        shape(*ups.shape, kind=F32),
        shape(width, LANES, kind=F32),
        shape(HD, HD, kind=F32),
        shape(TEAM, half, width),
        shape(3, half, width),
        shape(2, half, width),
        shape(2, half, width),
        shape(half, width),
    ]
    used = arrays + scratch + [a for a, place in shapes if place is VMEM]
    size = sum(a.size * a.dtype.itemsize for a in used)
    forwards = 8 * ((highs - 1) + highs + 2 * highs)
    sems = [
        (8, 2), (8, 2), (forwards,), (highs, 2, 2, 8), (chips,), (chips,), (2,), (5,), (4,), (3,), (4,),
        (STEPS, 6), (STEPS, 5), (STEPS, 3), (STEPS, 4), (7,),
    ]
    return pl.pallas_call(
        forward_kernel,
        out_shape=[a for a, _ in shapes],
        in_specs=[VMEM] * len(arrays),
        out_specs=[place for _, place in shapes],
        scratch_shapes=[pltpu.VMEM(a.shape, a.dtype) for a in scratch]
        + [DMA(n) for n in sems]
        + state_pass_scratch(highs),
        compiler_params=pltpu.CompilerParams(
            collective_id=0, has_side_effects=True, vmem_limit_bytes=min(size + (14 << 20), 62 << 20)
        ),
        name="forward",
    )(*arrays)


STEPS = 4


CROSS = [(0, 1), (1, 0)]


TILE = 256


def turn_rows(me, source, target):
    zh, y, highs = lax.axis_index("zh"), lax.axis_index("y"), lax.axis_size("zh")
    chunks, _, width = source.shape
    owners = highs * 8
    rows = width // owners
    for n in range(chunks):
        turned = source[n].T
        for chip in range(owners):
            at_zh, zl, at_y, x = chip // 8, chip // 4 % 2, chip // 2 % 2, chip % 2
            x_place = me.c if x == 1 else 1 - me.c
            y_place = y if at_y == 1 else 1 - y
            place = ((x_place * 2 + y_place) * highs + lax.rem(at_zh - zh + highs, highs)) * 2 + zl
            at = pl.ds(pl.multiple_of(place * rows, rows), rows)
            target[at, n * CHUNK : (n + 1) * CHUNK] = turned[chip * rows : (chip + 1) * rows]


def feed_forward_kernel(
    hidden, cots, pair_w, down_w,
    forth, back, pair_away, pair_keep, down_part,
    pair_v, down_v, act, grad_gate, grad_up, left_hidden, left_cots, tiles, tiles_got, down_away, down_keep,
    loads, tile_send, tile_arrive, side,
):
    me = Place()
    y = lax.axis_index("y")
    chunks, _, width = hidden.shape
    units = down_w.shape[1]
    tokens = chunks * CHUNK
    barrier = pltpu.get_barrier_semaphore()
    for to in ({"c": 1 - me.c}, {"y": 1 - y}):
        pl.semaphore_signal(barrier, inc=1, device_id=to, device_id_type=MESH)
    spans = [(n * TILE, min(TILE, units - n * TILE)) for n in range(-(-units // TILE))]

    def load(kind, n):
        start, size = spans[n]
        if kind == 2:
            return pltpu.make_async_copy(
                down_w.at[:, pl.ds(start, size)], down_v.at[:, pl.ds(start, size)], loads.at[2, n]
            )
        at = pl.ds(kind * units + start, size)
        return pltpu.make_async_copy(pair_w.at[:, at], pair_v.at[:, at], loads.at[kind, n])

    for n in range(len(spans)):
        for kind in range(3):
            load(kind, n).start()
    turn_rows(me, cots, left_cots)

    def units_step(start, size):
        at = pl.ds(start, size)
        rows = hidden[...].reshape(tokens, width)
        a = dot(rows, pair_v[:, at])
        b = dot(rows, pair_v[:, pl.ds(units + start, size)])
        da = dot(cots[...].reshape(tokens, width), down_v[:, at])
        sig = jax.nn.sigmoid(a)
        silu = a * sig
        act[:, at] = low(silu * b)
        grad_gate[:, at] = low(da * b * sig * (1.0 + a * (1.0 - sig)))
        grad_up[:, at] = low(da * silu)

    for n, (start, size) in enumerate(spans):
        for kind in range(3):
            load(kind, n).wait()
        if size < TILE:
            units_step(start, size)
    whole = units // TILE

    def whole_step(n, _):
        units_step(pl.multiple_of(n * TILE, TILE), TILE)
        return 0

    lax.fori_loop(0, whole, whole_step, 0)
    pl.semaphore_wait(barrier, 2)

    half = width // 2
    quarter = half // 2
    count = len(spans)

    def move(n):
        return copy_to(
            tiles.at[lax.rem(n, count)], tiles_got.at[n], tile_send.at[n], tile_arrive.at[n], {"c": 1 - me.c}
        )

    def send_tile(left, right, n, start, size):
        block = low(dot(left[pl.ds(0, half)], right[:, pl.ds(start, size)]))
        if size == TILE:
            tiles[lax.rem(n, count)] = block
        else:
            tiles[lax.rem(n, count), :, pl.ds(0, size)] = block
        move(n).start()

    def add_tile(left, right, n, start, size, away, keep, base):
        block = dot(left[pl.ds(half, half)], right[:, pl.ds(start, size)])
        move(n).wait_recv()
        block = low(block + tiles_got[n, :, pl.ds(0, size)].astype(F32))
        away[:, pl.ds(base + start, size)] = block[:quarter]
        keep[:, pl.ds(base + start, size)] = block[quarter:]

    def weight_grad(part, left, right, away, keep, base):
        first = part * count

        def send_step(n, _):
            if part:
                move(first + n - count).wait_send()
            send_tile(left, right, first + n, pl.multiple_of(n * TILE, TILE), TILE)
            return 0

        def add_step(n, _):
            add_tile(left, right, first + n, pl.multiple_of(n * TILE, TILE), TILE, away, keep, base)
            return 0

        lax.fori_loop(0, whole, send_step, 0)
        if whole < count:
            if part:
                move(first + whole - count).wait_send()
            send_tile(left, right, first + whole, *spans[whole])
        lax.fori_loop(0, whole, add_step, 0)
        if whole < count:
            add_tile(left, right, first + whole, *spans[whole], away, keep, base)

    weight_grad(0, left_cots, act, down_away, down_keep, 0)
    side_move = copy_to(down_away, down_part, side.at[0], side.at[1], {"y": 1 - y})
    side_move.start()

    def back_step(n, _):
        at = pl.ds(pl.multiple_of(n * TILE, TILE), TILE)
        block = dot_last(grad_gate[...], pair_v[at, pl.ds(0, units)])
        block = low(block + dot_last(grad_up[...], pair_v[at, pl.ds(units, units)]))
        ahead = low(dot_last(act[...], down_v[at]))
        for k in range(chunks):
            back[k, :, at] = block[k * CHUNK : (k + 1) * CHUNK]
            forth[k, :, at] = ahead[k * CHUNK : (k + 1) * CHUNK]
        return 0

    lax.fori_loop(0, width // TILE, back_step, 0)
    turn_rows(me, hidden, left_hidden)
    weight_grad(1, left_hidden, grad_gate, pair_away, pair_keep, 0)
    weight_grad(2, left_hidden, grad_up, pair_away, pair_keep, units)
    for n in range(2 * count, 3 * count):
        move(n).wait_send()
    side_move.wait()
    add_rows(down_part, down_keep, down_part)


def feed_forward(hidden, cots, pair_w, down_w):
    chunks, _, width = hidden.shape
    units = down_w.shape[1]
    tokens, half = chunks * CHUNK, width // 2
    count = -(-units // TILE)

    def shape(*dims, kind=BF):
        return jax.ShapeDtypeStruct(dims, kind)

    shapes = [
        shape(*hidden.shape),
        shape(*hidden.shape),
        shape(half // 2, 2 * units),
        shape(half // 2, 2 * units),
        shape(half // 2, units),
    ]
    scratch = [
        shape(width, 2 * units),
        shape(width, units),
        shape(tokens, units),
        shape(tokens, units),
        shape(tokens, units),
        shape(width, tokens),
        shape(width, tokens),
        shape(count, half, TILE),
        shape(3 * count, half, TILE),
        shape(half // 2, units),
        shape(half // 2, units),
    ]
    size = sum(a.size * a.dtype.itemsize for a in [hidden, cots] + shapes + scratch)
    sems = [(3, count), (3 * count,), (3 * count,), (2,)]
    return pl.pallas_call(
        feed_forward_kernel,
        out_shape=shapes,
        in_specs=[VMEM, VMEM, ANY, ANY],
        out_specs=[VMEM] * len(shapes),
        scratch_shapes=[pltpu.VMEM(a.shape, a.dtype) for a in scratch] + [DMA(n) for n in sems],
        compiler_params=pltpu.CompilerParams(
            collective_id=5, has_side_effects=True, vmem_limit_bytes=min(size + (10 << 20), 63 << 20)
        ),
        name="feed_forward",
    )(hidden, cots, pair_w, down_w)


def add_rows(out, *parts):
    def step(n, _):
        at = pl.ds(n * 16, 16)
        total = parts[0][at].astype(F32)
        for part in parts[1:]:
            total = total + part[at].astype(F32)
        out[at] = low(total)
        return 0

    lax.fori_loop(0, out.shape[0] // 16, step, 0)


def backward_kernel(*refs):
    (
        back, forth, cot, middle, gain, pair_away, pair_keep, downs, merge_w, gated, projected, mixed,
        cumulated, gate, befores, decay, low_rank, up_pad, head_gain, hidden, starts_row, starts_column,
        grad_middle, gain_grad, proj, ranks, heads, early_away, early_keep, gate_sum, up_sum, down_sum, left_hidden,
        result, got, relayed, staged, line, got2, relayed2, staged2, line2, branch, left_branch, douts, tiles, tiles_got,
        pair_side, gate_got, up_got, down_got, up_grad, state,
        send, arrive, send2, arrive2, side_send, side_arrive, high_send, high_arrive, tile_send, tile_arrive,
        send3, arrive3, twin_send, twin_arrive, here,
    ) = refs[:-STATE_REFS]
    me = Place()
    zh, y, highs = lax.axis_index("zh"), lax.axis_index("y"), lax.axis_size("zh")
    chunks, _, width = hidden.shape
    units = downs.shape[-1]
    first = ((zh * 2 + me.c) * 2 + y) * (chunks * CHUNK)
    greet_all(me)

    def columns(ref, part):
        return ref.at[:, :, :, pl.ds((part - 1) * units, units)]

    def source(part):
        return downs if part == 0 else columns(pair_side, part)

    sides = [
        copy_to(columns(pair_away, p), columns(pair_side, p), side_send.at[p], side_arrive.at[p], {"y": 1 - y})
        for p in (1, 2)
    ]
    high_got, high_sum = (down_got, gate_got, up_got), (down_sum, gate_sum, up_sum)
    highs_moves = [
        [
            copy_to(
                source(p).at[k],
                high_got[p].at[k - 1],
                high_send.at[p, k],
                high_arrive.at[p, k],
                {"zh": lax.rem(zh + k, highs)},
            )
            for k in range(1, highs)
        ]
        for p in range(3)
    ]

    def high_start(part):
        if part:
            sides[part - 1].wait()
            mine, there = columns(pair_keep, part), columns(pair_side, part)
            for k in range(highs):
                for m in range(2):
                    add_rows(there.at[k, m], mine.at[k, m], there.at[k, m])
        for move in highs_moves[part]:
            move.start()

    def high_add(part):
        there, out = high_got[part], high_sum[part]
        for k in range(1, highs):
            wait_for(there.at[k - 1], high_arrive.at[part, k])
        for m in range(2):
            add_rows(out.at[m], source(part).at[0, m], *(there.at[k - 1, m] for k in range(1, highs)))

    for move in sides:
        move.start()
    high_start(0)

    steps = send.shape[0]
    rows = cot.shape[0] // steps

    def part(ref, k, n):
        return ref.at[k, pl.ds(n * rows, rows)]

    sums = [
        MemberSum(
            me,
            lambda k, n=n: part(back, k, n),
            lambda k, n=n: part(got, k, n),
            lambda k, n=n: part(relayed, k, n),
            lambda k, n=n: part(staged, k, n),
            send.at[n],
            arrive.at[n],
            two="zl",
        )
        for n in range(steps)
    ]
    spreads = [
        HalvesSpread(
            me,
            line.at[pl.ds(n * rows, rows)],
            lambda k, n=n: part(branch, k, n),
            send2.at[n],
            arrive2.at[n],
        )
        for n in range(steps)
    ]
    forth_sums = [
        MemberSum(
            me,
            lambda k, n=n: part(forth, k, n),
            lambda k, n=n: part(got2, k, n),
            lambda k, n=n: part(relayed2, k, n),
            lambda k, n=n: part(staged2, k, n),
            send3.at[n],
            arrive3.at[n],
        )
        for n in range(steps)
    ]

    def twin_copy(n):
        return copy_to(
            line2.at[pl.ds(n * rows, rows)],
            part(result, me.c, n),
            twin_send.at[n],
            twin_arrive.at[n],
            {"c": 1 - me.c},
        )

    def own_copy(n):
        return pltpu.make_async_copy(line2.at[pl.ds(n * rows, rows)], part(result, me.c, n), here.at[n])

    for transfer in sums:
        transfer.start()

    turn_rows(me, hidden, left_hidden)
    for transfer in sums:
        transfer.relay()
    for n in range(steps):
        at = pl.ds(n * rows, rows)
        mid = middle[at]
        scale = lax.rsqrt(jnp.mean(mid * mid, -1, keepdims=True) + EPSILON)
        normed = mid * scale
        total = sums[n].total()
        gsum = jnp.sum(total * normed, axis=0, keepdims=True)
        gain_grad[...] = gsum if n == 0 else gain_grad[...] + gsum
        scaled = total * gain[...]
        out = cot[at].astype(F32) + scale * (
            scaled - normed * jnp.mean(scaled * normed, -1, keepdims=True)
        )
        grad_middle[at] = out
        line[at] = low(out)
        spreads[n].start()
        if n:
            spreads[n - 1].relay()
        if n == 2:
            high_start(1)
    spreads[steps - 1].relay()
    for transfer in spreads:
        transfer.wait()
    for transfer in forth_sums:
        transfer.start()

    heads[...] = jnp.zeros_like(heads)

    def head_step(n, _):
        grad = dot(branch[n], merge_w[...])
        out = mixed[n]
        scale = lax.rsqrt(jnp.mean(out * out, -1, keepdims=True) + HEAD_FLOOR)
        normed = out * scale
        u = projected[3, n]
        sig = jax.nn.sigmoid(u)
        dn = grad * (u * sig)
        proj[n, :, 3 * HD :] = low(grad * normed * head_gain[...] * sig * (1.0 + u * (1.0 - sig)))
        heads[17:18] = heads[17:18] + jnp.sum(dn * normed, axis=0, keepdims=True)
        scaled = dn * head_gain[...]
        douts[n] = low(scale * (scaled - normed * jnp.mean(scaled * normed, -1, keepdims=True)))
        return 0

    lax.fori_loop(0, chunks, head_step, 0)

    def masks(n):
        return keyed_mask(first + n * CHUNK, starts_row, starts_column)

    def query_rows(n, visible):
        return low(projected[0, n] * jnp.exp(cumulated[n]) * visible)

    state[...] = jnp.zeros_like(state)

    def local_step(i, _):
        n = chunks - 1 - i
        _, visible, keep, _ = masks(n)
        carry = keep * jnp.exp(cumulated[n, CHUNK - 1 :])
        state[...] = carry * state[...] + dot_rows(douts[n], query_rows(n, visible))
        return 0

    lax.fori_loop(0, chunks, local_step, 0)
    states = StatePass(True, state, decay, state, *refs[-STATE_REFS:])
    states.begin()
    high_start(2)

    turn_rows(me, branch, left_branch)
    half = width // 2
    quarter = half // 2

    def tile_move(n):
        return copy_to(tiles.at[n], tiles_got.at[n], tile_send.at[n], tile_arrive.at[n], {"c": 1 - me.c})

    def right_tile(kind, n):
        if kind == 0:
            return gated[...].reshape(chunks * CHUNK, HD)[:, n * TILE : (n + 1) * TILE]
        at = 3 * HD + n * TILE
        return proj[...].reshape(chunks * CHUNK, 4 * HD)[:, at : at + TILE]

    lefts = left_branch, left_hidden
    for kind in range(2):
        for n in range(HD // TILE):
            tile = kind * (HD // TILE) + n
            tiles[tile] = low(dot(lefts[kind][pl.ds(0, half)], right_tile(kind, n)))
            tile_move(tile).start()
    states.combine()
    for kind in range(2):
        for n in range(HD // TILE):
            tile = kind * (HD // TILE) + n
            block = dot(lefts[kind][pl.ds(half, half)], right_tile(kind, n))
            tile_move(tile).wait_recv()
            block = low(block + tiles_got[tile].astype(F32))
            at = slice(tile * TILE, (tile + 1) * TILE)
            early_away[:, at] = block[:quarter]
            early_keep[:, at] = block[quarter:]
    states.spread()
    for transfer in forth_sums:
        transfer.relay()
    states.finish()

    upper = (
        lax.broadcasted_iota(jnp.int32, (CHUNK, CHUNK), 0)
        <= lax.broadcasted_iota(jnp.int32, (CHUNK, CHUNK), 1)
    ).astype(F32)
    up_grad[...] = jnp.zeros_like(up_grad)

    def chunk_step(i, _):
        n = chunks - 1 - i
        pair, visible, keep, last = masks(n)
        b = cumulated[n]
        mid, end = b[CHUNK // 2 - 1 : CHUNK // 2], b[CHUNK - 1 :]
        q, k, v = projected[0, n], projected[1, n], low(projected[2, n])
        do = douts[n]
        eq, ek, el = jnp.exp(b - mid), jnp.exp(mid - b), jnp.exp(end - b) * last
        qh, kh, kc = low(q * eq), low(k * ek), k * el
        scores = low(jnp.where(pair, dot_last(qh, kh), 0.0))
        gs = low(jnp.where(pair, dot_last(do, v), 0.0))
        ds = low(state[...])
        proj[n, :, 2 * HD : 3 * HD] = low(dot_rows(scores, do) + dot_last(low(kc), ds))
        dq = dot(gs, kh) * eq + dot(do, low(befores[n])) * (jnp.exp(b) * visible)
        gkc = dot(v, ds)
        dk = dot_rows(gs, qh) * ek + gkc * el
        proj[n, :, :HD] = low(dq * HD ** (-0.5))
        proj[n, :, HD : 2 * HD] = low(dk)
        carry = keep * jnp.exp(end)
        extra = jnp.sum(gkc * kc, axis=0, keepdims=True)
        extra = extra + carry * jnp.sum(befores[n] * state[...], axis=0, keepdims=True)
        dlog = extra + jnp.dot(
            upper, dq * q - dk * k, precision=lax.Precision.HIGHEST, preferred_element_type=F32
        )
        state[...] = carry * state[...] + dot_rows(do, query_rows(n, visible))
        da = dlog * jax.nn.sigmoid(-gate[n]) / 16.0
        heads[16:17] = heads[16:17] + jnp.sum(da, axis=0, keepdims=True)
        dar = low(da)
        up_grad[...] = up_grad[...] + dot_rows(low_rank[n], dar)
        ranks[n] = low(dot_last(dar, up_pad[...]))
        return 0

    lax.fori_loop(0, chunks, chunk_step, 0)
    heads[0:16] = up_grad[2:18]
    for n in range(steps):
        at = pl.ds(n * rows, rows)
        line2[at] = low(middle[at] + forth_sums[n].total())
        twin_copy(n).start()
        own_copy(n).start()
    for p in range(3):
        high_add(p)
    for n in range(steps):
        twin_copy(n).wait()
        own_copy(n).wait()
    for transfer in forth_sums:
        transfer.wait_sent()
    for group in highs_moves:
        for move in group:
            move.wait_send()
    for transfer in sums:
        transfer.wait_sent()
    for tile in range(tiles.shape[0]):
        tile_move(tile).wait_send()
    states.wait_sent()


def backward(
    back, forth, cot, middle, gain, pair, downs, merge_w, gated, projected, mixed, cumulated, gate, befores, decay,
    low_rank, up_pad, head_gain, hidden, starts,
):
    highs, members, owner_rows, units = downs.shape
    rows, width = cot.shape
    chunks = hidden.shape[0]

    def shape(*dims, kind=BF):
        return jax.ShapeDtypeStruct(dims, kind)

    arrays = [
        back, forth, cot, middle, gain, *pair, downs, merge_w, gated, projected, mixed, cumulated, gate, befores, decay,
        low_rank, up_pad, head_gain, hidden, *starts_arrays(starts),
    ]
    away = {5}
    quarter = width // 4
    shapes = [
        shape(rows, width, kind=F32),
        shape(1, width, kind=F32),
        shape(chunks, CHUNK, 4 * HD),
        shape(chunks, CHUNK, LANES),
        shape(24, HD, kind=F32),
        shape(quarter, 2 * HD),
        shape(quarter, 2 * HD),
        shape(members, owner_rows, units),
        shape(members, owner_rows, units),
        shape(members, owner_rows, units),
        shape(width, chunks * CHUNK),
        shape(2, rows, width),
    ]
    tiles = 2 * HD // TILE
    scratch = [
        shape(2, rows, width),
        shape(1, rows, width),
        shape(1, rows, width),
        shape(rows, width),
        shape(2, rows, width),
        shape(1, rows, width),
        shape(1, rows, width),
        shape(rows, width),
        shape(TEAM, rows, width),
        shape(width, chunks * CHUNK),
        shape(chunks, CHUNK, HD),
        shape(tiles, width // 2, TILE),
        shape(tiles, width // 2, TILE),
        shape(highs, members, owner_rows, 2 * units),
        shape(highs - 1, members, owner_rows, units),
        shape(highs - 1, members, owner_rows, units),
        shape(highs - 1, members, owner_rows, units),
        shape(LANES, HD, kind=F32),
        shape(HD, HD, kind=F32),
    ]
    used = [a for n, a in enumerate(arrays) if n not in away] + shapes + scratch
    size = sum(a.size * a.dtype.itemsize for a in used)
    sems = [
        (STEPS, 3), (STEPS, 3), (STEPS, 5), (STEPS, 4), (3,), (3,), (3, highs), (3, highs), (tiles,), (tiles,),
        (STEPS, 3), (STEPS, 3), (STEPS,), (STEPS,), (STEPS,),
    ]
    return pl.pallas_call(
        backward_kernel,
        out_shape=shapes,
        in_specs=[ANY if n in away else VMEM for n in range(len(arrays))],
        out_specs=[VMEM] * len(shapes),
        scratch_shapes=[pltpu.VMEM(a.shape, a.dtype) for a in scratch]
        + [DMA(n) for n in sems]
        + state_pass_scratch(highs),
        compiler_params=pltpu.CompilerParams(
            collective_id=3, has_side_effects=True, vmem_limit_bytes=min(size + (14 << 20), 62 << 20)
        ),
        name="backward",
    )(*arrays)


def closing_kernel(*refs):
    (
        proj, ranks, mixer_w, left, own, grad_middle, gain, down, gain_two_grad, heads, early_away, early_keep,
        ups, gates, downs,
        out, mixer_grad, merge_grad, pair_grad, down_grad, wide_out, heads_out, gains_out,
        partial, got, relayed, staged, line, tiles, tiles_got, late_away, late_keep, late_side, early_side,
        late_got, early_got, late_sum, early_sum, late_home, early_home, ups_home, gate_home, down_home,
        wide, wide_got, heads_got, heads_sum, wide_twin, gain_grad, rank_grad,
        send, arrive, twin_send, twin_arrive, here, tile_send, tile_arrive, side_send, side_arrive,
        high_send, high_arrive, home_send, home_arrive,
        wide_send, wide_arrive, heads_send, heads_arrive, near, out_send, out_arrive, gain_send, gain_arrive,
    ) = refs
    me = Place()
    zh, y, highs = lax.axis_index("zh"), lax.axis_index("y"), lax.axis_size("zh")
    greet_all(me)
    steps = send.shape[0]
    rows, width = own.shape[0] // steps, own.shape[1]
    chunks = proj.shape[0]
    twin = {"c": 1 - me.c}

    def high_copies(kind, source, target):
        return [
            copy_to(
                source.at[k],
                target.at[k - 1],
                high_send.at[kind, k],
                high_arrive.at[kind, k],
                {"zh": lax.rem(zh + k, highs)},
            )
            for k in range(1, highs)
        ]

    def side_copy(kind, source, target):
        return copy_to(source, target, side_send.at[kind], side_arrive.at[kind], {"y": 1 - y})

    def home(kind, source, target):
        return Transfer(
            route_weights_home(me),
            lambda k: source.at[k],
            lambda k: target.at[k],
            home_send.at[kind],
            home_arrive.at[kind],
        )

    early_move = side_copy(3, early_away, early_side)
    late_moves = [side_copy(j, late_away.at[j], late_side.at[j]) for j in range(3)]
    high_moves = [high_copies(j, late_side.at[j], late_got.at[j]) for j in range(3)]
    high_moves += [high_copies(3, early_side, early_got)]
    homes = [home(j, late_sum.at[j], late_home.at[j]) for j in range(3)]
    homes += [home(3, early_sum, early_home), home(4, ups, ups_home)]
    homes += [home(5, gates, gate_home), home(6, downs, down_home)]
    group_out, group_arrive = [], []
    for n in range(highs):
        for f in range(4):
            to_zh, to_y, to_c = lax.rem(zh + n, highs), flip(y, f & 2), flip(me.c, f & 1)
            to = {"zh": to_zh, "y": to_y, "c": to_c}
            group_out.append((0, (zh * 2 + y) * 2 + me.c, to, n + f == 0))
            group_arrive.append(((to_zh * 2 + to_y) * 2 + to_c, n + f == 0))
    heads_move = Transfer(
        (group_out, group_arrive), lambda _: heads, lambda k: heads_got.at[k], heads_send, heads_arrive
    )
    heads_move.start()

    early_move.start()

    half = width // 2
    quarter = half // 2
    owner_rows = early_keep.shape[2]

    def tile_move(n):
        return copy_to(tiles.at[n], tiles_got.at[n], tile_send.at[n], tile_arrive.at[n], twin)

    def right_tile(n):
        return proj[:, :, pl.ds(pl.multiple_of(n * TILE, TILE), TILE)].reshape(chunks * CHUNK, TILE)

    def tile_step(n, _):
        tiles[n] = low(dot(left[pl.ds(0, half)], right_tile(n)))
        tile_move(n).start()
        return 0

    lax.fori_loop(0, 3 * HD // TILE, tile_step, 0)

    for n in range(chunks):
        partial[n, :, width:] = ranks[n]

    def hidden_step(n, _):
        at = pl.ds(pl.multiple_of(n * TILE, TILE), TILE)
        block = low(dot_last(proj[...].reshape(chunks * CHUNK, 4 * HD), mixer_w[at]))
        for k in range(chunks):
            partial[k, :, at] = block[k * CHUNK : (k + 1) * CHUNK]
        return 0

    lax.fori_loop(0, width // TILE, hidden_step, 0)

    def part(ref, k, n):
        return ref.at[k, pl.ds(n * rows, rows)]

    sums = [
        OwnersSum(
            me,
            lambda k, n=n: part(partial, k, n),
            lambda k, n=n: part(got, k, n),
            lambda k, n=n: part(relayed, k, n),
            lambda k, n=n: part(staged, k, n),
            send.at[n],
            arrive.at[n],
        )
        for n in range(steps)
    ]
    for transfer in sums:
        transfer.start()

    for j in range(3):
        for i in range(HD // TILE):
            n = j * (HD // TILE) + i
            block = dot(left[pl.ds(half, half)], right_tile(n))
            tile_move(n).wait_recv()
            block = low(block + tiles_got[n].astype(F32))
            columns = slice(i * TILE, (i + 1) * TILE)
            for k in range(highs):
                for m in range(2):
                    at = (k * 2 + m) * owner_rows
                    late_away[j, k, m, :, columns] = block[at : at + owner_rows]
                    late_keep[j, k, m, :, columns] = block[quarter + at : quarter + at + owner_rows]
        late_moves[j].start()
    for n in (6, 5, 4):
        homes[n].start()

    def side_add(move, keep, there):
        move.wait()
        for k in range(highs):
            for m in range(2):
                add_rows(there.at[k, m], keep.at[k, m], there.at[k, m])

    side_add(early_move, early_keep, early_side)
    for move in high_moves[3]:
        move.start()
    for transfer in sums:
        transfer.relay()
    for j in range(3):
        side_add(late_moves[j], late_keep.at[j], late_side.at[j])
        for move in high_moves[j]:
            move.start()

    def twin_copy(n):
        return copy_to(
            line.at[pl.ds(n * rows, rows)], part(out, me.c, n), twin_send.at[n], twin_arrive.at[n], twin
        )

    def own_copy(n):
        return pltpu.make_async_copy(line.at[pl.ds(n * rows, rows)], part(out, me.c, n), here.at[n])

    for n in range(steps):
        at = pl.ds(n * rows, rows)
        x = own[at].astype(F32)
        scale = lax.rsqrt(jnp.mean(x * x, -1, keepdims=True) + EPSILON)
        normed = x * scale
        total = sums[n].total()
        rank = low(total[:, width:])
        total = total[:, :width] + dot(rank, down[...])
        gsum = jnp.sum(total * normed, axis=0, keepdims=True)
        hidden = low(normed * gain[...])
        rsum = dot_rows(rank, hidden)
        gain_grad[...] = gsum if n == 0 else gain_grad[...] + gsum
        rank_grad[...] = rsum if n == 0 else rank_grad[...] + rsum
        scaled = total * gain[...]
        line[at] = low(
            grad_middle[at]
            + scale * (scaled - normed * jnp.mean(scaled * normed, -1, keepdims=True))
        )
        twin_copy(n).start()
        own_copy(n).start()

    for n in range(wide.shape[0]):
        at = slice(n * owner_rows, (n + 1) * owner_rows)
        wide[n, 0:1] = gain_grad[:, at]
        wide[n, 1:2] = gain_two_grad[:, at]
        wide[n, 2:8] = jnp.zeros((6, owner_rows), F32)
        wide[n, 8:24] = rank_grad[:16, at]
    spreads = Transfer(
        route_all(me), lambda k: wide.at[k], lambda k: wide_got.at[k], wide_send, wide_arrive
    )
    spreads.start()
    def high_add(kind, source, target, total):
        for k in range(1, highs):
            wait_for(target.at[k - 1], high_arrive.at[kind, k])
        for m in range(2):
            add_rows(total.at[m], source.at[0, m], *(target.at[k - 1, m] for k in range(1, highs)))
        homes[kind].start()


    heads_move.wait()
    total = heads_got[0]
    for n in range(1, highs * 4):
        total = total + heads_got[n]
    heads_sum[...] = total
    tail = gains_out.shape[1]
    gains = Transfer(
        route_member(me),
        lambda _: heads_sum.at[pl.ds(heads_sum.shape[0] - tail, tail)],
        lambda k: gains_out.at[k],
        gain_send,
        gain_arrive,
    )
    gains.start()
    moves = [
        copy_to(
            heads_sum,
            heads_out.at[me.x],
            out_send.at[n],
            out_arrive.at[me.x],
            {"zl": flip(me.zl, fz), "x": flip(me.x, fx)},
        )
        for n, (fz, fx) in enumerate(FLIPS[:3])
    ]

    @pl.when(me.c == me.zl)
    def _():
        for move in moves:
            move.start()
        heads_out[me.x] = heads_sum[...]

    spreads.wait()
    total = wide_got[0]
    for n in range(1, wide.shape[0]):
        total = total + wide_got[n]
    wide_out[...] = total
    swap = copy_to(wide_out, wide_twin, near.at[0], near.at[1], twin)
    swap.start()

    units = gates.shape[-1]

    def spread_columns(source, target, cols):
        for k in range(2):
            target[:, k * cols : (k + 1) * cols] = source[k].astype(F32)

    def spread_rows(source, target, cols):
        for k in range(2):
            target[k * cols : (k + 1) * cols] = source[k, :, :cols].astype(F32).T

    homes[6].wait()
    spread_rows(down_home, down_grad, units)
    homes[5].wait()
    spread_columns(gate_home, pair_grad.at[0], units)
    homes[4].wait()
    spread_columns(ups_home, pair_grad.at[1], units)
    high_add(3, early_side, early_got, early_sum)
    for k in range(2):
        own_slot = (me.c == me.zl) & (me.x == k)
        unless(own_slot, lambda k=k: wait_for(heads_out.at[k], out_arrive.at[k]))

    @pl.when(me.c == me.zl)
    def _():
        for move in moves:
            move.wait_send()

    swap.wait()
    wide_out[...] = wide_out[...] + wide_twin[...]
    gains.wait()
    for j in range(3):
        high_add(j, late_side.at[j], late_got.at[j], late_sum.at[j])
    homes[3].wait()
    spread_rows(early_home, merge_grad, HD)
    for k in range(2):
        mixer_grad[3, :, k * HD : (k + 1) * HD] = early_home[k, :, HD:].astype(F32)
    for j in range(3):
        homes[j].wait()
        spread_columns(late_home.at[j], mixer_grad.at[j], HD)
    for transfer in sums:
        transfer.wait_sent()
    for n in range(steps):
        twin_copy(n).wait()
        own_copy(n).wait()
    for group in high_moves:
        for move in group:
            move.wait_send()

    def tile_sent(n, _):
        tile_move(n).wait_send()
        return 0

    lax.fori_loop(0, tiles.shape[0], tile_sent, 0)


def closing(proj, ranks, mixer_w, left, own, grad_middle, gain, down, gain_two_grad, heads, early, ups, gates, downs):
    rows, width = own.shape
    chunks = proj.shape[0]
    highs, _, owner_rows, _ = early[0].shape
    units = ups.shape[-1]
    chips = highs * 8
    arrays = [
        proj, ranks, mixer_w, left, own, grad_middle, gain, down, gain_two_grad, heads, *early, ups, gates, downs,
    ]

    def shape(*dims, kind=BF):
        return jax.ShapeDtypeStruct(dims, kind)

    shapes = [
        shape(2, rows, width),
        shape(4, owner_rows, 2 * HD, kind=F32),
        shape(2 * HD, owner_rows, kind=F32),
        shape(2, owner_rows, 2 * units, kind=F32),
        shape(2 * units, owner_rows, kind=F32),
        shape(24, owner_rows, kind=F32),
        shape(2, *heads.shape, kind=F32),
        shape(TEAM, 8, heads.shape[1], kind=F32),
    ]
    tiles = 3 * HD // TILE
    late = (3, highs, 2, owner_rows, HD)
    scratch = [shape(chunks, CHUNK, width + LANES)]
    scratch += [shape(n, rows, width + LANES) for n in (3, 2, 2)] + [shape(rows, width)]
    scratch += [shape(tiles, width // 2, TILE)] * 2 + [shape(*late)] * 3 + [shape(*early[0].shape)]
    scratch += [
        shape(3, highs - 1, 2, owner_rows, HD),
        shape(highs - 1, 2, owner_rows, 2 * HD),
    ]
    sums = [shape(3, 2, owner_rows, HD), shape(2, owner_rows, 2 * HD)]
    scratch += sums + sums + [shape(2, owner_rows, units)] * 3
    scratch += [
        shape(chips, 24, owner_rows, kind=F32),
        shape(chips, 24, owner_rows, kind=F32),
        shape(highs * 4, *heads.shape, kind=F32),
        shape(*heads.shape, kind=F32),
        shape(24, owner_rows, kind=F32),
        shape(1, width, kind=F32),
        shape(LANES, width, kind=F32),
    ]
    size = sum(a.size * a.dtype.itemsize for a in arrays + shapes + scratch)
    sems = [
        (STEPS, 6), (STEPS, 5), (STEPS,), (STEPS,), (STEPS,), (tiles,), (tiles,), (4,), (4,), (4, highs), (4, highs),
        (7, 2), (7, 2), (chips,), (chips,), (highs * 4,), (highs * 4,), (2,), (3,), (2,), (TEAM,), (TEAM,),
    ]
    return pl.pallas_call(
        closing_kernel,
        out_shape=shapes,
        in_specs=[VMEM] * len(arrays),
        out_specs=[VMEM] * len(shapes),
        scratch_shapes=[pltpu.VMEM(a.shape, a.dtype) for a in scratch] + [DMA(n) for n in sems],
        compiler_params=pltpu.CompilerParams(
            collective_id=4, has_side_effects=True, vmem_limit_bytes=min(size + (10 << 20), 62 << 20)
        ),
        name="closing",
    )(*arrays)


def shards(
    tokens,
    cotangent,
    lengths,
    attn_gain,
    ffn_gain,
    mixer_in,
    decay_down,
    decay_up,
    decay_bias,
    head_gain,
    mixer_out,
    ffn_in,
    ffn_out,
):
    zh, zl, y, x, c = (lax.axis_index(a) for a in SEQ + ("c",))
    block, width = tokens.shape
    half = block // 2
    rows = mixer_in.shape[1]
    units = ffn_out.shape[0] // 2
    team_tokens = 2 * block
    rank = decay_down.shape[1]

    small = jnp.concatenate([attn_gain[:, None], ffn_gain[:, None], decay_down], axis=1)
    small = jnp.pad(small, ((0, 0), (0, LANES - small.shape[1])))
    up_head = lax.dynamic_slice_in_dim(decay_up, HD * x, HD, 1).astype(F32)
    bias_head = lax.dynamic_slice_in_dim(decay_bias, HD * x, HD, 0)
    ups = jnp.concatenate([up_head, bias_head[None], jnp.zeros((7, HD), F32)], axis=0)
    own = lax.dynamic_slice_in_dim(tokens, half * c, half, 0)
    own_dy = lax.dynamic_slice_in_dim(cotangent, half * c, half, 0)
    starts = jnp.cumsum(lengths) - lengths
    (
        mixer_w, merge_w, pair_w, down_w, gains, ffn_dy, hidden_one, low_rank, gate_input, cumulated, projected,
        mixed, gated, befores, decay, hidden_two, middle,
    ) = forward(
        mixer_in, mixer_out.T, ffn_in, ffn_out.T, small, ups, own, own_dy, starts, head_gain[None]
    )
    up_head = jnp.where(c == zl, up_head, lax.ppermute(up_head, "c", CROSS)).astype(BF)
    mixer_w, merge_w = mixer_w.reshape(width, 4 * HD), merge_w.reshape(width, HD)
    pair_w, down_w = pair_w.reshape(width, 2 * units), down_w.reshape(width, units)
    gain_one, gain_two, rank_down = gains[:1], gains[1:2], gains[2 : 2 + rank].astype(BF)
    forth, back, *pair_sides, down_part = feed_forward(hidden_two, ffn_dy, pair_w, down_w)
    highs = lax.axis_size("zh")
    pair_sides = [a.reshape(highs, 2, rows, 2 * units) for a in pair_sides]
    down_part = down_part.reshape(highs, 2, rows, units)
    pad_rank = ((0, LANES - rank), (0, 0))
    (
        grad_middle, grad_gain_two, grad_proj, grad_ranks, heads, early_away, early_keep, gate_sum, up_sum, down_sum,
        left_hidden, result,
    ) = backward(
        back, forth, own_dy, middle, gain_two, pair_sides, down_part, merge_w, gated, projected, mixed, cumulated,
        gate_input, befores, decay, low_rank, jnp.pad(up_head, pad_rank), head_gain[None], hidden_one, starts,
    )
    early_shape = (highs, 2, rows, 2 * HD)
    early_sums = early_away.reshape(early_shape), early_keep.reshape(early_shape)
    grad_inputs, mixer_home, merge_home, pair_home, down_home, wide, heads, gains = closing(
        grad_proj, grad_ranks, mixer_w, left_hidden, own, grad_middle, gain_one, jnp.pad(rank_down, pad_rank),
        grad_gain_two, heads, early_sums, up_sum, gate_sum, down_sum,
    )
    return (
        result.reshape(block, width),
        grad_inputs.reshape(block, width),
        wide[0],
        wide[1],
        mixer_home,
        wide[8 : 8 + rank].T,
        heads[:, :rank].transpose(1, 0, 2).reshape(rank, 2 * HD),
        heads[:, rank].reshape(2 * HD),
        jnp.sum(gains[:, rank + 1 - 16], axis=0),
        merge_home,
        pair_home,
        down_home,
    )


def solution(mesh):
    devices = mesh.devices
    inner = Mesh(devices.reshape(devices.shape[0] // 8, 2, 2, 2, devices.shape[1]), SEQ + ("c",))
    in_specs = (
        P(SEQ, None),
        P(SEQ, None),
        P(),
        P(SEQ),
        P(SEQ),
        P(None, SEQ, "c"),
        P(SEQ, None),
        P(None, "c"),
        P("c"),
        P(),
        P("c", SEQ),
        P(None, SEQ, "c"),
        P("c", SEQ),
    )
    out_specs = (
        P(SEQ, None),
        P(SEQ, None),
        P(SEQ),
        P(SEQ),
        P(None, SEQ, "c"),
        P(SEQ, None),
        P(None, "c"),
        P("c"),
        P(),
        P("c", SEQ),
        P(None, SEQ, "c"),
        P("c", SEQ),
    )
    return jax.shard_map(shards, mesh=inner, in_specs=in_specs, out_specs=out_specs, check_vma=False)
```

```python
import functools

import jax
import jax.numpy as jnp
from jax import lax
from jax.experimental import pallas as pl
from jax.experimental.pallas import tpu as pltpu
from jax.sharding import Mesh, PartitionSpec as P

HD = 512
CHUNK = 128
EPSILON = 1e-06
HEAD_FLOOR = 1.0
TEAM = 4

BF = jnp.bfloat16
F32 = jnp.float32
MESH = pl.DeviceIdType.MESH
ANY = pl.BlockSpec(memory_space=pl.ANY)
VMEM = pl.BlockSpec(memory_space=pltpu.VMEM)
DMA = pltpu.SemaphoreType.DMA

SEQ = ("zh", "zl", "y", "x")
FLIPS = ((1, 1), (0, 1), (1, 0), (0, 0))


def dot(a, b):
    return jnp.dot(a, b, preferred_element_type=F32)


def dot_rows(a, b):
    return lax.dot_general(a, b, (((0,), (0,)), ((), ())), preferred_element_type=F32)


def dot_last(a, b):
    return lax.dot_general(a, b, (((1,), (1,)), ((), ())), preferred_element_type=F32)


def low(v):
    return v.astype(BF)


def flip(index, by):
    return 1 - index if by else index


class Place:
    def __init__(self):
        self.zl, self.x, self.c = lax.axis_index("zl"), lax.axis_index("x"), lax.axis_index("c")
        self.member = self.zl * 2 + self.x


def greet_team(me, more=0):
    barrier = pltpu.get_barrier_semaphore()
    for n in range(1, 8):
        to = {"zl": flip(me.zl, n & 1), "x": flip(me.x, n & 2), "c": flip(me.c, n & 4)}
        pl.semaphore_signal(barrier, inc=1, device_id=to, device_id_type=MESH)
    pl.semaphore_wait(barrier, 7 + more)


def others(me):
    zh, y, highs = lax.axis_index("zh"), lax.axis_index("y"), lax.axis_size("zh")
    for k in range(highs):
        for n in range(8):
            yield lax.rem(zh + k, highs), flip(me.zl, n & 1), flip(y, n & 2), flip(me.x, n & 4), k + n == 0


def greet_all(me):
    barrier = pltpu.get_barrier_semaphore()
    count = 0
    for zh, zl, y, x, own in others(me):
        for f in range(2):
            if own and not f:
                continue
            to = {"zh": zh, "zl": zl, "y": y, "x": x, "c": flip(me.c, f)}
            pl.semaphore_signal(barrier, inc=1, device_id=to, device_id_type=MESH)
            count += 1
    pl.semaphore_wait(barrier, count)


def route_member(me):
    out, arrive = [], []
    for fz, fx in FLIPS:
        zl, x = flip(me.zl, fz), flip(me.x, fx)
        own = (fz, fx) == (0, 0)
        out.append((zl * 2 + x, me.member, {"zl": zl, "x": x}, own))
        arrive.append((zl * 2 + x, own))
    return out, arrive


def chip_index(zh, zl, y, x):
    return ((zh * 2 + zl) * 2 + y) * 2 + x


def route_all(me):
    mine = chip_index(lax.axis_index("zh"), me.zl, lax.axis_index("y"), me.x)
    out, arrive = [], []
    for zh, zl, y, x, own in others(me):
        chip = chip_index(zh, zl, y, x)
        out.append((chip, mine, {"zh": zh, "zl": zl, "y": y, "x": x}, own))
        arrive.append((chip, own))
    return out, arrive


def route_halves(me):
    mine = me.c == me.zl
    out, arrive = [], []
    for fz, fx in FLIPS:
        zl, x = flip(me.zl, fz), flip(me.x, fx)
        own = mine if (fz, fx) == (0, 0) else False
        out.append((0, me.x * 2 + me.c, {"zl": zl, "x": x, "c": me.zl}, own))
    for fc, fx in FLIPS:
        c, x = flip(me.c, fc), flip(me.x, fx)
        own = mine if (fc, fx) == (0, 0) else False
        arrive.append((x * 2 + c, own))
    return out, arrive


def route_owners(me):
    mine = me.c == me.zl
    out, arrive = [], []
    for fc, fx in FLIPS:
        c, x = flip(me.c, fc), flip(me.x, fx)
        own = mine if (fc, fx) == (0, 0) else False
        out.append((x * 2 + c, me.member, {"zl": me.c, "x": x, "c": c}, own))
    for fz, fx in FLIPS:
        zl, x = flip(me.zl, fz), flip(me.x, fx)
        own = mine if (fz, fx) == (0, 0) else False
        arrive.append((zl * 2 + x, own))
    return out, arrive


def route_weights(me):
    mine = (me.c == me.zl) & (me.c == me.x)
    out, arrive = [], []
    for f in (1, 0):
        x = flip(me.x, f)
        own = (me.c == me.zl) & (me.c == x) & (me.x == me.c) if not f else False
        out.append((x, me.zl, {"zl": me.c, "x": x, "c": me.x}, own))
    for f in (1, 0):
        zl = flip(me.zl, f)
        own = mine if not f else False
        arrive.append((zl, own))
    return out, arrive


def route_weights_home(me):
    mine = (me.c == me.zl) & (me.c == me.x)
    out, arrive = [], []
    for f in (1, 0):
        zl = flip(me.zl, f)
        own = mine if not f else False
        out.append((zl, me.x, {"zl": zl, "x": me.c, "c": me.zl}, own))
    for f in (1, 0):
        x = flip(me.x, f)
        own = mine if not f else False
        arrive.append((x, own))
    return out, arrive


def when(condition, run):
    if condition is True:
        run()
    elif condition is not False:
        pl.when(condition)(run)


def unless(condition, run):
    if condition is False:
        run()
    elif condition is not True:
        pl.when(jnp.logical_not(condition))(run)


class Transfer:
    def __init__(self, route, source, target, send, arrive):
        self.route, self.source, self.target, self.send, self.arrive = route, source, target, send, arrive

    def _remote(self, n):
        index, slot, to, own = self.route[0][n]
        return pltpu.make_async_remote_copy(
            src_ref=self.source(index),
            dst_ref=self.target(slot),
            send_sem=self.send.at[n],
            recv_sem=self.arrive.at[slot],
            device_id=to,
            device_id_type=MESH,
        )

    def _local(self, n):
        index, slot, to, own = self.route[0][n]
        return pltpu.make_async_copy(self.source(index), self.target(slot), self.send.at[n])

    def start(self):
        for n, (_, _, _, own) in enumerate(self.route[0]):
            unless(own, lambda: self._remote(n).start())
            when(own, lambda: self._local(n).start())

    def wait_arrive(self):
        for slot, own in self.route[1]:
            ref = self.target(slot)

            def arrived():
                pltpu.make_async_copy(ref, ref, self.arrive.at[slot]).wait()

            unless(own, arrived)

    def wait_local(self):
        for n, (_, _, _, own) in enumerate(self.route[0]):
            when(own, lambda: self._local(n).wait())

    def wait_sent(self):
        for n, (_, _, _, own) in enumerate(self.route[0]):
            unless(own, lambda: self._remote(n).wait_send())

    def wait(self):
        self.wait_arrive()
        self.wait_local()
        self.wait_sent()


def copy_to(src, dst, send, arrive, to):
    return pltpu.make_async_remote_copy(
        src_ref=src, dst_ref=dst, send_sem=send, recv_sem=arrive, device_id=to, device_id_type=MESH
    )


def wait_for(ref, sem):
    pltpu.make_async_copy(ref, ref, sem).wait()


def member_slots(me, two):
    along = me.zl * 2 + 1 - me.x, {"x": 1 - me.x}
    over = (1 - me.zl) * 2 + me.x, {"zl": 1 - me.zl}
    one, double = (over, along) if two == "x" else (along, over)
    return one[0], double[0], (1 - me.zl) * 2 + 1 - me.x, one[1], double[1]


class MemberSpread:
    def __init__(self, me, source, target, send, arrive, two="x"):
        self.target, self.arrive = target, arrive
        mine = me.member
        one, double, across, to_one, to_double = member_slots(me, two)
        self.slots = one, double, across
        self.direct = [
            copy_to(source, target(mine), send.at[0], arrive.at[mine], to_one),
            copy_to(source, target(mine), send.at[1], arrive.at[mine], to_double),
        ]
        self.local = pltpu.make_async_copy(source, target(mine), arrive.at[mine])
        self.forward = copy_to(target(one), target(one), send.at[2], arrive.at[one], to_double)

    def start(self):
        for copy in self.direct:
            copy.start()
        self.local.start()

    def relay(self):
        wait_for(self.target(self.slots[0]), self.arrive.at[self.slots[0]])
        self.forward.start()

    def wait(self):
        for slot in self.slots[1:]:
            wait_for(self.target(slot), self.arrive.at[slot])
        self.local.wait()
        for copy in self.direct + [self.forward]:
            copy.wait_send()


class HalvesSpread:
    def __init__(self, me, source, target, send, arrive):
        self.me, self.target, self.arrive = me, target, arrive
        mine = me.x * 2 + me.c
        self.home = me.c == me.zl
        self.direct = [
            copy_to(source, target(mine), send.at[0], arrive.at[mine], {"zl": 1 - me.zl, "c": me.zl}),
            copy_to(source, target(mine), send.at[1], arrive.at[mine], {"x": 1 - me.x, "c": me.zl}),
        ]
        self.near = copy_to(source, target(mine), send.at[2], arrive.at[mine], {"c": 1 - me.c})
        self.local = pltpu.make_async_copy(source, target(mine), send.at[2])
        self.near_slots = [me.x * 2 + c for c in range(2)]
        self.far_slots = [(1 - me.x) * 2 + c for c in range(2)]
        self.forwards = [
            copy_to(target(slot), target(slot), send.at[3 + c], arrive.at[slot], {"x": 1 - me.x})
            for c, slot in enumerate(self.near_slots)
        ]

    def start(self):
        for copy in self.direct:
            copy.start()
        pl.when(self.home)(self.local.start)
        unless(self.home, self.near.start)

    def relay(self):
        @pl.when(jnp.logical_not(self.home))
        def _():
            for slot, forward in zip(self.near_slots, self.forwards):
                wait_for(self.target(slot), self.arrive.at[slot])
                forward.start()

    def wait(self):
        me = self.me

        @pl.when(self.home)
        def _():
            self.local.wait()
            slot = me.x * 2 + 1 - me.c
            wait_for(self.target(slot), self.arrive.at[slot])

        for slot in self.far_slots:
            wait_for(self.target(slot), self.arrive.at[slot])
        for copy in self.direct:
            copy.wait_send()

        @pl.when(jnp.logical_not(self.home))
        def _():
            self.near.wait_send()
            for forward in self.forwards:
                forward.wait_send()


class MemberSum:
    def __init__(self, me, source, got, relayed, staged, send, arrive, two="x"):
        self.me, self.source, self.got, self.relayed, self.staged = me, source, got, relayed, staged
        self.arrive = arrive
        self.one, double, across, to_one, to_double = member_slots(me, two)
        self.direct = [
            copy_to(source(across), relayed(0), send.at[0], arrive.at[0], to_double),
            copy_to(source(double), got(0), send.at[1], arrive.at[1], to_double),
        ]
        self.onward = copy_to(staged(0), got(1), send.at[2], arrive.at[2], to_one)

    def start(self):
        for copy in self.direct:
            copy.start()

    def relay(self):
        wait_for(self.relayed(0), self.arrive.at[0])
        own = self.source(self.one)[...].astype(F32)
        self.staged(0)[...] = low(own + self.relayed(0)[...].astype(F32))
        self.onward.start()

    def total(self):
        wait_for(self.got(0), self.arrive.at[1])
        wait_for(self.got(1), self.arrive.at[2])
        total = self.source(self.me.member)[...].astype(F32)
        return total + self.got(0)[...].astype(F32) + self.got(1)[...].astype(F32)

    def wait_sent(self):
        for copy in self.direct + [self.onward]:
            copy.wait_send()


class OwnersSum:
    def __init__(self, me, source, got, relayed, staged, send, arrive):
        self.me, self.source, self.got, self.relayed, self.staged = me, source, got, relayed, staged
        self.arrive = arrive
        self.home = me.c == me.zl
        mine, other = me.x * 2, (1 - me.x) * 2
        self.near = copy_to(source(mine + 1 - me.c), got(0), send.at[0], arrive.at[0], {"c": 1 - me.c})
        self.local = pltpu.make_async_copy(source(mine + me.c), got(0), send.at[1])
        self.across = [
            copy_to(source(other + c), got(1), send.at[2 + c], arrive.at[1], {"x": 1 - me.x, "c": c})
            for c in range(2)
        ]
        self.first = [
            copy_to(source(other + c), relayed(c), send.at[2 + c], arrive.at[3 + c], {"x": 1 - me.x})
            for c in range(2)
        ]
        self.onward = [
            copy_to(staged(c), got(2), send.at[4 + c], arrive.at[2], {"zl": me.c, "c": c})
            for c in range(2)
        ]

    def start(self):
        @pl.when(self.home)
        def _():
            for copy in self.across + [self.near, self.local]:
                copy.start()

        @pl.when(jnp.logical_not(self.home))
        def _():
            for copy in self.first:
                copy.start()

    def relay(self):
        @pl.when(jnp.logical_not(self.home))
        def _():
            for c in range(2):
                wait_for(self.relayed(c), self.arrive.at[3 + c])
                own = self.source(self.me.x * 2 + c)[...].astype(F32)
                self.staged(c)[...] = low(own + self.relayed(c)[...].astype(F32))
                self.onward[c].start()

    def total(self):
        pl.when(self.home)(self.local.wait)
        unless(self.home, lambda: wait_for(self.got(0), self.arrive.at[0]))
        wait_for(self.got(1), self.arrive.at[1])
        wait_for(self.got(2), self.arrive.at[2])
        return sum(self.got(k)[...].astype(F32) for k in range(3))

    def wait_sent(self):
        @pl.when(self.home)
        def _():
            for copy in self.across + [self.near]:
                copy.wait_send()

        @pl.when(jnp.logical_not(self.home))
        def _():
            for copy in self.first + self.onward:
                copy.wait_send()


class Placed(Transfer):
    def __init__(self, route, source, there, target, send, arrive):
        super().__init__(route, source, target, send, arrive)
        self.there = there

    def _remote(self, n):
        index, slot, to, own = self.route[0][n]
        return pltpu.make_async_remote_copy(
            src_ref=self.source(index),
            dst_ref=self.there(slot),
            send_sem=self.send.at[n],
            recv_sem=self.arrive.at[slot],
            device_id=to,
            device_id_type=MESH,
        )


LANES = 128
RANKS = 32


def keyed_mask(start, starts_row, starts_column):
    rows = lax.broadcasted_iota(jnp.int32, (CHUNK, CHUNK), 0)
    columns = lax.broadcasted_iota(jnp.int32, (CHUNK, CHUNK), 1)
    ids = jnp.sum((rows + start >= starts_row[0:1]).astype(F32), axis=1, keepdims=True)
    places = lax.broadcasted_iota(jnp.int32, starts_column.shape, 1)
    ids_row = jnp.sum((places + start >= starts_column[...]).astype(F32), axis=0, keepdims=True)
    before = jnp.sum((starts_row[0:1] < start).astype(F32), axis=1, keepdims=True)
    final = ids_row[:, CHUNK - 1 :]
    pair = (rows >= columns) & (ids == ids_row)
    visible = (ids == before).astype(F32)
    keep = (final == before).astype(F32)
    return pair, visible, keep, (ids == final).astype(F32)


class StatePass:
    def __init__(self, back, local, decay, out, rounded, got, got_decay, sums, sum_decays, stage, stage_decay,
                 entering, leave, enter, send, arrive, far_send, far_arrive, leave_send, leave_arrive):
        self.__dict__.update(locals())
        self.zh, c, y = lax.axis_index("zh"), lax.axis_index("c"), lax.axis_index("y")
        self.highs = lax.axis_size("zh")
        self.mine = c * 2 + y
        self.quarter = local.shape[0] // 4
        self.partners = []
        for fc, fy in ((1, 1), (0, 1), (1, 0)):
            to_c, to_y = flip(c, fc), flip(y, fy)
            self.partners.append((to_c * 2 + to_y, {"c": to_c, "y": to_y}))
        self.order = range(3, -1, -1) if back else range(4)
        self.moves, self.outs = [], []

    def begin(self):
        self.rounded[...] = low(self.local[...])
        for n, (index, to) in enumerate(self.partners):
            rows = self.rounded.at[pl.ds(index * self.quarter, self.quarter)]
            self.moves.append(copy_to(rows, self.got.at[self.mine], self.send.at[0, n], self.arrive.at[0, self.mine], to))
            self.moves.append(
                copy_to(self.decay, self.got_decay.at[self.mine], self.send.at[1, n], self.arrive.at[1, self.mine], to)
            )
        for move in self.moves:
            move.start()
        self.got[self.mine] = self.rounded[pl.ds(self.mine * self.quarter, self.quarter)]
        self.got_decay[self.mine] = self.decay[...]

    def needs(self, source, target):
        return (source > target) if self.back else (source < target)

    def far(self, n, to):
        zh = self.zh
        return (
            copy_to(self.stage, self.sums.at[zh], self.far_send.at[0, n], self.far_arrive.at[0, zh], {"zh": to}),
            copy_to(
                self.stage_decay, self.sum_decays.at[zh], self.far_send.at[1, n], self.far_arrive.at[1, zh], {"zh": to}
            ),
        )

    def combine(self):
        for index, _ in self.partners:
            wait_for(self.got.at[index], self.arrive.at[0, index])
            wait_for(self.got_decay.at[index], self.arrive.at[1, index])
        total, total_decay = None, None
        for k in self.order:
            piece, d = self.got[k].astype(F32), self.got_decay[k][:1]
            total = piece if total is None else d * total + piece
            total_decay = d if total_decay is None else total_decay * d
        self.stage[...] = low(total)
        self.stage_decay[...] = jnp.broadcast_to(total_decay, self.stage_decay.shape)
        for n in range(1, self.highs):
            to = lax.rem(self.zh + n, self.highs)

            @pl.when(self.needs(self.zh, to))
            def _(n=n, to=to):
                for move in self.far(n, to):
                    move.start()

    def spread(self):
        self.entering[...] = jnp.zeros_like(self.entering)
        for n in range(self.highs):
            k = self.highs - 1 - n if self.back else n

            @pl.when(self.needs(k, self.zh))
            def _(k=k):
                wait_for(self.sums.at[k], self.far_arrive.at[0, k])
                wait_for(self.sum_decays.at[k], self.far_arrive.at[1, k])
                self.entering[...] = self.sum_decays[k][:1] * self.entering[...] + self.sums[k].astype(F32)

        state = self.entering[...]
        for k in self.order:
            self.leave[k] = low(state)
            state = self.got_decay[k][:1] * state + self.got[k].astype(F32)
        for n, (index, to) in enumerate(self.partners):
            self.outs.append(
                copy_to(
                    self.leave.at[index], self.enter.at[self.mine], self.leave_send.at[n],
                    self.leave_arrive.at[self.mine], to,
                )
            )
        for move in self.outs:
            move.start()
        self.enter[self.mine] = self.leave[self.mine]

    def finish(self):
        for index, _ in self.partners:
            wait_for(self.enter.at[index], self.leave_arrive.at[index])
        for k in range(4):
            self.out[pl.ds(k * self.quarter, self.quarter)] = self.enter[k].astype(F32)

    def wait_sent(self):
        for move in self.moves + self.outs:
            move.wait_send()
        for n in range(1, self.highs):
            to = lax.rem(self.zh + n, self.highs)

            @pl.when(self.needs(self.zh, to))
            def _(n=n, to=to):
                for move in self.far(n, to):
                    move.wait_send()


def state_pass_scratch(highs):
    quarter = HD // 4
    return [
        pltpu.VMEM((HD, HD), BF),
        pltpu.VMEM((4, quarter, HD), BF),
        pltpu.VMEM((4, 8, HD), F32),
        pltpu.VMEM((highs, quarter, HD), BF),
        pltpu.VMEM((highs, 8, HD), F32),
        pltpu.VMEM((quarter, HD), BF),
        pltpu.VMEM((8, HD), F32),
        pltpu.VMEM((quarter, HD), F32),
        pltpu.VMEM((4, quarter, HD), BF),
        pltpu.VMEM((4, quarter, HD), BF),
        DMA((2, 3)),
        DMA((2, 4)),
        DMA((2, highs)),
        DMA((2, highs)),
        DMA((3,)),
        DMA((4,)),
    ]


STATE_REFS = 16


def forward_kernel(*refs):
    (
        mixer_in, mixer_out, ffn_in, ffn_out, small, ups, own, cot, starts_row, starts_column, head_gain,
        mixer_w, merge_w, pair_w, down_w, gains, cots, hidden, low_rank, gate, cumulated, projected, mixed, gated,
        befores, decay, second, middle,
        mixer_v, merge_v, projected_v, updates, inputs, smalls, ups_got, state, partial, got, relayed, staged, line,
        own_send, own_arrive, far_send, arrive, small_send, small_arrive, ups_sem, inputs_send, inputs_arrive,
        cot_send, cot_arrive, sum_send, sum_arrive, spread_send, spread_arrive, saves,
    ) = refs[:-STATE_REFS]
    me = Place()
    zh, y, highs = lax.axis_index("zh"), lax.axis_index("y"), lax.axis_size("zh")
    units = down_w.shape[-1]
    width = own.shape[1]
    chunks = hidden.shape[0]
    first = ((zh * 2 + me.c) * 2 + y) * (chunks * CHUNK)
    greet_all(me)
    twin, side = {"c": 1 - me.c}, {"y": 1 - y}

    def own_source(part, k):
        if part < 5:
            at = pl.ds(pl.multiple_of(k * HD, HD), HD)
            return mixer_out.at[:, at] if part == 4 else mixer_in.at[part, :, at]
        at = pl.ds(pl.multiple_of(k * units, LANES), units)
        return ffn_out.at[:, at] if part == 7 else ffn_in.at[part - 5, :, at]

    def piece(at_zh, at_y, x, part, zl=slice(None)):
        if part < 4:
            return mixer_v.at[at_zh, zl, at_y, x, :, pl.ds(part * HD, HD)]
        if part == 4:
            return merge_v.at[at_zh, zl, at_y, x]
        if part < 7:
            return pair_w.at[at_zh, zl, at_y, x, :, pl.ds((part - 5) * units, units)]
        return down_w.at[at_zh, zl, at_y, x]

    firsts = [
        Placed(
            route_weights(me),
            lambda k, p=p: own_source(p, k),
            lambda zl, p=p: piece(zh, y, me.x, p, zl),
            lambda zl, p=p: piece(zh, y, me.c, p, zl),
            own_send.at[p],
            own_arrive.at[p],
        )
        for p in range(8)
    ]
    count = [0]
    sent = []

    def forward(at_zh, at_y, part, to, start=True):
        place = piece(at_zh, at_y, me.c, part)
        copy = copy_to(place, place, far_send.at[count[0]], arrive.at[at_zh, at_y, me.c, part], to)
        if start:
            copy.start()
        count[0] += 1
        sent.append(copy)
        return copy

    def arrived(at_zh, at_y, x, part):
        wait_for(piece(at_zh, at_y, x, part), arrive.at[at_zh, at_y, x, part])

    def own_high(part, start=True):
        firsts[part].wait_arrive()
        firsts[part].wait_local()
        return [forward(zh, y, part, {"zh": lax.rem(zh + k, highs)}, start) for k in range(1, highs)]

    def own_near(part):
        forward(zh, y, part, side)
        forward(zh, y, part, twin)

    def pass_high(part):
        for k in range(1, highs):
            at_zh = lax.rem(zh + k, highs)
            arrived(at_zh, y, me.c, part)
            forward(at_zh, y, part, side)
            forward(at_zh, y, part, twin)

    def pass_side(part):
        for k in range(highs):
            at_zh = lax.rem(zh + k, highs)
            arrived(at_zh, 1 - y, me.c, part)
            forward(at_zh, 1 - y, part, twin)

    def complete(part):
        for k in range(highs):
            at_zh = lax.rem(zh + k, highs)
            arrived(at_zh, y, 1 - me.c, part)
            arrived(at_zh, 1 - y, 1 - me.c, part)

    save_count = [0]
    saved = []

    def save(source, target):
        copy = pltpu.make_async_copy(source, target, saves.at[save_count[0]])
        copy.start()
        save_count[0] += 1
        saved.append(copy)

    order = (1, 2, 0, 3, 4)
    for part in order:
        firsts[part].start()
    move_small = Transfer(route_all(me), lambda _: small, lambda k: smalls.at[k], small_send, small_arrive)
    move_small.start()
    lend = copy_to(ups, ups_got, ups_sem.at[0], ups_sem.at[1], twin)
    lend.start()
    for part in order:
        own_high(part)
        if part in order[:2]:
            own_near(part)
    move_inputs = HalvesSpread(me, own, lambda k: inputs.at[k], inputs_send, inputs_arrive)
    move_cot = MemberSpread(me, cot, lambda k: cots.at[k], cot_send, cot_arrive)
    move_inputs.start()
    move_inputs.relay()
    pass_high(1)
    move_small.wait()
    lend.wait()
    owner_rows = smalls.shape[2]
    for n in range(smalls.shape[0]):
        gains[:, n * owner_rows : (n + 1) * owner_rows] = smalls[n].astype(F32)
    pass_high(2)
    for part in (5, 6, 7):
        firsts[part].start()
    for part in order[2:]:
        own_near(part)
    move_inputs.wait()

    up = jnp.where(me.c == me.zl, ups[...], ups_got[...])
    rank_up, bias = low(up[:16]), up[16:17]
    down = low(gains[...])
    lower = (
        lax.broadcasted_iota(jnp.int32, (CHUNK, CHUNK), 0)
        >= lax.broadcasted_iota(jnp.int32, (CHUNK, CHUNK), 1)
    ).astype(F32)

    def gates_step(n, _):
        x = inputs[n].astype(F32)
        scale = lax.rsqrt(jnp.mean(x * x, -1, keepdims=True) + EPSILON)
        h = low(x * scale * gains[0:1])
        hidden[n] = h
        z = low(dot_last(h, down))
        low_rank[n] = z
        a = dot(z[:, 2:18], rank_up) + bias
        gate[n] = a
        log_gate = (jnp.minimum(a, 0.0) - jnp.log1p(jnp.exp(-jnp.abs(a)))) / 16.0
        cumulated[n] = jnp.dot(
            lower, log_gate, precision=lax.Precision.HIGHEST, preferred_element_type=F32
        )
        return 0

    lax.fori_loop(0, chunks, gates_step, 0)

    def project(part):
        rows = hidden[...].reshape(chunks * CHUNK, width)
        block = mixer_v[:, :, :, :, :, pl.ds(part * HD, HD)].reshape(width, HD)
        result = dot(rows, block)
        if part == 0:
            result = result * HD ** (-0.5)
        projected_v[part] = result.reshape(chunks, CHUNK, HD)
        save(projected_v.at[part], projected.at[part])

    pass_side(1)
    pass_side(2)
    complete(1)
    project(1)
    complete(2)
    project(2)

    state[...] = jnp.zeros_like(state)
    decay[...] = jnp.ones_like(decay)

    def masks(n):
        return keyed_mask(first + n * CHUNK, starts_row, starts_column)

    def local_step(n, _):
        _, _, keep, last = masks(n)
        b = cumulated[n]
        end = b[CHUNK - 1 :]
        kc = low(projected_v[1, n] * jnp.exp(end - b) * last)
        update = dot_rows(low(projected_v[2, n]), kc)
        updates[n] = update
        carry = keep * jnp.exp(end)
        state[...] = carry * state[...] + update
        decay[...] = decay[...] * carry
        return 0

    lax.fori_loop(0, chunks, local_step, 0)
    states = StatePass(False, state, decay, state, *refs[-STATE_REFS:])
    states.begin()
    pass_high(0)
    states.combine()
    held = [copy for part in (5, 6, 7) for copy in own_high(part, False)]

    @pl.when(me.zl == 1)
    def _():
        for copy in held:
            copy.start()

    pass_high(3)
    pass_side(0)
    complete(0)
    project(0)
    pass_side(3)

    def inner_step(n, _):
        pair, _, _, _ = masks(n)
        b = cumulated[n]
        mid = b[CHUNK // 2 - 1 : CHUNK // 2]
        qh = low(projected_v[0, n] * jnp.exp(b - mid))
        kh = low(projected_v[1, n] * jnp.exp(mid - b))
        scores = low(jnp.where(pair, dot_last(qh, kh), 0.0))
        mixed[n] = dot(scores, low(projected_v[2, n]))
        return 0

    lax.fori_loop(0, chunks, inner_step, 0)
    states.spread()

    @pl.when(me.zl == 0)
    def _():
        for copy in held:
            copy.start()

    pass_high(4)
    for part in (5, 6, 7):
        own_near(part)
    complete(3)
    project(3)
    states.finish()

    def outer_step(n, _):
        _, visible, keep, _ = masks(n)
        b = cumulated[n]
        before = state[...]
        qd = low(projected_v[0, n] * jnp.exp(b) * visible)
        out = mixed[n] + dot_last(qd, low(before))
        mixed[n] = out
        befores[n] = low(before)
        state[...] = keep * jnp.exp(b[CHUNK - 1 :]) * before + updates[n]
        scale = lax.rsqrt(jnp.mean(out * out, -1, keepdims=True) + HEAD_FLOOR)
        u = projected_v[3, n]
        gated[n] = low(out * scale * head_gain[...] * (u * jax.nn.sigmoid(u)))
        return 0

    lax.fori_loop(0, chunks, outer_step, 0)
    pass_side(4)
    complete(4)

    def merge_step(n, _):
        partial[n] = low(dot_last(gated[n], merge_v[...].reshape(width, HD)))
        return 0

    lax.fori_loop(0, chunks, merge_step, 0)

    steps = sum_send.shape[0]
    rows = own.shape[0] // steps

    def rows_of(ref, k, n):
        return ref.at[k, pl.ds(n * rows, rows)]

    sums = [
        OwnersSum(
            me,
            lambda k, n=n: rows_of(partial, k, n),
            lambda k, n=n: rows_of(got, k, n),
            lambda k, n=n: rows_of(relayed, k, n),
            lambda k, n=n: rows_of(staged, k, n),
            sum_send.at[n],
            sum_arrive.at[n],
        )
        for n in range(steps)
    ]
    spreads = [
        MemberSpread(
            me,
            line.at[pl.ds(n * rows, rows)],
            lambda k, n=n: rows_of(second, k, n),
            spread_send.at[n],
            spread_arrive.at[n],
        )
        for n in range(steps)
    ]
    for transfer in sums:
        transfer.start()
    for transfer in sums:
        transfer.relay()
    pass_high(5)
    for n in range(steps):
        at = pl.ds(n * rows, rows)
        total = own[at].astype(F32) + sums[n].total()
        middle[at] = total
        scale = lax.rsqrt(jnp.mean(total * total, -1, keepdims=True) + EPSILON)
        line[at] = low(total * scale * gains[1:2])
        spreads[n].start()
        if n:
            spreads[n - 1].relay()
    spreads[steps - 1].relay()
    pass_high(6)
    pass_side(5)
    move_cot.start()
    save(mixer_v, mixer_w)
    save(merge_v, merge_w)
    pass_high(7)
    move_cot.relay()
    for part in (6, 7):
        pass_side(part)
    for part in (5, 6, 7):
        complete(part)
    for transfer in sums:
        transfer.wait_sent()
    for transfer in spreads:
        transfer.wait()
    states.wait_sent()
    move_cot.wait()
    for transfer in firsts:
        transfer.wait_sent()
    for copy in sent:
        copy.wait_send()
    for copy in saved:
        copy.wait()


def starts_arrays(starts):
    starts = jnp.pad(starts, (0, LANES - starts.shape[0]), constant_values=jnp.int32(1 << 30))
    return jnp.broadcast_to(starts[None], (8, LANES)), jnp.broadcast_to(starts[:16, None], (16, LANES))


def forward(mixer_in, mixer_out, ffn_in, ffn_out, small, ups, own, cot, starts, head_gain):
    highs = lax.axis_size("zh")
    chips = highs * 8
    rows, half, width = small.shape[1], own.shape[0], own.shape[1]
    units = ffn_out.shape[1] // 2
    chunks = TEAM * half // CHUNK

    def shape(*dims, kind=BF):
        return jax.ShapeDtypeStruct(dims, kind)

    shapes = [
        (shape(highs, 2, 2, 2, rows, 4 * HD), ANY),
        (shape(highs, 2, 2, 2, rows, HD), ANY),
        (shape(highs, 2, 2, 2, rows, 2 * units), ANY),
        (shape(highs, 2, 2, 2, rows, units), ANY),
        (shape(RANKS, width, kind=F32), VMEM),
        (shape(TEAM, half, width), ANY),
        (shape(chunks, CHUNK, width), VMEM),
        (shape(chunks, CHUNK, RANKS), VMEM),
        (shape(chunks, CHUNK, HD, kind=F32), VMEM),
        (shape(chunks, CHUNK, HD, kind=F32), VMEM),
        (shape(4, chunks, CHUNK, HD, kind=F32), ANY),
        (shape(chunks, CHUNK, HD, kind=F32), VMEM),
        (shape(chunks, CHUNK, HD), VMEM),
        (shape(chunks, HD, HD), VMEM),
        (shape(8, HD, kind=F32), VMEM),
        (shape(TEAM, half, width), VMEM),
        (shape(half, width, kind=F32), VMEM),
    ]
    arrays = [mixer_in, mixer_out, ffn_in, ffn_out, small, ups, own, cot, *starts_arrays(starts), head_gain]
    scratch = [
        shapes[0][0],
        shapes[1][0],
        shapes[10][0],
        shape(chunks, HD, HD, kind=F32),
        shape(TEAM, half, width),
        shape(chips, RANKS, rows),
        shape(*ups.shape, kind=F32),
        shape(HD, HD, kind=F32),
        shape(TEAM, half, width),
        shape(3, half, width),
        shape(2, half, width),
        shape(2, half, width),
        shape(half, width),
    ]
    used = arrays + scratch + [a for a, place in shapes if place is VMEM]
    size = sum(a.size * a.dtype.itemsize for a in used)
    forwards = 8 * ((highs - 1) + highs + 2 * highs)
    sems = [
        (8, 2), (8, 2), (forwards,), (highs, 2, 2, 8), (chips,), (chips,), (2,), (5,), (4,), (3,), (4,),
        (STEPS, 6), (STEPS, 5), (STEPS, 3), (STEPS, 4), (7,),
    ]
    return pl.pallas_call(
        forward_kernel,
        out_shape=[a for a, _ in shapes],
        in_specs=[VMEM] * len(arrays),
        out_specs=[place for _, place in shapes],
        scratch_shapes=[pltpu.VMEM(a.shape, a.dtype) for a in scratch]
        + [DMA(n) for n in sems]
        + state_pass_scratch(highs),
        compiler_params=pltpu.CompilerParams(
            collective_id=0, has_side_effects=True, vmem_limit_bytes=min(size + (14 << 20), 62 << 20)
        ),
        name="forward",
    )(*arrays)


STEPS = 4


CROSS = [(0, 1), (1, 0)]


TILE = 256


def turn_rows(me, source, target):
    zh, y, highs = lax.axis_index("zh"), lax.axis_index("y"), lax.axis_size("zh")
    chunks, _, width = source.shape
    owners = highs * 8
    rows = width // owners
    for n in range(chunks):
        turned = source[n].T
        for chip in range(owners):
            at_zh, zl, at_y, x = chip // 8, chip // 4 % 2, chip // 2 % 2, chip % 2
            x_place = me.c if x == 1 else 1 - me.c
            y_place = y if at_y == 1 else 1 - y
            place = ((x_place * 2 + y_place) * highs + lax.rem(at_zh - zh + highs, highs)) * 2 + zl
            at = pl.ds(pl.multiple_of(place * rows, rows), rows)
            target[at, n * CHUNK : (n + 1) * CHUNK] = turned[chip * rows : (chip + 1) * rows]


def feed_forward_kernel(
    hidden, cots, pair_w, down_w,
    forth, back, pair_away, pair_keep, down_part,
    pair_v, down_v, act, grad_gate, grad_up, left_hidden, left_cots, tiles, tiles_got, down_away, down_keep,
    loads, tile_send, tile_arrive, side,
):
    me = Place()
    y = lax.axis_index("y")
    chunks, _, width = hidden.shape
    units = down_w.shape[1]
    tokens = chunks * CHUNK
    barrier = pltpu.get_barrier_semaphore()
    for to in ({"c": 1 - me.c}, {"y": 1 - y}):
        pl.semaphore_signal(barrier, inc=1, device_id=to, device_id_type=MESH)
    spans = [(n * TILE, min(TILE, units - n * TILE)) for n in range(-(-units // TILE))]

    def load(kind, n):
        start, size = spans[n]
        if kind == 2:
            return pltpu.make_async_copy(
                down_w.at[:, pl.ds(start, size)], down_v.at[:, pl.ds(start, size)], loads.at[2, n]
            )
        at = pl.ds(kind * units + start, size)
        return pltpu.make_async_copy(pair_w.at[:, at], pair_v.at[:, at], loads.at[kind, n])

    for n in range(len(spans)):
        for kind in range(3):
            load(kind, n).start()
    turn_rows(me, cots, left_cots)

    def units_step(start, size):
        at = pl.ds(start, size)
        rows = hidden[...].reshape(tokens, width)
        a = dot(rows, pair_v[:, at])
        b = dot(rows, pair_v[:, pl.ds(units + start, size)])
        da = dot(cots[...].reshape(tokens, width), down_v[:, at])
        sig = jax.nn.sigmoid(a)
        silu = a * sig
        act[:, at] = low(silu * b)
        grad_gate[:, at] = low(da * b * sig * (1.0 + a * (1.0 - sig)))
        grad_up[:, at] = low(da * silu)

    for n, (start, size) in enumerate(spans):
        for kind in range(3):
            load(kind, n).wait()
        if size < TILE:
            units_step(start, size)
    whole = units // TILE

    def whole_step(n, _):
        units_step(pl.multiple_of(n * TILE, TILE), TILE)
        return 0

    lax.fori_loop(0, whole, whole_step, 0)
    pl.semaphore_wait(barrier, 2)

    half = width // 2
    quarter = half // 2
    count = len(spans)

    def move(n):
        return copy_to(
            tiles.at[lax.rem(n, count)], tiles_got.at[n], tile_send.at[n], tile_arrive.at[n], {"c": 1 - me.c}
        )

    def send_tile(left, right, n, start, size):
        block = low(dot(left[pl.ds(0, half)], right[:, pl.ds(start, size)]))
        if size == TILE:
            tiles[lax.rem(n, count)] = block
        else:
            tiles[lax.rem(n, count), :, pl.ds(0, size)] = block
        move(n).start()

    def add_tile(left, right, n, start, size, away, keep, base):
        block = dot(left[pl.ds(half, half)], right[:, pl.ds(start, size)])
        move(n).wait_recv()
        block = low(block + tiles_got[n, :, pl.ds(0, size)].astype(F32))
        away[:, pl.ds(base + start, size)] = block[:quarter]
        keep[:, pl.ds(base + start, size)] = block[quarter:]

    def weight_grad(part, left, right, away, keep, base):
        first = part * count

        def send_step(n, _):
            if part:
                move(first + n - count).wait_send()
            send_tile(left, right, first + n, pl.multiple_of(n * TILE, TILE), TILE)
            return 0

        def add_step(n, _):
            add_tile(left, right, first + n, pl.multiple_of(n * TILE, TILE), TILE, away, keep, base)
            return 0

        lax.fori_loop(0, whole, send_step, 0)
        if whole < count:
            if part:
                move(first + whole - count).wait_send()
            send_tile(left, right, first + whole, *spans[whole])
        lax.fori_loop(0, whole, add_step, 0)
        if whole < count:
            add_tile(left, right, first + whole, *spans[whole], away, keep, base)

    weight_grad(0, left_cots, act, down_away, down_keep, 0)
    side_move = copy_to(down_away, down_part, side.at[0], side.at[1], {"y": 1 - y})
    side_move.start()

    def back_step(n, _):
        at = pl.ds(pl.multiple_of(n * TILE, TILE), TILE)
        block = dot_last(grad_gate[...], pair_v[at, pl.ds(0, units)])
        block = low(block + dot_last(grad_up[...], pair_v[at, pl.ds(units, units)]))
        ahead = low(dot_last(act[...], down_v[at]))
        for k in range(chunks):
            back[k, :, at] = block[k * CHUNK : (k + 1) * CHUNK]
            forth[k, :, at] = ahead[k * CHUNK : (k + 1) * CHUNK]
        return 0

    lax.fori_loop(0, width // TILE, back_step, 0)
    turn_rows(me, hidden, left_hidden)
    weight_grad(1, left_hidden, grad_gate, pair_away, pair_keep, 0)
    weight_grad(2, left_hidden, grad_up, pair_away, pair_keep, units)
    for n in range(2 * count, 3 * count):
        move(n).wait_send()
    side_move.wait()
    add_rows(down_part, down_keep, down_part)


def feed_forward(hidden, cots, pair_w, down_w):
    chunks, _, width = hidden.shape
    units = down_w.shape[1]
    tokens, half = chunks * CHUNK, width // 2
    count = -(-units // TILE)

    def shape(*dims, kind=BF):
        return jax.ShapeDtypeStruct(dims, kind)

    shapes = [
        shape(*hidden.shape),
        shape(*hidden.shape),
        shape(half // 2, 2 * units),
        shape(half // 2, 2 * units),
        shape(half // 2, units),
    ]
    scratch = [
        shape(width, 2 * units),
        shape(width, units),
        shape(tokens, units),
        shape(tokens, units),
        shape(tokens, units),
        shape(width, tokens),
        shape(width, tokens),
        shape(count, half, TILE),
        shape(3 * count, half, TILE),
        shape(half // 2, units),
        shape(half // 2, units),
    ]
    size = sum(a.size * a.dtype.itemsize for a in [hidden, cots] + shapes + scratch)
    sems = [(3, count), (3 * count,), (3 * count,), (2,)]
    return pl.pallas_call(
        feed_forward_kernel,
        out_shape=shapes,
        in_specs=[VMEM, VMEM, ANY, ANY],
        out_specs=[VMEM] * len(shapes),
        scratch_shapes=[pltpu.VMEM(a.shape, a.dtype) for a in scratch] + [DMA(n) for n in sems],
        compiler_params=pltpu.CompilerParams(
            collective_id=5, has_side_effects=True, vmem_limit_bytes=min(size + (10 << 20), 63 << 20)
        ),
        name="feed_forward",
    )(hidden, cots, pair_w, down_w)


def add_rows(out, *parts):
    def step(n, _):
        at = pl.ds(n * 16, 16)
        total = parts[0][at].astype(F32)
        for part in parts[1:]:
            total = total + part[at].astype(F32)
        out[at] = low(total)
        return 0

    lax.fori_loop(0, out.shape[0] // 16, step, 0)


def backward_kernel(*refs):
    (
        back, forth, cot, middle, gain, pair_away, pair_keep, downs, merge_w, gated, projected, mixed,
        cumulated, gate, befores, decay, low_rank, up_pad, head_gain, hidden, starts_row, starts_column,
        grad_middle, gain_grad, proj, ranks, heads, early, gate_sum, up_sum, down_sum, left_hidden,
        result, got, relayed, staged, line, got2, relayed2, staged2, line2, branch, left_branch, douts, tiles, tiles_got,
        pair_side, gate_got, up_got, down_got, early_away, early_keep, up_grad, state,
        send, arrive, send2, arrive2, side_send, side_arrive, high_send, high_arrive, tile_send, tile_arrive,
        send3, arrive3, twin_send, twin_arrive, here,
    ) = refs[:-STATE_REFS]
    me = Place()
    zh, y, highs = lax.axis_index("zh"), lax.axis_index("y"), lax.axis_size("zh")
    chunks, _, width = hidden.shape
    units = downs.shape[-1]
    first = ((zh * 2 + me.c) * 2 + y) * (chunks * CHUNK)
    greet_all(me)

    def columns(ref, part):
        return ref.at[:, :, :, pl.ds((part - 1) * units, units)]

    def source(part):
        return downs if part == 0 else columns(pair_side, part)

    sides = [
        copy_to(columns(pair_away, p), columns(pair_side, p), side_send.at[p], side_arrive.at[p], {"y": 1 - y})
        for p in (1, 2)
    ]
    high_got, high_sum = (down_got, gate_got, up_got), (down_sum, gate_sum, up_sum)
    highs_moves = [
        [
            copy_to(
                source(p).at[k],
                high_got[p].at[k - 1],
                high_send.at[p, k],
                high_arrive.at[p, k],
                {"zh": lax.rem(zh + k, highs)},
            )
            for k in range(1, highs)
        ]
        for p in range(3)
    ]

    def high_start(part):
        if part:
            sides[part - 1].wait()
            mine, there = columns(pair_keep, part), columns(pair_side, part)
            for k in range(highs):
                for m in range(2):
                    add_rows(there.at[k, m], mine.at[k, m], there.at[k, m])
        for move in highs_moves[part]:
            move.start()

    def high_add(part):
        there, out = high_got[part], high_sum[part]
        for k in range(1, highs):
            wait_for(there.at[k - 1], high_arrive.at[part, k])
        for m in range(2):
            add_rows(out.at[m], source(part).at[0, m], *(there.at[k - 1, m] for k in range(1, highs)))

    for move in sides:
        move.start()
    high_start(0)

    steps = send.shape[0]
    rows = cot.shape[0] // steps

    def part(ref, k, n):
        return ref.at[k, pl.ds(n * rows, rows)]

    sums = [
        MemberSum(
            me,
            lambda k, n=n: part(back, k, n),
            lambda k, n=n: part(got, k, n),
            lambda k, n=n: part(relayed, k, n),
            lambda k, n=n: part(staged, k, n),
            send.at[n],
            arrive.at[n],
            two="zl",
        )
        for n in range(steps)
    ]
    spreads = [
        HalvesSpread(
            me,
            line.at[pl.ds(n * rows, rows)],
            lambda k, n=n: part(branch, k, n),
            send2.at[n],
            arrive2.at[n],
        )
        for n in range(steps)
    ]
    forth_sums = [
        MemberSum(
            me,
            lambda k, n=n: part(forth, k, n),
            lambda k, n=n: part(got2, k, n),
            lambda k, n=n: part(relayed2, k, n),
            lambda k, n=n: part(staged2, k, n),
            send3.at[n],
            arrive3.at[n],
        )
        for n in range(steps)
    ]

    def twin_copy(n):
        return copy_to(
            line2.at[pl.ds(n * rows, rows)],
            part(result, me.c, n),
            twin_send.at[n],
            twin_arrive.at[n],
            {"c": 1 - me.c},
        )

    def own_copy(n):
        return pltpu.make_async_copy(line2.at[pl.ds(n * rows, rows)], part(result, me.c, n), here.at[n])

    for transfer in sums:
        transfer.start()

    turn_rows(me, hidden, left_hidden)
    for transfer in sums:
        transfer.relay()
    for n in range(steps):
        at = pl.ds(n * rows, rows)
        mid = middle[at]
        scale = lax.rsqrt(jnp.mean(mid * mid, -1, keepdims=True) + EPSILON)
        normed = mid * scale
        total = sums[n].total()
        gsum = jnp.sum(total * normed, axis=0, keepdims=True)
        gain_grad[...] = gsum if n == 0 else gain_grad[...] + gsum
        scaled = total * gain[...]
        out = cot[at].astype(F32) + scale * (
            scaled - normed * jnp.mean(scaled * normed, -1, keepdims=True)
        )
        grad_middle[at] = out
        line[at] = low(out)
        spreads[n].start()
        if n:
            spreads[n - 1].relay()
        if n == 2:
            high_start(1)
    spreads[steps - 1].relay()
    for transfer in spreads:
        transfer.wait()
    for transfer in forth_sums:
        transfer.start()

    heads[...] = jnp.zeros_like(heads)

    def head_step(n, _):
        grad = dot(branch[n], merge_w[...])
        out = mixed[n]
        scale = lax.rsqrt(jnp.mean(out * out, -1, keepdims=True) + HEAD_FLOOR)
        normed = out * scale
        u = projected[3, n]
        sig = jax.nn.sigmoid(u)
        dn = grad * (u * sig)
        proj[n, :, 3 * HD :] = low(grad * normed * head_gain[...] * sig * (1.0 + u * (1.0 - sig)))
        heads[17:18] = heads[17:18] + jnp.sum(dn * normed, axis=0, keepdims=True)
        scaled = dn * head_gain[...]
        douts[n] = low(scale * (scaled - normed * jnp.mean(scaled * normed, -1, keepdims=True)))
        return 0

    lax.fori_loop(0, chunks, head_step, 0)

    def masks(n):
        return keyed_mask(first + n * CHUNK, starts_row, starts_column)

    def query_rows(n, visible):
        return low(projected[0, n] * jnp.exp(cumulated[n]) * visible)

    state[...] = jnp.zeros_like(state)

    def local_step(i, _):
        n = chunks - 1 - i
        _, visible, keep, _ = masks(n)
        carry = keep * jnp.exp(cumulated[n, CHUNK - 1 :])
        state[...] = carry * state[...] + dot_rows(douts[n], query_rows(n, visible))
        return 0

    lax.fori_loop(0, chunks, local_step, 0)
    states = StatePass(True, state, decay, state, *refs[-STATE_REFS:])
    states.begin()

    turn_rows(me, branch, left_branch)
    half = width // 2
    quarter = half // 2

    def tile_move(n):
        return copy_to(tiles.at[n], tiles_got.at[n], tile_send.at[n], tile_arrive.at[n], {"c": 1 - me.c})

    def right_tile(kind, n):
        if kind == 0:
            return gated[...].reshape(chunks * CHUNK, HD)[:, n * TILE : (n + 1) * TILE]
        at = 3 * HD + n * TILE
        return proj[...].reshape(chunks * CHUNK, 4 * HD)[:, at : at + TILE]

    lefts = left_branch, left_hidden
    for kind in range(2):
        for n in range(HD // TILE):
            tile = kind * (HD // TILE) + n
            tiles[tile] = low(dot(lefts[kind][pl.ds(0, half)], right_tile(kind, n)))
            tile_move(tile).start()
    states.combine()
    high_start(2)
    for kind in range(2):
        for n in range(HD // TILE):
            tile = kind * (HD // TILE) + n
            block = dot(lefts[kind][pl.ds(half, half)], right_tile(kind, n))
            tile_move(tile).wait_recv()
            block = low(block + tiles_got[tile].astype(F32))
            at = slice(tile * TILE, (tile + 1) * TILE)
            early_away[:, at] = block[:quarter]
            early_keep[:, at] = block[quarter:]
    early_move = copy_to(early_away, early, side_send.at[0], side_arrive.at[0], {"y": 1 - y})
    early_move.start()
    states.spread()
    for transfer in forth_sums:
        transfer.relay()
    states.finish()

    upper = (
        lax.broadcasted_iota(jnp.int32, (CHUNK, CHUNK), 0)
        <= lax.broadcasted_iota(jnp.int32, (CHUNK, CHUNK), 1)
    ).astype(F32)
    up_grad[...] = jnp.zeros_like(up_grad)

    def chunk_step(i, _):
        n = chunks - 1 - i
        pair, visible, keep, last = masks(n)
        b = cumulated[n]
        mid, end = b[CHUNK // 2 - 1 : CHUNK // 2], b[CHUNK - 1 :]
        q, k, v = projected[0, n], projected[1, n], low(projected[2, n])
        do = douts[n]
        eq, ek, el = jnp.exp(b - mid), jnp.exp(mid - b), jnp.exp(end - b) * last
        qh, kh, kc = low(q * eq), low(k * ek), k * el
        scores = low(jnp.where(pair, dot_last(qh, kh), 0.0))
        gs = low(jnp.where(pair, dot_last(do, v), 0.0))
        ds = low(state[...])
        proj[n, :, 2 * HD : 3 * HD] = low(dot_rows(scores, do) + dot_last(low(kc), ds))
        dq = dot(gs, kh) * eq + dot(do, low(befores[n])) * (jnp.exp(b) * visible)
        gkc = dot(v, ds)
        dk = dot_rows(gs, qh) * ek + gkc * el
        proj[n, :, :HD] = low(dq * HD ** (-0.5))
        proj[n, :, HD : 2 * HD] = low(dk)
        carry = keep * jnp.exp(end)
        extra = jnp.sum(gkc * kc, axis=0, keepdims=True)
        extra = extra + carry * jnp.sum(befores[n] * state[...], axis=0, keepdims=True)
        dlog = extra + jnp.dot(
            upper, dq * q - dk * k, precision=lax.Precision.HIGHEST, preferred_element_type=F32
        )
        state[...] = carry * state[...] + dot_rows(do, query_rows(n, visible))
        da = dlog * jax.nn.sigmoid(-gate[n]) / 16.0
        heads[16:17] = heads[16:17] + jnp.sum(da, axis=0, keepdims=True)
        dar = low(da)
        up_grad[...] = up_grad[...] + dot_rows(low_rank[n], dar)
        ranks[n] = low(dot_last(dar, up_pad[...]))
        return 0

    lax.fori_loop(0, chunks, chunk_step, 0)
    heads[0:16] = up_grad[2:18]
    for n in range(steps):
        at = pl.ds(n * rows, rows)
        line2[at] = low(middle[at] + forth_sums[n].total())
        twin_copy(n).start()
        own_copy(n).start()
    early_move.wait()
    add_rows(early, early_keep, early)
    for p in range(3):
        high_add(p)
    for n in range(steps):
        twin_copy(n).wait()
        own_copy(n).wait()
    for transfer in forth_sums:
        transfer.wait_sent()
    for group in highs_moves:
        for move in group:
            move.wait_send()
    for transfer in sums:
        transfer.wait_sent()
    for tile in range(tiles.shape[0]):
        tile_move(tile).wait_send()
    states.wait_sent()


def backward(
    back, forth, cot, middle, gain, pair, downs, merge_w, gated, projected, mixed, cumulated, gate, befores, decay,
    low_rank, up_pad, head_gain, hidden, starts,
):
    highs, members, owner_rows, units = downs.shape
    rows, width = cot.shape
    chunks = hidden.shape[0]

    def shape(*dims, kind=BF):
        return jax.ShapeDtypeStruct(dims, kind)

    arrays = [
        back, forth, cot, middle, gain, *pair, downs, merge_w, gated, projected, mixed, cumulated, gate, befores, decay,
        low_rank, up_pad, head_gain, hidden, *starts_arrays(starts),
    ]
    away = {5}
    quarter = width // 4
    shapes = [
        shape(rows, width, kind=F32),
        shape(1, width, kind=F32),
        shape(chunks, CHUNK, 4 * HD),
        shape(chunks, CHUNK, LANES),
        shape(24, HD, kind=F32),
        shape(quarter, 2 * HD),
        shape(members, owner_rows, units),
        shape(members, owner_rows, units),
        shape(members, owner_rows, units),
        shape(width, chunks * CHUNK),
        shape(2, rows, width),
    ]
    tiles = 2 * HD // TILE
    scratch = [
        shape(2, rows, width),
        shape(1, rows, width),
        shape(1, rows, width),
        shape(rows, width),
        shape(2, rows, width),
        shape(1, rows, width),
        shape(1, rows, width),
        shape(rows, width),
        shape(TEAM, rows, width),
        shape(width, chunks * CHUNK),
        shape(chunks, CHUNK, HD),
        shape(tiles, width // 2, TILE),
        shape(tiles, width // 2, TILE),
        shape(highs, members, owner_rows, 2 * units),
        shape(highs - 1, members, owner_rows, units),
        shape(highs - 1, members, owner_rows, units),
        shape(highs - 1, members, owner_rows, units),
        shape(quarter, 2 * HD),
        shape(quarter, 2 * HD),
        shape(RANKS, HD, kind=F32),
        shape(HD, HD, kind=F32),
    ]
    used = [a for n, a in enumerate(arrays) if n not in away] + shapes + scratch
    size = sum(a.size * a.dtype.itemsize for a in used)
    sems = [
        (STEPS, 3), (STEPS, 3), (STEPS, 5), (STEPS, 4), (3,), (3,), (3, highs), (3, highs), (tiles,), (tiles,),
        (STEPS, 3), (STEPS, 3), (STEPS,), (STEPS,), (STEPS,),
    ]
    return pl.pallas_call(
        backward_kernel,
        out_shape=shapes,
        in_specs=[ANY if n in away else VMEM for n in range(len(arrays))],
        out_specs=[VMEM] * len(shapes),
        scratch_shapes=[pltpu.VMEM(a.shape, a.dtype) for a in scratch]
        + [DMA(n) for n in sems]
        + state_pass_scratch(highs),
        compiler_params=pltpu.CompilerParams(
            collective_id=3, has_side_effects=True, vmem_limit_bytes=min(size + (14 << 20), 62 << 20)
        ),
        name="backward",
    )(*arrays)


def closing_kernel(*refs):
    (
        proj, ranks, mixer_w, left, own, grad_middle, gain, down, gain_two_grad, heads, early, ups, gates, downs,
        out, mixer_grad, merge_grad, pair_grad, down_grad, wide_out, heads_out, gains_out,
        partial, got, relayed, staged, line, tiles, tiles_got, late_away, late_keep, late_side,
        late_got, early_got, late_sum, early_sum, late_home, early_home, ups_home, gate_home, down_home,
        wide, wide_got, heads_got, heads_sum, wide_twin, gain_grad, rank_grad,
        send, arrive, twin_send, twin_arrive, here, tile_send, tile_arrive, side_send, side_arrive,
        high_send, high_arrive, home_send, home_arrive,
        wide_send, wide_arrive, heads_send, heads_arrive, near, out_send, out_arrive, gain_send, gain_arrive,
    ) = refs
    me = Place()
    zh, y, highs = lax.axis_index("zh"), lax.axis_index("y"), lax.axis_size("zh")
    greet_all(me)
    steps = send.shape[0]
    rows, width = own.shape[0] // steps, own.shape[1]
    chunks = proj.shape[0]
    twin = {"c": 1 - me.c}

    def high_copies(kind, source, target):
        return [
            copy_to(
                source.at[k],
                target.at[k - 1],
                high_send.at[kind, k],
                high_arrive.at[kind, k],
                {"zh": lax.rem(zh + k, highs)},
            )
            for k in range(1, highs)
        ]

    def side_copy(kind, source, target):
        return copy_to(source, target, side_send.at[kind], side_arrive.at[kind], {"y": 1 - y})

    def home(kind, source, target):
        return Transfer(
            route_weights_home(me),
            lambda k: source.at[k],
            lambda k: target.at[k],
            home_send.at[kind],
            home_arrive.at[kind],
        )

    late_moves = [side_copy(j, late_away.at[j], late_side.at[j]) for j in range(3)]
    high_moves = [high_copies(j, late_side.at[j], late_got.at[j]) for j in range(3)]
    high_moves += [high_copies(3, early, early_got)]
    homes = [home(j, late_sum.at[j], late_home.at[j]) for j in range(3)]
    homes += [home(3, early_sum, early_home), home(4, ups, ups_home)]
    homes += [home(5, gates, gate_home), home(6, downs, down_home)]
    group_out, group_arrive = [], []
    for n in range(highs):
        for f in range(4):
            to_zh, to_y, to_c = lax.rem(zh + n, highs), flip(y, f & 2), flip(me.c, f & 1)
            to = {"zh": to_zh, "y": to_y, "c": to_c}
            group_out.append((0, (zh * 2 + y) * 2 + me.c, to, n + f == 0))
            group_arrive.append(((to_zh * 2 + to_y) * 2 + to_c, n + f == 0))
    heads_move = Transfer(
        (group_out, group_arrive), lambda _: heads, lambda k: heads_got.at[k], heads_send, heads_arrive
    )
    heads_move.start()

    for move in high_moves[3]:
        move.start()

    half = width // 2
    quarter = half // 2
    owner_rows = early.shape[2]

    def tile_move(n):
        return copy_to(tiles.at[n], tiles_got.at[n], tile_send.at[n], tile_arrive.at[n], twin)

    def right_tile(n):
        return proj[:, :, pl.ds(pl.multiple_of(n * TILE, TILE), TILE)].reshape(chunks * CHUNK, TILE)

    def tile_step(n, _):
        tiles[n] = low(dot(left[pl.ds(0, half)], right_tile(n)))
        tile_move(n).start()
        return 0

    lax.fori_loop(0, 3 * HD // TILE, tile_step, 0)

    for n in range(chunks):
        partial[n, :, width:] = ranks[n]

    def hidden_step(n, _):
        at = pl.ds(pl.multiple_of(n * TILE, TILE), TILE)
        block = low(dot_last(proj[...].reshape(chunks * CHUNK, 4 * HD), mixer_w[at]))
        for k in range(chunks):
            partial[k, :, at] = block[k * CHUNK : (k + 1) * CHUNK]
        return 0

    lax.fori_loop(0, width // TILE, hidden_step, 0)

    def part(ref, k, n):
        return ref.at[k, pl.ds(n * rows, rows)]

    sums = [
        OwnersSum(
            me,
            lambda k, n=n: part(partial, k, n),
            lambda k, n=n: part(got, k, n),
            lambda k, n=n: part(relayed, k, n),
            lambda k, n=n: part(staged, k, n),
            send.at[n],
            arrive.at[n],
        )
        for n in range(steps)
    ]
    for transfer in sums:
        transfer.start()

    for j in range(3):
        for i in range(HD // TILE):
            n = j * (HD // TILE) + i
            block = dot(left[pl.ds(half, half)], right_tile(n))
            tile_move(n).wait_recv()
            block = low(block + tiles_got[n].astype(F32))
            columns = slice(i * TILE, (i + 1) * TILE)
            for k in range(highs):
                for m in range(2):
                    at = (k * 2 + m) * owner_rows
                    late_away[j, k, m, :, columns] = block[at : at + owner_rows]
                    late_keep[j, k, m, :, columns] = block[quarter + at : quarter + at + owner_rows]
        late_moves[j].start()
    for n in (6, 5, 4):
        homes[n].start()

    def side_add(move, keep, there):
        move.wait()
        for k in range(highs):
            for m in range(2):
                add_rows(there.at[k, m], keep.at[k, m], there.at[k, m])

    for transfer in sums:
        transfer.relay()
    for j in range(3):
        side_add(late_moves[j], late_keep.at[j], late_side.at[j])
        for move in high_moves[j]:
            move.start()

    def twin_copy(n):
        return copy_to(
            line.at[pl.ds(n * rows, rows)], part(out, me.c, n), twin_send.at[n], twin_arrive.at[n], twin
        )

    def own_copy(n):
        return pltpu.make_async_copy(line.at[pl.ds(n * rows, rows)], part(out, me.c, n), here.at[n])

    for n in range(steps):
        at = pl.ds(n * rows, rows)
        x = own[at].astype(F32)
        scale = lax.rsqrt(jnp.mean(x * x, -1, keepdims=True) + EPSILON)
        normed = x * scale
        total = sums[n].total()
        rank = low(total[:, width:])
        total = total[:, :width] + dot(rank, down[...])
        gsum = jnp.sum(total * normed, axis=0, keepdims=True)
        hidden = low(normed * gain[...])
        rsum = dot_rows(rank, hidden)
        gain_grad[...] = gsum if n == 0 else gain_grad[...] + gsum
        rank_grad[...] = rsum if n == 0 else rank_grad[...] + rsum
        scaled = total * gain[...]
        line[at] = low(
            grad_middle[at]
            + scale * (scaled - normed * jnp.mean(scaled * normed, -1, keepdims=True))
        )
        twin_copy(n).start()
        own_copy(n).start()

    for n in range(wide.shape[0]):
        at = slice(n * owner_rows, (n + 1) * owner_rows)
        wide[n, 0:1] = gain_grad[:, at]
        wide[n, 1:2] = gain_two_grad[:, at]
        wide[n, 2:8] = jnp.zeros((6, owner_rows), F32)
        wide[n, 8:24] = rank_grad[:16, at]
    spreads = Transfer(
        route_all(me), lambda k: wide.at[k], lambda k: wide_got.at[k], wide_send, wide_arrive
    )
    spreads.start()
    def high_add(kind, source, target, total):
        for k in range(1, highs):
            wait_for(target.at[k - 1], high_arrive.at[kind, k])
        for m in range(2):
            add_rows(total.at[m], source.at[0, m], *(target.at[k - 1, m] for k in range(1, highs)))
        homes[kind].start()


    heads_move.wait()
    total = heads_got[0]
    for n in range(1, highs * 4):
        total = total + heads_got[n]
    heads_sum[...] = total
    tail = gains_out.shape[1]
    gains = Transfer(
        route_member(me),
        lambda _: heads_sum.at[pl.ds(heads_sum.shape[0] - tail, tail)],
        lambda k: gains_out.at[k],
        gain_send,
        gain_arrive,
    )
    gains.start()
    moves = [
        copy_to(
            heads_sum,
            heads_out.at[me.x],
            out_send.at[n],
            out_arrive.at[me.x],
            {"zl": flip(me.zl, fz), "x": flip(me.x, fx)},
        )
        for n, (fz, fx) in enumerate(FLIPS[:3])
    ]

    @pl.when(me.c == me.zl)
    def _():
        for move in moves:
            move.start()
        heads_out[me.x] = heads_sum[...]

    spreads.wait()
    total = wide_got[0]
    for n in range(1, wide.shape[0]):
        total = total + wide_got[n]
    wide_out[...] = total
    swap = copy_to(wide_out, wide_twin, near.at[0], near.at[1], twin)
    swap.start()

    units = gates.shape[-1]

    def spread_columns(source, target, cols):
        for k in range(2):
            target[:, k * cols : (k + 1) * cols] = source[k].astype(F32)

    def spread_rows(source, target, cols):
        for k in range(2):
            target[k * cols : (k + 1) * cols] = source[k, :, :cols].astype(F32).T

    homes[6].wait()
    spread_rows(down_home, down_grad, units)
    homes[5].wait()
    spread_columns(gate_home, pair_grad.at[0], units)
    homes[4].wait()
    spread_columns(ups_home, pair_grad.at[1], units)
    high_add(3, early, early_got, early_sum)
    for k in range(2):
        own_slot = (me.c == me.zl) & (me.x == k)
        unless(own_slot, lambda k=k: wait_for(heads_out.at[k], out_arrive.at[k]))

    @pl.when(me.c == me.zl)
    def _():
        for move in moves:
            move.wait_send()

    swap.wait()
    wide_out[...] = wide_out[...] + wide_twin[...]
    gains.wait()
    for j in range(3):
        high_add(j, late_side.at[j], late_got.at[j], late_sum.at[j])
    homes[3].wait()
    spread_rows(early_home, merge_grad, HD)
    for k in range(2):
        mixer_grad[3, :, k * HD : (k + 1) * HD] = early_home[k, :, HD:].astype(F32)
    for j in range(3):
        homes[j].wait()
        spread_columns(late_home.at[j], mixer_grad.at[j], HD)
    for transfer in sums:
        transfer.wait_sent()
    for n in range(steps):
        twin_copy(n).wait()
        own_copy(n).wait()
    for group in high_moves:
        for move in group:
            move.wait_send()

    def tile_sent(n, _):
        tile_move(n).wait_send()
        return 0

    lax.fori_loop(0, tiles.shape[0], tile_sent, 0)


def closing(proj, ranks, mixer_w, left, own, grad_middle, gain, down, gain_two_grad, heads, early, ups, gates, downs):
    rows, width = own.shape
    chunks = proj.shape[0]
    highs, _, owner_rows, _ = early.shape
    units = ups.shape[-1]
    chips = highs * 8
    arrays = [
        proj, ranks, mixer_w, left, own, grad_middle, gain, down, gain_two_grad, heads, early, ups, gates, downs,
    ]

    def shape(*dims, kind=BF):
        return jax.ShapeDtypeStruct(dims, kind)

    shapes = [
        shape(2, rows, width),
        shape(4, owner_rows, 2 * HD, kind=F32),
        shape(2 * HD, owner_rows, kind=F32),
        shape(2, owner_rows, 2 * units, kind=F32),
        shape(2 * units, owner_rows, kind=F32),
        shape(24, owner_rows, kind=F32),
        shape(2, *heads.shape, kind=F32),
        shape(TEAM, 8, heads.shape[1], kind=F32),
    ]
    tiles = 3 * HD // TILE
    late = (3, highs, 2, owner_rows, HD)
    scratch = [shape(chunks, CHUNK, width + LANES)]
    scratch += [shape(n, rows, width + LANES) for n in (3, 2, 2)] + [shape(rows, width)]
    scratch += [shape(tiles, width // 2, TILE)] * 2 + [shape(*late)] * 3
    scratch += [
        shape(3, highs - 1, 2, owner_rows, HD),
        shape(highs - 1, 2, owner_rows, 2 * HD),
    ]
    sums = [shape(3, 2, owner_rows, HD), shape(2, owner_rows, 2 * HD)]
    scratch += sums + sums + [shape(2, owner_rows, units)] * 3
    scratch += [
        shape(chips, 24, owner_rows, kind=F32),
        shape(chips, 24, owner_rows, kind=F32),
        shape(highs * 4, *heads.shape, kind=F32),
        shape(*heads.shape, kind=F32),
        shape(24, owner_rows, kind=F32),
        shape(1, width, kind=F32),
        shape(LANES, width, kind=F32),
    ]
    size = sum(a.size * a.dtype.itemsize for a in arrays + shapes + scratch)
    sems = [
        (STEPS, 6), (STEPS, 5), (STEPS,), (STEPS,), (STEPS,), (tiles,), (tiles,), (3,), (3,), (4, highs), (4, highs),
        (7, 2), (7, 2), (chips,), (chips,), (highs * 4,), (highs * 4,), (2,), (3,), (2,), (TEAM,), (TEAM,),
    ]
    return pl.pallas_call(
        closing_kernel,
        out_shape=shapes,
        in_specs=[VMEM] * len(arrays),
        out_specs=[VMEM] * len(shapes),
        scratch_shapes=[pltpu.VMEM(a.shape, a.dtype) for a in scratch] + [DMA(n) for n in sems],
        compiler_params=pltpu.CompilerParams(
            collective_id=4, has_side_effects=True, vmem_limit_bytes=min(size + (10 << 20), 62 << 20)
        ),
        name="closing",
    )(*arrays)


def shards(
    tokens,
    cotangent,
    lengths,
    attn_gain,
    ffn_gain,
    mixer_in,
    decay_down,
    decay_up,
    decay_bias,
    head_gain,
    mixer_out,
    ffn_in,
    ffn_out,
):
    zh, zl, y, x, c = (lax.axis_index(a) for a in SEQ + ("c",))
    block, width = tokens.shape
    half = block // 2
    rows = mixer_in.shape[1]
    units = ffn_out.shape[0] // 2
    team_tokens = 2 * block
    rank = decay_down.shape[1]

    small = jnp.concatenate([attn_gain[None], ffn_gain[None], decay_down.T], axis=0)
    small = jnp.pad(small, ((0, RANKS - small.shape[0]), (0, 0)))
    up_head = lax.dynamic_slice_in_dim(decay_up, HD * x, HD, 1).astype(F32)
    bias_head = lax.dynamic_slice_in_dim(decay_bias, HD * x, HD, 0)
    ups = jnp.concatenate([up_head, bias_head[None], jnp.zeros((7, HD), F32)], axis=0)
    own = lax.dynamic_slice_in_dim(tokens, half * c, half, 0)
    own_dy = lax.dynamic_slice_in_dim(cotangent, half * c, half, 0)
    starts = jnp.cumsum(lengths) - lengths
    (
        mixer_w, merge_w, pair_w, down_w, gains, ffn_dy, hidden_one, low_rank, gate_input, cumulated, projected,
        mixed, gated, befores, decay, hidden_two, middle,
    ) = forward(
        mixer_in, mixer_out.T, ffn_in, ffn_out.T, small, ups, own, own_dy, starts, head_gain[None]
    )
    up_head = jnp.where(c == zl, up_head, lax.ppermute(up_head, "c", CROSS)).astype(BF)
    mixer_w, merge_w = mixer_w.reshape(width, 4 * HD), merge_w.reshape(width, HD)
    pair_w, down_w = pair_w.reshape(width, 2 * units), down_w.reshape(width, units)
    gain_one, gain_two, rank_down = gains[:1], gains[1:2], gains[2 : 2 + rank].astype(BF)
    forth, back, *pair_sides, down_part = feed_forward(hidden_two, ffn_dy, pair_w, down_w)
    highs = lax.axis_size("zh")
    pair_sides = [a.reshape(highs, 2, rows, 2 * units) for a in pair_sides]
    down_part = down_part.reshape(highs, 2, rows, units)
    pad_rank = ((0, LANES - rank), (0, 0))
    (
        grad_middle, grad_gain_two, grad_proj, grad_ranks, heads, early, gate_sum, up_sum, down_sum,
        left_hidden, result,
    ) = backward(
        back, forth, own_dy, middle, gain_two, pair_sides, down_part, merge_w, gated, projected, mixed, cumulated,
        gate_input, befores, decay, low_rank, jnp.pad(up_head, pad_rank), head_gain[None], hidden_one, starts,
    )
    early = early.reshape(highs, 2, rows, 2 * HD)
    grad_inputs, mixer_home, merge_home, pair_home, down_home, wide, heads, gains = closing(
        grad_proj, grad_ranks, mixer_w, left_hidden, own, grad_middle, gain_one, jnp.pad(rank_down, pad_rank),
        grad_gain_two, heads, early, up_sum, gate_sum, down_sum,
    )
    return (
        result.reshape(block, width),
        grad_inputs.reshape(block, width),
        wide[0],
        wide[1],
        mixer_home,
        wide[8 : 8 + rank].T,
        heads[:, :rank].transpose(1, 0, 2).reshape(rank, 2 * HD),
        heads[:, rank].reshape(2 * HD),
        jnp.sum(gains[:, rank + 1 - 16], axis=0),
        merge_home,
        pair_home,
        down_home,
    )


def solution(mesh):
    devices = mesh.devices
    inner = Mesh(devices.reshape(devices.shape[0] // 8, 2, 2, 2, devices.shape[1]), SEQ + ("c",))
    in_specs = (
        P(SEQ, None),
        P(SEQ, None),
        P(),
        P(SEQ),
        P(SEQ),
        P(None, SEQ, "c"),
        P(SEQ, None),
        P(None, "c"),
        P("c"),
        P(),
        P("c", SEQ),
        P(None, SEQ, "c"),
        P("c", SEQ),
    )
    out_specs = (
        P(SEQ, None),
        P(SEQ, None),
        P(SEQ),
        P(SEQ),
        P(None, SEQ, "c"),
        P(SEQ, None),
        P(None, "c"),
        P("c"),
        P(),
        P("c", SEQ),
        P(None, SEQ, "c"),
        P("c", SEQ),
    )
    return jax.shard_map(shards, mesh=inner, in_specs=in_specs, out_specs=out_specs, check_vma=False)
```

```python
import functools

import jax
import jax.numpy as jnp
from jax import lax
from jax.experimental import pallas as pl
from jax.experimental.pallas import tpu as pltpu
from jax.sharding import Mesh, PartitionSpec as P

HD = 512
CHUNK = 128
EPSILON = 1e-06
HEAD_FLOOR = 1.0
TEAM = 4

BF = jnp.bfloat16
F32 = jnp.float32
MESH = pl.DeviceIdType.MESH
ANY = pl.BlockSpec(memory_space=pl.ANY)
VMEM = pl.BlockSpec(memory_space=pltpu.VMEM)
DMA = pltpu.SemaphoreType.DMA

SEQ = ("zh", "zl", "y", "x")
FLIPS = ((1, 1), (0, 1), (1, 0), (0, 0))


def dot(a, b):
    return jnp.dot(a, b, preferred_element_type=F32)


def dot_rows(a, b):
    return lax.dot_general(a, b, (((0,), (0,)), ((), ())), preferred_element_type=F32)


def dot_last(a, b):
    return lax.dot_general(a, b, (((1,), (1,)), ((), ())), preferred_element_type=F32)


def low(v):
    return v.astype(BF)


def flip(index, by):
    return 1 - index if by else index


class Place:
    def __init__(self):
        self.zl, self.x, self.c = lax.axis_index("zl"), lax.axis_index("x"), lax.axis_index("c")
        self.member = self.zl * 2 + self.x


def greet_team(me, more=0):
    barrier = pltpu.get_barrier_semaphore()
    for n in range(1, 8):
        to = {"zl": flip(me.zl, n & 1), "x": flip(me.x, n & 2), "c": flip(me.c, n & 4)}
        pl.semaphore_signal(barrier, inc=1, device_id=to, device_id_type=MESH)
    pl.semaphore_wait(barrier, 7 + more)


def others(me):
    zh, y, highs = lax.axis_index("zh"), lax.axis_index("y"), lax.axis_size("zh")
    for k in range(highs):
        for n in range(8):
            yield lax.rem(zh + k, highs), flip(me.zl, n & 1), flip(y, n & 2), flip(me.x, n & 4), k + n == 0


def greet_all(me):
    barrier = pltpu.get_barrier_semaphore()
    count = 0
    for zh, zl, y, x, own in others(me):
        for f in range(2):
            if own and not f:
                continue
            to = {"zh": zh, "zl": zl, "y": y, "x": x, "c": flip(me.c, f)}
            pl.semaphore_signal(barrier, inc=1, device_id=to, device_id_type=MESH)
            count += 1
    pl.semaphore_wait(barrier, count)


def route_member(me):
    out, arrive = [], []
    for fz, fx in FLIPS:
        zl, x = flip(me.zl, fz), flip(me.x, fx)
        own = (fz, fx) == (0, 0)
        out.append((zl * 2 + x, me.member, {"zl": zl, "x": x}, own))
        arrive.append((zl * 2 + x, own))
    return out, arrive


def chip_index(zh, zl, y, x):
    return ((zh * 2 + zl) * 2 + y) * 2 + x


def route_all(me):
    mine = chip_index(lax.axis_index("zh"), me.zl, lax.axis_index("y"), me.x)
    out, arrive = [], []
    for zh, zl, y, x, own in others(me):
        chip = chip_index(zh, zl, y, x)
        out.append((chip, mine, {"zh": zh, "zl": zl, "y": y, "x": x}, own))
        arrive.append((chip, own))
    return out, arrive


def route_halves(me):
    mine = me.c == me.zl
    out, arrive = [], []
    for fz, fx in FLIPS:
        zl, x = flip(me.zl, fz), flip(me.x, fx)
        own = mine if (fz, fx) == (0, 0) else False
        out.append((0, me.x * 2 + me.c, {"zl": zl, "x": x, "c": me.zl}, own))
    for fc, fx in FLIPS:
        c, x = flip(me.c, fc), flip(me.x, fx)
        own = mine if (fc, fx) == (0, 0) else False
        arrive.append((x * 2 + c, own))
    return out, arrive


def route_owners(me):
    mine = me.c == me.zl
    out, arrive = [], []
    for fc, fx in FLIPS:
        c, x = flip(me.c, fc), flip(me.x, fx)
        own = mine if (fc, fx) == (0, 0) else False
        out.append((x * 2 + c, me.member, {"zl": me.c, "x": x, "c": c}, own))
    for fz, fx in FLIPS:
        zl, x = flip(me.zl, fz), flip(me.x, fx)
        own = mine if (fz, fx) == (0, 0) else False
        arrive.append((zl * 2 + x, own))
    return out, arrive


def route_weights(me):
    mine = (me.c == me.zl) & (me.c == me.x)
    out, arrive = [], []
    for f in (1, 0):
        x = flip(me.x, f)
        own = (me.c == me.zl) & (me.c == x) & (me.x == me.c) if not f else False
        out.append((x, me.zl, {"zl": me.c, "x": x, "c": me.x}, own))
    for f in (1, 0):
        zl = flip(me.zl, f)
        own = mine if not f else False
        arrive.append((zl, own))
    return out, arrive


def route_weights_home(me):
    mine = (me.c == me.zl) & (me.c == me.x)
    out, arrive = [], []
    for f in (1, 0):
        zl = flip(me.zl, f)
        own = mine if not f else False
        out.append((zl, me.x, {"zl": zl, "x": me.c, "c": me.zl}, own))
    for f in (1, 0):
        x = flip(me.x, f)
        own = mine if not f else False
        arrive.append((x, own))
    return out, arrive


def when(condition, run):
    if condition is True:
        run()
    elif condition is not False:
        pl.when(condition)(run)


def unless(condition, run):
    if condition is False:
        run()
    elif condition is not True:
        pl.when(jnp.logical_not(condition))(run)


class Transfer:
    def __init__(self, route, source, target, send, arrive):
        self.route, self.source, self.target, self.send, self.arrive = route, source, target, send, arrive

    def _remote(self, n):
        index, slot, to, own = self.route[0][n]
        return pltpu.make_async_remote_copy(
            src_ref=self.source(index),
            dst_ref=self.target(slot),
            send_sem=self.send.at[n],
            recv_sem=self.arrive.at[slot],
            device_id=to,
            device_id_type=MESH,
        )

    def _local(self, n):
        index, slot, to, own = self.route[0][n]
        return pltpu.make_async_copy(self.source(index), self.target(slot), self.send.at[n])

    def start(self):
        for n, (_, _, _, own) in enumerate(self.route[0]):
            unless(own, lambda: self._remote(n).start())
            when(own, lambda: self._local(n).start())

    def wait_arrive(self):
        for slot, own in self.route[1]:
            ref = self.target(slot)

            def arrived():
                pltpu.make_async_copy(ref, ref, self.arrive.at[slot]).wait()

            unless(own, arrived)

    def wait_local(self):
        for n, (_, _, _, own) in enumerate(self.route[0]):
            when(own, lambda: self._local(n).wait())

    def wait_sent(self):
        for n, (_, _, _, own) in enumerate(self.route[0]):
            unless(own, lambda: self._remote(n).wait_send())

    def wait(self):
        self.wait_arrive()
        self.wait_local()
        self.wait_sent()


def copy_to(src, dst, send, arrive, to):
    return pltpu.make_async_remote_copy(
        src_ref=src, dst_ref=dst, send_sem=send, recv_sem=arrive, device_id=to, device_id_type=MESH
    )


def wait_for(ref, sem):
    pltpu.make_async_copy(ref, ref, sem).wait()


def member_slots(me, two):
    along = me.zl * 2 + 1 - me.x, {"x": 1 - me.x}
    over = (1 - me.zl) * 2 + me.x, {"zl": 1 - me.zl}
    one, double = (over, along) if two == "x" else (along, over)
    return one[0], double[0], (1 - me.zl) * 2 + 1 - me.x, one[1], double[1]


class MemberSpread:
    def __init__(self, me, source, target, send, arrive, two="x"):
        self.target, self.arrive = target, arrive
        mine = me.member
        one, double, across, to_one, to_double = member_slots(me, two)
        self.slots = one, double, across
        self.direct = [
            copy_to(source, target(mine), send.at[0], arrive.at[mine], to_one),
            copy_to(source, target(mine), send.at[1], arrive.at[mine], to_double),
        ]
        self.local = pltpu.make_async_copy(source, target(mine), arrive.at[mine])
        self.forward = copy_to(target(one), target(one), send.at[2], arrive.at[one], to_double)

    def start(self):
        for copy in self.direct:
            copy.start()
        self.local.start()

    def relay(self):
        wait_for(self.target(self.slots[0]), self.arrive.at[self.slots[0]])
        self.forward.start()

    def wait(self):
        for slot in self.slots[1:]:
            wait_for(self.target(slot), self.arrive.at[slot])
        self.local.wait()
        for copy in self.direct + [self.forward]:
            copy.wait_send()


class HalvesSpread:
    def __init__(self, me, source, target, send, arrive):
        self.me, self.target, self.arrive = me, target, arrive
        mine = me.x * 2 + me.c
        self.home = me.c == me.zl
        self.direct = [
            copy_to(source, target(mine), send.at[0], arrive.at[mine], {"zl": 1 - me.zl, "c": me.zl}),
            copy_to(source, target(mine), send.at[1], arrive.at[mine], {"x": 1 - me.x, "c": me.zl}),
        ]
        self.near = copy_to(source, target(mine), send.at[2], arrive.at[mine], {"c": 1 - me.c})
        self.local = pltpu.make_async_copy(source, target(mine), send.at[2])
        self.near_slots = [me.x * 2 + c for c in range(2)]
        self.far_slots = [(1 - me.x) * 2 + c for c in range(2)]
        self.forwards = [
            copy_to(target(slot), target(slot), send.at[3 + c], arrive.at[slot], {"x": 1 - me.x})
            for c, slot in enumerate(self.near_slots)
        ]

    def start(self):
        for copy in self.direct:
            copy.start()
        pl.when(self.home)(self.local.start)
        unless(self.home, self.near.start)

    def relay(self):
        @pl.when(jnp.logical_not(self.home))
        def _():
            for slot, forward in zip(self.near_slots, self.forwards):
                wait_for(self.target(slot), self.arrive.at[slot])
                forward.start()

    def wait(self):
        me = self.me

        @pl.when(self.home)
        def _():
            self.local.wait()
            slot = me.x * 2 + 1 - me.c
            wait_for(self.target(slot), self.arrive.at[slot])

        for slot in self.far_slots:
            wait_for(self.target(slot), self.arrive.at[slot])
        for copy in self.direct:
            copy.wait_send()

        @pl.when(jnp.logical_not(self.home))
        def _():
            self.near.wait_send()
            for forward in self.forwards:
                forward.wait_send()


class MemberSum:
    def __init__(self, me, source, got, relayed, staged, send, arrive, two="x"):
        self.me, self.source, self.got, self.relayed, self.staged = me, source, got, relayed, staged
        self.arrive = arrive
        self.one, double, across, to_one, to_double = member_slots(me, two)
        self.direct = [
            copy_to(source(across), relayed(0), send.at[0], arrive.at[0], to_double),
            copy_to(source(double), got(0), send.at[1], arrive.at[1], to_double),
        ]
        self.onward = copy_to(staged(0), got(1), send.at[2], arrive.at[2], to_one)

    def start(self):
        for copy in self.direct:
            copy.start()

    def relay(self):
        wait_for(self.relayed(0), self.arrive.at[0])
        own = self.source(self.one)[...].astype(F32)
        self.staged(0)[...] = low(own + self.relayed(0)[...].astype(F32))
        self.onward.start()

    def total(self):
        wait_for(self.got(0), self.arrive.at[1])
        wait_for(self.got(1), self.arrive.at[2])
        total = self.source(self.me.member)[...].astype(F32)
        return total + self.got(0)[...].astype(F32) + self.got(1)[...].astype(F32)

    def wait_sent(self):
        for copy in self.direct + [self.onward]:
            copy.wait_send()


class OwnersSum:
    def __init__(self, me, source, got, relayed, staged, send, arrive):
        self.me, self.source, self.got, self.relayed, self.staged = me, source, got, relayed, staged
        self.arrive = arrive
        self.home = me.c == me.zl
        mine, other = me.x * 2, (1 - me.x) * 2
        self.near = copy_to(source(mine + 1 - me.c), got(0), send.at[0], arrive.at[0], {"c": 1 - me.c})
        self.local = pltpu.make_async_copy(source(mine + me.c), got(0), send.at[1])
        self.across = [
            copy_to(source(other + c), got(1), send.at[2 + c], arrive.at[1], {"x": 1 - me.x, "c": c})
            for c in range(2)
        ]
        self.first = [
            copy_to(source(other + c), relayed(c), send.at[2 + c], arrive.at[3 + c], {"x": 1 - me.x})
            for c in range(2)
        ]
        self.onward = [
            copy_to(staged(c), got(2), send.at[4 + c], arrive.at[2], {"zl": me.c, "c": c})
            for c in range(2)
        ]

    def start(self):
        @pl.when(self.home)
        def _():
            for copy in self.across + [self.near, self.local]:
                copy.start()

        @pl.when(jnp.logical_not(self.home))
        def _():
            for copy in self.first:
                copy.start()

    def relay(self):
        @pl.when(jnp.logical_not(self.home))
        def _():
            for c in range(2):
                wait_for(self.relayed(c), self.arrive.at[3 + c])
                own = self.source(self.me.x * 2 + c)[...].astype(F32)
                self.staged(c)[...] = low(own + self.relayed(c)[...].astype(F32))
                self.onward[c].start()

    def total(self):
        pl.when(self.home)(self.local.wait)
        unless(self.home, lambda: wait_for(self.got(0), self.arrive.at[0]))
        wait_for(self.got(1), self.arrive.at[1])
        wait_for(self.got(2), self.arrive.at[2])
        return sum(self.got(k)[...].astype(F32) for k in range(3))

    def wait_sent(self):
        @pl.when(self.home)
        def _():
            for copy in self.across + [self.near]:
                copy.wait_send()

        @pl.when(jnp.logical_not(self.home))
        def _():
            for copy in self.first + self.onward:
                copy.wait_send()


class Placed(Transfer):
    def __init__(self, route, source, there, target, send, arrive):
        super().__init__(route, source, target, send, arrive)
        self.there = there

    def _remote(self, n):
        index, slot, to, own = self.route[0][n]
        return pltpu.make_async_remote_copy(
            src_ref=self.source(index),
            dst_ref=self.there(slot),
            send_sem=self.send.at[n],
            recv_sem=self.arrive.at[slot],
            device_id=to,
            device_id_type=MESH,
        )


LANES = 128
RANKS = 32


def keyed_mask(start, starts_row, starts_column):
    rows = lax.broadcasted_iota(jnp.int32, (CHUNK, CHUNK), 0)
    columns = lax.broadcasted_iota(jnp.int32, (CHUNK, CHUNK), 1)
    ids = jnp.sum((rows + start >= starts_row[0:1]).astype(F32), axis=1, keepdims=True)
    places = lax.broadcasted_iota(jnp.int32, starts_column.shape, 1)
    ids_row = jnp.sum((places + start >= starts_column[...]).astype(F32), axis=0, keepdims=True)
    before = jnp.sum((starts_row[0:1] < start).astype(F32), axis=1, keepdims=True)
    final = ids_row[:, CHUNK - 1 :]
    pair = (rows >= columns) & (ids == ids_row)
    visible = (ids == before).astype(F32)
    keep = (final == before).astype(F32)
    return pair, visible, keep, (ids == final).astype(F32)


class StatePass:
    def __init__(self, back, local, decay, out, rounded, got, got_decay, sums, sum_decays, stage, stage_decay,
                 entering, leave, enter, send, arrive, far_send, far_arrive, leave_send, leave_arrive):
        self.__dict__.update(locals())
        self.zh, c, y = lax.axis_index("zh"), lax.axis_index("c"), lax.axis_index("y")
        self.highs = lax.axis_size("zh")
        self.mine = c * 2 + y
        self.quarter = local.shape[0] // 4
        self.partners = []
        for fc, fy in ((1, 1), (0, 1), (1, 0)):
            to_c, to_y = flip(c, fc), flip(y, fy)
            self.partners.append((to_c * 2 + to_y, {"c": to_c, "y": to_y}))
        self.order = range(3, -1, -1) if back else range(4)
        self.moves, self.outs = [], []

    def begin(self):
        self.rounded[...] = low(self.local[...])
        for n, (index, to) in enumerate(self.partners):
            rows = self.rounded.at[pl.ds(index * self.quarter, self.quarter)]
            self.moves.append(copy_to(rows, self.got.at[self.mine], self.send.at[0, n], self.arrive.at[0, self.mine], to))
            self.moves.append(
                copy_to(self.decay, self.got_decay.at[self.mine], self.send.at[1, n], self.arrive.at[1, self.mine], to)
            )
        for move in self.moves:
            move.start()
        self.got[self.mine] = self.rounded[pl.ds(self.mine * self.quarter, self.quarter)]
        self.got_decay[self.mine] = self.decay[...]

    def needs(self, source, target):
        return (source > target) if self.back else (source < target)

    def far(self, n, to):
        zh = self.zh
        return (
            copy_to(self.stage, self.sums.at[zh], self.far_send.at[0, n], self.far_arrive.at[0, zh], {"zh": to}),
            copy_to(
                self.stage_decay, self.sum_decays.at[zh], self.far_send.at[1, n], self.far_arrive.at[1, zh], {"zh": to}
            ),
        )

    def combine(self):
        for index, _ in self.partners:
            wait_for(self.got.at[index], self.arrive.at[0, index])
            wait_for(self.got_decay.at[index], self.arrive.at[1, index])
        total, total_decay = None, None
        for k in self.order:
            piece, d = self.got[k].astype(F32), self.got_decay[k][:1]
            total = piece if total is None else d * total + piece
            total_decay = d if total_decay is None else total_decay * d
        self.stage[...] = low(total)
        self.stage_decay[...] = jnp.broadcast_to(total_decay, self.stage_decay.shape)
        for n in range(1, self.highs):
            to = lax.rem(self.zh + n, self.highs)

            @pl.when(self.needs(self.zh, to))
            def _(n=n, to=to):
                for move in self.far(n, to):
                    move.start()

    def spread(self):
        self.entering[...] = jnp.zeros_like(self.entering)
        for n in range(self.highs):
            k = self.highs - 1 - n if self.back else n

            @pl.when(self.needs(k, self.zh))
            def _(k=k):
                wait_for(self.sums.at[k], self.far_arrive.at[0, k])
                wait_for(self.sum_decays.at[k], self.far_arrive.at[1, k])
                self.entering[...] = self.sum_decays[k][:1] * self.entering[...] + self.sums[k].astype(F32)

        state = self.entering[...]
        for k in self.order:
            self.leave[k] = low(state)
            state = self.got_decay[k][:1] * state + self.got[k].astype(F32)
        for n, (index, to) in enumerate(self.partners):
            self.outs.append(
                copy_to(
                    self.leave.at[index], self.enter.at[self.mine], self.leave_send.at[n],
                    self.leave_arrive.at[self.mine], to,
                )
            )
        for move in self.outs:
            move.start()
        self.enter[self.mine] = self.leave[self.mine]

    def finish(self):
        for index, _ in self.partners:
            wait_for(self.enter.at[index], self.leave_arrive.at[index])
        for k in range(4):
            self.out[pl.ds(k * self.quarter, self.quarter)] = self.enter[k].astype(F32)

    def wait_sent(self):
        for move in self.moves + self.outs:
            move.wait_send()
        for n in range(1, self.highs):
            to = lax.rem(self.zh + n, self.highs)

            @pl.when(self.needs(self.zh, to))
            def _(n=n, to=to):
                for move in self.far(n, to):
                    move.wait_send()


def state_pass_scratch(highs):
    quarter = HD // 4
    return [
        pltpu.VMEM((HD, HD), BF),
        pltpu.VMEM((4, quarter, HD), BF),
        pltpu.VMEM((4, 8, HD), F32),
        pltpu.VMEM((highs, quarter, HD), BF),
        pltpu.VMEM((highs, 8, HD), F32),
        pltpu.VMEM((quarter, HD), BF),
        pltpu.VMEM((8, HD), F32),
        pltpu.VMEM((quarter, HD), F32),
        pltpu.VMEM((4, quarter, HD), BF),
        pltpu.VMEM((4, quarter, HD), BF),
        DMA((2, 3)),
        DMA((2, 4)),
        DMA((2, highs)),
        DMA((2, highs)),
        DMA((3,)),
        DMA((4,)),
    ]


STATE_REFS = 16


def forward_kernel(*refs):
    (
        mixer_in, mixer_out, ffn_in, ffn_out, small, ups, own, cot, starts_row, starts_column, head_gain,
        mixer_w, merge_w, pair_w, down_w, gains, cots, hidden, low_rank, gate, cumulated, projected, mixed, gated,
        befores, decay, second, middle,
        mixer_v, merge_v, projected_v, updates, inputs, smalls, ups_got, state, partial, got, relayed, staged, line,
        own_send, own_arrive, far_send, arrive, small_send, small_arrive, ups_sem, inputs_send, inputs_arrive,
        cot_send, cot_arrive, sum_send, sum_arrive, spread_send, spread_arrive, saves,
    ) = refs[:-STATE_REFS]
    me = Place()
    zh, y, highs = lax.axis_index("zh"), lax.axis_index("y"), lax.axis_size("zh")
    units = down_w.shape[-1]
    width = own.shape[1]
    chunks = hidden.shape[0]
    first = ((zh * 2 + me.c) * 2 + y) * (chunks * CHUNK)
    greet_all(me)
    twin, side = {"c": 1 - me.c}, {"y": 1 - y}

    def own_source(part, k):
        if part < 5:
            at = pl.ds(pl.multiple_of(k * HD, HD), HD)
            return mixer_out.at[:, at] if part == 4 else mixer_in.at[part, :, at]
        at = pl.ds(pl.multiple_of(k * units, LANES), units)
        return ffn_out.at[:, at] if part == 7 else ffn_in.at[part - 5, :, at]

    def piece(at_zh, at_y, x, part, zl=slice(None)):
        if part < 4:
            return mixer_v.at[at_zh, zl, at_y, x, :, pl.ds(part * HD, HD)]
        if part == 4:
            return merge_v.at[at_zh, zl, at_y, x]
        if part < 7:
            return pair_w.at[at_zh, zl, at_y, x, :, pl.ds((part - 5) * units, units)]
        return down_w.at[at_zh, zl, at_y, x]

    firsts = [
        Placed(
            route_weights(me),
            lambda k, p=p: own_source(p, k),
            lambda zl, p=p: piece(zh, y, me.x, p, zl),
            lambda zl, p=p: piece(zh, y, me.c, p, zl),
            own_send.at[p],
            own_arrive.at[p],
        )
        for p in range(8)
    ]
    count = [0]
    sent = []

    def forward(at_zh, at_y, part, to, start=True):
        place = piece(at_zh, at_y, me.c, part)
        copy = copy_to(place, place, far_send.at[count[0]], arrive.at[at_zh, at_y, me.c, part], to)
        if start:
            copy.start()
        count[0] += 1
        sent.append(copy)
        return copy

    def arrived(at_zh, at_y, x, part):
        wait_for(piece(at_zh, at_y, x, part), arrive.at[at_zh, at_y, x, part])

    def own_high(part, start=True):
        firsts[part].wait_arrive()
        firsts[part].wait_local()
        return [forward(zh, y, part, {"zh": lax.rem(zh + k, highs)}, start) for k in range(1, highs)]

    def own_near(part):
        forward(zh, y, part, side)
        forward(zh, y, part, twin)

    def pass_high(part):
        for k in range(1, highs):
            at_zh = lax.rem(zh + k, highs)
            arrived(at_zh, y, me.c, part)
            forward(at_zh, y, part, side)
            forward(at_zh, y, part, twin)

    def pass_side(part):
        for k in range(highs):
            at_zh = lax.rem(zh + k, highs)
            arrived(at_zh, 1 - y, me.c, part)
            forward(at_zh, 1 - y, part, twin)

    def complete(part):
        for k in range(highs):
            at_zh = lax.rem(zh + k, highs)
            arrived(at_zh, y, 1 - me.c, part)
            arrived(at_zh, 1 - y, 1 - me.c, part)

    save_count = [0]
    saved = []

    def save(source, target):
        copy = pltpu.make_async_copy(source, target, saves.at[save_count[0]])
        copy.start()
        save_count[0] += 1
        saved.append(copy)

    order = (1, 2, 0, 3, 4)
    for part in order:
        firsts[part].start()
    move_small = Transfer(route_all(me), lambda _: small, lambda k: smalls.at[k], small_send, small_arrive)
    move_small.start()
    lend = copy_to(ups, ups_got, ups_sem.at[0], ups_sem.at[1], twin)
    lend.start()
    for part in order:
        own_high(part)
        if part in order[:2]:
            own_near(part)
    move_inputs = HalvesSpread(me, own, lambda k: inputs.at[k], inputs_send, inputs_arrive)
    move_cot = MemberSpread(me, cot, lambda k: cots.at[k], cot_send, cot_arrive)
    move_inputs.start()
    move_inputs.relay()
    pass_high(1)
    move_small.wait()
    lend.wait()
    owner_rows = smalls.shape[2]
    for n in range(smalls.shape[0]):
        gains[:, n * owner_rows : (n + 1) * owner_rows] = smalls[n].astype(F32)
    pass_high(2)
    for part in (5, 6, 7):
        firsts[part].start()
    for part in order[2:]:
        own_near(part)
    move_inputs.wait()

    up = jnp.where(me.c == me.zl, ups[...], ups_got[...])
    rank_up, bias = low(up[:16]), up[16:17]
    down = low(gains[...])
    lower = (
        lax.broadcasted_iota(jnp.int32, (CHUNK, CHUNK), 0)
        >= lax.broadcasted_iota(jnp.int32, (CHUNK, CHUNK), 1)
    ).astype(F32)

    def gates_step(n, _):
        x = inputs[n].astype(F32)
        scale = lax.rsqrt(jnp.mean(x * x, -1, keepdims=True) + EPSILON)
        h = low(x * scale * gains[0:1])
        hidden[n] = h
        z = low(dot_last(h, down))
        low_rank[n] = z
        a = dot(z[:, 2:18], rank_up) + bias
        gate[n] = a
        log_gate = (jnp.minimum(a, 0.0) - jnp.log1p(jnp.exp(-jnp.abs(a)))) / 16.0
        cumulated[n] = jnp.dot(
            lower, log_gate, precision=lax.Precision.HIGHEST, preferred_element_type=F32
        )
        return 0

    lax.fori_loop(0, chunks, gates_step, 0)

    def project(part):
        rows = hidden[...].reshape(chunks * CHUNK, width)
        block = mixer_v[:, :, :, :, :, pl.ds(part * HD, HD)].reshape(width, HD)
        result = dot(rows, block)
        if part == 0:
            result = result * HD ** (-0.5)
        projected_v[part] = result.reshape(chunks, CHUNK, HD)
        save(projected_v.at[part], projected.at[part])

    pass_side(1)
    pass_side(2)
    complete(1)
    project(1)
    complete(2)
    project(2)

    state[...] = jnp.zeros_like(state)
    decay[...] = jnp.ones_like(decay)

    def masks(n):
        return keyed_mask(first + n * CHUNK, starts_row, starts_column)

    def local_step(n, _):
        _, _, keep, last = masks(n)
        b = cumulated[n]
        end = b[CHUNK - 1 :]
        kc = low(projected_v[1, n] * jnp.exp(end - b) * last)
        update = dot_rows(low(projected_v[2, n]), kc)
        updates[n] = update
        carry = keep * jnp.exp(end)
        state[...] = carry * state[...] + update
        decay[...] = decay[...] * carry
        return 0

    lax.fori_loop(0, chunks, local_step, 0)
    states = StatePass(False, state, decay, state, *refs[-STATE_REFS:])
    states.begin()
    pass_high(0)
    states.combine()
    held = [copy for part in (5, 6, 7) for copy in own_high(part, False)]

    @pl.when(me.zl == 1)
    def _():
        for copy in held:
            copy.start()

    pass_high(3)
    pass_side(0)
    complete(0)
    project(0)
    pass_side(3)

    def inner_step(n, _):
        pair, _, _, _ = masks(n)
        b = cumulated[n]
        mid = b[CHUNK // 2 - 1 : CHUNK // 2]
        qh = low(projected_v[0, n] * jnp.exp(b - mid))
        kh = low(projected_v[1, n] * jnp.exp(mid - b))
        scores = low(jnp.where(pair, dot_last(qh, kh), 0.0))
        mixed[n] = dot(scores, low(projected_v[2, n]))
        return 0

    lax.fori_loop(0, chunks, inner_step, 0)
    states.spread()

    @pl.when(me.zl == 0)
    def _():
        for copy in held:
            copy.start()

    pass_high(4)
    for part in (5, 6, 7):
        own_near(part)
    complete(3)
    project(3)
    states.finish()

    def outer_step(n, _):
        _, visible, keep, _ = masks(n)
        b = cumulated[n]
        before = state[...]
        qd = low(projected_v[0, n] * jnp.exp(b) * visible)
        out = mixed[n] + dot_last(qd, low(before))
        mixed[n] = out
        befores[n] = low(before)
        state[...] = keep * jnp.exp(b[CHUNK - 1 :]) * before + updates[n]
        scale = lax.rsqrt(jnp.mean(out * out, -1, keepdims=True) + HEAD_FLOOR)
        u = projected_v[3, n]
        gated[n] = low(out * scale * head_gain[...] * (u * jax.nn.sigmoid(u)))
        return 0

    lax.fori_loop(0, chunks, outer_step, 0)
    pass_side(4)
    complete(4)

    def merge_step(n, _):
        partial[n] = low(dot_last(gated[n], merge_v[...].reshape(width, HD)))
        return 0

    lax.fori_loop(0, chunks, merge_step, 0)

    steps = sum_send.shape[0]
    rows = own.shape[0] // steps

    def rows_of(ref, k, n):
        return ref.at[k, pl.ds(n * rows, rows)]

    sums = [
        OwnersSum(
            me,
            lambda k, n=n: rows_of(partial, k, n),
            lambda k, n=n: rows_of(got, k, n),
            lambda k, n=n: rows_of(relayed, k, n),
            lambda k, n=n: rows_of(staged, k, n),
            sum_send.at[n],
            sum_arrive.at[n],
        )
        for n in range(steps)
    ]
    spreads = [
        MemberSpread(
            me,
            line.at[pl.ds(n * rows, rows)],
            lambda k, n=n: rows_of(second, k, n),
            spread_send.at[n],
            spread_arrive.at[n],
        )
        for n in range(steps)
    ]
    for transfer in sums:
        transfer.start()
    for transfer in sums:
        transfer.relay()
    pass_high(5)
    for n in range(steps):
        at = pl.ds(n * rows, rows)
        total = own[at].astype(F32) + sums[n].total()
        middle[at] = total
        scale = lax.rsqrt(jnp.mean(total * total, -1, keepdims=True) + EPSILON)
        line[at] = low(total * scale * gains[1:2])
        spreads[n].start()
        if n:
            spreads[n - 1].relay()
    spreads[steps - 1].relay()
    pass_high(6)
    pass_side(5)
    move_cot.start()
    save(mixer_v, mixer_w)
    save(merge_v, merge_w)
    pass_high(7)
    move_cot.relay()
    for part in (6, 7):
        pass_side(part)
    for part in (5, 6, 7):
        complete(part)
    for transfer in sums:
        transfer.wait_sent()
    for transfer in spreads:
        transfer.wait()
    states.wait_sent()
    move_cot.wait()
    for transfer in firsts:
        transfer.wait_sent()
    for copy in sent:
        copy.wait_send()
    for copy in saved:
        copy.wait()


def starts_arrays(starts):
    starts = jnp.pad(starts, (0, LANES - starts.shape[0]), constant_values=jnp.int32(1 << 30))
    return jnp.broadcast_to(starts[None], (8, LANES)), jnp.broadcast_to(starts[:16, None], (16, LANES))


def forward(mixer_in, mixer_out, ffn_in, ffn_out, small, ups, own, cot, starts, head_gain):
    highs = lax.axis_size("zh")
    chips = highs * 8
    rows, half, width = small.shape[1], own.shape[0], own.shape[1]
    units = ffn_out.shape[1] // 2
    chunks = TEAM * half // CHUNK

    def shape(*dims, kind=BF):
        return jax.ShapeDtypeStruct(dims, kind)

    shapes = [
        (shape(highs, 2, 2, 2, rows, 4 * HD), ANY),
        (shape(highs, 2, 2, 2, rows, HD), ANY),
        (shape(highs, 2, 2, 2, rows, 2 * units), ANY),
        (shape(highs, 2, 2, 2, rows, units), ANY),
        (shape(RANKS, width, kind=F32), VMEM),
        (shape(TEAM, half, width), ANY),
        (shape(chunks, CHUNK, width), VMEM),
        (shape(chunks, CHUNK, RANKS), VMEM),
        (shape(chunks, CHUNK, HD, kind=F32), VMEM),
        (shape(chunks, CHUNK, HD, kind=F32), VMEM),
        (shape(4, chunks, CHUNK, HD, kind=F32), ANY),
        (shape(chunks, CHUNK, HD, kind=F32), VMEM),
        (shape(chunks, CHUNK, HD), VMEM),
        (shape(chunks, HD, HD), VMEM),
        (shape(8, HD, kind=F32), VMEM),
        (shape(TEAM, half, width), VMEM),
        (shape(half, width, kind=F32), VMEM),
    ]
    arrays = [mixer_in, mixer_out, ffn_in, ffn_out, small, ups, own, cot, *starts_arrays(starts), head_gain]
    scratch = [
        shapes[0][0],
        shapes[1][0],
        shapes[10][0],
        shape(chunks, HD, HD, kind=F32),
        shape(TEAM, half, width),
        shape(chips, RANKS, rows),
        shape(*ups.shape, kind=F32),
        shape(HD, HD, kind=F32),
        shape(TEAM, half, width),
        shape(3, half, width),
        shape(2, half, width),
        shape(2, half, width),
        shape(half, width),
    ]
    used = arrays + scratch + [a for a, place in shapes if place is VMEM]
    size = sum(a.size * a.dtype.itemsize for a in used)
    forwards = 8 * ((highs - 1) + highs + 2 * highs)
    sems = [
        (8, 2), (8, 2), (forwards,), (highs, 2, 2, 8), (chips,), (chips,), (2,), (5,), (4,), (3,), (4,),
        (STEPS, 6), (STEPS, 5), (STEPS, 3), (STEPS, 4), (7,),
    ]
    return pl.pallas_call(
        forward_kernel,
        out_shape=[a for a, _ in shapes],
        in_specs=[VMEM] * len(arrays),
        out_specs=[place for _, place in shapes],
        scratch_shapes=[pltpu.VMEM(a.shape, a.dtype) for a in scratch]
        + [DMA(n) for n in sems]
        + state_pass_scratch(highs),
        compiler_params=pltpu.CompilerParams(
            collective_id=0, has_side_effects=True, vmem_limit_bytes=min(size + (14 << 20), 62 << 20)
        ),
        name="forward",
    )(*arrays)


STEPS = 4


CROSS = [(0, 1), (1, 0)]


TILE = 256


def turn_rows(me, source, target):
    zh, y, highs = lax.axis_index("zh"), lax.axis_index("y"), lax.axis_size("zh")
    chunks, _, width = source.shape
    owners = highs * 8
    rows = width // owners
    for n in range(chunks):
        turned = source[n].T
        for chip in range(owners):
            at_zh, zl, at_y, x = chip // 8, chip // 4 % 2, chip // 2 % 2, chip % 2
            x_place = me.c if x == 1 else 1 - me.c
            y_place = y if at_y == 1 else 1 - y
            place = ((x_place * 2 + y_place) * highs + lax.rem(at_zh - zh + highs, highs)) * 2 + zl
            at = pl.ds(pl.multiple_of(place * rows, rows), rows)
            target[at, n * CHUNK : (n + 1) * CHUNK] = turned[chip * rows : (chip + 1) * rows]


def feed_forward_kernel(
    hidden, cots, pair_w, down_w,
    forth, back, pair_away, pair_keep, down_part,
    forth_v, back_v, away_v, keep_v, pair_v, down_v, act, grad_gate, grad_up, left_hidden, left_cots, tiles, tiles_got, down_away, down_keep,
    loads, tile_send, tile_arrive, side_send, side_arrive, saves,
):
    me = Place()
    y = lax.axis_index("y")
    chunks, _, width = hidden.shape
    units = down_w.shape[1]
    tokens = chunks * CHUNK
    barrier = pltpu.get_barrier_semaphore()
    for to in ({"c": 1 - me.c}, {"y": 1 - y}):
        pl.semaphore_signal(barrier, inc=1, device_id=to, device_id_type=MESH)
    spans = [(n * TILE, min(TILE, units - n * TILE)) for n in range(-(-units // TILE))]

    def load(kind, n):
        start, size = spans[n]
        if kind == 2:
            return pltpu.make_async_copy(
                down_w.at[:, pl.ds(start, size)], down_v.at[:, pl.ds(start, size)], loads.at[2, n]
            )
        at = pl.ds(kind * units + start, size)
        return pltpu.make_async_copy(pair_w.at[:, at], pair_v.at[:, at], loads.at[kind, n])

    for n in range(len(spans)):
        for kind in range(3):
            load(kind, n).start()
    turn_rows(me, cots, left_cots)

    def units_step(start, size):
        at = pl.ds(start, size)
        rows = hidden[...].reshape(tokens, width)
        a = dot(rows, pair_v[:, at])
        b = dot(rows, pair_v[:, pl.ds(units + start, size)])
        da = dot(cots[...].reshape(tokens, width), down_v[:, at])
        sig = jax.nn.sigmoid(a)
        silu = a * sig
        act[:, at] = low(silu * b)
        grad_gate[:, at] = low(da * b * sig * (1.0 + a * (1.0 - sig)))
        grad_up[:, at] = low(da * silu)

    whole = units // TILE
    pl.semaphore_wait(barrier, 2)
    half = width // 2
    quarter = half // 2
    count = len(spans)

    def move(n):
        return copy_to(
            tiles.at[lax.rem(n, count)], tiles_got.at[n], tile_send.at[n], tile_arrive.at[n], {"c": 1 - me.c}
        )

    def send_tile(left, right, n, start, size):
        block = low(dot(left[pl.ds(0, half)], right[:, pl.ds(start, size)]))
        if size == TILE:
            tiles[lax.rem(n, count)] = block
        else:
            tiles[lax.rem(n, count), :, pl.ds(0, size)] = block
        move(n).start()

    def add_tile(left, right, n, start, size, away, keep, base):
        block = dot(left[pl.ds(half, half)], right[:, pl.ds(start, size)])
        move(n).wait_recv()
        block = low(block + tiles_got[n, :, pl.ds(0, size)].astype(F32))
        away[:, pl.ds(base + start, size)] = block[:quarter]
        keep[:, pl.ds(base + start, size)] = block[quarter:]

    def weight_grad(part, left, right, away, keep, base):
        first = part * count

        def send_step(n, _):
            if part:
                move(first + n - count).wait_send()
            send_tile(left, right, first + n, pl.multiple_of(n * TILE, TILE), TILE)
            return 0

        def add_step(n, _):
            add_tile(left, right, first + n, pl.multiple_of(n * TILE, TILE), TILE, away, keep, base)
            return 0

        lax.fori_loop(0, whole, send_step, 0)
        if whole < count:
            if part:
                move(first + whole - count).wait_send()
            send_tile(left, right, first + whole, *spans[whole])
        lax.fori_loop(0, whole, add_step, 0)
        if whole < count:
            add_tile(left, right, first + whole, *spans[whole], away, keep, base)

    def side_move(n, start, size):
        at = pl.ds(start, size)
        return copy_to(down_away.at[:, at], down_part.at[:, at], side_send.at[n], side_arrive.at[n], {"y": 1 - y})

    def down_tile(n, start, size):
        add_tile(left_cots, act, n, start, size, down_away, down_keep, 0)
        side_move(n, start, size).start()

    def tile_step(n, _):
        for kind in range(3):
            start = n * TILE if kind == 2 else kind * units + n * TILE
            at = pl.ds(pl.multiple_of(start, LANES), TILE)
            source, target = (down_w, down_v) if kind == 2 else (pair_w, pair_v)
            pltpu.make_async_copy(source.at[:, at], target.at[:, at], loads.at[kind, n]).wait()
        start = pl.multiple_of(n * TILE, TILE)
        units_step(start, TILE)
        send_tile(left_cots, act, n, start, TILE)

        @pl.when(n > 0)
        def _():
            down_tile(n - 1, pl.multiple_of((n - 1) * TILE, TILE), TILE)

        return 0

    lax.fori_loop(0, whole, tile_step, 0)
    if whole < count:
        for kind in range(3):
            load(kind, whole).wait()
        units_step(*spans[whole])
        send_tile(left_cots, act, whole, *spans[whole])
    down_tile(whole - 1, *spans[whole - 1])
    if whole < count:
        down_tile(whole, *spans[whole])

    def back_step(n, _):
        at = pl.ds(pl.multiple_of(n * TILE, TILE), TILE)
        block = dot_last(grad_gate[...], pair_v[at, pl.ds(0, units)])
        block = low(block + dot_last(grad_up[...], pair_v[at, pl.ds(units, units)]))
        ahead = low(dot_last(act[...], down_v[at]))
        for k in range(chunks):
            back_v[k, :, at] = block[k * CHUNK : (k + 1) * CHUNK]
            forth_v[k, :, at] = ahead[k * CHUNK : (k + 1) * CHUNK]
        return 0

    lax.fori_loop(0, width // TILE, back_step, 0)
    saved = [
        pltpu.make_async_copy(source, target, saves.at[n])
        for n, (source, target) in enumerate(
            ((back_v, back), (forth_v, forth), (away_v, pair_away), (keep_v, pair_keep))
        )
    ]
    for copy in saved[:2]:
        copy.start()
    turn_rows(me, hidden, left_hidden)
    weight_grad(1, left_hidden, grad_gate, away_v, keep_v, 0)
    weight_grad(2, left_hidden, grad_up, away_v, keep_v, units)
    for copy in saved[2:]:
        copy.start()
    for n in range(2 * count, 3 * count):
        move(n).wait_send()
    for n, span in enumerate(spans):
        side_move(n, *span).wait()
    add_rows(down_part, down_keep, down_part)
    for copy in saved:
        copy.wait()


def feed_forward(hidden, cots, pair_w, down_w):
    chunks, _, width = hidden.shape
    units = down_w.shape[1]
    tokens, half = chunks * CHUNK, width // 2
    count = -(-units // TILE)

    def shape(*dims, kind=BF):
        return jax.ShapeDtypeStruct(dims, kind)

    shapes = [
        shape(*hidden.shape),
        shape(*hidden.shape),
        shape(half // 2, 2 * units),
        shape(half // 2, 2 * units),
        shape(half // 2, units),
    ]
    scratch = shapes[:4] + [
        shape(width, 2 * units),
        shape(width, units),
        shape(tokens, units),
        shape(tokens, units),
        shape(tokens, units),
        shape(width, tokens),
        shape(width, tokens),
        shape(count, half, TILE),
        shape(3 * count, half, TILE),
        shape(half // 2, units),
        shape(half // 2, units),
    ]
    size = sum(a.size * a.dtype.itemsize for a in [hidden, cots] + shapes[4:] + scratch)
    sems = [(3, count), (3 * count,), (3 * count,), (count,), (count,), (4,)]
    return pl.pallas_call(
        feed_forward_kernel,
        out_shape=shapes,
        in_specs=[VMEM, VMEM, ANY, ANY],
        out_specs=[ANY] * 4 + [VMEM],
        scratch_shapes=[pltpu.VMEM(a.shape, a.dtype) for a in scratch] + [DMA(n) for n in sems],
        compiler_params=pltpu.CompilerParams(
            collective_id=5, has_side_effects=True, vmem_limit_bytes=min(size + (10 << 20), 63 << 20)
        ),
        name="feed_forward",
    )(hidden, cots, pair_w, down_w)


def add_rows(out, *parts):
    def step(n, _):
        at = pl.ds(n * 16, 16)
        total = parts[0][at].astype(F32)
        for part in parts[1:]:
            total = total + part[at].astype(F32)
        out[at] = low(total)
        return 0

    lax.fori_loop(0, out.shape[0] // 16, step, 0)


def backward_kernel(*refs):
    (
        back, forth, cot, middle, gain, pair_away, pair_keep_far, downs, merge_far, gated, projected_far, mixed_far,
        cumulated_far, gate_far, befores_far, decay, low_rank, up_pad, head_gain, hidden, starts_row, starts_column,
        grad_middle, gain_grad, proj, ranks, heads, early, gate_sum, up_sum, down_sum, left_hidden,
        result, got, relayed, staged, line, got2, relayed2, staged2, line2, branch, left_branch, douts, tiles, tiles_got,
        pair_keep, merge_w, projected, mixed, cumulated, gate, befores, pair_side, gate_got, up_got, down_got, early_away, early_keep, up_grad, state,
        send, arrive, send2, arrive2, side_send, side_arrive, high_send, high_arrive, tile_send, tile_arrive,
        send3, arrive3, twin_send, twin_arrive, here, loads,
    ) = refs[:-STATE_REFS]
    me = Place()
    zh, y, highs = lax.axis_index("zh"), lax.axis_index("y"), lax.axis_size("zh")
    chunks, _, width = hidden.shape
    units = downs.shape[-1]
    first = ((zh * 2 + me.c) * 2 + y) * (chunks * CHUNK)
    greet_all(me)
    loaded = [
        pltpu.make_async_copy(source, target, loads.at[n])
        for n, (source, target) in enumerate(
            (
                (pair_keep_far, pair_keep), (merge_far, merge_w), (mixed_far, mixed), (projected_far, projected),
                (cumulated_far, cumulated), (befores_far, befores), (gate_far, gate),
            )
        )
    ]
    for copy in loaded:
        copy.start()

    def columns(ref, part):
        return ref.at[:, :, :, pl.ds((part - 1) * units, units)]

    def source(part):
        return downs if part == 0 else columns(pair_side, part)

    sides = [
        copy_to(columns(pair_away, p), columns(pair_side, p), side_send.at[p], side_arrive.at[p], {"y": 1 - y})
        for p in (1, 2)
    ]
    high_got, high_sum = (down_got, gate_got, up_got), (down_sum, gate_sum, up_sum)
    highs_moves = [
        [
            copy_to(
                source(p).at[k],
                high_got[p].at[k - 1],
                high_send.at[p, k],
                high_arrive.at[p, k],
                {"zh": lax.rem(zh + k, highs)},
            )
            for k in range(1, highs)
        ]
        for p in range(3)
    ]

    def high_start(part):
        if part:
            sides[part - 1].wait()
            mine, there = columns(pair_keep, part), columns(pair_side, part)
            for k in range(highs):
                for m in range(2):
                    add_rows(there.at[k, m], mine.at[k, m], there.at[k, m])
        for move in highs_moves[part]:
            move.start()

    def high_add(part):
        there, out = high_got[part], high_sum[part]
        for k in range(1, highs):
            wait_for(there.at[k - 1], high_arrive.at[part, k])
        for m in range(2):
            add_rows(out.at[m], source(part).at[0, m], *(there.at[k - 1, m] for k in range(1, highs)))

    for move in sides:
        move.start()
    high_start(0)

    steps = send.shape[0]
    rows = cot.shape[0] // steps

    def part(ref, k, n):
        return ref.at[k, pl.ds(n * rows, rows)]

    sums = [
        MemberSum(
            me,
            lambda k, n=n: part(back, k, n),
            lambda k, n=n: part(got, k, n),
            lambda k, n=n: part(relayed, k, n),
            lambda k, n=n: part(staged, k, n),
            send.at[n],
            arrive.at[n],
            two="zl",
        )
        for n in range(steps)
    ]
    spreads = [
        HalvesSpread(
            me,
            line.at[pl.ds(n * rows, rows)],
            lambda k, n=n: part(branch, k, n),
            send2.at[n],
            arrive2.at[n],
        )
        for n in range(steps)
    ]
    forth_sums = [
        MemberSum(
            me,
            lambda k, n=n: part(forth, k, n),
            lambda k, n=n: part(got2, k, n),
            lambda k, n=n: part(relayed2, k, n),
            lambda k, n=n: part(staged2, k, n),
            send3.at[n],
            arrive3.at[n],
        )
        for n in range(steps)
    ]

    def twin_copy(n):
        return copy_to(
            line2.at[pl.ds(n * rows, rows)],
            part(result, me.c, n),
            twin_send.at[n],
            twin_arrive.at[n],
            {"c": 1 - me.c},
        )

    def own_copy(n):
        return pltpu.make_async_copy(line2.at[pl.ds(n * rows, rows)], part(result, me.c, n), here.at[n])

    for transfer in sums:
        transfer.start()

    turn_rows(me, hidden, left_hidden)
    for transfer in sums:
        transfer.relay()
    for n in range(steps):
        at = pl.ds(n * rows, rows)
        mid = middle[at]
        scale = lax.rsqrt(jnp.mean(mid * mid, -1, keepdims=True) + EPSILON)
        normed = mid * scale
        total = sums[n].total()
        gsum = jnp.sum(total * normed, axis=0, keepdims=True)
        gain_grad[...] = gsum if n == 0 else gain_grad[...] + gsum
        scaled = total * gain[...]
        out = cot[at].astype(F32) + scale * (
            scaled - normed * jnp.mean(scaled * normed, -1, keepdims=True)
        )
        grad_middle[at] = out
        line[at] = low(out)
        spreads[n].start()
        if n:
            spreads[n - 1].relay()
        if n == 2:
            loaded[0].wait()
            high_start(1)
    spreads[steps - 1].relay()
    for transfer in spreads:
        transfer.wait()
    for transfer in forth_sums:
        transfer.start()

    for copy in loaded[1:]:
        copy.wait()
    heads[...] = jnp.zeros_like(heads)

    def head_step(n, _):
        grad = dot(branch[n], merge_w[...])
        out = mixed[n]
        scale = lax.rsqrt(jnp.mean(out * out, -1, keepdims=True) + HEAD_FLOOR)
        normed = out * scale
        u = projected[3, n]
        sig = jax.nn.sigmoid(u)
        dn = grad * (u * sig)
        proj[n, :, 3 * HD :] = low(grad * normed * head_gain[...] * sig * (1.0 + u * (1.0 - sig)))
        heads[17:18] = heads[17:18] + jnp.sum(dn * normed, axis=0, keepdims=True)
        scaled = dn * head_gain[...]
        douts[n] = low(scale * (scaled - normed * jnp.mean(scaled * normed, -1, keepdims=True)))
        return 0

    lax.fori_loop(0, chunks, head_step, 0)

    def masks(n):
        return keyed_mask(first + n * CHUNK, starts_row, starts_column)

    def query_rows(n, visible):
        return low(projected[0, n] * jnp.exp(cumulated[n]) * visible)

    state[...] = jnp.zeros_like(state)

    def local_step(i, _):
        n = chunks - 1 - i
        _, visible, keep, _ = masks(n)
        carry = keep * jnp.exp(cumulated[n, CHUNK - 1 :])
        state[...] = carry * state[...] + dot_rows(douts[n], query_rows(n, visible))
        return 0

    lax.fori_loop(0, chunks, local_step, 0)
    states = StatePass(True, state, decay, state, *refs[-STATE_REFS:])
    states.begin()

    turn_rows(me, branch, left_branch)
    half = width // 2
    quarter = half // 2

    def tile_move(n):
        return copy_to(tiles.at[n], tiles_got.at[n], tile_send.at[n], tile_arrive.at[n], {"c": 1 - me.c})

    def right_tile(kind, n):
        if kind == 0:
            return gated[...].reshape(chunks * CHUNK, HD)[:, n * TILE : (n + 1) * TILE]
        at = 3 * HD + n * TILE
        return proj[...].reshape(chunks * CHUNK, 4 * HD)[:, at : at + TILE]

    lefts = left_branch, left_hidden
    for kind in range(2):
        for n in range(HD // TILE):
            tile = kind * (HD // TILE) + n
            tiles[tile] = low(dot(lefts[kind][pl.ds(0, half)], right_tile(kind, n)))
            tile_move(tile).start()
    states.combine()
    high_start(2)
    for kind in range(2):
        for n in range(HD // TILE):
            tile = kind * (HD // TILE) + n
            block = dot(lefts[kind][pl.ds(half, half)], right_tile(kind, n))
            tile_move(tile).wait_recv()
            block = low(block + tiles_got[tile].astype(F32))
            at = slice(tile * TILE, (tile + 1) * TILE)
            early_away[:, at] = block[:quarter]
            early_keep[:, at] = block[quarter:]
    early_move = copy_to(early_away, early, side_send.at[0], side_arrive.at[0], {"y": 1 - y})
    early_move.start()
    states.spread()
    for transfer in forth_sums:
        transfer.relay()
    states.finish()

    upper = (
        lax.broadcasted_iota(jnp.int32, (CHUNK, CHUNK), 0)
        <= lax.broadcasted_iota(jnp.int32, (CHUNK, CHUNK), 1)
    ).astype(F32)
    up_grad[...] = jnp.zeros_like(up_grad)

    def chunk_step(i, _):
        n = chunks - 1 - i
        pair, visible, keep, last = masks(n)
        b = cumulated[n]
        mid, end = b[CHUNK // 2 - 1 : CHUNK // 2], b[CHUNK - 1 :]
        q, k, v = projected[0, n], projected[1, n], low(projected[2, n])
        do = douts[n]
        eq, ek, el = jnp.exp(b - mid), jnp.exp(mid - b), jnp.exp(end - b) * last
        qh, kh, kc = low(q * eq), low(k * ek), k * el
        scores = low(jnp.where(pair, dot_last(qh, kh), 0.0))
        gs = low(jnp.where(pair, dot_last(do, v), 0.0))
        ds = low(state[...])
        proj[n, :, 2 * HD : 3 * HD] = low(dot_rows(scores, do) + dot_last(low(kc), ds))
        dq = dot(gs, kh) * eq + dot(do, low(befores[n])) * (jnp.exp(b) * visible)
        gkc = dot(v, ds)
        dk = dot_rows(gs, qh) * ek + gkc * el
        proj[n, :, :HD] = low(dq * HD ** (-0.5))
        proj[n, :, HD : 2 * HD] = low(dk)
        carry = keep * jnp.exp(end)
        extra = jnp.sum(gkc * kc, axis=0, keepdims=True)
        extra = extra + carry * jnp.sum(befores[n] * state[...], axis=0, keepdims=True)
        dlog = extra + jnp.dot(
            upper, dq * q - dk * k, precision=lax.Precision.HIGHEST, preferred_element_type=F32
        )
        state[...] = carry * state[...] + dot_rows(do, query_rows(n, visible))
        da = dlog * jax.nn.sigmoid(-gate[n]) / 16.0
        heads[16:17] = heads[16:17] + jnp.sum(da, axis=0, keepdims=True)
        dar = low(da)
        up_grad[...] = up_grad[...] + dot_rows(low_rank[n], dar)
        ranks[n] = low(dot_last(dar, up_pad[...]))
        return 0

    lax.fori_loop(0, chunks, chunk_step, 0)
    heads[0:16] = up_grad[2:18]
    for n in range(steps):
        at = pl.ds(n * rows, rows)
        line2[at] = low(middle[at] + forth_sums[n].total())
        twin_copy(n).start()
        own_copy(n).start()
    early_move.wait()
    add_rows(early, early_keep, early)
    for p in range(3):
        high_add(p)
    for n in range(steps):
        twin_copy(n).wait()
        own_copy(n).wait()
    for transfer in forth_sums:
        transfer.wait_sent()
    for group in highs_moves:
        for move in group:
            move.wait_send()
    for transfer in sums:
        transfer.wait_sent()
    for tile in range(tiles.shape[0]):
        tile_move(tile).wait_send()
    states.wait_sent()


def backward(
    back, forth, cot, middle, gain, pair, downs, merge_w, gated, projected, mixed, cumulated, gate, befores, decay,
    low_rank, up_pad, head_gain, hidden, starts,
):
    highs, members, owner_rows, units = downs.shape
    rows, width = cot.shape
    chunks = hidden.shape[0]

    def shape(*dims, kind=BF):
        return jax.ShapeDtypeStruct(dims, kind)

    arrays = [
        back, forth, cot, middle, gain, *pair, downs, merge_w, gated, projected, mixed, cumulated, gate, befores, decay,
        low_rank, up_pad, head_gain, hidden, *starts_arrays(starts),
    ]
    away = {5, 6, 8, 10, 11, 12, 13, 14}
    quarter = width // 4
    shapes = [
        shape(rows, width, kind=F32),
        shape(1, width, kind=F32),
        shape(chunks, CHUNK, 4 * HD),
        shape(chunks, CHUNK, LANES),
        shape(24, HD, kind=F32),
        shape(quarter, 2 * HD),
        shape(members, owner_rows, units),
        shape(members, owner_rows, units),
        shape(members, owner_rows, units),
        shape(width, chunks * CHUNK),
        shape(2, rows, width),
    ]
    tiles = 2 * HD // TILE
    scratch = [
        shape(2, rows, width),
        shape(1, rows, width),
        shape(1, rows, width),
        shape(rows, width),
        shape(2, rows, width),
        shape(1, rows, width),
        shape(1, rows, width),
        shape(rows, width),
        shape(TEAM, rows, width),
        shape(width, chunks * CHUNK),
        shape(chunks, CHUNK, HD),
        shape(tiles, width // 2, TILE),
        shape(tiles, width // 2, TILE),
        *(shape(*arrays[n].shape, kind=arrays[n].dtype) for n in (6, 8, 10, 11, 12, 13, 14)),
        shape(highs, members, owner_rows, 2 * units),
        shape(highs - 1, members, owner_rows, units),
        shape(highs - 1, members, owner_rows, units),
        shape(highs - 1, members, owner_rows, units),
        shape(quarter, 2 * HD),
        shape(quarter, 2 * HD),
        shape(RANKS, HD, kind=F32),
        shape(HD, HD, kind=F32),
    ]
    used = [a for n, a in enumerate(arrays) if n not in away] + shapes + scratch
    size = sum(a.size * a.dtype.itemsize for a in used)
    sems = [
        (STEPS, 3), (STEPS, 3), (STEPS, 5), (STEPS, 4), (3,), (3,), (3, highs), (3, highs), (tiles,), (tiles,),
        (STEPS, 3), (STEPS, 3), (STEPS,), (STEPS,), (STEPS,), (7,),
    ]
    return pl.pallas_call(
        backward_kernel,
        out_shape=shapes,
        in_specs=[ANY if n in away else VMEM for n in range(len(arrays))],
        out_specs=[VMEM] * len(shapes),
        scratch_shapes=[pltpu.VMEM(a.shape, a.dtype) for a in scratch]
        + [DMA(n) for n in sems]
        + state_pass_scratch(highs),
        compiler_params=pltpu.CompilerParams(
            collective_id=3, has_side_effects=True, vmem_limit_bytes=min(size + (14 << 20), 62 << 20)
        ),
        name="backward",
    )(*arrays)


def closing_kernel(*refs):
    (
        proj, ranks, mixer_far, left, own, grad_middle, gain, down, gain_two_grad, heads, early, ups, gates, downs,
        out, mixer_grad, merge_grad, pair_grad, down_grad, wide_out, heads_out, gains_out,
        mixer_w, partial, got, relayed, staged, line, tiles, tiles_got, late_away, late_keep, late_side,
        late_got, early_got, late_sum, early_sum, late_home, early_home, ups_home, gate_home, down_home,
        wide, wide_got, heads_got, heads_sum, wide_twin, gain_grad, rank_grad,
        send, arrive, twin_send, twin_arrive, here, tile_send, tile_arrive, side_send, side_arrive,
        high_send, high_arrive, home_send, home_arrive,
        wide_send, wide_arrive, heads_send, heads_arrive, near, out_send, out_arrive, gain_send, gain_arrive, loads,
    ) = refs
    me = Place()
    zh, y, highs = lax.axis_index("zh"), lax.axis_index("y"), lax.axis_size("zh")
    load = pltpu.make_async_copy(mixer_far, mixer_w, loads.at[0])
    load.start()
    greet_all(me)
    steps = send.shape[0]
    rows, width = own.shape[0] // steps, own.shape[1]
    chunks = proj.shape[0]
    twin = {"c": 1 - me.c}

    def high_copies(kind, source, target):
        return [
            copy_to(
                source.at[k],
                target.at[k - 1],
                high_send.at[kind, k],
                high_arrive.at[kind, k],
                {"zh": lax.rem(zh + k, highs)},
            )
            for k in range(1, highs)
        ]

    def side_copy(kind, source, target):
        return copy_to(source, target, side_send.at[kind], side_arrive.at[kind], {"y": 1 - y})

    def home(kind, source, target):
        return Transfer(
            route_weights_home(me),
            lambda k: source.at[k],
            lambda k: target.at[k],
            home_send.at[kind],
            home_arrive.at[kind],
        )

    late_moves = [side_copy(j, late_away.at[j], late_side.at[j]) for j in range(3)]
    high_moves = [high_copies(j, late_side.at[j], late_got.at[j]) for j in range(3)]
    high_moves += [high_copies(3, early, early_got)]
    homes = [home(j, late_sum.at[j], late_home.at[j]) for j in range(3)]
    homes += [home(3, early_sum, early_home), home(4, ups, ups_home)]
    homes += [home(5, gates, gate_home), home(6, downs, down_home)]
    group_out, group_arrive = [], []
    for n in range(highs):
        for f in range(4):
            to_zh, to_y, to_c = lax.rem(zh + n, highs), flip(y, f & 2), flip(me.c, f & 1)
            to = {"zh": to_zh, "y": to_y, "c": to_c}
            group_out.append((0, (zh * 2 + y) * 2 + me.c, to, n + f == 0))
            group_arrive.append(((to_zh * 2 + to_y) * 2 + to_c, n + f == 0))
    heads_move = Transfer(
        (group_out, group_arrive), lambda _: heads, lambda k: heads_got.at[k], heads_send, heads_arrive
    )
    heads_move.start()

    for move in high_moves[3]:
        move.start()

    half = width // 2
    quarter = half // 2
    owner_rows = early.shape[2]

    def tile_move(n):
        return copy_to(tiles.at[n], tiles_got.at[n], tile_send.at[n], tile_arrive.at[n], twin)

    def right_tile(n):
        return proj[:, :, pl.ds(pl.multiple_of(n * TILE, TILE), TILE)].reshape(chunks * CHUNK, TILE)

    def tile_step(n, _):
        tiles[n] = low(dot(left[pl.ds(0, half)], right_tile(n)))
        tile_move(n).start()
        return 0

    lax.fori_loop(0, 3 * HD // TILE, tile_step, 0)

    for n in range(chunks):
        partial[n, :, width:] = ranks[n]

    def hidden_step(n, _):
        at = pl.ds(pl.multiple_of(n * TILE, TILE), TILE)
        block = low(dot_last(proj[...].reshape(chunks * CHUNK, 4 * HD), mixer_w[at]))
        for k in range(chunks):
            partial[k, :, at] = block[k * CHUNK : (k + 1) * CHUNK]
        return 0

    load.wait()
    lax.fori_loop(0, width // TILE, hidden_step, 0)

    def part(ref, k, n):
        return ref.at[k, pl.ds(n * rows, rows)]

    sums = [
        OwnersSum(
            me,
            lambda k, n=n: part(partial, k, n),
            lambda k, n=n: part(got, k, n),
            lambda k, n=n: part(relayed, k, n),
            lambda k, n=n: part(staged, k, n),
            send.at[n],
            arrive.at[n],
        )
        for n in range(steps)
    ]
    for transfer in sums:
        transfer.start()

    for j in range(3):
        for i in range(HD // TILE):
            n = j * (HD // TILE) + i
            block = dot(left[pl.ds(half, half)], right_tile(n))
            tile_move(n).wait_recv()
            block = low(block + tiles_got[n].astype(F32))
            columns = slice(i * TILE, (i + 1) * TILE)
            for k in range(highs):
                for m in range(2):
                    at = (k * 2 + m) * owner_rows
                    late_away[j, k, m, :, columns] = block[at : at + owner_rows]
                    late_keep[j, k, m, :, columns] = block[quarter + at : quarter + at + owner_rows]
        late_moves[j].start()
    for n in (6, 5, 4):
        homes[n].start()

    def side_add(move, keep, there):
        move.wait()
        for k in range(highs):
            for m in range(2):
                add_rows(there.at[k, m], keep.at[k, m], there.at[k, m])

    for transfer in sums:
        transfer.relay()
    for j in range(3):
        side_add(late_moves[j], late_keep.at[j], late_side.at[j])
        for move in high_moves[j]:
            move.start()

    def twin_copy(n):
        return copy_to(
            line.at[pl.ds(n * rows, rows)], part(out, me.c, n), twin_send.at[n], twin_arrive.at[n], twin
        )

    def own_copy(n):
        return pltpu.make_async_copy(line.at[pl.ds(n * rows, rows)], part(out, me.c, n), here.at[n])

    for n in range(steps):
        at = pl.ds(n * rows, rows)
        x = own[at].astype(F32)
        scale = lax.rsqrt(jnp.mean(x * x, -1, keepdims=True) + EPSILON)
        normed = x * scale
        total = sums[n].total()
        rank = low(total[:, width:])
        total = total[:, :width] + dot(rank, down[...])
        gsum = jnp.sum(total * normed, axis=0, keepdims=True)
        hidden = low(normed * gain[...])
        rsum = dot_rows(rank, hidden)
        gain_grad[...] = gsum if n == 0 else gain_grad[...] + gsum
        rank_grad[...] = rsum if n == 0 else rank_grad[...] + rsum
        scaled = total * gain[...]
        line[at] = low(
            grad_middle[at]
            + scale * (scaled - normed * jnp.mean(scaled * normed, -1, keepdims=True))
        )
        twin_copy(n).start()
        own_copy(n).start()

    for n in range(wide.shape[0]):
        at = slice(n * owner_rows, (n + 1) * owner_rows)
        wide[n, 0:1] = gain_grad[:, at]
        wide[n, 1:2] = gain_two_grad[:, at]
        wide[n, 2:8] = jnp.zeros((6, owner_rows), F32)
        wide[n, 8:24] = rank_grad[:16, at]
    spreads = Transfer(
        route_all(me), lambda k: wide.at[k], lambda k: wide_got.at[k], wide_send, wide_arrive
    )
    spreads.start()
    def high_add(kind, source, target, total):
        for k in range(1, highs):
            wait_for(target.at[k - 1], high_arrive.at[kind, k])
        for m in range(2):
            add_rows(total.at[m], source.at[0, m], *(target.at[k - 1, m] for k in range(1, highs)))
        homes[kind].start()


    heads_move.wait()
    total = heads_got[0]
    for n in range(1, highs * 4):
        total = total + heads_got[n]
    heads_sum[...] = total
    tail = gains_out.shape[1]
    gains = Transfer(
        route_member(me),
        lambda _: heads_sum.at[pl.ds(heads_sum.shape[0] - tail, tail)],
        lambda k: gains_out.at[k],
        gain_send,
        gain_arrive,
    )
    gains.start()
    moves = [
        copy_to(
            heads_sum,
            heads_out.at[me.x],
            out_send.at[n],
            out_arrive.at[me.x],
            {"zl": flip(me.zl, fz), "x": flip(me.x, fx)},
        )
        for n, (fz, fx) in enumerate(FLIPS[:3])
    ]

    @pl.when(me.c == me.zl)
    def _():
        for move in moves:
            move.start()
        heads_out[me.x] = heads_sum[...]

    spreads.wait()
    total = wide_got[0]
    for n in range(1, wide.shape[0]):
        total = total + wide_got[n]
    wide_out[...] = total
    swap = copy_to(wide_out, wide_twin, near.at[0], near.at[1], twin)
    swap.start()

    units = gates.shape[-1]

    def spread_columns(source, target, cols):
        for k in range(2):
            target[:, k * cols : (k + 1) * cols] = source[k].astype(F32)

    def spread_rows(source, target, cols):
        for k in range(2):
            target[k * cols : (k + 1) * cols] = source[k, :, :cols].astype(F32).T

    homes[6].wait()
    spread_rows(down_home, down_grad, units)
    homes[5].wait()
    spread_columns(gate_home, pair_grad.at[0], units)
    homes[4].wait()
    spread_columns(ups_home, pair_grad.at[1], units)
    high_add(3, early, early_got, early_sum)
    for k in range(2):
        own_slot = (me.c == me.zl) & (me.x == k)
        unless(own_slot, lambda k=k: wait_for(heads_out.at[k], out_arrive.at[k]))

    @pl.when(me.c == me.zl)
    def _():
        for move in moves:
            move.wait_send()

    swap.wait()
    wide_out[...] = wide_out[...] + wide_twin[...]
    gains.wait()
    for j in range(3):
        high_add(j, late_side.at[j], late_got.at[j], late_sum.at[j])
    homes[3].wait()
    spread_rows(early_home, merge_grad, HD)
    for k in range(2):
        mixer_grad[3, :, k * HD : (k + 1) * HD] = early_home[k, :, HD:].astype(F32)
    for j in range(3):
        homes[j].wait()
        spread_columns(late_home.at[j], mixer_grad.at[j], HD)
    for transfer in sums:
        transfer.wait_sent()
    for n in range(steps):
        twin_copy(n).wait()
        own_copy(n).wait()
    for group in high_moves:
        for move in group:
            move.wait_send()

    def tile_sent(n, _):
        tile_move(n).wait_send()
        return 0

    lax.fori_loop(0, tiles.shape[0], tile_sent, 0)


def closing(proj, ranks, mixer_w, left, own, grad_middle, gain, down, gain_two_grad, heads, early, ups, gates, downs):
    rows, width = own.shape
    chunks = proj.shape[0]
    highs, _, owner_rows, _ = early.shape
    units = ups.shape[-1]
    chips = highs * 8
    arrays = [
        proj, ranks, mixer_w, left, own, grad_middle, gain, down, gain_two_grad, heads, early, ups, gates, downs,
    ]

    def shape(*dims, kind=BF):
        return jax.ShapeDtypeStruct(dims, kind)

    shapes = [
        shape(2, rows, width),
        shape(4, owner_rows, 2 * HD, kind=F32),
        shape(2 * HD, owner_rows, kind=F32),
        shape(2, owner_rows, 2 * units, kind=F32),
        shape(2 * units, owner_rows, kind=F32),
        shape(24, owner_rows, kind=F32),
        shape(2, *heads.shape, kind=F32),
        shape(TEAM, 8, heads.shape[1], kind=F32),
    ]
    tiles = 3 * HD // TILE
    late = (3, highs, 2, owner_rows, HD)
    scratch = [shape(*mixer_w.shape), shape(chunks, CHUNK, width + LANES)]
    scratch += [shape(n, rows, width + LANES) for n in (3, 2, 2)] + [shape(rows, width)]
    scratch += [shape(tiles, width // 2, TILE)] * 2 + [shape(*late)] * 3
    scratch += [
        shape(3, highs - 1, 2, owner_rows, HD),
        shape(highs - 1, 2, owner_rows, 2 * HD),
    ]
    sums = [shape(3, 2, owner_rows, HD), shape(2, owner_rows, 2 * HD)]
    scratch += sums + sums + [shape(2, owner_rows, units)] * 3
    scratch += [
        shape(chips, 24, owner_rows, kind=F32),
        shape(chips, 24, owner_rows, kind=F32),
        shape(highs * 4, *heads.shape, kind=F32),
        shape(*heads.shape, kind=F32),
        shape(24, owner_rows, kind=F32),
        shape(1, width, kind=F32),
        shape(LANES, width, kind=F32),
    ]
    size = sum(a.size * a.dtype.itemsize for a in arrays[:2] + arrays[3:] + shapes + scratch)
    sems = [
        (STEPS, 6), (STEPS, 5), (STEPS,), (STEPS,), (STEPS,), (tiles,), (tiles,), (3,), (3,), (4, highs), (4, highs),
        (7, 2), (7, 2), (chips,), (chips,), (highs * 4,), (highs * 4,), (2,), (3,), (2,), (TEAM,), (TEAM,), (1,),
    ]
    return pl.pallas_call(
        closing_kernel,
        out_shape=shapes,
        in_specs=[ANY if n == 2 else VMEM for n in range(len(arrays))],
        out_specs=[VMEM] * len(shapes),
        scratch_shapes=[pltpu.VMEM(a.shape, a.dtype) for a in scratch] + [DMA(n) for n in sems],
        compiler_params=pltpu.CompilerParams(
            collective_id=4, has_side_effects=True, vmem_limit_bytes=min(size + (10 << 20), 62 << 20)
        ),
        name="closing",
    )(*arrays)


def shards(
    tokens,
    cotangent,
    lengths,
    attn_gain,
    ffn_gain,
    mixer_in,
    decay_down,
    decay_up,
    decay_bias,
    head_gain,
    mixer_out,
    ffn_in,
    ffn_out,
):
    zh, zl, y, x, c = (lax.axis_index(a) for a in SEQ + ("c",))
    block, width = tokens.shape
    half = block // 2
    rows = mixer_in.shape[1]
    units = ffn_out.shape[0] // 2
    team_tokens = 2 * block
    rank = decay_down.shape[1]

    small = jnp.concatenate([attn_gain[None], ffn_gain[None], decay_down.T], axis=0)
    small = jnp.pad(small, ((0, RANKS - small.shape[0]), (0, 0)))
    up_head = lax.dynamic_slice_in_dim(decay_up, HD * x, HD, 1).astype(F32)
    bias_head = lax.dynamic_slice_in_dim(decay_bias, HD * x, HD, 0)
    ups = jnp.concatenate([up_head, bias_head[None], jnp.zeros((7, HD), F32)], axis=0)
    own = lax.dynamic_slice_in_dim(tokens, half * c, half, 0)
    own_dy = lax.dynamic_slice_in_dim(cotangent, half * c, half, 0)
    starts = jnp.cumsum(lengths) - lengths
    (
        mixer_w, merge_w, pair_w, down_w, gains, ffn_dy, hidden_one, low_rank, gate_input, cumulated, projected,
        mixed, gated, befores, decay, hidden_two, middle,
    ) = forward(
        mixer_in, mixer_out.T, ffn_in, ffn_out.T, small, ups, own, own_dy, starts, head_gain[None]
    )
    up_head = jnp.where(c == zl, up_head, lax.ppermute(up_head, "c", CROSS)).astype(BF)
    mixer_w, merge_w = mixer_w.reshape(width, 4 * HD), merge_w.reshape(width, HD)
    pair_w, down_w = pair_w.reshape(width, 2 * units), down_w.reshape(width, units)
    gain_one, gain_two, rank_down = gains[:1], gains[1:2], gains[2 : 2 + rank].astype(BF)
    forth, back, *pair_sides, down_part = feed_forward(hidden_two, ffn_dy, pair_w, down_w)
    highs = lax.axis_size("zh")
    pair_sides = [a.reshape(highs, 2, rows, 2 * units) for a in pair_sides]
    down_part = down_part.reshape(highs, 2, rows, units)
    pad_rank = ((0, LANES - rank), (0, 0))
    (
        grad_middle, grad_gain_two, grad_proj, grad_ranks, heads, early, gate_sum, up_sum, down_sum,
        left_hidden, result,
    ) = backward(
        back, forth, own_dy, middle, gain_two, pair_sides, down_part, merge_w, gated, projected, mixed, cumulated,
        gate_input, befores, decay, low_rank, jnp.pad(up_head, pad_rank), head_gain[None], hidden_one, starts,
    )
    early = early.reshape(highs, 2, rows, 2 * HD)
    grad_inputs, mixer_home, merge_home, pair_home, down_home, wide, heads, gains = closing(
        grad_proj, grad_ranks, mixer_w, left_hidden, own, grad_middle, gain_one, jnp.pad(rank_down, pad_rank),
        grad_gain_two, heads, early, up_sum, gate_sum, down_sum,
    )
    return (
        result.reshape(block, width),
        grad_inputs.reshape(block, width),
        wide[0],
        wide[1],
        mixer_home,
        wide[8 : 8 + rank].T,
        heads[:, :rank].transpose(1, 0, 2).reshape(rank, 2 * HD),
        heads[:, rank].reshape(2 * HD),
        jnp.sum(gains[:, rank + 1 - 16], axis=0),
        merge_home,
        pair_home,
        down_home,
    )


def solution(mesh):
    devices = mesh.devices
    inner = Mesh(devices.reshape(devices.shape[0] // 8, 2, 2, 2, devices.shape[1]), SEQ + ("c",))
    in_specs = (
        P(SEQ, None),
        P(SEQ, None),
        P(),
        P(SEQ),
        P(SEQ),
        P(None, SEQ, "c"),
        P(SEQ, None),
        P(None, "c"),
        P("c"),
        P(),
        P("c", SEQ),
        P(None, SEQ, "c"),
        P("c", SEQ),
    )
    out_specs = (
        P(SEQ, None),
        P(SEQ, None),
        P(SEQ),
        P(SEQ),
        P(None, SEQ, "c"),
        P(SEQ, None),
        P(None, "c"),
        P("c"),
        P(),
        P("c", SEQ),
        P(None, SEQ, "c"),
        P("c", SEQ),
    )
    return jax.shard_map(shards, mesh=inner, in_specs=in_specs, out_specs=out_specs, check_vma=False)
```

```python
import functools

import jax
import jax.numpy as jnp
from jax import lax
from jax.experimental import pallas as pl
from jax.experimental.pallas import tpu as pltpu
from jax.sharding import Mesh, PartitionSpec as P

HD = 512
CHUNK = 128
EPSILON = 1e-06
HEAD_FLOOR = 1.0
TEAM = 4

BF = jnp.bfloat16
F32 = jnp.float32
MESH = pl.DeviceIdType.MESH
ANY = pl.BlockSpec(memory_space=pl.ANY)
VMEM = pl.BlockSpec(memory_space=pltpu.VMEM)
DMA = pltpu.SemaphoreType.DMA

SEQ = ("zh", "zl", "y", "x")
FLIPS = ((1, 1), (0, 1), (1, 0), (0, 0))


def dot(a, b):
    return jnp.dot(a, b, preferred_element_type=F32)


def dot_rows(a, b):
    return lax.dot_general(a, b, (((0,), (0,)), ((), ())), preferred_element_type=F32)


def dot_last(a, b):
    return lax.dot_general(a, b, (((1,), (1,)), ((), ())), preferred_element_type=F32)


def low(v):
    return v.astype(BF)


def flip(index, by):
    return 1 - index if by else index


class Place:
    def __init__(self):
        self.zl, self.x, self.c = lax.axis_index("zl"), lax.axis_index("x"), lax.axis_index("c")
        self.member = self.zl * 2 + self.x

    def half(self, ref):
        rows = ref.shape[0] // 2
        return ref.at[pl.ds(pl.multiple_of(self.c * rows, rows), rows)]


def greet_team(me, more=0):
    barrier = pltpu.get_barrier_semaphore()
    for n in range(1, 8):
        to = {"zl": flip(me.zl, n & 1), "x": flip(me.x, n & 2), "c": flip(me.c, n & 4)}
        pl.semaphore_signal(barrier, inc=1, device_id=to, device_id_type=MESH)
    pl.semaphore_wait(barrier, 7 + more)


def others(me):
    zh, y, highs = lax.axis_index("zh"), lax.axis_index("y"), lax.axis_size("zh")
    for k in range(highs):
        for n in range(8):
            yield lax.rem(zh + k, highs), flip(me.zl, n & 1), flip(y, n & 2), flip(me.x, n & 4), k + n == 0


def greet_all(me):
    barrier = pltpu.get_barrier_semaphore()
    count = 0
    for zh, zl, y, x, own in others(me):
        for f in range(2):
            if own and not f:
                continue
            to = {"zh": zh, "zl": zl, "y": y, "x": x, "c": flip(me.c, f)}
            pl.semaphore_signal(barrier, inc=1, device_id=to, device_id_type=MESH)
            count += 1
    pl.semaphore_wait(barrier, count)


def route_member(me):
    out, arrive = [], []
    for fz, fx in FLIPS:
        zl, x = flip(me.zl, fz), flip(me.x, fx)
        own = (fz, fx) == (0, 0)
        out.append((zl * 2 + x, me.member, {"zl": zl, "x": x}, own))
        arrive.append((zl * 2 + x, own))
    return out, arrive


def chip_index(zh, zl, y, x):
    return ((zh * 2 + zl) * 2 + y) * 2 + x


def route_all(me):
    mine = chip_index(lax.axis_index("zh"), me.zl, lax.axis_index("y"), me.x)
    out, arrive = [], []
    for zh, zl, y, x, own in others(me):
        chip = chip_index(zh, zl, y, x)
        out.append((chip, mine, {"zh": zh, "zl": zl, "y": y, "x": x}, own))
        arrive.append((chip, own))
    return out, arrive


def route_halves(me):
    mine = me.c == me.zl
    out, arrive = [], []
    for fz, fx in FLIPS:
        zl, x = flip(me.zl, fz), flip(me.x, fx)
        own = mine if (fz, fx) == (0, 0) else False
        out.append((0, me.x * 2 + me.c, {"zl": zl, "x": x, "c": me.zl}, own))
    for fc, fx in FLIPS:
        c, x = flip(me.c, fc), flip(me.x, fx)
        own = mine if (fc, fx) == (0, 0) else False
        arrive.append((x * 2 + c, own))
    return out, arrive


def route_owners(me):
    mine = me.c == me.zl
    out, arrive = [], []
    for fc, fx in FLIPS:
        c, x = flip(me.c, fc), flip(me.x, fx)
        own = mine if (fc, fx) == (0, 0) else False
        out.append((x * 2 + c, me.member, {"zl": me.c, "x": x, "c": c}, own))
    for fz, fx in FLIPS:
        zl, x = flip(me.zl, fz), flip(me.x, fx)
        own = mine if (fz, fx) == (0, 0) else False
        arrive.append((zl * 2 + x, own))
    return out, arrive


def route_weights(me):
    mine = (me.c == me.zl) & (me.c == me.x)
    out, arrive = [], []
    for f in (1, 0):
        x = flip(me.x, f)
        own = (me.c == me.zl) & (me.c == x) & (me.x == me.c) if not f else False
        out.append((x, me.zl, {"zl": me.c, "x": x, "c": me.x}, own))
    for f in (1, 0):
        zl = flip(me.zl, f)
        own = mine if not f else False
        arrive.append((zl, own))
    return out, arrive


def route_weights_home(me):
    mine = (me.c == me.zl) & (me.c == me.x)
    out, arrive = [], []
    for f in (1, 0):
        zl = flip(me.zl, f)
        own = mine if not f else False
        out.append((zl, me.x, {"zl": zl, "x": me.c, "c": me.zl}, own))
    for f in (1, 0):
        x = flip(me.x, f)
        own = mine if not f else False
        arrive.append((x, own))
    return out, arrive


def when(condition, run):
    if condition is True:
        run()
    elif condition is not False:
        pl.when(condition)(run)


def unless(condition, run):
    if condition is False:
        run()
    elif condition is not True:
        pl.when(jnp.logical_not(condition))(run)


class Transfer:
    def __init__(self, route, source, target, send, arrive):
        self.route, self.source, self.target, self.send, self.arrive = route, source, target, send, arrive

    def _remote(self, n):
        index, slot, to, own = self.route[0][n]
        return pltpu.make_async_remote_copy(
            src_ref=self.source(index),
            dst_ref=self.target(slot),
            send_sem=self.send.at[n],
            recv_sem=self.arrive.at[slot],
            device_id=to,
            device_id_type=MESH,
        )

    def _local(self, n):
        index, slot, to, own = self.route[0][n]
        return pltpu.make_async_copy(self.source(index), self.target(slot), self.send.at[n])

    def start(self):
        for n, (_, _, _, own) in enumerate(self.route[0]):
            unless(own, lambda: self._remote(n).start())
            when(own, lambda: self._local(n).start())

    def wait_arrive(self):
        for slot, own in self.route[1]:
            ref = self.target(slot)

            def arrived():
                pltpu.make_async_copy(ref, ref, self.arrive.at[slot]).wait()

            unless(own, arrived)

    def wait_local(self):
        for n, (_, _, _, own) in enumerate(self.route[0]):
            when(own, lambda: self._local(n).wait())

    def wait_sent(self):
        for n, (_, _, _, own) in enumerate(self.route[0]):
            unless(own, lambda: self._remote(n).wait_send())

    def wait(self):
        self.wait_arrive()
        self.wait_local()
        self.wait_sent()


def copy_to(src, dst, send, arrive, to):
    return pltpu.make_async_remote_copy(
        src_ref=src, dst_ref=dst, send_sem=send, recv_sem=arrive, device_id=to, device_id_type=MESH
    )


def wait_for(ref, sem):
    pltpu.make_async_copy(ref, ref, sem).wait()


def member_slots(me, two):
    along = me.zl * 2 + 1 - me.x, {"x": 1 - me.x}
    over = (1 - me.zl) * 2 + me.x, {"zl": 1 - me.zl}
    one, double = (over, along) if two == "x" else (along, over)
    return one[0], double[0], (1 - me.zl) * 2 + 1 - me.x, one[1], double[1]


class MemberSpread:
    def __init__(self, me, source, target, send, arrive, two="x"):
        self.target, self.arrive = target, arrive
        mine = me.member
        one, double, across, to_one, to_double = member_slots(me, two)
        self.slots = one, double, across
        self.direct = [
            copy_to(source, target(mine), send.at[0], arrive.at[mine], to_one),
            copy_to(source, target(mine), send.at[1], arrive.at[mine], to_double),
        ]
        self.local = pltpu.make_async_copy(source, target(mine), arrive.at[mine])
        self.forward = copy_to(target(one), target(one), send.at[2], arrive.at[one], to_double)

    def start(self):
        for copy in self.direct:
            copy.start()
        self.local.start()

    def relay(self):
        wait_for(self.target(self.slots[0]), self.arrive.at[self.slots[0]])
        self.forward.start()

    def wait(self):
        for slot in self.slots[1:]:
            wait_for(self.target(slot), self.arrive.at[slot])
        self.local.wait()
        for copy in self.direct + [self.forward]:
            copy.wait_send()


class HalvesSpread:
    def __init__(self, me, source, target, send, arrive):
        self.me, self.target, self.arrive = me, target, arrive
        mine = me.x * 2 + me.c
        self.home = me.c == me.zl
        self.direct = [
            copy_to(source, target(mine), send.at[0], arrive.at[mine], {"zl": 1 - me.zl, "c": me.zl}),
            copy_to(source, target(mine), send.at[1], arrive.at[mine], {"x": 1 - me.x, "c": me.zl}),
        ]
        self.near = copy_to(source, target(mine), send.at[2], arrive.at[mine], {"c": 1 - me.c})
        self.local = pltpu.make_async_copy(source, target(mine), send.at[2])
        self.near_slots = [me.x * 2 + c for c in range(2)]
        self.far_slots = [(1 - me.x) * 2 + c for c in range(2)]
        self.forwards = [
            copy_to(target(slot), target(slot), send.at[3 + c], arrive.at[slot], {"x": 1 - me.x})
            for c, slot in enumerate(self.near_slots)
        ]

    def start(self):
        for copy in self.direct:
            copy.start()
        pl.when(self.home)(self.local.start)
        unless(self.home, self.near.start)

    def relay(self):
        @pl.when(jnp.logical_not(self.home))
        def _():
            for slot, forward in zip(self.near_slots, self.forwards):
                wait_for(self.target(slot), self.arrive.at[slot])
                forward.start()

    def wait(self):
        me = self.me

        @pl.when(self.home)
        def _():
            self.local.wait()
            slot = me.x * 2 + 1 - me.c
            wait_for(self.target(slot), self.arrive.at[slot])

        for slot in self.far_slots:
            wait_for(self.target(slot), self.arrive.at[slot])
        for copy in self.direct:
            copy.wait_send()

        @pl.when(jnp.logical_not(self.home))
        def _():
            self.near.wait_send()
            for forward in self.forwards:
                forward.wait_send()


class MemberSum:
    def __init__(self, me, source, got, relayed, staged, send, arrive, two="x"):
        self.me, self.source, self.got, self.relayed, self.staged = me, source, got, relayed, staged
        self.arrive = arrive
        self.one, double, across, to_one, to_double = member_slots(me, two)
        self.direct = [
            copy_to(source(across), relayed(0), send.at[0], arrive.at[0], to_double),
            copy_to(source(double), got(0), send.at[1], arrive.at[1], to_double),
        ]
        self.onward = copy_to(staged(0), got(1), send.at[2], arrive.at[2], to_one)

    def start(self):
        for copy in self.direct:
            copy.start()

    def relay(self):
        wait_for(self.relayed(0), self.arrive.at[0])
        own = self.source(self.one)[...].astype(F32)
        self.staged(0)[...] = low(own + self.relayed(0)[...].astype(F32))
        self.onward.start()

    def total(self):
        wait_for(self.got(0), self.arrive.at[1])
        wait_for(self.got(1), self.arrive.at[2])
        total = self.source(self.me.member)[...].astype(F32)
        return total + self.got(0)[...].astype(F32) + self.got(1)[...].astype(F32)

    def wait_sent(self):
        for copy in self.direct + [self.onward]:
            copy.wait_send()


class OwnersSum:
    def __init__(self, me, source, got, relayed, staged, send, arrive):
        self.me, self.source, self.got, self.relayed, self.staged = me, source, got, relayed, staged
        self.arrive = arrive
        self.home = me.c == me.zl
        mine, other = me.x * 2, (1 - me.x) * 2
        self.near = copy_to(source(mine + 1 - me.c), got(0), send.at[0], arrive.at[0], {"c": 1 - me.c})
        self.local = pltpu.make_async_copy(source(mine + me.c), got(0), send.at[1])
        self.across = [
            copy_to(source(other + c), got(1), send.at[2 + c], arrive.at[1], {"x": 1 - me.x, "c": c})
            for c in range(2)
        ]
        self.first = [
            copy_to(source(other + c), relayed(c), send.at[2 + c], arrive.at[3 + c], {"x": 1 - me.x})
            for c in range(2)
        ]
        self.onward = [
            copy_to(staged(c), got(2), send.at[4 + c], arrive.at[2], {"zl": me.c, "c": c})
            for c in range(2)
        ]

    def start(self):
        @pl.when(self.home)
        def _():
            for copy in self.across + [self.near, self.local]:
                copy.start()

        @pl.when(jnp.logical_not(self.home))
        def _():
            for copy in self.first:
                copy.start()

    def relay(self):
        @pl.when(jnp.logical_not(self.home))
        def _():
            for c in range(2):
                wait_for(self.relayed(c), self.arrive.at[3 + c])
                own = self.source(self.me.x * 2 + c)[...].astype(F32)
                self.staged(c)[...] = low(own + self.relayed(c)[...].astype(F32))
                self.onward[c].start()

    def total(self):
        pl.when(self.home)(self.local.wait)
        unless(self.home, lambda: wait_for(self.got(0), self.arrive.at[0]))
        wait_for(self.got(1), self.arrive.at[1])
        wait_for(self.got(2), self.arrive.at[2])
        return sum(self.got(k)[...].astype(F32) for k in range(3))

    def wait_sent(self):
        @pl.when(self.home)
        def _():
            for copy in self.across + [self.near]:
                copy.wait_send()

        @pl.when(jnp.logical_not(self.home))
        def _():
            for copy in self.first + self.onward:
                copy.wait_send()


class Placed(Transfer):
    def __init__(self, route, source, there, target, send, arrive):
        super().__init__(route, source, target, send, arrive)
        self.there = there

    def _remote(self, n):
        index, slot, to, own = self.route[0][n]
        return pltpu.make_async_remote_copy(
            src_ref=self.source(index),
            dst_ref=self.there(slot),
            send_sem=self.send.at[n],
            recv_sem=self.arrive.at[slot],
            device_id=to,
            device_id_type=MESH,
        )


LANES = 128
RANKS = 32


def keyed_mask(start, starts_row, starts_column):
    rows = lax.broadcasted_iota(jnp.int32, (CHUNK, CHUNK), 0)
    columns = lax.broadcasted_iota(jnp.int32, (CHUNK, CHUNK), 1)
    ids = jnp.sum((rows + start >= starts_row[0:1]).astype(F32), axis=1, keepdims=True)
    places = lax.broadcasted_iota(jnp.int32, starts_column.shape, 1)
    ids_row = jnp.sum((places + start >= starts_column[...]).astype(F32), axis=0, keepdims=True)
    before = jnp.sum((starts_row[0:1] < start).astype(F32), axis=1, keepdims=True)
    final = ids_row[:, CHUNK - 1 :]
    pair = (rows >= columns) & (ids == ids_row)
    visible = (ids == before).astype(F32)
    keep = (final == before).astype(F32)
    return pair, visible, keep, (ids == final).astype(F32)


class StatePass:
    def __init__(self, back, local, decay, out, rounded, got, got_decay, sums, sum_decays, stage, stage_decay,
                 entering, leave, enter, send, arrive, far_send, far_arrive, leave_send, leave_arrive):
        self.__dict__.update(locals())
        self.zh, c, y = lax.axis_index("zh"), lax.axis_index("c"), lax.axis_index("y")
        self.highs = lax.axis_size("zh")
        self.mine = c * 2 + y
        self.quarter = local.shape[0] // 4
        self.partners = []
        for fc, fy in ((1, 1), (0, 1), (1, 0)):
            to_c, to_y = flip(c, fc), flip(y, fy)
            self.partners.append((to_c * 2 + to_y, {"c": to_c, "y": to_y}))
        self.order = range(3, -1, -1) if back else range(4)
        self.moves, self.outs = [], []

    def begin(self):
        self.rounded[...] = low(self.local[...])
        for n, (index, to) in enumerate(self.partners):
            rows = self.rounded.at[pl.ds(index * self.quarter, self.quarter)]
            self.moves.append(copy_to(rows, self.got.at[self.mine], self.send.at[0, n], self.arrive.at[0, self.mine], to))
            self.moves.append(
                copy_to(self.decay, self.got_decay.at[self.mine], self.send.at[1, n], self.arrive.at[1, self.mine], to)
            )
        for move in self.moves:
            move.start()
        self.got[self.mine] = self.rounded[pl.ds(self.mine * self.quarter, self.quarter)]
        self.got_decay[self.mine] = self.decay[...]

    def needs(self, source, target):
        return (source > target) if self.back else (source < target)

    def far(self, n, to):
        zh = self.zh
        return (
            copy_to(self.stage, self.sums.at[zh], self.far_send.at[0, n], self.far_arrive.at[0, zh], {"zh": to}),
            copy_to(
                self.stage_decay, self.sum_decays.at[zh], self.far_send.at[1, n], self.far_arrive.at[1, zh], {"zh": to}
            ),
        )

    def combine(self):
        for index, _ in self.partners:
            wait_for(self.got.at[index], self.arrive.at[0, index])
            wait_for(self.got_decay.at[index], self.arrive.at[1, index])
        total, total_decay = None, None
        for k in self.order:
            piece, d = self.got[k].astype(F32), self.got_decay[k][:1]
            total = piece if total is None else d * total + piece
            total_decay = d if total_decay is None else total_decay * d
        self.stage[...] = low(total)
        self.stage_decay[...] = jnp.broadcast_to(total_decay, self.stage_decay.shape)
        for n in range(1, self.highs):
            to = lax.rem(self.zh + n, self.highs)

            @pl.when(self.needs(self.zh, to))
            def _(n=n, to=to):
                for move in self.far(n, to):
                    move.start()

    def spread(self):
        self.entering[...] = jnp.zeros_like(self.entering)
        for n in range(self.highs):
            k = self.highs - 1 - n if self.back else n

            @pl.when(self.needs(k, self.zh))
            def _(k=k):
                wait_for(self.sums.at[k], self.far_arrive.at[0, k])
                wait_for(self.sum_decays.at[k], self.far_arrive.at[1, k])
                self.entering[...] = self.sum_decays[k][:1] * self.entering[...] + self.sums[k].astype(F32)

        state = self.entering[...]
        for k in self.order:
            self.leave[k] = low(state)
            state = self.got_decay[k][:1] * state + self.got[k].astype(F32)
        for n, (index, to) in enumerate(self.partners):
            self.outs.append(
                copy_to(
                    self.leave.at[index], self.enter.at[self.mine], self.leave_send.at[n],
                    self.leave_arrive.at[self.mine], to,
                )
            )
        for move in self.outs:
            move.start()
        self.enter[self.mine] = self.leave[self.mine]

    def finish(self):
        for index, _ in self.partners:
            wait_for(self.enter.at[index], self.leave_arrive.at[index])
        for k in range(4):
            self.out[pl.ds(k * self.quarter, self.quarter)] = self.enter[k].astype(F32)

    def wait_sent(self):
        for move in self.moves + self.outs:
            move.wait_send()
        for n in range(1, self.highs):
            to = lax.rem(self.zh + n, self.highs)

            @pl.when(self.needs(self.zh, to))
            def _(n=n, to=to):
                for move in self.far(n, to):
                    move.wait_send()


def state_pass_scratch(highs):
    quarter = HD // 4
    return [
        pltpu.VMEM((HD, HD), BF),
        pltpu.VMEM((4, quarter, HD), BF),
        pltpu.VMEM((4, 8, HD), F32),
        pltpu.VMEM((highs, quarter, HD), BF),
        pltpu.VMEM((highs, 8, HD), F32),
        pltpu.VMEM((quarter, HD), BF),
        pltpu.VMEM((8, HD), F32),
        pltpu.VMEM((quarter, HD), F32),
        pltpu.VMEM((4, quarter, HD), BF),
        pltpu.VMEM((4, quarter, HD), BF),
        DMA((2, 3)),
        DMA((2, 4)),
        DMA((2, highs)),
        DMA((2, highs)),
        DMA((3,)),
        DMA((4,)),
    ]


STATE_REFS = 16


def forward_kernel(*refs):
    (
        mixer_in, mixer_out, ffn_in, ffn_out, small, ups, tokens, cotangent, starts_row, starts_column, head_gain,
        mixer_w, merge_w, pair_w, down_w, gains, cots, hidden_far, low_rank, gate_far, cumulated_far, projected, mixed_far,
        gated_far, befores_far, decay, second, middle_far,
        hidden, gate, cumulated, mixed, gated, befores, middle, mixer_v, merge_v, projected_v, updates, inputs, smalls, ups_got, state, partial, got, relayed, staged, line,
        own_send, own_arrive, far_send, arrive, small_send, small_arrive, ups_sem, inputs_send, inputs_arrive,
        cot_send, cot_arrive, sum_send, sum_arrive, spread_send, spread_arrive, saves,
    ) = refs[:-STATE_REFS]
    me = Place()
    own, cot = me.half(tokens), me.half(cotangent)
    zh, y, highs = lax.axis_index("zh"), lax.axis_index("y"), lax.axis_size("zh")
    units = down_w.shape[-1]
    width = tokens.shape[1]
    chunks = hidden.shape[0]
    first = ((zh * 2 + me.c) * 2 + y) * (chunks * CHUNK)
    greet_all(me)
    twin, side = {"c": 1 - me.c}, {"y": 1 - y}

    def own_source(part, k):
        if part < 5:
            at = pl.ds(pl.multiple_of(k * HD, HD), HD)
            return mixer_out.at[:, at] if part == 4 else mixer_in.at[part, :, at]
        at = pl.ds(pl.multiple_of(k * units, LANES), units)
        return ffn_out.at[:, at] if part == 7 else ffn_in.at[part - 5, :, at]

    def piece(at_zh, at_y, x, part, zl=slice(None)):
        if part < 4:
            return mixer_v.at[at_zh, zl, at_y, x, :, pl.ds(part * HD, HD)]
        if part == 4:
            return merge_v.at[at_zh, zl, at_y, x]
        if part < 7:
            return pair_w.at[at_zh, zl, at_y, x, :, pl.ds((part - 5) * units, units)]
        return down_w.at[at_zh, zl, at_y, x]

    firsts = [
        Placed(
            route_weights(me),
            lambda k, p=p: own_source(p, k),
            lambda zl, p=p: piece(zh, y, me.x, p, zl),
            lambda zl, p=p: piece(zh, y, me.c, p, zl),
            own_send.at[p],
            own_arrive.at[p],
        )
        for p in range(8)
    ]
    count = [0]
    sent = []

    def forward(at_zh, at_y, part, to, start=True):
        place = piece(at_zh, at_y, me.c, part)
        copy = copy_to(place, place, far_send.at[count[0]], arrive.at[at_zh, at_y, me.c, part], to)
        if start:
            copy.start()
        count[0] += 1
        sent.append(copy)
        return copy

    def arrived(at_zh, at_y, x, part):
        wait_for(piece(at_zh, at_y, x, part), arrive.at[at_zh, at_y, x, part])

    def own_high(part, start=True):
        firsts[part].wait_arrive()
        firsts[part].wait_local()
        return [forward(zh, y, part, {"zh": lax.rem(zh + k, highs)}, start) for k in range(1, highs)]

    def own_near(part):
        forward(zh, y, part, side)
        forward(zh, y, part, twin)

    def pass_high(part):
        for k in range(1, highs):
            at_zh = lax.rem(zh + k, highs)
            arrived(at_zh, y, me.c, part)
            forward(at_zh, y, part, side)
            forward(at_zh, y, part, twin)

    def pass_side(part):
        for k in range(highs):
            at_zh = lax.rem(zh + k, highs)
            arrived(at_zh, 1 - y, me.c, part)
            forward(at_zh, 1 - y, part, twin)

    def complete(part):
        for k in range(highs):
            at_zh = lax.rem(zh + k, highs)
            arrived(at_zh, y, 1 - me.c, part)
            arrived(at_zh, 1 - y, 1 - me.c, part)

    save_count = [0]
    saved = []

    def save(source, target):
        copy = pltpu.make_async_copy(source, target, saves.at[save_count[0]])
        copy.start()
        save_count[0] += 1
        saved.append(copy)

    order = (1, 2, 0, 3, 4)
    for part in order:
        firsts[part].start()
    move_small = Transfer(route_all(me), lambda _: small, lambda k: smalls.at[k], small_send, small_arrive)
    move_small.start()
    lend = copy_to(ups, ups_got, ups_sem.at[0], ups_sem.at[1], twin)
    lend.start()
    for part in order:
        own_high(part)
        if part in order[:2]:
            own_near(part)
    move_inputs = HalvesSpread(me, own, lambda k: inputs.at[k], inputs_send, inputs_arrive)
    move_cot = MemberSpread(me, cot, lambda k: cots.at[k], cot_send, cot_arrive)
    move_inputs.start()
    move_inputs.relay()
    pass_high(1)
    move_small.wait()
    lend.wait()
    owner_rows = smalls.shape[2]
    for n in range(smalls.shape[0]):
        gains[:, n * owner_rows : (n + 1) * owner_rows] = smalls[n].astype(F32)
    pass_high(2)
    for part in (5, 6, 7):
        firsts[part].start()
    for part in order[2:]:
        own_near(part)
    move_inputs.wait()

    up = jnp.where(me.c == me.zl, ups[...], ups_got[...])
    rank_up, bias = low(up[:16]), up[16:17]
    down = low(gains[...])
    lower = (
        lax.broadcasted_iota(jnp.int32, (CHUNK, CHUNK), 0)
        >= lax.broadcasted_iota(jnp.int32, (CHUNK, CHUNK), 1)
    ).astype(F32)

    def gates_step(n, _):
        x = inputs[n].astype(F32)
        scale = lax.rsqrt(jnp.mean(x * x, -1, keepdims=True) + EPSILON)
        h = low(x * scale * gains[0:1])
        hidden[n] = h
        z = low(dot_last(h, down))
        low_rank[n] = z
        a = dot(z[:, 2:18], rank_up) + bias
        gate[n] = a
        log_gate = (jnp.minimum(a, 0.0) - jnp.log1p(jnp.exp(-jnp.abs(a)))) / 16.0
        cumulated[n] = jnp.dot(
            lower, log_gate, precision=lax.Precision.HIGHEST, preferred_element_type=F32
        )
        return 0

    lax.fori_loop(0, chunks, gates_step, 0)
    save(hidden, hidden_far)
    save(gate, gate_far)
    save(cumulated, cumulated_far)

    def project(part):
        rows = hidden[...].reshape(chunks * CHUNK, width)
        block = mixer_v[:, :, :, :, :, pl.ds(part * HD, HD)].reshape(width, HD)
        result = dot(rows, block)
        if part == 0:
            result = result * HD ** (-0.5)
        projected_v[part] = result.reshape(chunks, CHUNK, HD)
        save(projected_v.at[part], projected.at[part])

    pass_side(1)
    pass_side(2)
    complete(1)
    project(1)
    complete(2)
    project(2)

    state[...] = jnp.zeros_like(state)
    decay[...] = jnp.ones_like(decay)

    def masks(n):
        return keyed_mask(first + n * CHUNK, starts_row, starts_column)

    def local_step(n, _):
        _, _, keep, last = masks(n)
        b = cumulated[n]
        end = b[CHUNK - 1 :]
        kc = low(projected_v[1, n] * jnp.exp(end - b) * last)
        update = dot_rows(low(projected_v[2, n]), kc)
        updates[n] = update
        carry = keep * jnp.exp(end)
        state[...] = carry * state[...] + update
        decay[...] = decay[...] * carry
        return 0

    lax.fori_loop(0, chunks, local_step, 0)
    states = StatePass(False, state, decay, state, *refs[-STATE_REFS:])
    states.begin()
    pass_high(0)
    states.combine()
    held = [own_high(part, False) for part in (5, 6, 7)]

    @pl.when(me.zl == 1)
    def _():
        for copy in sum(held, []):
            copy.start()

    pass_high(3)
    pass_side(0)
    complete(0)
    project(0)
    pass_side(3)

    def inner_step(n, _):
        pair, _, _, _ = masks(n)
        b = cumulated[n]
        mid = b[CHUNK // 2 - 1 : CHUNK // 2]
        qh = low(projected_v[0, n] * jnp.exp(b - mid))
        kh = low(projected_v[1, n] * jnp.exp(mid - b))
        scores = low(jnp.where(pair, dot_last(qh, kh), 0.0))
        mixed[n] = dot(scores, low(projected_v[2, n]))
        return 0

    lax.fori_loop(0, chunks, inner_step, 0)
    states.spread()

    @pl.when(me.zl == 0)
    def _():
        for copy in sum(held[:1], []):
            copy.start()

    pass_high(4)
    for part in (5, 6, 7):
        own_near(part)
    complete(3)
    project(3)
    states.finish()

    def outer_step(n, _):
        _, visible, keep, _ = masks(n)
        b = cumulated[n]
        before = state[...]
        qd = low(projected_v[0, n] * jnp.exp(b) * visible)
        out = mixed[n] + dot_last(qd, low(before))
        mixed[n] = out
        befores[n] = low(before)
        state[...] = keep * jnp.exp(b[CHUNK - 1 :]) * before + updates[n]
        scale = lax.rsqrt(jnp.mean(out * out, -1, keepdims=True) + HEAD_FLOOR)
        u = projected_v[3, n]
        gated[n] = low(out * scale * head_gain[...] * (u * jax.nn.sigmoid(u)))
        return 0

    lax.fori_loop(0, chunks, outer_step, 0)
    save(mixed, mixed_far)
    save(gated, gated_far)
    save(befores, befores_far)
    pass_side(4)
    complete(4)

    def merge_step(n, _):
        partial[n] = low(dot_last(gated[n], merge_v[...].reshape(width, HD)))
        return 0

    lax.fori_loop(0, chunks, merge_step, 0)

    steps = sum_send.shape[0]
    rows = tokens.shape[0] // 2 // steps

    def rows_of(ref, k, n):
        return ref.at[k, pl.ds(n * rows, rows)]

    sums = [
        OwnersSum(
            me,
            lambda k, n=n: rows_of(partial, k, n),
            lambda k, n=n: rows_of(got, k, n),
            lambda k, n=n: rows_of(relayed, k, n),
            lambda k, n=n: rows_of(staged, k, n),
            sum_send.at[n],
            sum_arrive.at[n],
        )
        for n in range(steps)
    ]
    spreads = [
        MemberSpread(
            me,
            line.at[pl.ds(n * rows, rows)],
            lambda k, n=n: rows_of(second, k, n),
            spread_send.at[n],
            spread_arrive.at[n],
        )
        for n in range(steps)
    ]
    for transfer in sums:
        transfer.start()
    for transfer in sums:
        transfer.relay()
    for n in range(steps):
        at = pl.ds(n * rows, rows)
        total = own[at].astype(F32) + sums[n].total()
        middle[at] = total
        scale = lax.rsqrt(jnp.mean(total * total, -1, keepdims=True) + EPSILON)
        line[at] = low(total * scale * gains[1:2])
        spreads[n].start()
        if n:
            spreads[n - 1].relay()
    spreads[steps - 1].relay()
    @pl.when(me.zl == 0)
    def _():
        for copy in sum(held[1:], []):
            copy.start()

    pass_high(5)
    pass_high(6)
    pass_side(5)
    move_cot.start()
    save(middle, middle_far)
    save(mixer_v, mixer_w)
    save(merge_v, merge_w)
    pass_high(7)
    move_cot.relay()
    for part in (6, 7):
        pass_side(part)
    for part in (5, 6, 7):
        complete(part)
    for transfer in sums:
        transfer.wait_sent()
    for transfer in spreads:
        transfer.wait()
    states.wait_sent()
    move_cot.wait()
    for transfer in firsts:
        transfer.wait_sent()
    for copy in sent:
        copy.wait_send()
    for copy in saved:
        copy.wait()


def starts_arrays(starts):
    starts = jnp.pad(starts, (0, LANES - starts.shape[0]), constant_values=jnp.int32(1 << 30))
    return jnp.broadcast_to(starts[None], (8, LANES)), jnp.broadcast_to(starts[:16, None], (16, LANES))


def forward(mixer_in, mixer_out, ffn_in, ffn_out, small, ups, tokens, cotangent, starts, head_gain):
    highs = lax.axis_size("zh")
    chips = highs * 8
    rows, half, width = small.shape[1], tokens.shape[0] // 2, tokens.shape[1]
    units = ffn_out.shape[1] // 2
    chunks = TEAM * half // CHUNK

    def shape(*dims, kind=BF):
        return jax.ShapeDtypeStruct(dims, kind)

    shapes = [
        (shape(highs, 2, 2, 2, rows, 4 * HD), ANY),
        (shape(highs, 2, 2, 2, rows, HD), ANY),
        (shape(highs, 2, 2, 2, rows, 2 * units), ANY),
        (shape(highs, 2, 2, 2, rows, units), ANY),
        (shape(RANKS, width, kind=F32), VMEM),
        (shape(TEAM, half, width), ANY),
        (shape(chunks, CHUNK, width), ANY),
        (shape(chunks, CHUNK, RANKS), VMEM),
        (shape(chunks, CHUNK, HD, kind=F32), ANY),
        (shape(chunks, CHUNK, HD, kind=F32), ANY),
        (shape(4, chunks, CHUNK, HD, kind=F32), ANY),
        (shape(chunks, CHUNK, HD, kind=F32), ANY),
        (shape(chunks, CHUNK, HD), ANY),
        (shape(chunks, HD, HD), ANY),
        (shape(8, HD, kind=F32), VMEM),
        (shape(TEAM, half, width), ANY),
        (shape(half, width, kind=F32), ANY),
    ]
    arrays = [mixer_in, mixer_out, ffn_in, ffn_out, small, ups, tokens, cotangent, *starts_arrays(starts), head_gain]
    scratch = [shapes[n][0] for n in (6, 8, 9, 11, 12, 13, 16)]
    scratch += [
        shapes[0][0],
        shapes[1][0],
        shapes[10][0],
        shape(chunks, HD, HD, kind=F32),
        shape(TEAM, half, width),
        shape(chips, RANKS, rows),
        shape(*ups.shape, kind=F32),
        shape(HD, HD, kind=F32),
        shape(TEAM, half, width),
        shape(3, half, width),
        shape(2, half, width),
        shape(2, half, width),
        shape(half, width),
    ]
    used = arrays + scratch + [a for a, place in shapes if place is VMEM]
    size = sum(a.size * a.dtype.itemsize for a in used)
    forwards = 8 * ((highs - 1) + highs + 2 * highs)
    sems = [
        (8, 2), (8, 2), (forwards,), (highs, 2, 2, 8), (chips,), (chips,), (2,), (5,), (4,), (3,), (4,),
        (STEPS, 6), (STEPS, 5), (STEPS, 3), (STEPS, 4), (14,),
    ]
    return pl.pallas_call(
        forward_kernel,
        out_shape=[a for a, _ in shapes],
        in_specs=[VMEM] * len(arrays),
        out_specs=[place for _, place in shapes],
        scratch_shapes=[pltpu.VMEM(a.shape, a.dtype) for a in scratch]
        + [DMA(n) for n in sems]
        + state_pass_scratch(highs),
        compiler_params=pltpu.CompilerParams(
            collective_id=0, has_side_effects=True, vmem_limit_bytes=min(size + (14 << 20), 62 << 20)
        ),
        name="forward",
    )(*arrays)


STEPS = 4


CROSS = [(0, 1), (1, 0)]


TILE = 256


def turn_rows(me, source, target):
    zh, y, highs = lax.axis_index("zh"), lax.axis_index("y"), lax.axis_size("zh")
    chunks, _, width = source.shape
    owners = highs * 8
    rows = width // owners
    for n in range(chunks):
        turned = source[n].T
        for chip in range(owners):
            at_zh, zl, at_y, x = chip // 8, chip // 4 % 2, chip // 2 % 2, chip % 2
            x_place = me.c if x == 1 else 1 - me.c
            y_place = y if at_y == 1 else 1 - y
            place = ((x_place * 2 + y_place) * highs + lax.rem(at_zh - zh + highs, highs)) * 2 + zl
            at = pl.ds(pl.multiple_of(place * rows, rows), rows)
            target[at, n * CHUNK : (n + 1) * CHUNK] = turned[chip * rows : (chip + 1) * rows]


def feed_forward_kernel(
    hidden, cots, pair_w, down_w,
    forth, back, pair_away, pair_keep, down_part,
    forth_v, back_v, away_v, keep_v, pair_v, down_v, act, grad_gate, grad_up, left_hidden, left_cots, tiles, tiles_got, down_away, down_keep,
    loads, tile_send, tile_arrive, side_send, side_arrive, saves,
):
    me = Place()
    y = lax.axis_index("y")
    chunks, _, width = hidden.shape
    units = down_w.shape[1]
    tokens = chunks * CHUNK
    barrier = pltpu.get_barrier_semaphore()
    for to in ({"c": 1 - me.c}, {"y": 1 - y}):
        pl.semaphore_signal(barrier, inc=1, device_id=to, device_id_type=MESH)
    spans = [(n * TILE, min(TILE, units - n * TILE)) for n in range(-(-units // TILE))]

    def load(kind, n):
        start, size = spans[n]
        if kind == 2:
            return pltpu.make_async_copy(
                down_w.at[:, pl.ds(start, size)], down_v.at[:, pl.ds(start, size)], loads.at[2, n]
            )
        at = pl.ds(kind * units + start, size)
        return pltpu.make_async_copy(pair_w.at[:, at], pair_v.at[:, at], loads.at[kind, n])

    for n in range(len(spans)):
        for kind in range(3):
            load(kind, n).start()
    turn_rows(me, cots, left_cots)

    def units_step(start, size):
        at = pl.ds(start, size)
        rows = hidden[...].reshape(tokens, width)
        a = dot(rows, pair_v[:, at])
        b = dot(rows, pair_v[:, pl.ds(units + start, size)])
        da = dot(cots[...].reshape(tokens, width), down_v[:, at])
        sig = jax.nn.sigmoid(a)
        silu = a * sig
        act[:, at] = low(silu * b)
        grad_gate[:, at] = low(da * b * sig * (1.0 + a * (1.0 - sig)))
        grad_up[:, at] = low(da * silu)

    whole = units // TILE
    pl.semaphore_wait(barrier, 2)
    half = width // 2
    quarter = half // 2
    count = len(spans)

    def move(n):
        return copy_to(
            tiles.at[lax.rem(n, count)], tiles_got.at[n], tile_send.at[n], tile_arrive.at[n], {"c": 1 - me.c}
        )

    def send_tile(left, right, n, start, size):
        block = low(dot(left[pl.ds(0, half)], right[:, pl.ds(start, size)]))
        if size == TILE:
            tiles[lax.rem(n, count)] = block
        else:
            tiles[lax.rem(n, count), :, pl.ds(0, size)] = block
        move(n).start()

    def add_tile(left, right, n, start, size, away, keep, base):
        block = dot(left[pl.ds(half, half)], right[:, pl.ds(start, size)])
        move(n).wait_recv()
        block = low(block + tiles_got[n, :, pl.ds(0, size)].astype(F32))
        away[:, pl.ds(base + start, size)] = block[:quarter]
        keep[:, pl.ds(base + start, size)] = block[quarter:]

    def weight_grad(part, left, right, away, keep, base):
        first = part * count

        def send_step(n, _):
            if part:
                move(first + n - count).wait_send()
            send_tile(left, right, first + n, pl.multiple_of(n * TILE, TILE), TILE)
            return 0

        def add_step(n, _):
            add_tile(left, right, first + n, pl.multiple_of(n * TILE, TILE), TILE, away, keep, base)
            return 0

        lax.fori_loop(0, whole, send_step, 0)
        if whole < count:
            if part:
                move(first + whole - count).wait_send()
            send_tile(left, right, first + whole, *spans[whole])
        lax.fori_loop(0, whole, add_step, 0)
        if whole < count:
            add_tile(left, right, first + whole, *spans[whole], away, keep, base)

    def side_move(n, start, size):
        at = pl.ds(start, size)
        return copy_to(down_away.at[:, at], down_part.at[:, at], side_send.at[n], side_arrive.at[n], {"y": 1 - y})

    def down_tile(n, start, size):
        add_tile(left_cots, act, n, start, size, down_away, down_keep, 0)
        side_move(n, start, size).start()

    def tile_step(n, _):
        for kind in range(3):
            start = n * TILE if kind == 2 else kind * units + n * TILE
            at = pl.ds(pl.multiple_of(start, LANES), TILE)
            source, target = (down_w, down_v) if kind == 2 else (pair_w, pair_v)
            pltpu.make_async_copy(source.at[:, at], target.at[:, at], loads.at[kind, n]).wait()
        start = pl.multiple_of(n * TILE, TILE)
        units_step(start, TILE)
        send_tile(left_cots, act, n, start, TILE)

        @pl.when(n > 0)
        def _():
            down_tile(n - 1, pl.multiple_of((n - 1) * TILE, TILE), TILE)

        return 0

    lax.fori_loop(0, whole, tile_step, 0)
    if whole < count:
        for kind in range(3):
            load(kind, whole).wait()
        units_step(*spans[whole])
        send_tile(left_cots, act, whole, *spans[whole])
    down_tile(whole - 1, *spans[whole - 1])
    if whole < count:
        down_tile(whole, *spans[whole])

    def back_step(n, _):
        at = pl.ds(pl.multiple_of(n * TILE, TILE), TILE)
        block = dot_last(grad_gate[...], pair_v[at, pl.ds(0, units)])
        block = low(block + dot_last(grad_up[...], pair_v[at, pl.ds(units, units)]))
        ahead = low(dot_last(act[...], down_v[at]))
        for k in range(chunks):
            back_v[k, :, at] = block[k * CHUNK : (k + 1) * CHUNK]
            forth_v[k, :, at] = ahead[k * CHUNK : (k + 1) * CHUNK]
        return 0

    lax.fori_loop(0, width // TILE, back_step, 0)
    saved = [
        pltpu.make_async_copy(source, target, saves.at[n])
        for n, (source, target) in enumerate(
            ((back_v, back), (forth_v, forth), (away_v, pair_away), (keep_v, pair_keep))
        )
    ]
    for copy in saved[:2]:
        copy.start()
    turn_rows(me, hidden, left_hidden)
    weight_grad(1, left_hidden, grad_gate, away_v, keep_v, 0)
    weight_grad(2, left_hidden, grad_up, away_v, keep_v, units)
    for copy in saved[2:]:
        copy.start()
    for n in range(2 * count, 3 * count):
        move(n).wait_send()
    for n, span in enumerate(spans):
        side_move(n, *span).wait()
    add_rows(down_part, down_keep, down_part)
    for copy in saved:
        copy.wait()


def feed_forward(hidden, cots, pair_w, down_w):
    chunks, _, width = hidden.shape
    units = down_w.shape[1]
    tokens, half = chunks * CHUNK, width // 2
    count = -(-units // TILE)

    def shape(*dims, kind=BF):
        return jax.ShapeDtypeStruct(dims, kind)

    shapes = [
        shape(*hidden.shape),
        shape(*hidden.shape),
        shape(half // 2, 2 * units),
        shape(half // 2, 2 * units),
        shape(half // 2, units),
    ]
    scratch = shapes[:4] + [
        shape(width, 2 * units),
        shape(width, units),
        shape(tokens, units),
        shape(tokens, units),
        shape(tokens, units),
        shape(width, tokens),
        shape(width, tokens),
        shape(count, half, TILE),
        shape(3 * count, half, TILE),
        shape(half // 2, units),
        shape(half // 2, units),
    ]
    size = sum(a.size * a.dtype.itemsize for a in [hidden, cots] + shapes[4:] + scratch)
    sems = [(3, count), (3 * count,), (3 * count,), (count,), (count,), (4,)]
    return pl.pallas_call(
        feed_forward_kernel,
        out_shape=shapes,
        in_specs=[VMEM, VMEM, ANY, ANY],
        out_specs=[ANY] * 4 + [VMEM],
        scratch_shapes=[pltpu.VMEM(a.shape, a.dtype) for a in scratch] + [DMA(n) for n in sems],
        compiler_params=pltpu.CompilerParams(
            collective_id=5, has_side_effects=True, vmem_limit_bytes=min(size + (10 << 20), 63 << 20)
        ),
        name="feed_forward",
    )(hidden, cots, pair_w, down_w)


def add_rows(out, *parts):
    def step(n, _):
        at = pl.ds(n * 16, 16)
        total = parts[0][at].astype(F32)
        for part in parts[1:]:
            total = total + part[at].astype(F32)
        out[at] = low(total)
        return 0

    lax.fori_loop(0, out.shape[0] // 16, step, 0)


def backward_kernel(*refs):
    (
        back, forth, cotangent, middle, gain, pair_away, pair_keep_far, downs, merge_far, gated, projected_far, mixed_far,
        cumulated_far, gate_far, befores_far, decay, low_rank, up_pad, head_gain, hidden, starts_row, starts_column,
        grad_middle, gain_grad, proj, ranks, heads, early, gate_sum, up_sum, down_sum, left_hidden,
        result, got, relayed, staged, line, got2, relayed2, staged2, line2, branch, left_branch, douts, tiles, tiles_got,
        pair_keep, merge_w, projected, mixed, cumulated, gate, befores, pair_side, gate_got, up_got, down_got, early_away, early_keep, up_grad, state,
        send, arrive, send2, arrive2, side_send, side_arrive, high_send, high_arrive, tile_send, tile_arrive,
        send3, arrive3, twin_send, twin_arrive, here, loads,
    ) = refs[:-STATE_REFS]
    me = Place()
    cot = me.half(cotangent)
    zh, y, highs = lax.axis_index("zh"), lax.axis_index("y"), lax.axis_size("zh")
    chunks, _, width = hidden.shape
    units = downs.shape[-1]
    first = ((zh * 2 + me.c) * 2 + y) * (chunks * CHUNK)
    greet_all(me)
    loaded = [
        pltpu.make_async_copy(source, target, loads.at[n])
        for n, (source, target) in enumerate(
            (
                (pair_keep_far, pair_keep), (merge_far, merge_w), (mixed_far, mixed), (projected_far, projected),
                (cumulated_far, cumulated), (befores_far, befores), (gate_far, gate),
            )
        )
    ]
    for copy in loaded:
        copy.start()

    def columns(ref, part):
        return ref.at[:, :, :, pl.ds((part - 1) * units, units)]

    def source(part):
        return downs if part == 0 else columns(pair_side, part)

    sides = [
        copy_to(columns(pair_away, p), columns(pair_side, p), side_send.at[p], side_arrive.at[p], {"y": 1 - y})
        for p in (1, 2)
    ]
    high_got, high_sum = (down_got, gate_got, up_got), (down_sum, gate_sum, up_sum)
    highs_moves = [
        [
            copy_to(
                source(p).at[k],
                high_got[p].at[k - 1],
                high_send.at[p, k],
                high_arrive.at[p, k],
                {"zh": lax.rem(zh + k, highs)},
            )
            for k in range(1, highs)
        ]
        for p in range(3)
    ]

    def high_start(part):
        if part:
            sides[part - 1].wait()
            mine, there = columns(pair_keep, part), columns(pair_side, part)
            for k in range(highs):
                for m in range(2):
                    add_rows(there.at[k, m], mine.at[k, m], there.at[k, m])
        for move in highs_moves[part]:
            move.start()

    def high_add(part):
        there, out = high_got[part], high_sum[part]
        for k in range(1, highs):
            wait_for(there.at[k - 1], high_arrive.at[part, k])
        for m in range(2):
            add_rows(out.at[m], source(part).at[0, m], *(there.at[k - 1, m] for k in range(1, highs)))

    for move in sides:
        move.start()
    high_start(0)

    steps = send.shape[0]
    rows = cotangent.shape[0] // 2 // steps

    def part(ref, k, n):
        return ref.at[k, pl.ds(n * rows, rows)]

    sums = [
        MemberSum(
            me,
            lambda k, n=n: part(back, k, n),
            lambda k, n=n: part(got, k, n),
            lambda k, n=n: part(relayed, k, n),
            lambda k, n=n: part(staged, k, n),
            send.at[n],
            arrive.at[n],
            two="zl",
        )
        for n in range(steps)
    ]
    spreads = [
        HalvesSpread(
            me,
            line.at[pl.ds(n * rows, rows)],
            lambda k, n=n: part(branch, k, n),
            send2.at[n],
            arrive2.at[n],
        )
        for n in range(steps)
    ]
    forth_sums = [
        MemberSum(
            me,
            lambda k, n=n: part(forth, k, n),
            lambda k, n=n: part(got2, k, n),
            lambda k, n=n: part(relayed2, k, n),
            lambda k, n=n: part(staged2, k, n),
            send3.at[n],
            arrive3.at[n],
        )
        for n in range(steps)
    ]

    def twin_copy(n):
        return copy_to(
            line2.at[pl.ds(n * rows, rows)],
            part(result, me.c, n),
            twin_send.at[n],
            twin_arrive.at[n],
            {"c": 1 - me.c},
        )

    def own_copy(n):
        return pltpu.make_async_copy(line2.at[pl.ds(n * rows, rows)], part(result, me.c, n), here.at[n])

    for transfer in sums:
        transfer.start()

    turn_rows(me, hidden, left_hidden)
    for transfer in sums:
        transfer.relay()
    for n in range(steps):
        at = pl.ds(n * rows, rows)
        mid = middle[at]
        scale = lax.rsqrt(jnp.mean(mid * mid, -1, keepdims=True) + EPSILON)
        normed = mid * scale
        total = sums[n].total()
        gsum = jnp.sum(total * normed, axis=0, keepdims=True)
        gain_grad[...] = gsum if n == 0 else gain_grad[...] + gsum
        scaled = total * gain[...]
        out = cot[at].astype(F32) + scale * (
            scaled - normed * jnp.mean(scaled * normed, -1, keepdims=True)
        )
        grad_middle[at] = out
        line[at] = low(out)
        spreads[n].start()
        if n:
            spreads[n - 1].relay()
        if n == 2:
            loaded[0].wait()
            high_start(1)
    spreads[steps - 1].relay()
    for transfer in spreads:
        transfer.wait()
    for transfer in forth_sums:
        transfer.start()

    for copy in loaded[1:]:
        copy.wait()
    heads[...] = jnp.zeros_like(heads)

    def head_step(n, _):
        grad = dot(branch[n], merge_w[...])
        out = mixed[n]
        scale = lax.rsqrt(jnp.mean(out * out, -1, keepdims=True) + HEAD_FLOOR)
        normed = out * scale
        u = projected[3, n]
        sig = jax.nn.sigmoid(u)
        dn = grad * (u * sig)
        proj[n, :, 3 * HD :] = low(grad * normed * head_gain[...] * sig * (1.0 + u * (1.0 - sig)))
        heads[17:18] = heads[17:18] + jnp.sum(dn * normed, axis=0, keepdims=True)
        scaled = dn * head_gain[...]
        douts[n] = low(scale * (scaled - normed * jnp.mean(scaled * normed, -1, keepdims=True)))
        return 0

    lax.fori_loop(0, chunks, head_step, 0)

    def masks(n):
        return keyed_mask(first + n * CHUNK, starts_row, starts_column)

    def query_rows(n, visible):
        return low(projected[0, n] * jnp.exp(cumulated[n]) * visible)

    state[...] = jnp.zeros_like(state)

    def local_step(i, _):
        n = chunks - 1 - i
        _, visible, keep, _ = masks(n)
        carry = keep * jnp.exp(cumulated[n, CHUNK - 1 :])
        state[...] = carry * state[...] + dot_rows(douts[n], query_rows(n, visible))
        return 0

    lax.fori_loop(0, chunks, local_step, 0)
    states = StatePass(True, state, decay, state, *refs[-STATE_REFS:])
    states.begin()

    turn_rows(me, branch, left_branch)
    half = width // 2
    quarter = half // 2

    def tile_move(n):
        return copy_to(tiles.at[n], tiles_got.at[n], tile_send.at[n], tile_arrive.at[n], {"c": 1 - me.c})

    def right_tile(kind, n):
        if kind == 0:
            return gated[...].reshape(chunks * CHUNK, HD)[:, n * TILE : (n + 1) * TILE]
        at = 3 * HD + n * TILE
        return proj[...].reshape(chunks * CHUNK, 4 * HD)[:, at : at + TILE]

    lefts = left_branch, left_hidden
    for kind in range(2):
        for n in range(HD // TILE):
            tile = kind * (HD // TILE) + n
            tiles[tile] = low(dot(lefts[kind][pl.ds(0, half)], right_tile(kind, n)))
            tile_move(tile).start()
    states.combine()
    high_start(2)
    for kind in range(2):
        for n in range(HD // TILE):
            tile = kind * (HD // TILE) + n
            block = dot(lefts[kind][pl.ds(half, half)], right_tile(kind, n))
            tile_move(tile).wait_recv()
            block = low(block + tiles_got[tile].astype(F32))
            at = slice(tile * TILE, (tile + 1) * TILE)
            early_away[:, at] = block[:quarter]
            early_keep[:, at] = block[quarter:]
    early_move = copy_to(early_away, early, side_send.at[0], side_arrive.at[0], {"y": 1 - y})
    early_move.start()
    states.spread()
    for transfer in forth_sums:
        transfer.relay()
    states.finish()

    upper = (
        lax.broadcasted_iota(jnp.int32, (CHUNK, CHUNK), 0)
        <= lax.broadcasted_iota(jnp.int32, (CHUNK, CHUNK), 1)
    ).astype(F32)
    up_grad[...] = jnp.zeros_like(up_grad)

    def chunk_step(i, _):
        n = chunks - 1 - i
        pair, visible, keep, last = masks(n)
        b = cumulated[n]
        mid, end = b[CHUNK // 2 - 1 : CHUNK // 2], b[CHUNK - 1 :]
        q, k, v = projected[0, n], projected[1, n], low(projected[2, n])
        do = douts[n]
        eq, ek, el = jnp.exp(b - mid), jnp.exp(mid - b), jnp.exp(end - b) * last
        qh, kh, kc = low(q * eq), low(k * ek), k * el
        scores = low(jnp.where(pair, dot_last(qh, kh), 0.0))
        gs = low(jnp.where(pair, dot_last(do, v), 0.0))
        ds = low(state[...])
        proj[n, :, 2 * HD : 3 * HD] = low(dot_rows(scores, do) + dot_last(low(kc), ds))
        dq = dot(gs, kh) * eq + dot(do, low(befores[n])) * (jnp.exp(b) * visible)
        gkc = dot(v, ds)
        dk = dot_rows(gs, qh) * ek + gkc * el
        proj[n, :, :HD] = low(dq * HD ** (-0.5))
        proj[n, :, HD : 2 * HD] = low(dk)
        carry = keep * jnp.exp(end)
        extra = jnp.sum(gkc * kc, axis=0, keepdims=True)
        extra = extra + carry * jnp.sum(befores[n] * state[...], axis=0, keepdims=True)
        dlog = extra + jnp.dot(
            upper, dq * q - dk * k, precision=lax.Precision.HIGHEST, preferred_element_type=F32
        )
        state[...] = carry * state[...] + dot_rows(do, query_rows(n, visible))
        da = dlog * jax.nn.sigmoid(-gate[n]) / 16.0
        heads[16:17] = heads[16:17] + jnp.sum(da, axis=0, keepdims=True)
        dar = low(da)
        up_grad[...] = up_grad[...] + dot_rows(low_rank[n], dar)
        ranks[n] = low(dot_last(dar, up_pad[...]))
        return 0

    lax.fori_loop(0, chunks, chunk_step, 0)
    heads[0:16] = up_grad[2:18]
    for n in range(steps):
        at = pl.ds(n * rows, rows)
        line2[at] = low(middle[at] + forth_sums[n].total())
        twin_copy(n).start()
        own_copy(n).start()
    early_move.wait()
    add_rows(early, early_keep, early)
    for p in range(3):
        high_add(p)
    for n in range(steps):
        twin_copy(n).wait()
        own_copy(n).wait()
    for transfer in forth_sums:
        transfer.wait_sent()
    for group in highs_moves:
        for move in group:
            move.wait_send()
    for transfer in sums:
        transfer.wait_sent()
    for tile in range(tiles.shape[0]):
        tile_move(tile).wait_send()
    states.wait_sent()


def backward(
    back, forth, cot, middle, gain, pair, downs, merge_w, gated, projected, mixed, cumulated, gate, befores, decay,
    low_rank, up_pad, head_gain, hidden, starts,
):
    highs, members, owner_rows, units = downs.shape
    rows, width = cot.shape[0] // 2, cot.shape[1]
    chunks = hidden.shape[0]

    def shape(*dims, kind=BF):
        return jax.ShapeDtypeStruct(dims, kind)

    arrays = [
        back, forth, cot, middle, gain, *pair, downs, merge_w, gated, projected, mixed, cumulated, gate, befores, decay,
        low_rank, up_pad, head_gain, hidden, *starts_arrays(starts),
    ]
    away = {5, 6, 8, 10, 11, 12, 13, 14}
    quarter = width // 4
    shapes = [
        shape(rows, width, kind=F32),
        shape(1, width, kind=F32),
        shape(chunks, CHUNK, 4 * HD),
        shape(chunks, CHUNK, LANES),
        shape(24, HD, kind=F32),
        shape(quarter, 2 * HD),
        shape(members, owner_rows, units),
        shape(members, owner_rows, units),
        shape(members, owner_rows, units),
        shape(width, chunks * CHUNK),
        shape(2, rows, width),
    ]
    tiles = 2 * HD // TILE
    scratch = [
        shape(2, rows, width),
        shape(1, rows, width),
        shape(1, rows, width),
        shape(rows, width),
        shape(2, rows, width),
        shape(1, rows, width),
        shape(1, rows, width),
        shape(rows, width),
        shape(TEAM, rows, width),
        shape(width, chunks * CHUNK),
        shape(chunks, CHUNK, HD),
        shape(tiles, width // 2, TILE),
        shape(tiles, width // 2, TILE),
        *(shape(*arrays[n].shape, kind=arrays[n].dtype) for n in (6, 8, 10, 11, 12, 13, 14)),
        shape(highs, members, owner_rows, 2 * units),
        shape(highs - 1, members, owner_rows, units),
        shape(highs - 1, members, owner_rows, units),
        shape(highs - 1, members, owner_rows, units),
        shape(quarter, 2 * HD),
        shape(quarter, 2 * HD),
        shape(RANKS, HD, kind=F32),
        shape(HD, HD, kind=F32),
    ]
    used = [a for n, a in enumerate(arrays) if n not in away] + shapes + scratch
    size = sum(a.size * a.dtype.itemsize for a in used)
    sems = [
        (STEPS, 3), (STEPS, 3), (STEPS, 5), (STEPS, 4), (3,), (3,), (3, highs), (3, highs), (tiles,), (tiles,),
        (STEPS, 3), (STEPS, 3), (STEPS,), (STEPS,), (STEPS,), (7,),
    ]
    return pl.pallas_call(
        backward_kernel,
        out_shape=shapes,
        in_specs=[ANY if n in away else VMEM for n in range(len(arrays))],
        out_specs=[VMEM] * len(shapes),
        scratch_shapes=[pltpu.VMEM(a.shape, a.dtype) for a in scratch]
        + [DMA(n) for n in sems]
        + state_pass_scratch(highs),
        compiler_params=pltpu.CompilerParams(
            collective_id=3, has_side_effects=True, vmem_limit_bytes=min(size + (14 << 20), 62 << 20)
        ),
        name="backward",
    )(*arrays)


def closing_kernel(*refs):
    (
        proj, ranks, mixer_far, left, tokens, grad_middle, gain, down, gain_two_grad, heads, early, ups, gates, downs,
        out, mixer_grad, merge_grad, pair_grad, down_grad, wide_out, heads_out, gains_out,
        mixer_w, partial, got, relayed, staged, line, tiles, tiles_got, late_away, late_keep, late_side,
        late_got, early_got, late_sum, early_sum, late_home, early_home, ups_home, gate_home, down_home,
        wide, wide_got, heads_got, heads_sum, wide_twin, gain_grad, rank_grad,
        send, arrive, twin_send, twin_arrive, here, tile_send, tile_arrive, side_send, side_arrive,
        high_send, high_arrive, home_send, home_arrive,
        wide_send, wide_arrive, heads_send, heads_arrive, near, out_send, out_arrive, gain_send, gain_arrive, loads,
    ) = refs
    me = Place()
    own = me.half(tokens)
    zh, y, highs = lax.axis_index("zh"), lax.axis_index("y"), lax.axis_size("zh")
    load = pltpu.make_async_copy(mixer_far, mixer_w, loads.at[0])
    load.start()
    greet_all(me)
    steps = send.shape[0]
    rows, width = tokens.shape[0] // 2 // steps, tokens.shape[1]
    chunks = proj.shape[0]
    twin = {"c": 1 - me.c}

    def high_copies(kind, source, target):
        return [
            copy_to(
                source.at[k],
                target.at[k - 1],
                high_send.at[kind, k],
                high_arrive.at[kind, k],
                {"zh": lax.rem(zh + k, highs)},
            )
            for k in range(1, highs)
        ]

    def side_copy(kind, source, target):
        return copy_to(source, target, side_send.at[kind], side_arrive.at[kind], {"y": 1 - y})

    def home(kind, source, target):
        return Transfer(
            route_weights_home(me),
            lambda k: source.at[k],
            lambda k: target.at[k],
            home_send.at[kind],
            home_arrive.at[kind],
        )

    late_moves = [side_copy(j, late_away.at[j], late_side.at[j]) for j in range(3)]
    high_moves = [high_copies(j, late_side.at[j], late_got.at[j]) for j in range(3)]
    high_moves += [high_copies(3, early, early_got)]
    homes = [home(j, late_sum.at[j], late_home.at[j]) for j in range(3)]
    homes += [home(3, early_sum, early_home), home(4, ups, ups_home)]
    homes += [home(5, gates, gate_home), home(6, downs, down_home)]
    group_out, group_arrive = [], []
    for n in range(highs):
        for f in range(4):
            to_zh, to_y, to_c = lax.rem(zh + n, highs), flip(y, f & 2), flip(me.c, f & 1)
            to = {"zh": to_zh, "y": to_y, "c": to_c}
            group_out.append((0, (zh * 2 + y) * 2 + me.c, to, n + f == 0))
            group_arrive.append(((to_zh * 2 + to_y) * 2 + to_c, n + f == 0))
    heads_move = Transfer(
        (group_out, group_arrive), lambda _: heads, lambda k: heads_got.at[k], heads_send, heads_arrive
    )
    heads_move.start()

    for move in high_moves[3]:
        move.start()

    half = width // 2
    quarter = half // 2
    owner_rows = early.shape[2]

    def tile_move(n):
        return copy_to(tiles.at[n], tiles_got.at[n], tile_send.at[n], tile_arrive.at[n], twin)

    def right_tile(n):
        return proj[:, :, pl.ds(pl.multiple_of(n * TILE, TILE), TILE)].reshape(chunks * CHUNK, TILE)

    def tile_step(n, _):
        tiles[n] = low(dot(left[pl.ds(0, half)], right_tile(n)))
        tile_move(n).start()
        return 0

    lax.fori_loop(0, 3 * HD // TILE, tile_step, 0)

    for n in range(chunks):
        partial[n, :, width:] = ranks[n]

    def hidden_step(n, _):
        at = pl.ds(pl.multiple_of(n * TILE, TILE), TILE)
        block = low(dot_last(proj[...].reshape(chunks * CHUNK, 4 * HD), mixer_w[at]))
        for k in range(chunks):
            partial[k, :, at] = block[k * CHUNK : (k + 1) * CHUNK]
        return 0

    load.wait()
    lax.fori_loop(0, width // TILE, hidden_step, 0)

    def part(ref, k, n):
        return ref.at[k, pl.ds(n * rows, rows)]

    sums = [
        OwnersSum(
            me,
            lambda k, n=n: part(partial, k, n),
            lambda k, n=n: part(got, k, n),
            lambda k, n=n: part(relayed, k, n),
            lambda k, n=n: part(staged, k, n),
            send.at[n],
            arrive.at[n],
        )
        for n in range(steps)
    ]
    for transfer in sums:
        transfer.start()

    for j in range(3):
        for i in range(HD // TILE):
            n = j * (HD // TILE) + i
            block = dot(left[pl.ds(half, half)], right_tile(n))
            tile_move(n).wait_recv()
            block = low(block + tiles_got[n].astype(F32))
            columns = slice(i * TILE, (i + 1) * TILE)
            for k in range(highs):
                for m in range(2):
                    at = (k * 2 + m) * owner_rows
                    late_away[j, k, m, :, columns] = block[at : at + owner_rows]
                    late_keep[j, k, m, :, columns] = block[quarter + at : quarter + at + owner_rows]
        late_moves[j].start()
    for n in (6, 5, 4):
        homes[n].start()

    def side_add(move, keep, there):
        move.wait()
        for k in range(highs):
            for m in range(2):
                add_rows(there.at[k, m], keep.at[k, m], there.at[k, m])

    for transfer in sums:
        transfer.relay()
    for j in range(3):
        side_add(late_moves[j], late_keep.at[j], late_side.at[j])
        for move in high_moves[j]:
            move.start()

    def twin_copy(n):
        return copy_to(
            line.at[pl.ds(n * rows, rows)], part(out, me.c, n), twin_send.at[n], twin_arrive.at[n], twin
        )

    def own_copy(n):
        return pltpu.make_async_copy(line.at[pl.ds(n * rows, rows)], part(out, me.c, n), here.at[n])

    for n in range(steps):
        at = pl.ds(n * rows, rows)
        x = own[at].astype(F32)
        scale = lax.rsqrt(jnp.mean(x * x, -1, keepdims=True) + EPSILON)
        normed = x * scale
        total = sums[n].total()
        rank = low(total[:, width:])
        total = total[:, :width] + dot(rank, down[...])
        gsum = jnp.sum(total * normed, axis=0, keepdims=True)
        hidden = low(normed * gain[...])
        rsum = dot_rows(rank, hidden)
        gain_grad[...] = gsum if n == 0 else gain_grad[...] + gsum
        rank_grad[...] = rsum if n == 0 else rank_grad[...] + rsum
        scaled = total * gain[...]
        line[at] = low(
            grad_middle[at]
            + scale * (scaled - normed * jnp.mean(scaled * normed, -1, keepdims=True))
        )
        twin_copy(n).start()
        own_copy(n).start()

    for n in range(wide.shape[0]):
        at = slice(n * owner_rows, (n + 1) * owner_rows)
        wide[n, 0:1] = gain_grad[:, at]
        wide[n, 1:2] = gain_two_grad[:, at]
        wide[n, 2:8] = jnp.zeros((6, owner_rows), F32)
        wide[n, 8:24] = rank_grad[:16, at]
    spreads = Transfer(
        route_all(me), lambda k: wide.at[k], lambda k: wide_got.at[k], wide_send, wide_arrive
    )
    spreads.start()
    def high_add(kind, source, target, total):
        for k in range(1, highs):
            wait_for(target.at[k - 1], high_arrive.at[kind, k])
        for m in range(2):
            add_rows(total.at[m], source.at[0, m], *(target.at[k - 1, m] for k in range(1, highs)))
        homes[kind].start()


    heads_move.wait()
    total = heads_got[0]
    for n in range(1, highs * 4):
        total = total + heads_got[n]
    heads_sum[...] = total
    tail = gains_out.shape[1]
    gains = Transfer(
        route_member(me),
        lambda _: heads_sum.at[pl.ds(heads_sum.shape[0] - tail, tail)],
        lambda k: gains_out.at[k],
        gain_send,
        gain_arrive,
    )
    gains.start()
    moves = [
        copy_to(
            heads_sum,
            heads_out.at[me.x],
            out_send.at[n],
            out_arrive.at[me.x],
            {"zl": flip(me.zl, fz), "x": flip(me.x, fx)},
        )
        for n, (fz, fx) in enumerate(FLIPS[:3])
    ]

    @pl.when(me.c == me.zl)
    def _():
        for move in moves:
            move.start()
        heads_out[me.x] = heads_sum[...]

    spreads.wait()
    total = wide_got[0]
    for n in range(1, wide.shape[0]):
        total = total + wide_got[n]
    wide_out[...] = total
    swap = copy_to(wide_out, wide_twin, near.at[0], near.at[1], twin)
    swap.start()

    units = gates.shape[-1]

    def spread_columns(source, target, cols):
        for k in range(2):
            target[:, k * cols : (k + 1) * cols] = source[k].astype(F32)

    def spread_rows(source, target, cols):
        for k in range(2):
            target[k * cols : (k + 1) * cols] = source[k, :, :cols].astype(F32).T

    homes[6].wait()
    spread_rows(down_home, down_grad, units)
    homes[5].wait()
    spread_columns(gate_home, pair_grad.at[0], units)
    homes[4].wait()
    spread_columns(ups_home, pair_grad.at[1], units)
    high_add(3, early, early_got, early_sum)
    for k in range(2):
        own_slot = (me.c == me.zl) & (me.x == k)
        unless(own_slot, lambda k=k: wait_for(heads_out.at[k], out_arrive.at[k]))

    @pl.when(me.c == me.zl)
    def _():
        for move in moves:
            move.wait_send()

    swap.wait()
    wide_out[...] = wide_out[...] + wide_twin[...]
    gains.wait()
    for j in range(3):
        high_add(j, late_side.at[j], late_got.at[j], late_sum.at[j])
    homes[3].wait()
    spread_rows(early_home, merge_grad, HD)
    for k in range(2):
        mixer_grad[3, :, k * HD : (k + 1) * HD] = early_home[k, :, HD:].astype(F32)
    for j in range(3):
        homes[j].wait()
        spread_columns(late_home.at[j], mixer_grad.at[j], HD)
    for transfer in sums:
        transfer.wait_sent()
    for n in range(steps):
        twin_copy(n).wait()
        own_copy(n).wait()
    for group in high_moves:
        for move in group:
            move.wait_send()

    def tile_sent(n, _):
        tile_move(n).wait_send()
        return 0

    lax.fori_loop(0, tiles.shape[0], tile_sent, 0)


def closing(proj, ranks, mixer_w, left, own, grad_middle, gain, down, gain_two_grad, heads, early, ups, gates, downs):
    rows, width = own.shape[0] // 2, own.shape[1]
    chunks = proj.shape[0]
    highs, _, owner_rows, _ = early.shape
    units = ups.shape[-1]
    chips = highs * 8
    arrays = [
        proj, ranks, mixer_w, left, own, grad_middle, gain, down, gain_two_grad, heads, early, ups, gates, downs,
    ]

    def shape(*dims, kind=BF):
        return jax.ShapeDtypeStruct(dims, kind)

    shapes = [
        shape(2, rows, width),
        shape(4, owner_rows, 2 * HD, kind=F32),
        shape(2 * HD, owner_rows, kind=F32),
        shape(2, owner_rows, 2 * units, kind=F32),
        shape(2 * units, owner_rows, kind=F32),
        shape(24, owner_rows, kind=F32),
        shape(2, *heads.shape, kind=F32),
        shape(TEAM, 8, heads.shape[1], kind=F32),
    ]
    tiles = 3 * HD // TILE
    late = (3, highs, 2, owner_rows, HD)
    scratch = [shape(*mixer_w.shape), shape(chunks, CHUNK, width + LANES)]
    scratch += [shape(n, rows, width + LANES) for n in (3, 2, 2)] + [shape(rows, width)]
    scratch += [shape(tiles, width // 2, TILE)] * 2 + [shape(*late)] * 3
    scratch += [
        shape(3, highs - 1, 2, owner_rows, HD),
        shape(highs - 1, 2, owner_rows, 2 * HD),
    ]
    sums = [shape(3, 2, owner_rows, HD), shape(2, owner_rows, 2 * HD)]
    scratch += sums + sums + [shape(2, owner_rows, units)] * 3
    scratch += [
        shape(chips, 24, owner_rows, kind=F32),
        shape(chips, 24, owner_rows, kind=F32),
        shape(highs * 4, *heads.shape, kind=F32),
        shape(*heads.shape, kind=F32),
        shape(24, owner_rows, kind=F32),
        shape(1, width, kind=F32),
        shape(LANES, width, kind=F32),
    ]
    size = sum(a.size * a.dtype.itemsize for a in arrays[:2] + arrays[3:] + shapes + scratch)
    sems = [
        (STEPS, 6), (STEPS, 5), (STEPS,), (STEPS,), (STEPS,), (tiles,), (tiles,), (3,), (3,), (4, highs), (4, highs),
        (7, 2), (7, 2), (chips,), (chips,), (highs * 4,), (highs * 4,), (2,), (3,), (2,), (TEAM,), (TEAM,), (1,),
    ]
    return pl.pallas_call(
        closing_kernel,
        out_shape=shapes,
        in_specs=[ANY if n == 2 else VMEM for n in range(len(arrays))],
        out_specs=[VMEM] * len(shapes),
        scratch_shapes=[pltpu.VMEM(a.shape, a.dtype) for a in scratch] + [DMA(n) for n in sems],
        compiler_params=pltpu.CompilerParams(
            collective_id=4, has_side_effects=True, vmem_limit_bytes=min(size + (10 << 20), 62 << 20)
        ),
        name="closing",
    )(*arrays)


def shards(
    tokens,
    cotangent,
    lengths,
    attn_gain,
    ffn_gain,
    mixer_in,
    decay_down,
    decay_up,
    decay_bias,
    head_gain,
    mixer_out,
    ffn_in,
    ffn_out,
):
    zh, zl, y, x, c = (lax.axis_index(a) for a in SEQ + ("c",))
    block, width = tokens.shape
    half = block // 2
    rows = mixer_in.shape[1]
    units = ffn_out.shape[0] // 2
    team_tokens = 2 * block
    rank = decay_down.shape[1]

    small = jnp.concatenate([attn_gain[None], ffn_gain[None], decay_down.T], axis=0)
    small = jnp.pad(small, ((0, RANKS - small.shape[0]), (0, 0)))
    up_head = lax.dynamic_slice_in_dim(decay_up, HD * x, HD, 1).astype(F32)
    bias_head = lax.dynamic_slice_in_dim(decay_bias, HD * x, HD, 0)
    ups = jnp.concatenate([up_head, bias_head[None], jnp.zeros((7, HD), F32)], axis=0)
    starts = jnp.cumsum(lengths) - lengths
    (
        mixer_w, merge_w, pair_w, down_w, gains, ffn_dy, hidden_one, low_rank, gate_input, cumulated, projected,
        mixed, gated, befores, decay, hidden_two, middle,
    ) = forward(
        mixer_in, mixer_out.T, ffn_in, ffn_out.T, small, ups, tokens, cotangent, starts, head_gain[None]
    )
    up_head = jnp.where(c == zl, up_head, lax.ppermute(up_head, "c", CROSS)).astype(BF)
    mixer_w, merge_w = mixer_w.reshape(width, 4 * HD), merge_w.reshape(width, HD)
    pair_w, down_w = pair_w.reshape(width, 2 * units), down_w.reshape(width, units)
    gain_one, gain_two, rank_down = gains[:1], gains[1:2], gains[2 : 2 + rank].astype(BF)
    forth, back, *pair_sides, down_part = feed_forward(hidden_two, ffn_dy, pair_w, down_w)
    highs = lax.axis_size("zh")
    pair_sides = [a.reshape(highs, 2, rows, 2 * units) for a in pair_sides]
    down_part = down_part.reshape(highs, 2, rows, units)
    pad_rank = ((0, LANES - rank), (0, 0))
    (
        grad_middle, grad_gain_two, grad_proj, grad_ranks, heads, early, gate_sum, up_sum, down_sum,
        left_hidden, result,
    ) = backward(
        back, forth, cotangent, middle, gain_two, pair_sides, down_part, merge_w, gated, projected, mixed, cumulated,
        gate_input, befores, decay, low_rank, jnp.pad(up_head, pad_rank), head_gain[None], hidden_one, starts,
    )
    early = early.reshape(highs, 2, rows, 2 * HD)
    grad_inputs, mixer_home, merge_home, pair_home, down_home, wide, heads, gains = closing(
        grad_proj, grad_ranks, mixer_w, left_hidden, tokens, grad_middle, gain_one, jnp.pad(rank_down, pad_rank),
        grad_gain_two, heads, early, up_sum, gate_sum, down_sum,
    )
    return (
        result.reshape(block, width),
        grad_inputs.reshape(block, width),
        wide[0],
        wide[1],
        mixer_home,
        wide[8 : 8 + rank].T,
        heads[:, :rank].transpose(1, 0, 2).reshape(rank, 2 * HD),
        heads[:, rank].reshape(2 * HD),
        jnp.sum(gains[:, rank + 1 - 16], axis=0),
        merge_home,
        pair_home,
        down_home,
    )


def solution(mesh):
    devices = mesh.devices
    inner = Mesh(devices.reshape(devices.shape[0] // 8, 2, 2, 2, devices.shape[1]), SEQ + ("c",))
    in_specs = (
        P(SEQ, None),
        P(SEQ, None),
        P(),
        P(SEQ),
        P(SEQ),
        P(None, SEQ, "c"),
        P(SEQ, None),
        P(None, "c"),
        P("c"),
        P(),
        P("c", SEQ),
        P(None, SEQ, "c"),
        P("c", SEQ),
    )
    out_specs = (
        P(SEQ, None),
        P(SEQ, None),
        P(SEQ),
        P(SEQ),
        P(None, SEQ, "c"),
        P(SEQ, None),
        P(None, "c"),
        P("c"),
        P(),
        P("c", SEQ),
        P(None, SEQ, "c"),
        P("c", SEQ),
    )
    return jax.shard_map(shards, mesh=inner, in_specs=in_specs, out_specs=out_specs, check_vma=False)
```

```python
import functools

import jax
import jax.numpy as jnp
from jax import lax
from jax.experimental import pallas as pl
from jax.experimental.pallas import tpu as pltpu
from jax.sharding import Mesh, PartitionSpec as P

HD = 512
CHUNK = 128
EPSILON = 1e-06
HEAD_FLOOR = 1.0
TEAM = 4

BF = jnp.bfloat16
F32 = jnp.float32
MESH = pl.DeviceIdType.MESH
ANY = pl.BlockSpec(memory_space=pl.ANY)
VMEM = pl.BlockSpec(memory_space=pltpu.VMEM)
DMA = pltpu.SemaphoreType.DMA

SEQ = ("zh", "zl", "y", "x")
FLIPS = ((1, 1), (0, 1), (1, 0), (0, 0))


def dot(a, b):
    return jnp.dot(a, b, preferred_element_type=F32)


def dot_rows(a, b):
    return lax.dot_general(a, b, (((0,), (0,)), ((), ())), preferred_element_type=F32)


def dot_last(a, b):
    return lax.dot_general(a, b, (((1,), (1,)), ((), ())), preferred_element_type=F32)


def low(v):
    return v.astype(BF)


def flip(index, by):
    return 1 - index if by else index


class Place:
    def __init__(self):
        self.zl, self.x, self.c = lax.axis_index("zl"), lax.axis_index("x"), lax.axis_index("c")
        self.member = self.zl * 2 + self.x

    def half(self, ref):
        rows = ref.shape[0] // 2
        return ref.at[pl.ds(pl.multiple_of(self.c * rows, rows), rows)]


def greet_team(me, more=0):
    barrier = pltpu.get_barrier_semaphore()
    for n in range(1, 8):
        to = {"zl": flip(me.zl, n & 1), "x": flip(me.x, n & 2), "c": flip(me.c, n & 4)}
        pl.semaphore_signal(barrier, inc=1, device_id=to, device_id_type=MESH)
    pl.semaphore_wait(barrier, 7 + more)


def others(me):
    zh, y, highs = lax.axis_index("zh"), lax.axis_index("y"), lax.axis_size("zh")
    for k in range(highs):
        for n in range(8):
            yield lax.rem(zh + k, highs), flip(me.zl, n & 1), flip(y, n & 2), flip(me.x, n & 4), k + n == 0


def greet_all(me):
    barrier = pltpu.get_barrier_semaphore()
    count = 0
    for zh, zl, y, x, own in others(me):
        for f in range(2):
            if own and not f:
                continue
            to = {"zh": zh, "zl": zl, "y": y, "x": x, "c": flip(me.c, f)}
            pl.semaphore_signal(barrier, inc=1, device_id=to, device_id_type=MESH)
            count += 1
    pl.semaphore_wait(barrier, count)


def route_member(me):
    out, arrive = [], []
    for fz, fx in FLIPS:
        zl, x = flip(me.zl, fz), flip(me.x, fx)
        own = (fz, fx) == (0, 0)
        out.append((zl * 2 + x, me.member, {"zl": zl, "x": x}, own))
        arrive.append((zl * 2 + x, own))
    return out, arrive


def chip_index(zh, zl, y, x):
    return ((zh * 2 + zl) * 2 + y) * 2 + x


def route_all(me):
    mine = chip_index(lax.axis_index("zh"), me.zl, lax.axis_index("y"), me.x)
    out, arrive = [], []
    for zh, zl, y, x, own in others(me):
        chip = chip_index(zh, zl, y, x)
        out.append((chip, mine, {"zh": zh, "zl": zl, "y": y, "x": x}, own))
        arrive.append((chip, own))
    return out, arrive


def route_halves(me):
    mine = me.c == me.zl
    out, arrive = [], []
    for fz, fx in FLIPS:
        zl, x = flip(me.zl, fz), flip(me.x, fx)
        own = mine if (fz, fx) == (0, 0) else False
        out.append((0, me.x * 2 + me.c, {"zl": zl, "x": x, "c": me.zl}, own))
    for fc, fx in FLIPS:
        c, x = flip(me.c, fc), flip(me.x, fx)
        own = mine if (fc, fx) == (0, 0) else False
        arrive.append((x * 2 + c, own))
    return out, arrive


def route_owners(me):
    mine = me.c == me.zl
    out, arrive = [], []
    for fc, fx in FLIPS:
        c, x = flip(me.c, fc), flip(me.x, fx)
        own = mine if (fc, fx) == (0, 0) else False
        out.append((x * 2 + c, me.member, {"zl": me.c, "x": x, "c": c}, own))
    for fz, fx in FLIPS:
        zl, x = flip(me.zl, fz), flip(me.x, fx)
        own = mine if (fz, fx) == (0, 0) else False
        arrive.append((zl * 2 + x, own))
    return out, arrive


def route_weights(me):
    mine = (me.c == me.zl) & (me.c == me.x)
    out, arrive = [], []
    for f in (1, 0):
        x = flip(me.x, f)
        own = (me.c == me.zl) & (me.c == x) & (me.x == me.c) if not f else False
        out.append((x, me.zl, {"zl": me.c, "x": x, "c": me.x}, own))
    for f in (1, 0):
        zl = flip(me.zl, f)
        own = mine if not f else False
        arrive.append((zl, own))
    return out, arrive


def route_weights_home(me):
    mine = (me.c == me.zl) & (me.c == me.x)
    out, arrive = [], []
    for f in (1, 0):
        zl = flip(me.zl, f)
        own = mine if not f else False
        out.append((zl, me.x, {"zl": zl, "x": me.c, "c": me.zl}, own))
    for f in (1, 0):
        x = flip(me.x, f)
        own = mine if not f else False
        arrive.append((x, own))
    return out, arrive


def when(condition, run):
    if condition is True:
        run()
    elif condition is not False:
        pl.when(condition)(run)


def unless(condition, run):
    if condition is False:
        run()
    elif condition is not True:
        pl.when(jnp.logical_not(condition))(run)


class Transfer:
    def __init__(self, route, source, target, send, arrive):
        self.route, self.source, self.target, self.send, self.arrive = route, source, target, send, arrive

    def _remote(self, n):
        index, slot, to, own = self.route[0][n]
        return pltpu.make_async_remote_copy(
            src_ref=self.source(index),
            dst_ref=self.target(slot),
            send_sem=self.send.at[n],
            recv_sem=self.arrive.at[slot],
            device_id=to,
            device_id_type=MESH,
        )

    def _local(self, n):
        index, slot, to, own = self.route[0][n]
        return pltpu.make_async_copy(self.source(index), self.target(slot), self.send.at[n])

    def start(self):
        for n, (_, _, _, own) in enumerate(self.route[0]):
            unless(own, lambda: self._remote(n).start())
            when(own, lambda: self._local(n).start())

    def wait_arrive(self):
        for slot, own in self.route[1]:
            ref = self.target(slot)

            def arrived():
                pltpu.make_async_copy(ref, ref, self.arrive.at[slot]).wait()

            unless(own, arrived)

    def wait_local(self):
        for n, (_, _, _, own) in enumerate(self.route[0]):
            when(own, lambda: self._local(n).wait())

    def wait_sent(self):
        for n, (_, _, _, own) in enumerate(self.route[0]):
            unless(own, lambda: self._remote(n).wait_send())

    def wait(self):
        self.wait_arrive()
        self.wait_local()
        self.wait_sent()


def copy_to(src, dst, send, arrive, to):
    return pltpu.make_async_remote_copy(
        src_ref=src, dst_ref=dst, send_sem=send, recv_sem=arrive, device_id=to, device_id_type=MESH
    )


def wait_for(ref, sem):
    pltpu.make_async_copy(ref, ref, sem).wait()


def member_slots(me, two):
    along = me.zl * 2 + 1 - me.x, {"x": 1 - me.x}
    over = (1 - me.zl) * 2 + me.x, {"zl": 1 - me.zl}
    one, double = (over, along) if two == "x" else (along, over)
    return one[0], double[0], (1 - me.zl) * 2 + 1 - me.x, one[1], double[1]


class MemberSpread:
    def __init__(self, me, source, target, send, arrive, two="x"):
        self.target, self.arrive = target, arrive
        mine = me.member
        one, double, across, to_one, to_double = member_slots(me, two)
        self.slots = one, double, across
        self.direct = [
            copy_to(source, target(mine), send.at[0], arrive.at[mine], to_one),
            copy_to(source, target(mine), send.at[1], arrive.at[mine], to_double),
        ]
        self.local = pltpu.make_async_copy(source, target(mine), arrive.at[mine])
        self.forward = copy_to(target(one), target(one), send.at[2], arrive.at[one], to_double)

    def start(self):
        for copy in self.direct:
            copy.start()
        self.local.start()

    def relay(self):
        wait_for(self.target(self.slots[0]), self.arrive.at[self.slots[0]])
        self.forward.start()

    def wait(self):
        for slot in self.slots[1:]:
            wait_for(self.target(slot), self.arrive.at[slot])
        self.local.wait()
        for copy in self.direct + [self.forward]:
            copy.wait_send()


class HalvesSpread:
    def __init__(self, me, source, target, send, arrive):
        self.me, self.target, self.arrive = me, target, arrive
        mine = me.x * 2 + me.c
        self.home = me.c == me.zl
        self.direct = [
            copy_to(source, target(mine), send.at[0], arrive.at[mine], {"zl": 1 - me.zl, "c": me.zl}),
            copy_to(source, target(mine), send.at[1], arrive.at[mine], {"x": 1 - me.x, "c": me.zl}),
        ]
        self.near = copy_to(source, target(mine), send.at[2], arrive.at[mine], {"c": 1 - me.c})
        self.local = pltpu.make_async_copy(source, target(mine), send.at[2])
        self.near_slots = [me.x * 2 + c for c in range(2)]
        self.far_slots = [(1 - me.x) * 2 + c for c in range(2)]
        self.forwards = [
            copy_to(target(slot), target(slot), send.at[3 + c], arrive.at[slot], {"x": 1 - me.x})
            for c, slot in enumerate(self.near_slots)
        ]

    def start(self):
        for copy in self.direct:
            copy.start()
        pl.when(self.home)(self.local.start)
        unless(self.home, self.near.start)

    def relay(self):
        @pl.when(jnp.logical_not(self.home))
        def _():
            for slot, forward in zip(self.near_slots, self.forwards):
                wait_for(self.target(slot), self.arrive.at[slot])
                forward.start()

    def wait(self):
        me = self.me

        @pl.when(self.home)
        def _():
            self.local.wait()
            slot = me.x * 2 + 1 - me.c
            wait_for(self.target(slot), self.arrive.at[slot])

        for slot in self.far_slots:
            wait_for(self.target(slot), self.arrive.at[slot])
        for copy in self.direct:
            copy.wait_send()

        @pl.when(jnp.logical_not(self.home))
        def _():
            self.near.wait_send()
            for forward in self.forwards:
                forward.wait_send()


class MemberSum:
    def __init__(self, me, source, got, relayed, staged, send, arrive, two="x"):
        self.me, self.source, self.got, self.relayed, self.staged = me, source, got, relayed, staged
        self.arrive = arrive
        self.one, double, across, to_one, to_double = member_slots(me, two)
        self.direct = [
            copy_to(source(across), relayed(0), send.at[0], arrive.at[0], to_double),
            copy_to(source(double), got(0), send.at[1], arrive.at[1], to_double),
        ]
        self.onward = copy_to(staged(0), got(1), send.at[2], arrive.at[2], to_one)

    def start(self):
        for copy in self.direct:
            copy.start()

    def relay(self):
        wait_for(self.relayed(0), self.arrive.at[0])
        own = self.source(self.one)[...].astype(F32)
        self.staged(0)[...] = low(own + self.relayed(0)[...].astype(F32))
        self.onward.start()

    def total(self):
        wait_for(self.got(0), self.arrive.at[1])
        wait_for(self.got(1), self.arrive.at[2])
        total = self.source(self.me.member)[...].astype(F32)
        return total + self.got(0)[...].astype(F32) + self.got(1)[...].astype(F32)

    def wait_sent(self):
        for copy in self.direct + [self.onward]:
            copy.wait_send()


class OwnersSum:
    def __init__(self, me, source, got, relayed, staged, send, arrive):
        self.me, self.source, self.got, self.relayed, self.staged = me, source, got, relayed, staged
        self.arrive = arrive
        self.home = me.c == me.zl
        mine, other = me.x * 2, (1 - me.x) * 2
        self.near = copy_to(source(mine + 1 - me.c), got(0), send.at[0], arrive.at[0], {"c": 1 - me.c})
        self.local = pltpu.make_async_copy(source(mine + me.c), got(0), send.at[1])
        self.across = [
            copy_to(source(other + c), got(1), send.at[2 + c], arrive.at[1], {"x": 1 - me.x, "c": c})
            for c in range(2)
        ]
        self.first = [
            copy_to(source(other + c), relayed(c), send.at[2 + c], arrive.at[3 + c], {"x": 1 - me.x})
            for c in range(2)
        ]
        self.onward = [
            copy_to(staged(c), got(2), send.at[4 + c], arrive.at[2], {"zl": me.c, "c": c})
            for c in range(2)
        ]

    def start(self):
        @pl.when(self.home)
        def _():
            for copy in self.across + [self.near, self.local]:
                copy.start()

        @pl.when(jnp.logical_not(self.home))
        def _():
            for copy in self.first:
                copy.start()

    def relay(self):
        @pl.when(jnp.logical_not(self.home))
        def _():
            for c in range(2):
                wait_for(self.relayed(c), self.arrive.at[3 + c])
                own = self.source(self.me.x * 2 + c)[...].astype(F32)
                self.staged(c)[...] = low(own + self.relayed(c)[...].astype(F32))
                self.onward[c].start()

    def total(self):
        pl.when(self.home)(self.local.wait)
        unless(self.home, lambda: wait_for(self.got(0), self.arrive.at[0]))
        wait_for(self.got(1), self.arrive.at[1])
        wait_for(self.got(2), self.arrive.at[2])
        return sum(self.got(k)[...].astype(F32) for k in range(3))

    def wait_sent(self):
        @pl.when(self.home)
        def _():
            for copy in self.across + [self.near]:
                copy.wait_send()

        @pl.when(jnp.logical_not(self.home))
        def _():
            for copy in self.first + self.onward:
                copy.wait_send()


class Placed(Transfer):
    def __init__(self, route, source, there, target, send, arrive):
        super().__init__(route, source, target, send, arrive)
        self.there = there

    def _remote(self, n):
        index, slot, to, own = self.route[0][n]
        return pltpu.make_async_remote_copy(
            src_ref=self.source(index),
            dst_ref=self.there(slot),
            send_sem=self.send.at[n],
            recv_sem=self.arrive.at[slot],
            device_id=to,
            device_id_type=MESH,
        )


LANES = 128
RANKS = 32


def keyed_mask(start, starts_row, starts_column):
    rows = lax.broadcasted_iota(jnp.int32, (CHUNK, CHUNK), 0)
    columns = lax.broadcasted_iota(jnp.int32, (CHUNK, CHUNK), 1)
    ids = jnp.sum((rows + start >= starts_row[0:1]).astype(F32), axis=1, keepdims=True)
    places = lax.broadcasted_iota(jnp.int32, starts_column.shape, 1)
    ids_row = jnp.sum((places + start >= starts_column[...]).astype(F32), axis=0, keepdims=True)
    before = jnp.sum((starts_row[0:1] < start).astype(F32), axis=1, keepdims=True)
    final = ids_row[:, CHUNK - 1 :]
    pair = (rows >= columns) & (ids == ids_row)
    visible = (ids == before).astype(F32)
    keep = (final == before).astype(F32)
    return pair, visible, keep, (ids == final).astype(F32)


class StatePass:
    def __init__(self, back, local, decay, out, rounded, got, got_decay, sums, sum_decays, stage, stage_decay,
                 entering, leave, enter, send, arrive, far_send, far_arrive, leave_send, leave_arrive):
        self.__dict__.update(locals())
        self.zh, c, y = lax.axis_index("zh"), lax.axis_index("c"), lax.axis_index("y")
        self.highs = lax.axis_size("zh")
        self.mine = c * 2 + y
        self.quarter = local.shape[0] // 4
        self.partners = []
        for fc, fy in ((1, 1), (0, 1), (1, 0)):
            to_c, to_y = flip(c, fc), flip(y, fy)
            self.partners.append((to_c * 2 + to_y, {"c": to_c, "y": to_y}))
        self.order = range(3, -1, -1) if back else range(4)
        self.moves, self.outs = [], []

    def begin(self):
        self.rounded[...] = low(self.local[...])
        for n, (index, to) in enumerate(self.partners):
            rows = self.rounded.at[pl.ds(index * self.quarter, self.quarter)]
            self.moves.append(copy_to(rows, self.got.at[self.mine], self.send.at[0, n], self.arrive.at[0, self.mine], to))
            self.moves.append(
                copy_to(self.decay, self.got_decay.at[self.mine], self.send.at[1, n], self.arrive.at[1, self.mine], to)
            )
        for move in self.moves:
            move.start()
        self.got[self.mine] = self.rounded[pl.ds(self.mine * self.quarter, self.quarter)]
        self.got_decay[self.mine] = self.decay[...]

    def needs(self, source, target):
        return (source > target) if self.back else (source < target)

    def far(self, n, to):
        zh = self.zh
        return (
            copy_to(self.stage, self.sums.at[zh], self.far_send.at[0, n], self.far_arrive.at[0, zh], {"zh": to}),
            copy_to(
                self.stage_decay, self.sum_decays.at[zh], self.far_send.at[1, n], self.far_arrive.at[1, zh], {"zh": to}
            ),
        )

    def combine(self):
        for index, _ in self.partners:
            wait_for(self.got.at[index], self.arrive.at[0, index])
            wait_for(self.got_decay.at[index], self.arrive.at[1, index])
        total, total_decay = None, None
        for k in self.order:
            piece, d = self.got[k].astype(F32), self.got_decay[k][:1]
            total = piece if total is None else d * total + piece
            total_decay = d if total_decay is None else total_decay * d
        self.stage[...] = low(total)
        self.stage_decay[...] = jnp.broadcast_to(total_decay, self.stage_decay.shape)
        for n in range(1, self.highs):
            to = lax.rem(self.zh + n, self.highs)

            @pl.when(self.needs(self.zh, to))
            def _(n=n, to=to):
                for move in self.far(n, to):
                    move.start()

    def spread(self):
        self.entering[...] = jnp.zeros_like(self.entering)
        for n in range(self.highs):
            k = self.highs - 1 - n if self.back else n

            @pl.when(self.needs(k, self.zh))
            def _(k=k):
                wait_for(self.sums.at[k], self.far_arrive.at[0, k])
                wait_for(self.sum_decays.at[k], self.far_arrive.at[1, k])
                self.entering[...] = self.sum_decays[k][:1] * self.entering[...] + self.sums[k].astype(F32)

        state = self.entering[...]
        for k in self.order:
            self.leave[k] = low(state)
            state = self.got_decay[k][:1] * state + self.got[k].astype(F32)
        for n, (index, to) in enumerate(self.partners):
            self.outs.append(
                copy_to(
                    self.leave.at[index], self.enter.at[self.mine], self.leave_send.at[n],
                    self.leave_arrive.at[self.mine], to,
                )
            )
        for move in self.outs:
            move.start()
        self.enter[self.mine] = self.leave[self.mine]

    def finish(self):
        for index, _ in self.partners:
            wait_for(self.enter.at[index], self.leave_arrive.at[index])
        for k in range(4):
            self.out[pl.ds(k * self.quarter, self.quarter)] = self.enter[k].astype(F32)

    def wait_sent(self):
        for move in self.moves + self.outs:
            move.wait_send()
        for n in range(1, self.highs):
            to = lax.rem(self.zh + n, self.highs)

            @pl.when(self.needs(self.zh, to))
            def _(n=n, to=to):
                for move in self.far(n, to):
                    move.wait_send()


def state_pass_scratch(highs):
    quarter = HD // 4
    return [
        pltpu.VMEM((HD, HD), BF),
        pltpu.VMEM((4, quarter, HD), BF),
        pltpu.VMEM((4, 8, HD), F32),
        pltpu.VMEM((highs, quarter, HD), BF),
        pltpu.VMEM((highs, 8, HD), F32),
        pltpu.VMEM((quarter, HD), BF),
        pltpu.VMEM((8, HD), F32),
        pltpu.VMEM((quarter, HD), F32),
        pltpu.VMEM((4, quarter, HD), BF),
        pltpu.VMEM((4, quarter, HD), BF),
        DMA((2, 3)),
        DMA((2, 4)),
        DMA((2, highs)),
        DMA((2, highs)),
        DMA((3,)),
        DMA((4,)),
    ]


STATE_REFS = 16


def forward_kernel(*refs):
    (
        mixer_in, mixer_out, ffn_in, ffn_out, small, ups, tokens, cotangent, starts_row, starts_column, head_gain,
        mixer_w, merge_w, pair_w, down_w, gains, cots, hidden_far, low_rank, gate_far, cumulated_far, projected, mixed_far,
        gated_far, befores_far, decay, second, middle_far,
        hidden, gate, cumulated, mixed, gated, befores, middle, mixer_v, merge_v, projected_v, updates, inputs, smalls, ups_got, state, partial, got, relayed, staged, line,
        own_send, own_arrive, far_send, arrive, small_send, small_arrive, ups_sem, inputs_send, inputs_arrive,
        cot_send, cot_arrive, sum_send, sum_arrive, spread_send, spread_arrive, saves,
    ) = refs[:-STATE_REFS]
    me = Place()
    own, cot = me.half(tokens), me.half(cotangent)
    zh, y, highs = lax.axis_index("zh"), lax.axis_index("y"), lax.axis_size("zh")
    units = down_w.shape[-1]
    width = tokens.shape[1]
    chunks = hidden.shape[0]
    first = ((zh * 2 + me.c) * 2 + y) * (chunks * CHUNK)
    greet_all(me)
    twin, side = {"c": 1 - me.c}, {"y": 1 - y}

    def own_source(part, k):
        if part < 5:
            at = pl.ds(pl.multiple_of(k * HD, HD), HD)
            return mixer_out.at[:, at] if part == 4 else mixer_in.at[part, :, at]
        at = pl.ds(pl.multiple_of(k * units, LANES), units)
        return ffn_out.at[:, at] if part == 7 else ffn_in.at[part - 5, :, at]

    def piece(at_zh, at_y, x, part, zl=slice(None)):
        if part < 4:
            return mixer_v.at[at_zh, zl, at_y, x, :, pl.ds(part * HD, HD)]
        if part == 4:
            return merge_v.at[at_zh, zl, at_y, x]
        if part < 7:
            return pair_w.at[at_zh, zl, at_y, x, :, pl.ds((part - 5) * units, units)]
        return down_w.at[at_zh, zl, at_y, x]

    firsts = [
        Placed(
            route_weights(me),
            lambda k, p=p: own_source(p, k),
            lambda zl, p=p: piece(zh, y, me.x, p, zl),
            lambda zl, p=p: piece(zh, y, me.c, p, zl),
            own_send.at[p],
            own_arrive.at[p],
        )
        for p in range(8)
    ]
    count = [0]
    sent = []

    def forward(at_zh, at_y, part, to, start=True):
        place = piece(at_zh, at_y, me.c, part)
        copy = copy_to(place, place, far_send.at[count[0]], arrive.at[at_zh, at_y, me.c, part], to)
        if start:
            copy.start()
        count[0] += 1
        sent.append(copy)
        return copy

    def arrived(at_zh, at_y, x, part):
        wait_for(piece(at_zh, at_y, x, part), arrive.at[at_zh, at_y, x, part])

    def own_high(part, start=True):
        firsts[part].wait_arrive()
        firsts[part].wait_local()
        return [forward(zh, y, part, {"zh": lax.rem(zh + k, highs)}, start) for k in range(1, highs)]

    def own_near(part):
        forward(zh, y, part, side)
        forward(zh, y, part, twin)

    def pass_high(part):
        for k in range(1, highs):
            at_zh = lax.rem(zh + k, highs)
            arrived(at_zh, y, me.c, part)
            forward(at_zh, y, part, side)
            forward(at_zh, y, part, twin)

    def pass_side(part):
        for k in range(highs):
            at_zh = lax.rem(zh + k, highs)
            arrived(at_zh, 1 - y, me.c, part)
            forward(at_zh, 1 - y, part, twin)

    def complete(part):
        for k in range(highs):
            at_zh = lax.rem(zh + k, highs)
            arrived(at_zh, y, 1 - me.c, part)
            arrived(at_zh, 1 - y, 1 - me.c, part)

    save_count = [0]
    saved = []

    def save(source, target):
        copy = pltpu.make_async_copy(source, target, saves.at[save_count[0]])
        copy.start()
        save_count[0] += 1
        saved.append(copy)

    order = (1, 2, 0, 3, 4)
    for part in order:
        firsts[part].start()
    move_small = Transfer(route_all(me), lambda _: small, lambda k: smalls.at[k], small_send, small_arrive)
    move_small.start()
    lend = copy_to(ups, ups_got, ups_sem.at[0], ups_sem.at[1], twin)
    lend.start()
    for part in order:
        own_high(part)
        if part in order[:2]:
            own_near(part)
    move_inputs = HalvesSpread(me, own, lambda k: inputs.at[k], inputs_send, inputs_arrive)
    move_cot = MemberSpread(me, cot, lambda k: cots.at[k], cot_send, cot_arrive)
    move_inputs.start()
    move_inputs.relay()
    pass_high(1)
    move_small.wait()
    lend.wait()
    owner_rows = smalls.shape[2]
    for n in range(smalls.shape[0]):
        gains[:, n * owner_rows : (n + 1) * owner_rows] = smalls[n].astype(F32)
    pass_high(2)
    for part in (5, 6, 7):
        firsts[part].start()
    for part in order[2:]:
        own_near(part)
    move_inputs.wait()

    up = jnp.where(me.c == me.zl, ups[...], ups_got[...])
    rank_up, bias = low(up[:16]), up[16:17]
    down = low(gains[...])
    lower = (
        lax.broadcasted_iota(jnp.int32, (CHUNK, CHUNK), 0)
        >= lax.broadcasted_iota(jnp.int32, (CHUNK, CHUNK), 1)
    ).astype(F32)

    def gates_step(n, _):
        x = inputs[n].astype(F32)
        scale = lax.rsqrt(jnp.mean(x * x, -1, keepdims=True) + EPSILON)
        h = low(x * scale * gains[0:1])
        hidden[n] = h
        z = low(dot_last(h, down))
        low_rank[n] = z
        a = dot(z[:, 2:18], rank_up) + bias
        gate[n] = a
        log_gate = (jnp.minimum(a, 0.0) - jnp.log1p(jnp.exp(-jnp.abs(a)))) / 16.0
        cumulated[n] = jnp.dot(
            lower, log_gate, precision=lax.Precision.HIGHEST, preferred_element_type=F32
        )
        return 0

    lax.fori_loop(0, chunks, gates_step, 0)
    save(hidden, hidden_far)
    save(gate, gate_far)
    save(cumulated, cumulated_far)

    def project(part):
        rows = hidden[...].reshape(chunks * CHUNK, width)
        block = mixer_v[:, :, :, :, :, pl.ds(part * HD, HD)].reshape(width, HD)
        result = dot(rows, block)
        if part == 0:
            result = result * HD ** (-0.5)
        projected_v[part] = result.reshape(chunks, CHUNK, HD)
        save(projected_v.at[part], projected.at[part])

    pass_side(1)
    pass_side(2)
    complete(1)
    project(1)
    complete(2)
    project(2)

    state[...] = jnp.zeros_like(state)
    decay[...] = jnp.ones_like(decay)

    def masks(n):
        return keyed_mask(first + n * CHUNK, starts_row, starts_column)

    def local_step(n, _):
        _, _, keep, last = masks(n)
        b = cumulated[n]
        end = b[CHUNK - 1 :]
        kc = low(projected_v[1, n] * jnp.exp(end - b) * last)
        update = dot_rows(low(projected_v[2, n]), kc)
        updates[n] = update
        carry = keep * jnp.exp(end)
        state[...] = carry * state[...] + update
        decay[...] = decay[...] * carry
        return 0

    lax.fori_loop(0, chunks, local_step, 0)
    states = StatePass(False, state, decay, state, *refs[-STATE_REFS:])
    states.begin()
    pass_high(0)
    states.combine()
    held = [own_high(part, False) for part in (5, 6, 7)]

    @pl.when(me.zl == 1)
    def _():
        for copy in sum(held, []):
            copy.start()

    pass_high(3)
    pass_side(0)
    complete(0)
    project(0)
    pass_side(3)

    def inner_step(n, _):
        pair, _, _, _ = masks(n)
        b = cumulated[n]
        mid = b[CHUNK // 2 - 1 : CHUNK // 2]
        qh = low(projected_v[0, n] * jnp.exp(b - mid))
        kh = low(projected_v[1, n] * jnp.exp(mid - b))
        scores = low(jnp.where(pair, dot_last(qh, kh), 0.0))
        mixed[n] = dot(scores, low(projected_v[2, n]))
        return 0

    lax.fori_loop(0, chunks, inner_step, 0)
    states.spread()

    @pl.when(me.zl == 0)
    def _():
        for copy in sum(held[:1], []):
            copy.start()

    pass_high(4)
    for part in (5, 6, 7):
        own_near(part)
    complete(3)
    project(3)
    states.finish()

    def outer_step(n, _):
        _, visible, keep, _ = masks(n)
        b = cumulated[n]
        before = state[...]
        qd = low(projected_v[0, n] * jnp.exp(b) * visible)
        out = mixed[n] + dot_last(qd, low(before))
        mixed[n] = out
        befores[n] = low(before)
        state[...] = keep * jnp.exp(b[CHUNK - 1 :]) * before + updates[n]
        scale = lax.rsqrt(jnp.mean(out * out, -1, keepdims=True) + HEAD_FLOOR)
        u = projected_v[3, n]
        gated[n] = low(out * scale * head_gain[...] * (u * jax.nn.sigmoid(u)))
        return 0

    lax.fori_loop(0, chunks, outer_step, 0)
    save(mixed, mixed_far)
    save(gated, gated_far)
    save(befores, befores_far)
    pass_side(4)
    complete(4)

    def merge_step(n, _):
        partial[n] = low(dot_last(gated[n], merge_v[...].reshape(width, HD)))
        return 0

    lax.fori_loop(0, chunks, merge_step, 0)

    steps = sum_send.shape[0]
    rows = tokens.shape[0] // 2 // steps

    def rows_of(ref, k, n):
        return ref.at[k, pl.ds(n * rows, rows)]

    sums = [
        OwnersSum(
            me,
            lambda k, n=n: rows_of(partial, k, n),
            lambda k, n=n: rows_of(got, k, n),
            lambda k, n=n: rows_of(relayed, k, n),
            lambda k, n=n: rows_of(staged, k, n),
            sum_send.at[n],
            sum_arrive.at[n],
        )
        for n in range(steps)
    ]
    spreads = [
        MemberSpread(
            me,
            line.at[pl.ds(n * rows, rows)],
            lambda k, n=n: rows_of(second, k, n),
            spread_send.at[n],
            spread_arrive.at[n],
        )
        for n in range(steps)
    ]
    for transfer in sums:
        transfer.start()
    for transfer in sums:
        transfer.relay()
    for n in range(steps):
        at = pl.ds(n * rows, rows)
        total = own[at].astype(F32) + sums[n].total()
        middle[at] = total
        scale = lax.rsqrt(jnp.mean(total * total, -1, keepdims=True) + EPSILON)
        line[at] = low(total * scale * gains[1:2])
        spreads[n].start()
        if n:
            spreads[n - 1].relay()
    spreads[steps - 1].relay()
    @pl.when(me.zl == 0)
    def _():
        for copy in sum(held[1:], []):
            copy.start()

    pass_high(5)
    pass_high(6)
    pass_side(5)
    move_cot.start()
    save(middle, middle_far)
    save(mixer_v, mixer_w)
    save(merge_v, merge_w)
    pass_high(7)
    move_cot.relay()
    for part in (6, 7):
        pass_side(part)
    for part in (5, 6, 7):
        complete(part)
    for transfer in sums:
        transfer.wait_sent()
    for transfer in spreads:
        transfer.wait()
    states.wait_sent()
    move_cot.wait()
    for transfer in firsts:
        transfer.wait_sent()
    for copy in sent:
        copy.wait_send()
    for copy in saved:
        copy.wait()


def starts_arrays(starts):
    starts = jnp.pad(starts, (0, LANES - starts.shape[0]), constant_values=jnp.int32(1 << 30))
    return jnp.broadcast_to(starts[None], (8, LANES)), jnp.broadcast_to(starts[:16, None], (16, LANES))


def forward(mixer_in, mixer_out, ffn_in, ffn_out, small, ups, tokens, cotangent, starts, head_gain):
    highs = lax.axis_size("zh")
    chips = highs * 8
    rows, half, width = small.shape[1], tokens.shape[0] // 2, tokens.shape[1]
    units = ffn_out.shape[1] // 2
    chunks = TEAM * half // CHUNK

    def shape(*dims, kind=BF):
        return jax.ShapeDtypeStruct(dims, kind)

    shapes = [
        (shape(highs, 2, 2, 2, rows, 4 * HD), ANY),
        (shape(highs, 2, 2, 2, rows, HD), ANY),
        (shape(highs, 2, 2, 2, rows, 2 * units), ANY),
        (shape(highs, 2, 2, 2, rows, units), ANY),
        (shape(RANKS, width, kind=F32), VMEM),
        (shape(TEAM, half, width), ANY),
        (shape(chunks, CHUNK, width), ANY),
        (shape(chunks, CHUNK, RANKS), VMEM),
        (shape(chunks, CHUNK, HD, kind=F32), ANY),
        (shape(chunks, CHUNK, HD, kind=F32), ANY),
        (shape(4, chunks, CHUNK, HD, kind=F32), ANY),
        (shape(chunks, CHUNK, HD, kind=F32), ANY),
        (shape(chunks, CHUNK, HD), ANY),
        (shape(chunks, HD, HD), ANY),
        (shape(8, HD, kind=F32), VMEM),
        (shape(TEAM, half, width), ANY),
        (shape(half, width, kind=F32), ANY),
    ]
    arrays = [mixer_in, mixer_out, ffn_in, ffn_out, small, ups, tokens, cotangent, *starts_arrays(starts), head_gain]
    scratch = [shapes[n][0] for n in (6, 8, 9, 11, 12, 13, 16)]
    scratch += [
        shapes[0][0],
        shapes[1][0],
        shapes[10][0],
        shape(chunks, HD, HD, kind=F32),
        shape(TEAM, half, width),
        shape(chips, RANKS, rows),
        shape(*ups.shape, kind=F32),
        shape(HD, HD, kind=F32),
        shape(TEAM, half, width),
        shape(3, half, width),
        shape(2, half, width),
        shape(2, half, width),
        shape(half, width),
    ]
    used = arrays + scratch + [a for a, place in shapes if place is VMEM]
    size = sum(a.size * a.dtype.itemsize for a in used)
    forwards = 8 * ((highs - 1) + highs + 2 * highs)
    sems = [
        (8, 2), (8, 2), (forwards,), (highs, 2, 2, 8), (chips,), (chips,), (2,), (5,), (4,), (3,), (4,),
        (STEPS, 6), (STEPS, 5), (STEPS, 3), (STEPS, 4), (14,),
    ]
    return pl.pallas_call(
        forward_kernel,
        out_shape=[a for a, _ in shapes],
        in_specs=[VMEM] * len(arrays),
        out_specs=[place for _, place in shapes],
        scratch_shapes=[pltpu.VMEM(a.shape, a.dtype) for a in scratch]
        + [DMA(n) for n in sems]
        + state_pass_scratch(highs),
        compiler_params=pltpu.CompilerParams(
            collective_id=0, has_side_effects=True, vmem_limit_bytes=min(size + (14 << 20), 62 << 20)
        ),
        name="forward",
    )(*arrays)


STEPS = 4


CROSS = [(0, 1), (1, 0)]


TILE = 256


def turn_rows(me, source, target):
    zh, y, highs = lax.axis_index("zh"), lax.axis_index("y"), lax.axis_size("zh")
    chunks, _, width = source.shape
    owners = highs * 8
    rows = width // owners
    for n in range(chunks):
        turned = source[n].T
        for chip in range(owners):
            at_zh, zl, at_y, x = chip // 8, chip // 4 % 2, chip // 2 % 2, chip % 2
            x_place = me.c if x == 1 else 1 - me.c
            y_place = y if at_y == 1 else 1 - y
            place = ((x_place * 2 + y_place) * highs + lax.rem(at_zh - zh + highs, highs)) * 2 + zl
            at = pl.ds(pl.multiple_of(place * rows, rows), rows)
            target[at, n * CHUNK : (n + 1) * CHUNK] = turned[chip * rows : (chip + 1) * rows]


def feed_forward_kernel(
    hidden, cots, pair_w, down_w,
    forth, back, pair_away, pair_keep, down_part,
    forth_v, back_v, away_v, keep_v, pair_v, down_v, act, grad_gate, grad_up, left_hidden, left_cots, tiles, tiles_got, down_away, down_keep,
    loads, tile_send, tile_arrive, side_send, side_arrive, saves,
):
    me = Place()
    y = lax.axis_index("y")
    chunks, _, width = hidden.shape
    units = down_w.shape[1]
    tokens = chunks * CHUNK
    barrier = pltpu.get_barrier_semaphore()
    for to in ({"c": 1 - me.c}, {"y": 1 - y}):
        pl.semaphore_signal(barrier, inc=1, device_id=to, device_id_type=MESH)
    spans = [(n * TILE, min(TILE, units - n * TILE)) for n in range(-(-units // TILE))]

    def load(kind, n):
        start, size = spans[n]
        if kind == 2:
            return pltpu.make_async_copy(
                down_w.at[:, pl.ds(start, size)], down_v.at[:, pl.ds(start, size)], loads.at[2, n]
            )
        at = pl.ds(kind * units + start, size)
        return pltpu.make_async_copy(pair_w.at[:, at], pair_v.at[:, at], loads.at[kind, n])

    for n in range(len(spans)):
        for kind in range(3):
            load(kind, n).start()
    turn_rows(me, cots, left_cots)

    def units_step(start, size):
        at = pl.ds(start, size)
        rows = hidden[...].reshape(tokens, width)
        a = dot(rows, pair_v[:, at])
        b = dot(rows, pair_v[:, pl.ds(units + start, size)])
        da = dot(cots[...].reshape(tokens, width), down_v[:, at])
        sig = jax.nn.sigmoid(a)
        silu = a * sig
        act[:, at] = low(silu * b)
        grad_gate[:, at] = low(da * b * sig * (1.0 + a * (1.0 - sig)))
        grad_up[:, at] = low(da * silu)

    whole = units // TILE
    pl.semaphore_wait(barrier, 2)
    half = width // 2
    quarter = half // 2
    count = len(spans)

    def move(n):
        return copy_to(
            tiles.at[lax.rem(n, count)], tiles_got.at[n], tile_send.at[n], tile_arrive.at[n], {"c": 1 - me.c}
        )

    def send_tile(left, right, n, start, size):
        block = low(dot(left[pl.ds(0, half)], right[:, pl.ds(start, size)]))
        if size == TILE:
            tiles[lax.rem(n, count)] = block
        else:
            tiles[lax.rem(n, count), :, pl.ds(0, size)] = block
        move(n).start()

    def add_tile(left, right, n, start, size, away, keep, base):
        block = dot(left[pl.ds(half, half)], right[:, pl.ds(start, size)])
        move(n).wait_recv()
        block = low(block + tiles_got[n, :, pl.ds(0, size)].astype(F32))
        away[:, pl.ds(base + start, size)] = block[:quarter]
        keep[:, pl.ds(base + start, size)] = block[quarter:]

    def weight_grad(part, left, right, away, keep, base):
        first = part * count

        def send_step(n, _):
            if part:
                move(first + n - count).wait_send()
            send_tile(left, right, first + n, pl.multiple_of(n * TILE, TILE), TILE)
            return 0

        def add_step(n, _):
            add_tile(left, right, first + n, pl.multiple_of(n * TILE, TILE), TILE, away, keep, base)
            return 0

        lax.fori_loop(0, whole, send_step, 0)
        if whole < count:
            if part:
                move(first + whole - count).wait_send()
            send_tile(left, right, first + whole, *spans[whole])
        lax.fori_loop(0, whole, add_step, 0)
        if whole < count:
            add_tile(left, right, first + whole, *spans[whole], away, keep, base)

    def side_move(n, start, size):
        at = pl.ds(start, size)
        return copy_to(down_away.at[:, at], down_part.at[:, at], side_send.at[n], side_arrive.at[n], {"y": 1 - y})

    def down_tile(n, start, size):
        add_tile(left_cots, act, n, start, size, down_away, down_keep, 0)
        side_move(n, start, size).start()

    def tile_step(n, _):
        for kind in range(3):
            start = n * TILE if kind == 2 else kind * units + n * TILE
            at = pl.ds(pl.multiple_of(start, LANES), TILE)
            source, target = (down_w, down_v) if kind == 2 else (pair_w, pair_v)
            pltpu.make_async_copy(source.at[:, at], target.at[:, at], loads.at[kind, n]).wait()
        start = pl.multiple_of(n * TILE, TILE)
        units_step(start, TILE)
        send_tile(left_cots, act, n, start, TILE)

        @pl.when(n > 0)
        def _():
            down_tile(n - 1, pl.multiple_of((n - 1) * TILE, TILE), TILE)

        return 0

    lax.fori_loop(0, whole, tile_step, 0)
    if whole < count:
        for kind in range(3):
            load(kind, whole).wait()
        units_step(*spans[whole])
        send_tile(left_cots, act, whole, *spans[whole])
    down_tile(whole - 1, *spans[whole - 1])
    if whole < count:
        down_tile(whole, *spans[whole])

    def back_step(n, _):
        at = pl.ds(pl.multiple_of(n * TILE, TILE), TILE)
        block = dot_last(grad_gate[...], pair_v[at, pl.ds(0, units)])
        block = low(block + dot_last(grad_up[...], pair_v[at, pl.ds(units, units)]))
        ahead = low(dot_last(act[...], down_v[at]))
        for k in range(chunks):
            back_v[k, :, at] = block[k * CHUNK : (k + 1) * CHUNK]
            forth_v[k, :, at] = ahead[k * CHUNK : (k + 1) * CHUNK]
        return 0

    lax.fori_loop(0, width // TILE, back_step, 0)
    saved = [
        pltpu.make_async_copy(source, target, saves.at[n])
        for n, (source, target) in enumerate(
            ((back_v, back), (forth_v, forth), (away_v, pair_away), (keep_v, pair_keep))
        )
    ]
    for copy in saved[:2]:
        copy.start()
    turn_rows(me, hidden, left_hidden)
    weight_grad(1, left_hidden, grad_gate, away_v, keep_v, 0)
    weight_grad(2, left_hidden, grad_up, away_v, keep_v, units)
    for copy in saved[2:]:
        copy.start()
    for n in range(2 * count, 3 * count):
        move(n).wait_send()
    for n, span in enumerate(spans):
        side_move(n, *span).wait()
    add_rows(down_part, down_keep, down_part)
    for copy in saved:
        copy.wait()


def feed_forward(hidden, cots, pair_w, down_w):
    chunks, _, width = hidden.shape
    units = down_w.shape[1]
    tokens, half = chunks * CHUNK, width // 2
    count = -(-units // TILE)

    def shape(*dims, kind=BF):
        return jax.ShapeDtypeStruct(dims, kind)

    shapes = [
        shape(*hidden.shape),
        shape(*hidden.shape),
        shape(half // 2, 2 * units),
        shape(half // 2, 2 * units),
        shape(half // 2, units),
    ]
    scratch = shapes[:4] + [
        shape(width, 2 * units),
        shape(width, units),
        shape(tokens, units),
        shape(tokens, units),
        shape(tokens, units),
        shape(width, tokens),
        shape(width, tokens),
        shape(count, half, TILE),
        shape(3 * count, half, TILE),
        shape(half // 2, units),
        shape(half // 2, units),
    ]
    size = sum(a.size * a.dtype.itemsize for a in [hidden, cots] + shapes[4:] + scratch)
    sems = [(3, count), (3 * count,), (3 * count,), (count,), (count,), (4,)]
    return pl.pallas_call(
        feed_forward_kernel,
        out_shape=shapes,
        in_specs=[VMEM, VMEM, ANY, ANY],
        out_specs=[ANY] * 4 + [VMEM],
        scratch_shapes=[pltpu.VMEM(a.shape, a.dtype) for a in scratch] + [DMA(n) for n in sems],
        compiler_params=pltpu.CompilerParams(
            collective_id=5, has_side_effects=True, vmem_limit_bytes=min(size + (10 << 20), 63 << 20)
        ),
        name="feed_forward",
    )(hidden, cots, pair_w, down_w)


def add_rows(out, *parts):
    def step(n, _):
        at = pl.ds(n * 16, 16)
        total = parts[0][at].astype(F32)
        for part in parts[1:]:
            total = total + part[at].astype(F32)
        out[at] = low(total)
        return 0

    lax.fori_loop(0, out.shape[0] // 16, step, 0)


def backward_kernel(*refs):
    (
        back, forth, cotangent, middle, gain, pair_away, pair_keep_far, downs, merge_far, gated, projected_far, mixed_far,
        cumulated_far, gate_far, befores_far, decay, low_rank, up_pad, head_gain, hidden, starts_row, starts_column,
        grad_middle, gain_grad, proj, ranks, heads, early, gate_sum, up_sum, down_sum, left_hidden,
        result, got, relayed, staged, line, got2, relayed2, staged2, line2, branch, left_branch, douts, tiles, tiles_got,
        pair_keep, merge_w, projected, mixed, cumulated, gate, befores, pair_side, gate_got, up_got, down_got, early_away, early_keep, up_grad, state,
        send, arrive, send2, arrive2, side_send, side_arrive, high_send, high_arrive, tile_send, tile_arrive,
        send3, arrive3, twin_send, twin_arrive, here, loads,
    ) = refs[:-STATE_REFS]
    me = Place()
    cot = me.half(cotangent)
    zh, y, highs = lax.axis_index("zh"), lax.axis_index("y"), lax.axis_size("zh")
    chunks, _, width = hidden.shape
    units = downs.shape[-1]
    first = ((zh * 2 + me.c) * 2 + y) * (chunks * CHUNK)
    greet_all(me)
    loaded = [
        pltpu.make_async_copy(source, target, loads.at[n])
        for n, (source, target) in enumerate(
            (
                (pair_keep_far, pair_keep), (merge_far, merge_w), (mixed_far, mixed), (projected_far, projected),
                (cumulated_far, cumulated), (befores_far, befores), (gate_far, gate),
            )
        )
    ]
    for copy in loaded:
        copy.start()

    def columns(ref, part):
        return ref.at[:, :, :, pl.ds((part - 1) * units, units)]

    def source(part):
        return downs if part == 0 else columns(pair_side, part)

    sides = [
        copy_to(columns(pair_away, p), columns(pair_side, p), side_send.at[p], side_arrive.at[p], {"y": 1 - y})
        for p in (1, 2)
    ]
    high_got, high_sum = (down_got, gate_got, up_got), (down_sum, gate_sum, up_sum)
    highs_moves = [
        [
            copy_to(
                source(p).at[k],
                high_got[p].at[k - 1],
                high_send.at[p, k],
                high_arrive.at[p, k],
                {"zh": lax.rem(zh + k, highs)},
            )
            for k in range(1, highs)
        ]
        for p in range(3)
    ]

    def high_start(part):
        if part:
            sides[part - 1].wait()
            mine, there = columns(pair_keep, part), columns(pair_side, part)
            for k in range(highs):
                for m in range(2):
                    add_rows(there.at[k, m], mine.at[k, m], there.at[k, m])
        for move in highs_moves[part]:
            move.start()

    def high_add(part):
        there, out = high_got[part], high_sum[part]
        for k in range(1, highs):
            wait_for(there.at[k - 1], high_arrive.at[part, k])
        for m in range(2):
            add_rows(out.at[m], source(part).at[0, m], *(there.at[k - 1, m] for k in range(1, highs)))

    for move in sides:
        move.start()
    high_start(0)

    steps = send.shape[0]
    rows = cotangent.shape[0] // 2 // steps

    def part(ref, k, n):
        return ref.at[k, pl.ds(n * rows, rows)]

    sums = [
        MemberSum(
            me,
            lambda k, n=n: part(back, k, n),
            lambda k, n=n: part(got, k, n),
            lambda k, n=n: part(relayed, k, n),
            lambda k, n=n: part(staged, k, n),
            send.at[n],
            arrive.at[n],
            two="zl",
        )
        for n in range(steps)
    ]
    spreads = [
        HalvesSpread(
            me,
            line.at[pl.ds(n * rows, rows)],
            lambda k, n=n: part(branch, k, n),
            send2.at[n],
            arrive2.at[n],
        )
        for n in range(steps)
    ]
    forth_sums = [
        MemberSum(
            me,
            lambda k, n=n: part(forth, k, n),
            lambda k, n=n: part(got2, k, n),
            lambda k, n=n: part(relayed2, k, n),
            lambda k, n=n: part(staged2, k, n),
            send3.at[n],
            arrive3.at[n],
        )
        for n in range(steps)
    ]

    def twin_copy(n):
        return copy_to(
            line2.at[pl.ds(n * rows, rows)],
            part(result, me.c, n),
            twin_send.at[n],
            twin_arrive.at[n],
            {"c": 1 - me.c},
        )

    def own_copy(n):
        return pltpu.make_async_copy(line2.at[pl.ds(n * rows, rows)], part(result, me.c, n), here.at[n])

    for transfer in sums:
        transfer.start()

    turn_rows(me, hidden, left_hidden)
    for transfer in sums:
        transfer.relay()
    for n in range(steps):
        at = pl.ds(n * rows, rows)
        mid = middle[at]
        scale = lax.rsqrt(jnp.mean(mid * mid, -1, keepdims=True) + EPSILON)
        normed = mid * scale
        total = sums[n].total()
        gsum = jnp.sum(total * normed, axis=0, keepdims=True)
        gain_grad[...] = gsum if n == 0 else gain_grad[...] + gsum
        scaled = total * gain[...]
        out = cot[at].astype(F32) + scale * (
            scaled - normed * jnp.mean(scaled * normed, -1, keepdims=True)
        )
        grad_middle[at] = out
        line[at] = low(out)
        spreads[n].start()
        if n:
            spreads[n - 1].relay()
        if n == 2:
            loaded[0].wait()
            high_start(1)
    spreads[steps - 1].relay()
    for transfer in spreads:
        transfer.wait()
    for transfer in forth_sums:
        transfer.start()

    for copy in loaded[1:]:
        copy.wait()
    heads[...] = jnp.zeros_like(heads)

    def head_step(n, _):
        grad = dot(branch[n], merge_w[...])
        out = mixed[n]
        scale = lax.rsqrt(jnp.mean(out * out, -1, keepdims=True) + HEAD_FLOOR)
        normed = out * scale
        u = projected[3, n]
        sig = jax.nn.sigmoid(u)
        dn = grad * (u * sig)
        proj[n, :, 3 * HD :] = low(grad * normed * head_gain[...] * sig * (1.0 + u * (1.0 - sig)))
        heads[17:18] = heads[17:18] + jnp.sum(dn * normed, axis=0, keepdims=True)
        scaled = dn * head_gain[...]
        douts[n] = low(scale * (scaled - normed * jnp.mean(scaled * normed, -1, keepdims=True)))
        return 0

    lax.fori_loop(0, chunks, head_step, 0)

    def masks(n):
        return keyed_mask(first + n * CHUNK, starts_row, starts_column)

    def query_rows(n, visible):
        return low(projected[0, n] * jnp.exp(cumulated[n]) * visible)

    state[...] = jnp.zeros_like(state)

    def local_step(i, _):
        n = chunks - 1 - i
        _, visible, keep, _ = masks(n)
        carry = keep * jnp.exp(cumulated[n, CHUNK - 1 :])
        state[...] = carry * state[...] + dot_rows(douts[n], query_rows(n, visible))
        return 0

    lax.fori_loop(0, chunks, local_step, 0)
    states = StatePass(True, state, decay, state, *refs[-STATE_REFS:])
    states.begin()

    turn_rows(me, branch, left_branch)
    half = width // 2
    quarter = half // 2

    def tile_move(n):
        return copy_to(tiles.at[n], tiles_got.at[n], tile_send.at[n], tile_arrive.at[n], {"c": 1 - me.c})

    def right_tile(kind, n):
        if kind == 0:
            return gated[...].reshape(chunks * CHUNK, HD)[:, n * TILE : (n + 1) * TILE]
        at = 3 * HD + n * TILE
        return proj[...].reshape(chunks * CHUNK, 4 * HD)[:, at : at + TILE]

    lefts = left_branch, left_hidden
    for kind in range(2):
        for n in range(HD // TILE):
            tile = kind * (HD // TILE) + n
            tiles[tile] = low(dot(lefts[kind][pl.ds(0, half)], right_tile(kind, n)))
            tile_move(tile).start()
    states.combine()
    high_start(2)
    for kind in range(2):
        for n in range(HD // TILE):
            tile = kind * (HD // TILE) + n
            block = dot(lefts[kind][pl.ds(half, half)], right_tile(kind, n))
            tile_move(tile).wait_recv()
            block = low(block + tiles_got[tile].astype(F32))
            at = slice(tile * TILE, (tile + 1) * TILE)
            early_away[:, at] = block[:quarter]
            early_keep[:, at] = block[quarter:]
    early_move = copy_to(early_away, early, side_send.at[0], side_arrive.at[0], {"y": 1 - y})
    early_move.start()
    states.spread()
    for transfer in forth_sums:
        transfer.relay()
    states.finish()

    upper = (
        lax.broadcasted_iota(jnp.int32, (CHUNK, CHUNK), 0)
        <= lax.broadcasted_iota(jnp.int32, (CHUNK, CHUNK), 1)
    ).astype(F32)
    up_grad[...] = jnp.zeros_like(up_grad)

    def chunk_step(i, _):
        n = chunks - 1 - i
        pair, visible, keep, last = masks(n)
        b = cumulated[n]
        mid, end = b[CHUNK // 2 - 1 : CHUNK // 2], b[CHUNK - 1 :]
        q, k, v = projected[0, n], projected[1, n], low(projected[2, n])
        do = douts[n]
        eq, ek, el = jnp.exp(b - mid), jnp.exp(mid - b), jnp.exp(end - b) * last
        qh, kh, kc = low(q * eq), low(k * ek), k * el
        scores = low(jnp.where(pair, dot_last(qh, kh), 0.0))
        gs = low(jnp.where(pair, dot_last(do, v), 0.0))
        ds = low(state[...])
        proj[n, :, 2 * HD : 3 * HD] = low(dot_rows(scores, do) + dot_last(low(kc), ds))
        dq = dot(gs, kh) * eq + dot(do, low(befores[n])) * (jnp.exp(b) * visible)
        gkc = dot(v, ds)
        dk = dot_rows(gs, qh) * ek + gkc * el
        proj[n, :, :HD] = low(dq * HD ** (-0.5))
        proj[n, :, HD : 2 * HD] = low(dk)
        carry = keep * jnp.exp(end)
        extra = jnp.sum(gkc * kc, axis=0, keepdims=True)
        extra = extra + carry * jnp.sum(befores[n] * state[...], axis=0, keepdims=True)
        dlog = extra + jnp.dot(
            upper, dq * q - dk * k, precision=lax.Precision.HIGHEST, preferred_element_type=F32
        )
        state[...] = carry * state[...] + dot_rows(do, query_rows(n, visible))
        da = dlog * jax.nn.sigmoid(-gate[n]) / 16.0
        heads[16:17] = heads[16:17] + jnp.sum(da, axis=0, keepdims=True)
        dar = low(da)
        up_grad[...] = up_grad[...] + dot_rows(low_rank[n], dar)
        ranks[n] = low(dot_last(dar, up_pad[...]))
        return 0

    lax.fori_loop(0, chunks, chunk_step, 0)
    heads[0:16] = up_grad[2:18]
    for n in range(steps):
        at = pl.ds(n * rows, rows)
        line2[at] = low(middle[at] + forth_sums[n].total())
        twin_copy(n).start()
        own_copy(n).start()
    early_move.wait()
    add_rows(early, early_keep, early)
    for p in range(3):
        high_add(p)
    for n in range(steps):
        twin_copy(n).wait()
        own_copy(n).wait()
    for transfer in forth_sums:
        transfer.wait_sent()
    for group in highs_moves:
        for move in group:
            move.wait_send()
    for transfer in sums:
        transfer.wait_sent()
    for tile in range(tiles.shape[0]):
        tile_move(tile).wait_send()
    states.wait_sent()


def backward(
    back, forth, cot, middle, gain, pair, downs, merge_w, gated, projected, mixed, cumulated, gate, befores, decay,
    low_rank, up_pad, head_gain, hidden, starts,
):
    highs, members, owner_rows, units = downs.shape
    rows, width = cot.shape[0] // 2, cot.shape[1]
    chunks = hidden.shape[0]

    def shape(*dims, kind=BF):
        return jax.ShapeDtypeStruct(dims, kind)

    arrays = [
        back, forth, cot, middle, gain, *pair, downs, merge_w, gated, projected, mixed, cumulated, gate, befores, decay,
        low_rank, up_pad, head_gain, hidden, *starts_arrays(starts),
    ]
    away = {5, 6, 8, 10, 11, 12, 13, 14}
    quarter = width // 4
    shapes = [
        shape(rows, width, kind=F32),
        shape(1, width, kind=F32),
        shape(chunks, CHUNK, 4 * HD),
        shape(chunks, CHUNK, LANES),
        shape(24, HD, kind=F32),
        shape(quarter, 2 * HD),
        shape(members, owner_rows, units),
        shape(members, owner_rows, units),
        shape(members, owner_rows, units),
        shape(width, chunks * CHUNK),
        shape(2, rows, width),
    ]
    tiles = 2 * HD // TILE
    scratch = [
        shape(2, rows, width),
        shape(1, rows, width),
        shape(1, rows, width),
        shape(rows, width),
        shape(2, rows, width),
        shape(1, rows, width),
        shape(1, rows, width),
        shape(rows, width),
        shape(TEAM, rows, width),
        shape(width, chunks * CHUNK),
        shape(chunks, CHUNK, HD),
        shape(tiles, width // 2, TILE),
        shape(tiles, width // 2, TILE),
        *(shape(*arrays[n].shape, kind=arrays[n].dtype) for n in (6, 8, 10, 11, 12, 13, 14)),
        shape(highs, members, owner_rows, 2 * units),
        shape(highs - 1, members, owner_rows, units),
        shape(highs - 1, members, owner_rows, units),
        shape(highs - 1, members, owner_rows, units),
        shape(quarter, 2 * HD),
        shape(quarter, 2 * HD),
        shape(RANKS, HD, kind=F32),
        shape(HD, HD, kind=F32),
    ]
    used = [a for n, a in enumerate(arrays) if n not in away] + shapes + scratch
    size = sum(a.size * a.dtype.itemsize for a in used)
    sems = [
        (STEPS, 3), (STEPS, 3), (STEPS, 5), (STEPS, 4), (3,), (3,), (3, highs), (3, highs), (tiles,), (tiles,),
        (STEPS, 3), (STEPS, 3), (STEPS,), (STEPS,), (STEPS,), (7,),
    ]
    return pl.pallas_call(
        backward_kernel,
        out_shape=shapes,
        in_specs=[ANY if n in away else VMEM for n in range(len(arrays))],
        out_specs=[VMEM] * len(shapes),
        scratch_shapes=[pltpu.VMEM(a.shape, a.dtype) for a in scratch]
        + [DMA(n) for n in sems]
        + state_pass_scratch(highs),
        compiler_params=pltpu.CompilerParams(
            collective_id=3, has_side_effects=True, vmem_limit_bytes=min(size + (14 << 20), 62 << 20)
        ),
        name="backward",
    )(*arrays)


def closing_kernel(*refs):
    (
        proj, ranks, mixer_far, left, tokens, grad_middle, gain, down, gain_two_grad, heads, early, ups, gates, downs,
        out, mixer_grad, merge_grad, pair_grad, down_grad, wide_out, heads_out, gains_out,
        mixer_w, partial, got, relayed, staged, line, tiles, tiles_got, late_away, late_keep, late_side,
        late_got, early_got, late_sum, early_sum, late_home, early_home, ups_home, gate_home, down_home,
        wide, wide_got, heads_got, heads_sum, wide_twin, gain_grad, rank_grad,
        send, arrive, twin_send, twin_arrive, here, tile_send, tile_arrive, side_send, side_arrive,
        high_send, high_arrive, home_send, home_arrive,
        wide_send, wide_arrive, heads_send, heads_arrive, near, out_send, out_arrive, gain_send, gain_arrive, loads,
    ) = refs
    me = Place()
    own = me.half(tokens)
    zh, y, highs = lax.axis_index("zh"), lax.axis_index("y"), lax.axis_size("zh")
    load = pltpu.make_async_copy(mixer_far, mixer_w, loads.at[0])
    load.start()
    greet_all(me)
    steps = send.shape[0]
    rows, width = tokens.shape[0] // 2 // steps, tokens.shape[1]
    chunks = proj.shape[0]
    twin = {"c": 1 - me.c}

    def high_copies(kind, source, target):
        return [
            copy_to(
                source.at[k],
                target.at[k - 1],
                high_send.at[kind, k],
                high_arrive.at[kind, k],
                {"zh": lax.rem(zh + k, highs)},
            )
            for k in range(1, highs)
        ]

    def side_copy(kind, source, target):
        return copy_to(source, target, side_send.at[kind], side_arrive.at[kind], {"y": 1 - y})

    def home(kind, source, target):
        return Transfer(
            route_weights_home(me),
            lambda k: source.at[k],
            lambda k: target.at[k],
            home_send.at[kind],
            home_arrive.at[kind],
        )

    late_moves = [side_copy(j, late_away.at[j], late_side.at[j]) for j in range(3)]
    high_moves = [high_copies(j, late_side.at[j], late_got.at[j]) for j in range(3)]
    high_moves += [high_copies(3, early, early_got)]
    homes = [home(j, late_sum.at[j], late_home.at[j]) for j in range(3)]
    homes += [home(3, early_sum, early_home), home(4, ups, ups_home)]
    homes += [home(5, gates, gate_home), home(6, downs, down_home)]
    group_out, group_arrive = [], []
    for n in range(highs):
        for f in range(4):
            to_zh, to_y, to_c = lax.rem(zh + n, highs), flip(y, f & 2), flip(me.c, f & 1)
            to = {"zh": to_zh, "y": to_y, "c": to_c}
            group_out.append((0, (zh * 2 + y) * 2 + me.c, to, n + f == 0))
            group_arrive.append(((to_zh * 2 + to_y) * 2 + to_c, n + f == 0))
    heads_move = Transfer(
        (group_out, group_arrive), lambda _: heads, lambda k: heads_got.at[k], heads_send, heads_arrive
    )
    heads_move.start()

    for move in high_moves[3]:
        move.start()

    half = width // 2
    quarter = half // 2
    owner_rows = early.shape[2]

    def tile_move(n):
        return copy_to(tiles.at[n], tiles_got.at[n], tile_send.at[n], tile_arrive.at[n], twin)

    def right_tile(n):
        return proj[:, :, pl.ds(pl.multiple_of(n * TILE, TILE), TILE)].reshape(chunks * CHUNK, TILE)

    def tile_step(n, _):
        tiles[n] = low(dot(left[pl.ds(0, half)], right_tile(n)))
        tile_move(n).start()
        return 0

    lax.fori_loop(0, 3 * HD // TILE, tile_step, 0)

    for n in range(chunks):
        partial[n, :, width:] = ranks[n]

    def hidden_step(n, _):
        at = pl.ds(pl.multiple_of(n * TILE, TILE), TILE)
        block = low(dot_last(proj[...].reshape(chunks * CHUNK, 4 * HD), mixer_w[at]))
        for k in range(chunks):
            partial[k, :, at] = block[k * CHUNK : (k + 1) * CHUNK]
        return 0

    load.wait()
    lax.fori_loop(0, width // TILE, hidden_step, 0)

    def part(ref, k, n):
        return ref.at[k, pl.ds(n * rows, rows)]

    sums = [
        OwnersSum(
            me,
            lambda k, n=n: part(partial, k, n),
            lambda k, n=n: part(got, k, n),
            lambda k, n=n: part(relayed, k, n),
            lambda k, n=n: part(staged, k, n),
            send.at[n],
            arrive.at[n],
        )
        for n in range(steps)
    ]
    for transfer in sums:
        transfer.start()

    for j in range(3):
        for i in range(HD // TILE):
            n = j * (HD // TILE) + i
            block = dot(left[pl.ds(half, half)], right_tile(n))
            tile_move(n).wait_recv()
            block = low(block + tiles_got[n].astype(F32))
            columns = slice(i * TILE, (i + 1) * TILE)
            for k in range(highs):
                for m in range(2):
                    at = (k * 2 + m) * owner_rows
                    late_away[j, k, m, :, columns] = block[at : at + owner_rows]
                    late_keep[j, k, m, :, columns] = block[quarter + at : quarter + at + owner_rows]
        late_moves[j].start()
    for n in (6, 5, 4):
        homes[n].start()

    def side_add(move, keep, there):
        move.wait()
        for k in range(highs):
            for m in range(2):
                add_rows(there.at[k, m], keep.at[k, m], there.at[k, m])

    for transfer in sums:
        transfer.relay()
    for j in range(3):
        side_add(late_moves[j], late_keep.at[j], late_side.at[j])
        for move in high_moves[j]:
            move.start()

    def high_add(kind, source, target, total):
        for k in range(1, highs):
            wait_for(target.at[k - 1], high_arrive.at[kind, k])
        for m in range(2):
            add_rows(total.at[m], source.at[0, m], *(target.at[k - 1, m] for k in range(1, highs)))
        homes[kind].start()


    high_add(3, early, early_got, early_sum)
    for j in range(3):
        high_add(j, late_side.at[j], late_got.at[j], late_sum.at[j])

    def twin_copy(n):
        return copy_to(
            line.at[pl.ds(n * rows, rows)], part(out, me.c, n), twin_send.at[n], twin_arrive.at[n], twin
        )

    def own_copy(n):
        return pltpu.make_async_copy(line.at[pl.ds(n * rows, rows)], part(out, me.c, n), here.at[n])

    for n in range(steps):
        at = pl.ds(n * rows, rows)
        x = own[at].astype(F32)
        scale = lax.rsqrt(jnp.mean(x * x, -1, keepdims=True) + EPSILON)
        normed = x * scale
        total = sums[n].total()
        rank = low(total[:, width:])
        total = total[:, :width] + dot(rank, down[...])
        gsum = jnp.sum(total * normed, axis=0, keepdims=True)
        hidden = low(normed * gain[...])
        rsum = dot_rows(rank, hidden)
        gain_grad[...] = gsum if n == 0 else gain_grad[...] + gsum
        rank_grad[...] = rsum if n == 0 else rank_grad[...] + rsum
        scaled = total * gain[...]
        line[at] = low(
            grad_middle[at]
            + scale * (scaled - normed * jnp.mean(scaled * normed, -1, keepdims=True))
        )
        twin_copy(n).start()
        own_copy(n).start()

    for n in range(wide.shape[0]):
        at = slice(n * owner_rows, (n + 1) * owner_rows)
        wide[n, 0:1] = gain_grad[:, at]
        wide[n, 1:2] = gain_two_grad[:, at]
        wide[n, 2:8] = jnp.zeros((6, owner_rows), F32)
        wide[n, 8:24] = rank_grad[:16, at]
    spreads = Transfer(
        route_all(me), lambda k: wide.at[k], lambda k: wide_got.at[k], wide_send, wide_arrive
    )
    spreads.start()
    heads_move.wait()
    total = heads_got[0]
    for n in range(1, highs * 4):
        total = total + heads_got[n]
    heads_sum[...] = total
    tail = gains_out.shape[1]
    gains = Transfer(
        route_member(me),
        lambda _: heads_sum.at[pl.ds(heads_sum.shape[0] - tail, tail)],
        lambda k: gains_out.at[k],
        gain_send,
        gain_arrive,
    )
    gains.start()
    moves = [
        copy_to(
            heads_sum,
            heads_out.at[me.x],
            out_send.at[n],
            out_arrive.at[me.x],
            {"zl": flip(me.zl, fz), "x": flip(me.x, fx)},
        )
        for n, (fz, fx) in enumerate(FLIPS[:3])
    ]

    @pl.when(me.c == me.zl)
    def _():
        for move in moves:
            move.start()
        heads_out[me.x] = heads_sum[...]

    spreads.wait()
    total = wide_got[0]
    for n in range(1, wide.shape[0]):
        total = total + wide_got[n]
    wide_out[...] = total
    swap = copy_to(wide_out, wide_twin, near.at[0], near.at[1], twin)
    swap.start()

    units = gates.shape[-1]

    def spread_columns(source, target, cols):
        for k in range(2):
            target[:, k * cols : (k + 1) * cols] = source[k].astype(F32)

    def spread_rows(source, target, cols):
        for k in range(2):
            target[k * cols : (k + 1) * cols] = source[k, :, :cols].astype(F32).T

    homes[6].wait()
    spread_rows(down_home, down_grad, units)
    homes[5].wait()
    spread_columns(gate_home, pair_grad.at[0], units)
    homes[4].wait()
    spread_columns(ups_home, pair_grad.at[1], units)
    for k in range(2):
        own_slot = (me.c == me.zl) & (me.x == k)
        unless(own_slot, lambda k=k: wait_for(heads_out.at[k], out_arrive.at[k]))

    @pl.when(me.c == me.zl)
    def _():
        for move in moves:
            move.wait_send()

    swap.wait()
    wide_out[...] = wide_out[...] + wide_twin[...]
    gains.wait()
    homes[3].wait()
    spread_rows(early_home, merge_grad, HD)
    for k in range(2):
        mixer_grad[3, :, k * HD : (k + 1) * HD] = early_home[k, :, HD:].astype(F32)
    for j in range(3):
        homes[j].wait()
        spread_columns(late_home.at[j], mixer_grad.at[j], HD)
    for transfer in sums:
        transfer.wait_sent()
    for n in range(steps):
        twin_copy(n).wait()
        own_copy(n).wait()
    for group in high_moves:
        for move in group:
            move.wait_send()

    def tile_sent(n, _):
        tile_move(n).wait_send()
        return 0

    lax.fori_loop(0, tiles.shape[0], tile_sent, 0)


def closing(proj, ranks, mixer_w, left, own, grad_middle, gain, down, gain_two_grad, heads, early, ups, gates, downs):
    rows, width = own.shape[0] // 2, own.shape[1]
    chunks = proj.shape[0]
    highs, _, owner_rows, _ = early.shape
    units = ups.shape[-1]
    chips = highs * 8
    arrays = [
        proj, ranks, mixer_w, left, own, grad_middle, gain, down, gain_two_grad, heads, early, ups, gates, downs,
    ]

    def shape(*dims, kind=BF):
        return jax.ShapeDtypeStruct(dims, kind)

    shapes = [
        shape(2, rows, width),
        shape(4, owner_rows, 2 * HD, kind=F32),
        shape(2 * HD, owner_rows, kind=F32),
        shape(2, owner_rows, 2 * units, kind=F32),
        shape(2 * units, owner_rows, kind=F32),
        shape(24, owner_rows, kind=F32),
        shape(2, *heads.shape, kind=F32),
        shape(TEAM, 8, heads.shape[1], kind=F32),
    ]
    tiles = 3 * HD // TILE
    late = (3, highs, 2, owner_rows, HD)
    scratch = [shape(*mixer_w.shape), shape(chunks, CHUNK, width + LANES)]
    scratch += [shape(n, rows, width + LANES) for n in (3, 2, 2)] + [shape(rows, width)]
    scratch += [shape(tiles, width // 2, TILE)] * 2 + [shape(*late)] * 3
    scratch += [
        shape(3, highs - 1, 2, owner_rows, HD),
        shape(highs - 1, 2, owner_rows, 2 * HD),
    ]
    sums = [shape(3, 2, owner_rows, HD), shape(2, owner_rows, 2 * HD)]
    scratch += sums + sums + [shape(2, owner_rows, units)] * 3
    scratch += [
        shape(chips, 24, owner_rows, kind=F32),
        shape(chips, 24, owner_rows, kind=F32),
        shape(highs * 4, *heads.shape, kind=F32),
        shape(*heads.shape, kind=F32),
        shape(24, owner_rows, kind=F32),
        shape(1, width, kind=F32),
        shape(LANES, width, kind=F32),
    ]
    size = sum(a.size * a.dtype.itemsize for a in arrays[:2] + arrays[3:] + shapes + scratch)
    sems = [
        (STEPS, 6), (STEPS, 5), (STEPS,), (STEPS,), (STEPS,), (tiles,), (tiles,), (3,), (3,), (4, highs), (4, highs),
        (7, 2), (7, 2), (chips,), (chips,), (highs * 4,), (highs * 4,), (2,), (3,), (2,), (TEAM,), (TEAM,), (1,),
    ]
    return pl.pallas_call(
        closing_kernel,
        out_shape=shapes,
        in_specs=[ANY if n == 2 else VMEM for n in range(len(arrays))],
        out_specs=[VMEM] * len(shapes),
        scratch_shapes=[pltpu.VMEM(a.shape, a.dtype) for a in scratch] + [DMA(n) for n in sems],
        compiler_params=pltpu.CompilerParams(
            collective_id=4, has_side_effects=True, vmem_limit_bytes=min(size + (10 << 20), 62 << 20)
        ),
        name="closing",
    )(*arrays)


def shards(
    tokens,
    cotangent,
    lengths,
    attn_gain,
    ffn_gain,
    mixer_in,
    decay_down,
    decay_up,
    decay_bias,
    head_gain,
    mixer_out,
    ffn_in,
    ffn_out,
):
    zh, zl, y, x, c = (lax.axis_index(a) for a in SEQ + ("c",))
    block, width = tokens.shape
    half = block // 2
    rows = mixer_in.shape[1]
    units = ffn_out.shape[0] // 2
    team_tokens = 2 * block
    rank = decay_down.shape[1]

    small = jnp.concatenate([attn_gain[None], ffn_gain[None], decay_down.T], axis=0)
    small = jnp.pad(small, ((0, RANKS - small.shape[0]), (0, 0)))
    up_head = lax.dynamic_slice_in_dim(decay_up, HD * x, HD, 1).astype(F32)
    bias_head = lax.dynamic_slice_in_dim(decay_bias, HD * x, HD, 0)
    ups = jnp.concatenate([up_head, bias_head[None], jnp.zeros((7, HD), F32)], axis=0)
    starts = jnp.cumsum(lengths) - lengths
    (
        mixer_w, merge_w, pair_w, down_w, gains, ffn_dy, hidden_one, low_rank, gate_input, cumulated, projected,
        mixed, gated, befores, decay, hidden_two, middle,
    ) = forward(
        mixer_in, mixer_out.T, ffn_in, ffn_out.T, small, ups, tokens, cotangent, starts, head_gain[None]
    )
    up_head = jnp.where(c == zl, up_head, lax.ppermute(up_head, "c", CROSS)).astype(BF)
    mixer_w, merge_w = mixer_w.reshape(width, 4 * HD), merge_w.reshape(width, HD)
    pair_w, down_w = pair_w.reshape(width, 2 * units), down_w.reshape(width, units)
    gain_one, gain_two, rank_down = gains[:1], gains[1:2], gains[2 : 2 + rank].astype(BF)
    forth, back, *pair_sides, down_part = feed_forward(hidden_two, ffn_dy, pair_w, down_w)
    highs = lax.axis_size("zh")
    pair_sides = [a.reshape(highs, 2, rows, 2 * units) for a in pair_sides]
    down_part = down_part.reshape(highs, 2, rows, units)
    pad_rank = ((0, LANES - rank), (0, 0))
    (
        grad_middle, grad_gain_two, grad_proj, grad_ranks, heads, early, gate_sum, up_sum, down_sum,
        left_hidden, result,
    ) = backward(
        back, forth, cotangent, middle, gain_two, pair_sides, down_part, merge_w, gated, projected, mixed, cumulated,
        gate_input, befores, decay, low_rank, jnp.pad(up_head, pad_rank), head_gain[None], hidden_one, starts,
    )
    early = early.reshape(highs, 2, rows, 2 * HD)
    grad_inputs, mixer_home, merge_home, pair_home, down_home, wide, heads, gains = closing(
        grad_proj, grad_ranks, mixer_w, left_hidden, tokens, grad_middle, gain_one, jnp.pad(rank_down, pad_rank),
        grad_gain_two, heads, early, up_sum, gate_sum, down_sum,
    )
    return (
        result.reshape(block, width),
        grad_inputs.reshape(block, width),
        wide[0],
        wide[1],
        mixer_home,
        wide[8 : 8 + rank].T,
        heads[:, :rank].transpose(1, 0, 2).reshape(rank, 2 * HD),
        heads[:, rank].reshape(2 * HD),
        jnp.sum(gains[:, rank + 1 - 16], axis=0),
        merge_home,
        pair_home,
        down_home,
    )


def solution(mesh):
    devices = mesh.devices
    inner = Mesh(devices.reshape(devices.shape[0] // 8, 2, 2, 2, devices.shape[1]), SEQ + ("c",))
    in_specs = (
        P(SEQ, None),
        P(SEQ, None),
        P(),
        P(SEQ),
        P(SEQ),
        P(None, SEQ, "c"),
        P(SEQ, None),
        P(None, "c"),
        P("c"),
        P(),
        P("c", SEQ),
        P(None, SEQ, "c"),
        P("c", SEQ),
    )
    out_specs = (
        P(SEQ, None),
        P(SEQ, None),
        P(SEQ),
        P(SEQ),
        P(None, SEQ, "c"),
        P(SEQ, None),
        P(None, "c"),
        P("c"),
        P(),
        P("c", SEQ),
        P(None, SEQ, "c"),
        P("c", SEQ),
    )
    return jax.shard_map(shards, mesh=inner, in_specs=in_specs, out_specs=out_specs, check_vma=False)
```
